32 devices in a mesh: dp: 32 (over z, y, x, core).
Axes of the slice: x: 2, y: 2, z: 4, core: 2. Of those that a mesh axis runs over, the one named last changes fastest.
Arguments:
- images: bfloat16 [512, 14, 14, 384], P('dp'), may hold values from -6 to 6
- mix_weight: float32 [512], P('dp'), may hold values from 0.5 to 1
- partner: int32 [512], P('dp'), may hold values from 0 to 511, as said below
- keep_mask: int32 [512], P('dp'), may hold values 0 or 1
- cotangent: bfloat16 [512, 7, 7, 768], P('dp'), may hold values from -6 to 6
- weight_in: float32 [1536, 384], P('dp')
- weight_out: float32 [1536, 384], P('dp')
- weight_down: float32 [1536, 768], P('dp'), may hold values from -0.15625 to 0.15625
- small_params: float32 [23808], P('dp')
- first_in: float32 [1536, 384], P('dp'), may hold values from -0.0009765625 to 0.0009765625
- second_in: float32 [1536, 384], P('dp'), may hold values from 4.196208e-10 to 1.6784832e-09
- first_out: float32 [1536, 384], P('dp'), may hold values from -0.0009765625 to 0.0009765625
- second_out: float32 [1536, 384], P('dp'), may hold values from 4.196208e-10 to 1.6784832e-09
- first_down: float32 [1536, 768], P('dp'), may hold values from -0.0009765625 to 0.0009765625
- second_down: float32 [1536, 768], P('dp'), may hold values from 4.196208e-10 to 1.6784832e-09
- first_small: float32 [23808], P('dp'), may hold values from -0.0009765625 to 0.0009765625
- second_small: float32 [23808], P('dp'), may hold values from 4.196208e-10 to 1.6784832e-09
Outputs:
- output: bfloat16 [512, 7, 7, 768], P('dp')
- images_grad: float32 [512, 14, 14, 384], P('dp')
- grad_norm: float32 [], replicated
- new_first_in: float32 [1536, 384], P('dp')
- new_second_in: float32 [1536, 384], P('dp')
- new_weight_in: float32 [1536, 384], P('dp')
- new_first_out: float32 [1536, 384], P('dp')
- new_second_out: float32 [1536, 384], P('dp')
- new_weight_out: float32 [1536, 384], P('dp')
- new_first_down: float32 [1536, 768], P('dp')
- new_second_down: float32 [1536, 768], P('dp')
- new_weight_down: float32 [1536, 768], P('dp')
- new_first_small: float32 [23808], P('dp')
- new_second_small: float32 [23808], P('dp')
- new_small_params: float32 [23808], P('dp')
The draws below stay inside these ranges and needn't reach their ends.
Inputs may be any that keep to these rules, and one draw needn't show every extreme that they name: The partner of each image lies in the same aligned block of 16 images (one device's), and within each block the partners are a permutation of its images.
All inputs are finite; a program needn't handle non-finite values. No bound on the sum of `keep_mask` on one device may be relied on, other than what follows from the above.
Results may differ from the reference program's by a relative error of at most 0.0089.
Values may be sent and summed in bfloat16 or wider, within the bound.
No kernel may reach another device: no remote copies, remote signals or barrier semaphores. Data moves between devices by JAX's collectives and lax.ppermute only.
A program may use at most 192 MiB of HBM per device.

```python
import math
import jax
import jax.numpy as jnp
from jax import lax

D = 384
FF = 1536
IMG_DEV = 16
SIDE = 14
STEP = 10
HALF = 7
IMAGES = 512
SMALLN = 23808
PARAMS = 2383104


def rising_matrix(key, fan_in):
    row_frac = jnp.arange(FF, dtype=jnp.float32)[:, None] / FF
    noise_draw = jax.random.normal(key, (FF, D), jnp.float32)
    rise_scale = 0.6 + 1.2 * row_frac
    return noise_draw * rise_scale * fan_in ** (-0.5)


def draw_weight_in(key, part):
    key = jax.random.fold_in(key, 11)
    return rising_matrix(key, D)


def draw_weight_out(key, part):
    key = jax.random.fold_in(key, 17)
    return rising_matrix(key, FF)


def draw_small_params(key, part):
    key = jax.random.fold_in(key, 23)
    key_rough, key_level = jax.random.split(key)
    position = jnp.arange(SMALLN, dtype=jnp.int32)
    rough = jax.random.normal(key_rough, (SMALLN,), jnp.float32)
    low_end = 0.6
    rise_span = 1.2
    level_draw = jax.random.uniform(key_level, (SMALLN,), jnp.float32)
    kernel_end = 49 * D
    gain_one_at = 50 * D
    layer_at = 53 * D + FF
    gain_two_at = 54 * D + FF
    used_end = 58 * D + FF
    channel = ((position - gain_two_at) % D).astype(jnp.float32) / D
    gain_like = 0.7 + 0.6 * level_draw
    values = 0.3 * rough
    values = jnp.where(position < kernel_end, rough / 7.0, values)
    values = jnp.where((position >= gain_one_at) & (position < gain_one_at + D), gain_like, values)
    values = jnp.where((position >= layer_at) & (position < layer_at + D), gain_like, values)
    values = jnp.where((position >= gain_two_at) & (position < gain_two_at + D), (low_end + rise_span * channel) * (0.8 + 0.4 * level_draw), values)
    values = jnp.where(position >= used_end, 0.0, values)
    return values


def draw_partner(key, part):
    key = jax.random.fold_in(key, 5)
    blocks = IMAGES // IMG_DEV
    scores = jax.random.randint(key, (blocks, IMG_DEV), 0, 1 << 20) * IMG_DEV + jnp.arange(IMG_DEV, dtype=jnp.int32)[None, :]
    order_idx = jnp.argsort(scores, axis=1, stable=True).astype(jnp.int32)
    return (order_idx + IMG_DEV * jnp.arange(blocks, dtype=jnp.int32)[:, None]).reshape(IMAGES)


def set_ends(values, key, smallest, largest):
    place = [jax.random.randint(jax.random.fold_in(key, axis), (), 0, length) for axis, length in enumerate(values.shape)]
    widest = values.shape.index(max(values.shape))
    next_to = place[:widest] + [(place[widest] + 1) % values.shape[widest]] + place[widest + 1:]
    return values.at[tuple(place)].set(smallest).at[tuple(next_to)].set(largest)


def steps_of(rng, extent, cuts, smallest, high):
    loudness = 1.0
    for axis_at, parts in cuts:
        steps = jax.random.uniform(jax.random.fold_in(jax.random.fold_in(rng, 6), axis_at), (parts,), jnp.float32, smallest / len(cuts), high / len(cuts))
        loudness = loudness * jnp.repeat(jnp.exp(steps), extent[axis_at] // parts).reshape((-1,) + (1,) * (len(extent) - 1 - axis_at))
    return loudness


def bell_draw(rng, shape, spread, most, cuts=(), kind=jnp.bfloat16):
    factor_of = steps_of(rng, shape, cuts, -0.22, 0.18) if cuts else 1.0
    entries = jax.random.normal(rng, shape, jnp.float32) * spread * factor_of
    return jnp.minimum(jnp.maximum(entries, -most), most).astype(kind)


def setup_inputs(seed: int = 0) -> dict:
    key_of = jax.random.split(jax.random.key(seed), 18)
    images = bell_draw(key_of[0], (IMAGES, SIDE, SIDE, D), 1.0, 6.0, ((0, 32),))
    mix_weight = jnp.clip(0.5 + 0.5 * jax.random.uniform(key_of[1], (IMAGES,), jnp.float32) ** steps_of(key_of[1], (IMAGES,), ((0, 32),), -0.2, 0.2), 0.5, 1.0)
    partner = draw_partner(jax.random.fold_in(key_of[17], 71), 0)
    keep_mask = set_ends((jax.random.randint(key_of[3], (IMAGES,), 0, 5) < 4).astype(jnp.int32), jax.random.fold_in(key_of[3], 1), 0, 1)
    cotangent = bell_draw(key_of[4], (IMAGES, HALF, HALF, 2 * D), 1.0, 6.0, ((0, 32),))
    weight_in = draw_weight_in(jax.random.fold_in(key_of[17], 71), 0)
    weight_out = draw_weight_out(jax.random.fold_in(key_of[17], 71), 0)
    weight_down = bell_draw(key_of[7], (4 * D, 2 * D), (4 * D) ** -0.5, 0.15625, ((0, 32),), jnp.float32)
    small_params = draw_small_params(jax.random.fold_in(key_of[17], 71), 0)
    first_in = bell_draw(key_of[9], (FF, D), (0.11 * PARAMS ** -0.5), 0.0009765625, ((0, 32),), jnp.float32)
    second_in = jnp.clip(jnp.exp(math.log(1.678483241285278e-09) - 1.3862944 * jax.random.uniform(key_of[10], (FF, D), jnp.float32) ** steps_of(key_of[10], (FF, D), ((0, 32),), -0.2, 0.2)), 4.196208103213195e-10, 1.678483241285278e-09)
    first_out = bell_draw(key_of[11], (FF, D), (0.11 * PARAMS ** -0.5), 0.0009765625, ((0, 32),), jnp.float32)
    second_out = jnp.clip(jnp.exp(math.log(1.678483241285278e-09) - 1.3862944 * jax.random.uniform(key_of[12], (FF, D), jnp.float32) ** steps_of(key_of[12], (FF, D), ((0, 32),), -0.2, 0.2)), 4.196208103213195e-10, 1.678483241285278e-09)
    first_down = bell_draw(key_of[13], (4 * D, 2 * D), (0.11 * PARAMS ** -0.5), 0.0009765625, ((0, 32),), jnp.float32)
    second_down = jnp.clip(jnp.exp(math.log(1.678483241285278e-09) - 1.3862944 * jax.random.uniform(key_of[14], (4 * D, 2 * D), jnp.float32) ** steps_of(key_of[14], (4 * D, 2 * D), ((0, 32),), -0.2, 0.2)), 4.196208103213195e-10, 1.678483241285278e-09)
    first_small = bell_draw(key_of[15], (SMALLN,), (0.11 * PARAMS ** -0.5), 0.0009765625, ((0, 32),), jnp.float32)
    second_small = jnp.clip(jnp.exp(math.log(1.678483241285278e-09) - 1.3862944 * jax.random.uniform(key_of[16], (SMALLN,), jnp.float32) ** steps_of(key_of[16], (SMALLN,), ((0, 32),), -0.2, 0.2)), 4.196208103213195e-10, 1.678483241285278e-09)
    return {"images": images, "mix_weight": mix_weight, "partner": partner, "keep_mask": keep_mask, "cotangent": cotangent, "weight_in": weight_in, "weight_out": weight_out, "weight_down": weight_down, "small_params": small_params, "first_in": first_in, "second_in": second_in, "first_out": first_out, "second_out": second_out, "first_down": first_down, "second_down": second_down, "first_small": first_small, "second_small": second_small}


LN_EPS = 1e-06
DROP_RATE = 0.2
RATE_MATRIX = 0.05
RATE_VECTOR = 0.3
LAYER_DECAY = 0.8
BETA_ONE = 0.9
BETA_TWO = 0.999
ADAM_EPS = 1e-08
WEIGHT_DECAY = 0.05
CLIP_NORM = 1.0
PRECISE = lax.Precision.HIGHEST

@jax.custom_vjp
def low(v):
    return lax.optimization_barrier(v.astype(jnp.bfloat16)).astype(jnp.float32)

@jax.custom_vjp
def low_back(v):
    return v

def low_keep(v):
    return (low(v), None)

def low_pass(kept, grad):
    return (grad,)

def back_keep(v):
    return (v, None)

def back_low(kept, grad):
    return (low(grad),)
low.defvjp(low_keep, low_pass)
low_back.defvjp(back_keep, back_low)

def split_small(small_vec):
    sizes_list = [49 * D, D, D, D, FF, D, D, D, D, 2 * D]
    pieces = []
    begin_at = 0
    for length in sizes_list:
        pieces.append(small_vec[begin_at:begin_at + length])
        begin_at = begin_at + length
    pieces[0] = pieces[0].reshape(49, D)
    return pieces

def layer_norm(values, gain_vec, bias_vec):
    average = lax.optimization_barrier(jnp.mean(values, axis=-1, keepdims=True))
    centred = values - average
    variance = lax.optimization_barrier(jnp.mean(centred * centred, axis=-1, keepdims=True))
    return centred * lax.rsqrt(variance + LN_EPS) * gain_vec + bias_vec

def block_forward(images_blk, mix_blk, local_blk, scale_blk, weight_in, weight_out, weight_down, small_vec):
    depth_kernel, depth_bias, gain_one, bias_one, hidden_bias, out_bias, layer_scale, gain_two, bias_two, down_bias = split_small(small_vec)
    images_dev = images_blk.shape[0]
    mix_col = mix_blk[:, None, None, None]
    mixed_in = mix_col * images_blk + (1.0 - mix_col) * images_blk[local_blk]
    padded = jnp.pad(mixed_in, ((0, 0), (3, 3), (3, 3), (0, 0)))
    conv_out = jnp.zeros_like(mixed_in) + depth_bias
    for row_off in range(7):
        for col_off in range(7):
            conv_out = conv_out + padded[:, row_off:row_off + SIDE, col_off:col_off + SIDE, :] * depth_kernel[row_off * 7 + col_off]
    pixels = images_dev * SIDE * SIDE
    normed_one = low(layer_norm(conv_out, gain_one, bias_one)).reshape(pixels, D)
    hidden_pre = low_back(jnp.dot(normed_one, weight_in.T, precision=PRECISE, preferred_element_type=jnp.float32) + hidden_bias)
    hidden_act = low(jax.nn.gelu(hidden_pre, approximate=False))
    branch = low_back(jnp.dot(hidden_act, weight_out, precision=PRECISE, preferred_element_type=jnp.float32) + out_bias)
    residual = mixed_in + scale_blk[:, None, None, None] * layer_scale * branch.reshape(images_dev, SIDE, SIDE, D)
    normed_two = low(layer_norm(residual, gain_two, bias_two))
    patches = normed_two.reshape(images_dev, HALF, 2, HALF, 2, D).transpose(0, 1, 3, 5, 2, 4).reshape(images_dev * HALF * HALF, 4 * D)
    result = jnp.dot(patches, weight_down, precision=PRECISE, preferred_element_type=jnp.float32) + down_bias
    return result.reshape(images_dev, HALF, HALF, 2 * D)

def adamw_step(weight, first_mom, second, gradient, step_rate, decay_rate):
    first_mom = BETA_ONE * first_mom + (1.0 - BETA_ONE) * gradient
    second = BETA_TWO * second + (1.0 - BETA_TWO) * gradient * gradient
    first_hat = first_mom / (1.0 - BETA_ONE ** STEP)
    second_hat = second / (1.0 - BETA_TWO ** STEP)
    weight = weight - step_rate * (first_hat / (jnp.sqrt(second_hat) + ADAM_EPS) + decay_rate * weight)
    return (first_mom, second, weight)

def reference(images, mix_weight, partner, keep_mask, cotangent, weight_in, weight_out, weight_down, small_params, first_in, second_in, first_out, second_out, first_down, second_down, first_small, second_small):
    blocks = IMAGES // IMG_DEV
    local_partner = partner.reshape(blocks, IMG_DEV) - IMG_DEV * jnp.arange(blocks, dtype=jnp.int32)[:, None]
    keep_scale = keep_mask.astype(jnp.float32) / (1.0 - DROP_RATE)
    mix_blocks = mix_weight.reshape(blocks, IMG_DEV)
    scale_blocks = keep_scale.reshape(blocks, IMG_DEV)
    checked = jax.checkpoint(block_forward)

    def whole_layer(images_all, layer_in, layer_out, layer_down, small_vec):
        lowered = (low(layer_in), low(layer_out), low(layer_down), low(small_vec))

        def one_block(carried, block_item):
            return (carried, checked(block_item[0], block_item[1], block_item[2], block_item[3], *lowered))
        shaped = images_all.reshape(blocks, IMG_DEV, SIDE, SIDE, D)
        _, outputs = lax.scan(one_block, jnp.zeros((), jnp.float32), (shaped, mix_blocks, local_partner, scale_blocks))
        return outputs.reshape(IMAGES, HALF, HALF, 2 * D)
    result, pullback = jax.vjp(whole_layer, images.astype(jnp.float32), weight_in, weight_out, weight_down, small_params)
    images_grad, grad_in, grad_out, grad_down, grad_small = pullback(cotangent.astype(jnp.float32))
    squares_sum = jnp.sum(grad_in * grad_in) + jnp.sum(grad_out * grad_out) + jnp.sum(grad_down * grad_down) + jnp.sum(grad_small * grad_small)
    grad_norm = jnp.sqrt(squares_sum)
    factor = CLIP_NORM / jnp.maximum(grad_norm, CLIP_NORM)
    position = jnp.arange(SMALLN, dtype=jnp.int32)
    small_rate = jnp.where(position < 54 * D + FF, LAYER_DECAY * RATE_VECTOR, RATE_VECTOR)
    small_decay = jnp.where(position < 49 * D, WEIGHT_DECAY, 0.0)
    new_in = adamw_step(weight_in, first_in, second_in, grad_in * factor, LAYER_DECAY * RATE_MATRIX, WEIGHT_DECAY)
    new_out = adamw_step(weight_out, first_out, second_out, grad_out * factor, LAYER_DECAY * RATE_MATRIX, WEIGHT_DECAY)
    new_down = adamw_step(weight_down, first_down, second_down, grad_down * factor, RATE_MATRIX, WEIGHT_DECAY)
    new_small = adamw_step(small_params, first_small, second_small, grad_small * factor, small_rate, small_decay)
    return (result.astype(jnp.bfloat16), images_grad, grad_norm, new_in[0], new_in[1], new_in[2], new_out[0], new_out[1], new_out[2], new_down[0], new_down[1], new_down[2], new_small[0], new_small[1], new_small[2])
```

```python
import functools
import jax
import jax.numpy as jnp
from jax import lax
from jax.experimental import pallas as pl
from jax.experimental.pallas import tpu as pltpu
from jax.sharding import PartitionSpec as P

STEP = 10
DROP_RATE = 0.2
RATE_MATRIX = 0.05
RATE_VECTOR = 0.3
LAYER_DECAY = 0.8
BETA_ONE = 0.9
BETA_TWO = 0.999
ADAM_EPS = 1e-08
WEIGHT_DECAY = 0.05
CLIP_NORM = 1.0
D = 384
FF = 1536
LN_EPS = 1e-06
F32 = jnp.float32
BF16 = jnp.bfloat16
VMEM = pl.BlockSpec(memory_space=pltpu.VMEM)
ROWS = (((0,), (0,)), ((), ()))
COLS = (((1,), (1,)), ((), ()))


def limit(mib):
    return pltpu.CompilerParams(vmem_limit_bytes=mib << 20)


def shaped(shape, dtype):
    return jax.ShapeDtypeStruct(shape, dtype)


def conv_rows(src, taps, h, t, lanes, side, base, flip):
    def one(ky, acc):
        acc = list(acc)
        x = [src[h + ky - 3, w, t, lanes] for w in range(side)]
        for kx in range(7):
            tap = taps[48 - (ky * 7 + kx) if flip else ky * 7 + kx, :, lanes]
            for w in range(side):
                if 0 <= w + kx - 3 < side:
                    acc[w] = acc[w] + x[w + kx - 3] * tap
        return tuple(acc)

    first = jnp.maximum(3 - h, 0)
    last = jnp.minimum(7, side + 3 - h)
    return lax.fori_loop(first, last, one, tuple(base))


def conv_kernel(sel_ref, mix_ref, img_ref, dk_ref, vec_ref, mixed_ref, unit_ref, inv_ref, norm_ref, taps):
    side, _, imgs, _ = img_ref.shape
    for t in range(49):
        taps[t] = jnp.broadcast_to(dk_ref[t : t + 1, :], (8, D))
    mix = mix_ref[...][None]
    rest = 1.0 - mix

    def mixing(h, _):
        x = img_ref[h].reshape(side * imgs, D)
        other = jnp.dot(sel_ref[...], x, preferred_element_type=F32).reshape(side, imgs, D)
        mixed_ref[h] = mix * x.reshape(side, imgs, D).astype(F32) + rest * other
        return 0

    lax.fori_loop(0, side, mixing, 0)

    def conv(h, _):
        for t in range(imgs // 8):
            at = pl.ds(t * 8, 8)
            for g in range(D // 128):
                lanes = pl.ds(g * 128, 128)
                base = jnp.broadcast_to(vec_ref[0:1, lanes], (8, 128))
                acc = conv_rows(mixed_ref, taps, h, at, lanes, side, [base] * side, False)
                for w in range(side):
                    unit_ref[h, w, at, lanes] = acc[w]
        return 0

    lax.fori_loop(0, side, conv, 0)
    gain = vec_ref[1:2, :][None]
    bias = vec_ref[2:3, :][None]

    def norm(h, _):
        v = unit_ref[h]
        c = v - jnp.mean(v, axis=-1, keepdims=True)
        inv = lax.rsqrt(jnp.mean(c * c, axis=-1, keepdims=True) + LN_EPS)
        unit = c * inv
        unit_ref[h] = unit
        inv_ref[h] = inv
        norm_ref[h] = (unit * gain + bias).astype(BF16)
        return 0

    lax.fori_loop(0, side, norm, 0)


def conv_forward(sel, mix, img, dk, vec):
    side, _, imgs, _ = img.shape
    full = (side, side, imgs, D)
    return pl.pallas_call(
        conv_kernel,
        out_shape=(shaped(full, F32), shaped(full, F32), shaped(full[:3] + (1,), F32), shaped(full, BF16)),
        in_specs=[VMEM] * 5,
        out_specs=(VMEM,) * 4,
        scratch_shapes=[pltpu.VMEM((49, 8, D), F32)],
        compiler_params=limit(24),
    )(sel, mix, img, dk, vec)


def hidden_kernel(block, chunk, norm_ref, win_ref, wout_ref, hb_ref, vec_ref, kl_ref, mixed_ref, act_ref, dg_ref, branch_ref, unit_ref, inv_ref, out_ref):
    rows = norm_ref.shape[0]
    imgs = kl_ref.shape[0]
    gain = vec_ref[5:6, :][None]
    bias = vec_ref[6:7, :][None]

    def body(i, _):
        at = pl.ds(pl.multiple_of(i * block, block), block)
        x = norm_ref[at, :]
        branch = jnp.broadcast_to(vec_ref[3:4, :], (block, D))
        for j in range(FF // chunk):
            cols = pl.ds(j * chunk, chunk)
            pre = lax.dot_general(x, win_ref[cols, :], COLS, preferred_element_type=F32) + hb_ref[:, cols]
            phi = 0.5 + 0.5 * lax.erf(pre * 0.7071067811865476)
            bell = jnp.exp2(pre * pre * -0.7213475204444817) * 0.3989422804014327
            act = (pre * phi).astype(BF16)
            act_ref[at, cols] = act
            dg_ref[at, cols] = (phi + pre * bell).astype(BF16)
            branch = branch + jnp.dot(act, wout_ref[cols, :], preferred_element_type=F32)
        branch_ref[at, :] = branch
        shape = (block // imgs, imgs, D)
        v = mixed_ref[at, :].reshape(shape) + kl_ref[...][None] * branch.reshape(shape)
        c = v - jnp.mean(v, axis=-1, keepdims=True)
        inv = lax.rsqrt(jnp.mean(c * c, axis=-1, keepdims=True) + LN_EPS)
        unit = c * inv
        unit_ref[at, :] = unit.reshape(block, D)
        inv_ref[at, :] = inv.reshape(block, 1)
        out_ref[at, :] = (unit * gain + bias).astype(BF16).reshape(block, D)
        return 0

    lax.fori_loop(0, rows // block, body, 0)


def hidden_forward(norm, win, wout, hb, vec, kl, mixed, block=224, chunk=512):
    rows = norm.shape[0]
    return pl.pallas_call(
        functools.partial(hidden_kernel, block, chunk),
        out_shape=(
            shaped((rows, FF), BF16),
            shaped((rows, FF), BF16),
            shaped((rows, D), F32),
            shaped((rows, D), F32),
            shaped((rows, 1), F32),
            shaped((rows, D), BF16),
        ),
        in_specs=[VMEM] * 7,
        out_specs=(VMEM,) * 6,
        compiler_params=limit(24),
    )(norm, win, wout, hb, vec, kl, mixed)


def down_kernel(norm_ref, dy_ref, wd_ref, unit_ref, inv_ref, branch_ref, vec_ref, keep_ref, db_ref, out_ref, gd_ref, res_ref, bb_ref, sums_ref, gdb_ref, acc):
    half, _, _, _, imgs, _ = norm_ref.shape
    rows = half * half * imgs
    dy = dy_ref[...].reshape(rows, 2 * D)
    acc[...] = jnp.broadcast_to(db_ref[...], acc.shape)
    sums_ref[...] = jnp.zeros(sums_ref.shape, F32)
    shape = (half * half, imgs, D)
    gain = vec_ref[5:6, :][None]
    keep = keep_ref[...][None]
    scale = keep * vec_ref[4:5, :][None]

    def part(k, _):
        a = k // 2
        b = k % 2
        x = norm_ref[:, a, :, b].reshape(rows, D)
        acc[...] += jnp.dot(x, wd_ref[k], preferred_element_type=F32)
        gd_ref[k] = lax.dot_general(x, dy, ROWS, preferred_element_type=F32)
        back = lax.dot_general(dy, wd_ref[k], COLS, preferred_element_type=F32).reshape(shape)
        unit = unit_ref[:, a, :, b].reshape(shape)
        sums_ref[0] += jnp.sum(back * unit, axis=0)
        sums_ref[1] += jnp.sum(back, axis=0)
        scaled = back * gain
        m1 = jnp.mean(scaled, axis=-1, keepdims=True)
        m2 = jnp.mean(scaled * unit, axis=-1, keepdims=True)
        inv = inv_ref[:, a, :, b].reshape(half * half, imgs, 1)
        res = inv * (scaled - m1 - unit * m2)
        res_ref[:, a, :, b] = res.reshape(half, half, imgs, D)
        sums_ref[2] += jnp.sum(res * keep * branch_ref[:, a, :, b].reshape(shape), axis=0)
        bb = (res * scale).astype(BF16)
        bb_ref[:, a, :, b] = bb.reshape(half, half, imgs, D)
        sums_ref[3] += jnp.sum(bb.astype(F32), axis=0)
        return 0

    lax.fori_loop(0, 4, part, 0)
    out_ref[...] = acc[...].astype(BF16).reshape(out_ref.shape)
    gdb_ref[...] = jnp.sum(dy.astype(F32).reshape(half * half, imgs, 2 * D), axis=0)


def down_both(norm, dy, wd, unit, inv, branch, vec, keep, db):
    half, _, _, _, imgs, _ = norm.shape
    return pl.pallas_call(
        down_kernel,
        out_shape=(
            shaped((half, half, imgs, 2 * D), BF16),
            shaped((4, D, 2 * D), F32),
            shaped(norm.shape, F32),
            shaped(norm.shape, BF16),
            shaped((4, imgs, D), F32),
            shaped((imgs, 2 * D), F32),
        ),
        in_specs=[VMEM] * 9,
        out_specs=(VMEM,) * 6,
        scratch_shapes=[pltpu.VMEM((half * half * imgs, 2 * D), F32)],
        compiler_params=limit(28),
    )(norm, dy, wd, unit, inv, branch, vec, keep, db)


def grad_out_kernel(act_ref, bb_ref, g_ref):
    def body(j, _):
        cols = pl.ds(pl.multiple_of(j * 256, 256), 256)
        g_ref[cols, :] = lax.dot_general(act_ref[:, cols], bb_ref[...], ROWS, preferred_element_type=F32)
        return 0

    lax.fori_loop(0, FF // 256, body, 0)


def grad_out_of(act, bb):
    return pl.pallas_call(
        grad_out_kernel,
        out_shape=shaped((FF, D), F32),
        in_specs=[VMEM] * 2,
        out_specs=VMEM,
        compiler_params=limit(24),
    )(act, bb)


def hidden_back_kernel(block, bb_ref, wout_ref, win_ref, dg_ref, norm_ref, unit_ref, inv_ref, vec_ref, gi_ref, conv_ref, hb_ref, sums_ref, pre):
    rows = bb_ref.shape[0]
    imgs = sums_ref.shape[1]
    shape = (block // imgs, imgs, D)
    gain = vec_ref[1:2, :][None]
    gi_ref[...] = jnp.zeros(gi_ref.shape, F32)
    hb_ref[...] = jnp.zeros(hb_ref.shape, F32)
    sums_ref[...] = jnp.zeros(sums_ref.shape, F32)
    chunk = 512

    def body(i, _):
        at = pl.ds(pl.multiple_of(i * block, block), block)
        b = bb_ref[at, :]
        x = norm_ref[at, :]
        back = jnp.zeros((block, D), F32)
        for j in range(FF // chunk):
            cols = pl.ds(j * chunk, chunk)
            act = lax.dot_general(b, wout_ref[cols, :], COLS, preferred_element_type=F32)
            p = (act * dg_ref[at, cols].astype(F32)).astype(BF16)
            hb_ref[:, cols] += jnp.sum(p.astype(F32).reshape(block // imgs, imgs, chunk), axis=0)
            back = back + jnp.dot(p, win_ref[cols, :], preferred_element_type=F32)
            gi_ref[cols, :] += lax.dot_general(p, x, ROWS, preferred_element_type=F32)
        back = back.reshape(shape)
        unit = unit_ref[at, :].reshape(shape)
        sums_ref[0] += jnp.sum(back * unit, axis=0)
        sums_ref[1] += jnp.sum(back, axis=0)
        scaled = back * gain
        m1 = jnp.mean(scaled, axis=-1, keepdims=True)
        m2 = jnp.mean(scaled * unit, axis=-1, keepdims=True)
        out = inv_ref[at, :].reshape(shape[:2] + (1,)) * (scaled - m1 - unit * m2)
        sums_ref[2] += jnp.sum(out, axis=0)
        conv_ref[at, :] = out.reshape(block, D)
        return 0

    lax.fori_loop(0, rows // block, body, 0)


def hidden_back(bb, wout, win, dg, norm, unit, inv, vec, imgs, block=784):
    rows = bb.shape[0]
    return pl.pallas_call(
        functools.partial(hidden_back_kernel, block),
        out_shape=(
            shaped((FF, D), F32),
            shaped((rows, D), F32),
            shaped((imgs, FF), F32),
            shaped((3, imgs, D), F32),
        ),
        in_specs=[VMEM] * 8,
        out_specs=(VMEM,) * 4,
        scratch_shapes=[pltpu.VMEM((8, 128), F32)],
        compiler_params=limit(32),
    )(bb, wout, win, dg, norm, unit, inv, vec)


def taps_kernel(mixed_ref, conv_ref, g_ref):
    side, _, imgs, _ = mixed_ref.shape

    def per_ky(ky, _):
        first = jnp.maximum(3 - ky, 0)
        last = jnp.minimum(side, side + 3 - ky)
        for g in range(D // 128):
            lanes = pl.ds(g * 128, 128)

            def row(h, acc):
                acc = list(acc)
                for t in range(imgs // 8):
                    at = pl.ds(t * 8, 8)
                    x = [mixed_ref[h + ky - 3, w, at, lanes] for w in range(side)]
                    for w in range(side):
                        d = conv_ref[h, w, at, lanes]
                        for kx in range(7):
                            if 0 <= w + kx - 3 < side:
                                acc[kx] = acc[kx] + x[w + kx - 3] * d
                return tuple(acc)

            acc = lax.fori_loop(first, last, row, (jnp.zeros((8, 128), F32),) * 7)
            for kx in range(7):
                g_ref[ky * 7 + kx, :, lanes] = jnp.sum(acc[kx], axis=0, keepdims=True)
        return 0

    lax.fori_loop(0, 7, per_ky, 0)


def taps_grad(mixed, conv):
    return pl.pallas_call(
        taps_kernel,
        out_shape=shaped((49, 1, D), F32),
        in_specs=[VMEM] * 2,
        out_specs=VMEM,
        compiler_params=limit(24),
    )(mixed, conv)


def images_kernel(conv_ref, res_ref, dk_ref, mix_ref, sel_ref, g_ref, taps):
    side, _, imgs, _ = conv_ref.shape
    for t in range(49):
        taps[t] = jnp.broadcast_to(dk_ref[t : t + 1, :], (8, D))
    mix = mix_ref[...][None]
    rest = 1.0 - mix

    def row(h, _):
        for t in range(imgs // 8):
            at = pl.ds(t * 8, 8)
            for g in range(D // 128):
                lanes = pl.ds(g * 128, 128)
                base = [res_ref[h, w, at, lanes] for w in range(side)]
                acc = conv_rows(conv_ref, taps, h, at, lanes, side, base, True)
                for w in range(side):
                    g_ref[h, w, at, lanes] = acc[w]
        return 0

    lax.fori_loop(0, side, row, 0)

    def unmix(h, _):
        v = g_ref[h]
        part = (rest * v).reshape(side * imgs, D)
        high = part.astype(BF16)
        low = (part - high.astype(F32)).astype(BF16)
        back = jnp.dot(sel_ref[...], high, preferred_element_type=F32) + jnp.dot(sel_ref[...], low, preferred_element_type=F32)
        g_ref[h] = mix * v + back.reshape(side, imgs, D)
        return 0

    lax.fori_loop(0, side, unmix, 0)


def images_back(conv, res, dk, mix, selt):
    return pl.pallas_call(
        images_kernel,
        out_shape=shaped(conv.shape, F32),
        in_specs=[VMEM] * 5,
        out_specs=VMEM,
        scratch_shapes=[pltpu.VMEM((49, 8, D), F32)],
        compiler_params=limit(24),
    )(conv, res, dk, mix, selt)


def swap(x, bit, n):
    return lax.ppermute(x, "dp", [(i, i ^ bit) for i in range(n)])


def bits_of(n):
    return [1 << k for k in range(n.bit_length() - 1)]


def is_set(bit):
    return (lax.axis_index("dp") & bit) != 0


def gather_tree(shard, n, order):
    have = shard
    met = []
    for bit in order:
        other = swap(have, bit, n)
        axis = sum(1 for b in met if b > bit)
        mine = is_set(bit)
        low = jnp.where(mine, other, have)
        high = jnp.where(mine, have, other)
        have = jnp.stack([low, high], axis=axis)
        met.append(bit)
    return have.reshape((n,) + shard.shape)


def scatter_tree(total, n, order):
    shape = total.shape[1:]
    left = sorted(order, reverse=True)
    have = total.reshape((2,) * len(left) + shape)
    for bit in order:
        axis = left.index(bit)
        mine = is_set(bit).astype(jnp.int32)
        keep = lax.dynamic_index_in_dim(have, mine, axis, keepdims=False)
        send = lax.dynamic_index_in_dim(have, 1 - mine, axis, keepdims=False)
        have = keep.astype(F32) + swap(send.astype(BF16), bit, n).astype(F32)
        left.remove(bit)
    return have


def adamw_step(weight, first_mom, second, gradient, step_rate, decay_rate):
    first_mom = BETA_ONE * first_mom + (1.0 - BETA_ONE) * gradient
    second = BETA_TWO * second + (1.0 - BETA_TWO) * gradient * gradient
    first_hat = first_mom / (1.0 - BETA_ONE**STEP)
    second_hat = second / (1.0 - BETA_TWO**STEP)
    weight = weight - step_rate * (first_hat / (jnp.sqrt(second_hat) + ADAM_EPS) + decay_rate * weight)
    return (first_mom, second, weight)


def local(n, images, mix_weight, partner, keep_mask, cotangent, weight_in, weight_out, weight_down, small_params,
          first_in, second_in, first_out, second_out, first_down, second_down, first_small, second_small):
    imgs, side = images.shape[:2]
    half = side // 2
    pixels = side * side * imgs
    bits = bits_of(n)
    up = bits[1:] + bits[:1]
    small = gather_tree(small_params.astype(BF16), n, up).reshape(-1, D).astype(F32)
    pair = jnp.concatenate([weight_in, weight_out], axis=1).astype(BF16)
    pair = gather_tree(pair, n, up).reshape(FF, 2 * D)
    win = pair[:, :D]
    wout = pair[:, D:]
    wd = lax.all_gather(weight_down.astype(BF16), "dp", axis=0, tiled=True).reshape(D, 4, 2 * D).transpose(1, 0, 2)

    dk = small[:49]
    vec = jnp.concatenate([small[49:52], small[56:60], small[56:57]], axis=0)
    hb = small[52:56].reshape(1, FF)
    db = small[60:62].reshape(1, 2 * D)
    place = partner - lax.axis_index("dp") * imgs
    spot = jnp.arange(side * imgs, dtype=jnp.int32)
    target = jnp.tile(place, side) + (spot // imgs) * imgs
    sel = target[:, None] == spot[None, :]
    selt = (target[None, :] == spot[:, None]).astype(BF16)
    sel = sel.astype(BF16)
    mix = jnp.broadcast_to(mix_weight[:, None], (imgs, D))
    keep = jnp.broadcast_to((keep_mask.astype(F32) / (1.0 - DROP_RATE))[:, None], (imgs, D))

    img = images.transpose(1, 2, 0, 3)
    dy = cotangent.transpose(1, 2, 0, 3)
    flat = lambda a: a.reshape(pixels, a.shape[-1])
    paired = lambda a: a.reshape(half, 2, half, 2, imgs, a.shape[-1])
    square = lambda a: a.reshape(side, side, imgs, a.shape[-1])
    mixed, unit1, inv1, norm1 = conv_forward(sel, mix, img, dk, vec)
    act, dg, branch, unit2, inv2, norm2 = hidden_forward(flat(norm1), win, wout, hb, vec, keep * vec[4:5], flat(mixed))
    out, gd, res, bb, sums2, gdb = down_both(
        paired(norm2), dy, wd, paired(unit2), paired(inv2), paired(branch), vec, keep, db
    )
    gd = gd.astype(BF16).transpose(1, 0, 2).reshape(n, FF // n, 2 * D)
    gd = scatter_tree(gd, n, [1, 4, 2] + bits[3:])
    go = grad_out_of(act, flat(bb)).reshape(n, FF // n, D)
    go = scatter_tree(go, n, [1, 2, 4] + bits[3:])
    gi, back_conv, ghb, sums1 = hidden_back(flat(bb), wout, win, dg, flat(norm1), flat(unit1), flat(inv1), vec, imgs)
    gi = scatter_tree(gi.reshape(n, FF // n, D), n, [1, 8, 2, 4] + bits[4:])
    back_conv = square(back_conv)
    gk = taps_grad(mixed, back_conv)
    one = jnp.sum(sums1, axis=1)
    two = jnp.sum(sums2, axis=1)
    gs = jnp.concatenate(
        [
            gk.reshape(49, D),
            one[2:3],
            one[0:2],
            jnp.sum(ghb, axis=0).reshape(4, D),
            two[3:4],
            two[2:3],
            two[0:2],
            jnp.sum(gdb, axis=0).reshape(2, D),
        ],
        axis=0,
    )
    gs = scatter_tree(gs.reshape(n, -1), n, up[-1:] + up[:-1])
    images_grad = images_back(back_conv, square(res), dk, mix, selt)

    squares = sum(jnp.sum(g * g) for g in (gi, go, gd, gs)).reshape(1, 1)
    for bit in bits:
        squares = squares + swap(squares, bit, n)
    grad_norm = jnp.sqrt(squares[0, 0])
    factor = CLIP_NORM / jnp.maximum(grad_norm, CLIP_NORM)
    shard_len = gs.shape[0]
    position = lax.axis_index("dp") * shard_len + jnp.arange(shard_len, dtype=jnp.int32)
    small_rate = jnp.where(position < 54 * D + FF, LAYER_DECAY * RATE_VECTOR, RATE_VECTOR)
    small_decay = jnp.where(position < 49 * D, WEIGHT_DECAY, 0.0)
    new_in = adamw_step(weight_in, first_in, second_in, gi * factor, LAYER_DECAY * RATE_MATRIX, WEIGHT_DECAY)
    new_out = adamw_step(weight_out, first_out, second_out, go * factor, LAYER_DECAY * RATE_MATRIX, WEIGHT_DECAY)
    new_down = adamw_step(weight_down, first_down, second_down, gd * factor, RATE_MATRIX, WEIGHT_DECAY)
    new_small = adamw_step(small_params, first_small, second_small, gs * factor, small_rate, small_decay)
    return (
        out.transpose(2, 0, 1, 3),
        images_grad.transpose(2, 0, 1, 3),
        grad_norm,
        *new_in,
        *new_out,
        *new_down,
        *new_small,
    )


def solution(mesh):
    four = P("dp", None, None, None)
    two = P("dp", None)
    one = P("dp")
    return jax.shard_map(
        functools.partial(local, mesh.shape["dp"]),
        mesh=mesh,
        in_specs=(four, one, one, one, four, two, two, two, one) + (two,) * 6 + (one,) * 2,
        out_specs=(four, four, P()) + (two,) * 9 + (one,) * 3,
        check_vma=False,
    )
```

```python
import functools
import jax
import jax.numpy as jnp
import numpy as np
from jax import lax
from jax.experimental import pallas as pl
from jax.experimental.pallas import tpu as pltpu
from jax.sharding import PartitionSpec as P

STEP = 10
DROP_RATE = 0.2
RATE_MATRIX = 0.05
RATE_VECTOR = 0.3
LAYER_DECAY = 0.8
BETA_ONE = 0.9
BETA_TWO = 0.999
ADAM_EPS = 1e-08
WEIGHT_DECAY = 0.05
CLIP_NORM = 1.0
D = 384
FF = 1536
LN_EPS = 1e-06
F32 = jnp.float32
BF16 = jnp.bfloat16
VMEM = pl.BlockSpec(memory_space=pltpu.VMEM)
SMEM = pl.BlockSpec(memory_space=pltpu.SMEM)
HBM = pl.BlockSpec(memory_space=pltpu.HBM)
ROWS = (((0,), (0,)), ((), ()))
COLS = (((1,), (1,)), ((), ()))
DEPTH_BIAS, GAIN_ONE, BIAS_ONE, HIDDEN_BIAS, OUT_BIAS, LAYER_SCALE, GAIN_TWO, BIAS_TWO, DOWN_BIAS = 49, 50, 51, 52, 56, 57, 58, 59, 60


def near(shape, dtype):
    return jax.ShapeDtypeStruct(shape, dtype)


def far(shape, dtype):
    return pltpu.HBM(shape, dtype)


def held(x):
    return pltpu.with_memory_space_constraint(x, pltpu.HBM)


def dma(src, dst, sem):
    return pltpu.make_async_copy(src, dst, sem)


def start(copies):
    for copy in copies:
        copy.start()


def wait(copies):
    for copy in copies:
        copy.wait()


def kernel_call(body, out, specs, scratch, args, after, us, mib, aliases=None):
    specs = specs + [HBM] * len(after)
    args = tuple(args) + tuple(after)
    args = [held(x) if spec is HBM else x for spec, x in zip(specs, args)]
    return pl.pallas_call(
        body,
        out_shape=tuple(out),
        in_specs=specs,
        out_specs=tuple(HBM if isinstance(x, type(far((8, 128), F32))) else VMEM for x in out),
        scratch_shapes=scratch,
        input_output_aliases=aliases or {},
        cost_estimate=pl.CostEstimate(flops=int(us * 1e9), bytes_accessed=0, transcendentals=0),
        compiler_params=pltpu.CompilerParams(vmem_limit_bytes=mib << 20),
    )(*args)


def norm_of(v):
    c = v - jnp.mean(v, axis=-1, keepdims=True)
    inv = lax.rsqrt(jnp.mean(c * c, axis=-1, keepdims=True) + LN_EPS)
    return c * inv, inv


def norm_back(back, unit, inv, gain):
    scaled = back * gain
    m1 = jnp.mean(scaled, axis=-1, keepdims=True)
    m2 = jnp.mean(scaled * unit, axis=-1, keepdims=True)
    return inv * (scaled - m1 - unit * m2)


def conv_rows(src, taps, h, t, lanes, side, base, flip):
    def one(ky, acc):
        acc = list(acc)
        x = [src[h + ky - 3, w, t, lanes] for w in range(side)]
        for kx in range(7):
            tap = taps[48 - (ky * 7 + kx) if flip else ky * 7 + kx, :, lanes]
            for w in range(side):
                if 0 <= w + kx - 3 < side:
                    acc[w] = acc[w] + x[w + kx - 3] * tap
        return tuple(acc)

    first = jnp.maximum(3 - h, 0)
    last = jnp.minimum(7, side + 3 - h)
    return lax.fori_loop(first, last, one, tuple(base))


def conv_kernel(begin, end, fresh, *refs):
    if fresh:
        small_hbm, img_hbm, sel_ref, mix_ref = refs[:4]
        mixed_hbm, unit_hbm, inv_hbm, norm_hbm, small_ref, mixed_ref, taps, conv_ref, unit_ref, inv_ref, norm_ref, sem, img_ref = refs[-13:]
    else:
        small_hbm, mixed_hbm = refs[:2]
        unit_hbm, inv_hbm, norm_hbm, small_ref, mixed_ref, taps, conv_ref, unit_ref, inv_ref, norm_ref, sem = refs[-11:]
    side, _, imgs, _ = mixed_ref.shape
    low = max(begin - 3, 0)
    high = side if fresh else min(end + 3, side)
    rows = end - begin
    load = dma(small_hbm, small_ref, sem.at[4, 0])
    load.start()

    def enter(h):
        if fresh:
            return dma(img_hbm.at[h], img_ref.at[h], sem.at[3, h])
        return dma(mixed_hbm.at[h], mixed_ref.at[h], sem.at[3, h])

    def store(h):
        return dma(mixed_ref.at[h], mixed_hbm.at[h], sem.at[5, h])

    for h in range(low, high):
        enter(h).start()
    load.wait()
    for t in range(49):
        taps[t] = jnp.broadcast_to(small_ref[t : t + 1, :], (8, D))
    if fresh:
        mix = mix_ref[...][None]
        rest = 1.0 - mix

        def blend(h, _):
            enter(h).wait()
            x = img_ref[h].reshape(side * imgs, D)
            other = jnp.dot(sel_ref[...], x, preferred_element_type=F32).reshape(side, imgs, D)
            mixed_ref[h] = mix * x.reshape(side, imgs, D).astype(F32) + rest * other
            store(h).start()
            return 0

        lax.fori_loop(0, side, blend, 0)
    else:
        for h in range(low, min(begin + 3, high)):
            enter(h).wait()

    def conv(r, _):
        h = r + begin
        if not fresh:

            @pl.when(h + 3 < high)
            def _():
                enter(h + 3).wait()

        for t in range(imgs // 8):
            at = pl.ds(t * 8, 8)
            for g in range(D // 128):
                lanes = pl.ds(g * 128, 128)
                base = jnp.broadcast_to(small_ref[DEPTH_BIAS : DEPTH_BIAS + 1, lanes], (8, 128))
                acc = conv_rows(mixed_ref, taps, h, at, lanes, side, [base] * side, False)
                for w in range(side):
                    conv_ref[r, w, at, lanes] = acc[w]
        return 0

    lax.fori_loop(0, rows, conv, 0)
    gain = small_ref[GAIN_ONE : GAIN_ONE + 1, :][None]
    bias = small_ref[BIAS_ONE : BIAS_ONE + 1, :][None]

    def leave(r):
        return (
            dma(unit_ref.at[r], unit_hbm.at[r + begin], sem.at[0, r]),
            dma(inv_ref.at[r], inv_hbm.at[r + begin], sem.at[1, r]),
            dma(norm_ref.at[r], norm_hbm.at[r + begin], sem.at[2, r]),
        )

    def norm(r, _):
        unit, inv = norm_of(conv_ref[r])
        unit_ref[r] = unit.astype(BF16)
        inv_ref[r] = inv
        norm_ref[r] = (unit * gain + bias).astype(BF16)
        start(leave(r))
        return 0

    lax.fori_loop(0, rows, norm, 0)
    for r in range(rows):
        wait(leave(r))
    if fresh:
        for h in range(side):
            store(h).wait()


def conv_forward(small, inputs, begin, end, so_far=(), after=()):
    fresh = not so_far
    full = inputs[0].shape
    side = full[0]
    thin = full[:3] + (1,)
    rows = end - begin
    out = [far(full, BF16), far(thin, F32), far(full, BF16)]
    scratch = [
        pltpu.VMEM(small.shape, F32),
        pltpu.VMEM(full, F32),
        pltpu.VMEM((49, 8, D), F32),
        pltpu.VMEM((rows,) + full[1:], F32),
        pltpu.VMEM((rows,) + full[1:], BF16),
        pltpu.VMEM((rows,) + thin[1:], F32),
        pltpu.VMEM((rows,) + full[1:], BF16),
        pltpu.SemaphoreType.DMA((6, side)),
    ]
    specs = [HBM] * 2
    if fresh:
        out = [far(full, F32)] + out
        scratch.append(pltpu.VMEM(full, BF16))
        specs = [HBM] * 2 + [VMEM] * 2
    return kernel_call(
        functools.partial(conv_kernel, begin, end, fresh),
        out,
        specs + [HBM] * len(so_far),
        scratch,
        (small,) + tuple(inputs) + tuple(so_far),
        after,
        21 * rows / side + 3 * fresh,
        28,
        {2 + k: k for k in range(len(so_far))},
    )


def hidden_kernel(block, norm_hbm, mixed_hbm, near_hbm, far_hbm, small_hbm, hb_ref, keep_ref, *rest):
    act_hbm, dg_hbm, branch_hbm, unit_hbm, inv_hbm, out_hbm = rest[-20:-14]
    near_ref, far_ref, small_ref, norm_ref, mixed_ref, act_ref, dg_ref, branch_ref, unit_ref, inv_ref, out_ref, isem, osem, wsem = rest[-14:]
    rows = norm_hbm.shape[0]
    steps = rows // block
    imgs = keep_ref.shape[0]
    shape = (block // imgs, imgs, D)
    wide = near_ref.shape[0]

    def spot(i):
        return pl.ds(pl.multiple_of(i * block, block), block)

    def enter(i):
        s = i % 2
        return (
            dma(norm_hbm.at[spot(i), :], norm_ref.at[s], isem.at[0, s]),
            dma(mixed_hbm.at[spot(i), :], mixed_ref.at[s], isem.at[1, s]),
        )

    def leave(i):
        s = i % 2
        pairs = ((act_ref, act_hbm), (dg_ref, dg_hbm), (branch_ref, branch_hbm), (unit_ref, unit_hbm), (inv_ref, inv_hbm), (out_ref, out_hbm))
        return [dma(a.at[s], b.at[spot(i), :], osem.at[k, s]) for k, (a, b) in enumerate(pairs)]

    loads = (dma(small_hbm, small_ref, wsem.at[0]), dma(near_hbm, near_ref, wsem.at[1]), dma(far_hbm, far_ref, wsem.at[2]))
    start(enter(0))
    start(loads)
    wait(loads)
    scale = (keep_ref[...] * small_ref[LAYER_SCALE : LAYER_SCALE + 1, :])[None]
    gain = small_ref[GAIN_TWO : GAIN_TWO + 1, :][None]
    bias = small_ref[BIAS_TWO : BIAS_TWO + 1, :][None]

    def body(i, _):
        s = i % 2

        @pl.when(i + 1 < steps)
        def _():
            start(enter(i + 1))

        @pl.when(i >= 2)
        def _():
            wait(leave(i - 2))

        wait(enter(i))
        x = norm_ref[s]
        branch = jnp.broadcast_to(small_ref[OUT_BIAS : OUT_BIAS + 1, :], (block, D))
        for j, pair_ref in enumerate((near_ref, far_ref)):
            cols = pl.ds(j * wide, wide)
            pre = lax.dot_general(x, pair_ref[:, :D], COLS, preferred_element_type=F32) + hb_ref[:, cols]
            phi = 0.5 + 0.5 * lax.erf(pre * 0.7071067811865476)
            bell = jnp.exp2(pre * pre * -0.7213475204444817) * 0.3989422804014327
            act = (pre * phi).astype(BF16)
            act_ref[s, :, cols] = act
            dg_ref[s, :, cols] = (phi + pre * bell).astype(BF16)
            branch = branch + jnp.dot(act, pair_ref[:, D:], preferred_element_type=F32)
        branch_ref[s] = branch.astype(BF16)
        unit, inv = norm_of(mixed_ref[s].reshape(shape) + scale * branch.reshape(shape))
        unit_ref[s] = unit.astype(BF16).reshape(block, D)
        inv_ref[s] = inv.reshape(block, 1)
        out_ref[s] = (unit * gain + bias).astype(BF16).reshape(block, D)
        start(leave(i))
        return 0

    lax.fori_loop(0, steps, body, 0)
    for i in range(max(steps - 2, 0), steps):
        wait(leave(i))


def hidden_forward(norm, mixed, pair, small, hb, keep, after=(), block=448):
    rows = norm.shape[0]
    two = lambda width, dtype: pltpu.VMEM((2, block, width), dtype)
    return kernel_call(
        functools.partial(hidden_kernel, block),
        [far((rows, FF), BF16)] * 2 + [far((rows, D), BF16)] * 2 + [far((rows, 1), F32), far((rows, D), BF16)],
        [HBM] * 5 + [VMEM] * 2,
        [pltpu.VMEM(pair[0].shape, BF16)] * 2
        + [pltpu.VMEM(small.shape, F32), two(D, BF16), two(D, F32), two(FF, BF16), two(FF, BF16)]
        + [two(D, BF16), two(D, BF16), two(1, F32), two(D, BF16)]
        + [pltpu.SemaphoreType.DMA((2, 2)), pltpu.SemaphoreType.DMA((6, 2)), pltpu.SemaphoreType.DMA((3,))],
        (norm, mixed, *pair, small, hb, keep),
        after,
        17,
        32,
    )


def grad_down_kernel(origin_ref, norm_hbm, dy_hbm, *rest):
    near_ref, far_ref, gdb_ref, dy_ref, norm_ref, wide, sem = rest[-7:]
    half, _, _, _, imgs, _ = norm_hbm.shape
    rows = half * half * imgs
    enter = [dma(dy_hbm, dy_ref, sem.at[4])]
    enter += [dma(norm_hbm.at[:, k // 2, :, k % 2], norm_ref.at[k], sem.at[k]) for k in range(4)]
    start(enter)
    enter[0].wait()
    dy = dy_ref[...].reshape(rows, 2 * D)
    gdb_ref[...] = jnp.sum(dy.astype(F32).reshape(half * half, imgs, 2 * D), axis=0)
    for k in range(4):
        enter[k + 1].wait()
        x = norm_ref[k].reshape(rows, D)
        for g in range(6):
            wide[g, pl.ds(k, D, stride=4), :] = lax.dot_general(
                x, dy[:, g * 128 : (g + 1) * 128], ROWS, preferred_element_type=F32
            )
    pieces = origin_ref.shape[0]
    deep = 4 * D // pieces
    for half_ref, first in ((near_ref, 0), (far_ref, pieces // 2)):
        def move(j, _):
            begin = pl.multiple_of(origin_ref[first + j] * deep, 16)
            to = pl.multiple_of(j * deep, 16)
            for g in range(6):
                half_ref[pl.ds(to, deep), pl.ds(g * 128, 128)] = wide[g, pl.ds(begin, deep), :].astype(BF16)
            return 0

        lax.fori_loop(0, pieces // 2, move, 0)


def grad_down(origin, norm, dy, after=()):
    half = dy.shape[0]
    imgs = dy.shape[2]
    return kernel_call(
        grad_down_kernel,
        [near((2 * D, 2 * D), BF16)] * 2 + [near((imgs, 2 * D), F32)],
        [SMEM] + [HBM] * 2,
        [
            pltpu.VMEM(dy.shape, BF16),
            pltpu.VMEM((4, half, half, imgs, D), BF16),
            pltpu.VMEM((6, 4 * D, 128), F32),
            pltpu.SemaphoreType.DMA((5,)),
        ],
        (origin, norm, dy),
        after,
        8,
        24,
    )


def down_kernel(origin_ref, norm_hbm, unit_hbm, inv_hbm, branch_hbm, near_hbm, far_hbm, dy_hbm, small_hbm, keep_ref, db_ref, *rest):
    out_ref, bb_hbm, sums_ref, res_hbm = rest[-20:-16]
    near_ref, far_ref, dy_ref, small_ref, norm_ref, unit_ref, inv_ref, branch_ref, bb_ref, res_ref, acc, wide, wk, wsem, isem, osem = rest[-16:]
    half, _, _, _, imgs, _ = norm_hbm.shape
    rows = half * half * imgs
    loads = [dma(near_hbm, near_ref, wsem.at[0]), dma(far_hbm, far_ref, wsem.at[1]), dma(dy_hbm, dy_ref, wsem.at[2]), dma(small_hbm, small_ref, wsem.at[3])]
    start(loads)

    def enter(k):
        pairs = ((norm_hbm, norm_ref), (unit_hbm, unit_ref), (inv_hbm, inv_ref), (branch_hbm, branch_ref))
        return [dma(a.at[:, k // 2, :, k % 2], b.at[k], isem.at[j, k]) for j, (a, b) in enumerate(pairs)]

    def leave(k):
        pairs = ((bb_ref, bb_hbm), (res_ref, res_hbm))
        return [dma(a.at[k], b.at[:, k // 2, :, k % 2], osem.at[j, k]) for j, (a, b) in enumerate(pairs)]

    for k in range(4):
        start(enter(k))
    pieces = origin_ref.shape[0]
    deep = 4 * D // pieces
    for half_ref, load, first in ((near_ref, loads[0], 0), (far_ref, loads[1], pieces // 2)):
        load.wait()

        def move(j, _):
            begin = pl.multiple_of(origin_ref[first + j] * deep, 16)
            to = pl.multiple_of(j * deep, 16)
            for g in range(6):
                wide[g, pl.ds(begin, deep), :] = half_ref[pl.ds(to, deep), pl.ds(g * 128, 128)].astype(F32)
            return 0

        lax.fori_loop(0, pieces // 2, move, 0)
    for g in range(6):
        for k in range(4):
            wk[k, :, pl.ds(g * 128, 128)] = wide[g, pl.ds(k, D, stride=4), :].astype(BF16)
    acc[...] = jnp.broadcast_to(db_ref[...], acc.shape)
    sums_ref[...] = jnp.zeros(sums_ref.shape, F32)
    shape = (half * half, imgs, D)
    loads[2].wait()
    loads[3].wait()
    gain = small_ref[GAIN_TWO : GAIN_TWO + 1, :][None]
    keep = keep_ref[...][None]
    scale = keep * small_ref[LAYER_SCALE : LAYER_SCALE + 1, :][None]

    def part(k, _):
        wait(enter(k))
        x = norm_ref[k].reshape(rows, D)
        acc[...] += jnp.dot(x, wk[k], preferred_element_type=F32)
        back = lax.dot_general(dy_ref[...].reshape(rows, 2 * D), wk[k], COLS, preferred_element_type=F32).reshape(shape)
        unit = unit_ref[k].reshape(shape).astype(F32)
        sums_ref[0] += jnp.sum(back * unit, axis=0)
        sums_ref[1] += jnp.sum(back, axis=0)
        res = norm_back(back, unit, inv_ref[k].reshape(half * half, imgs, 1), gain)
        res_ref[k] = res.reshape(half, half, imgs, D)
        kept = res * keep
        sums_ref[2] += jnp.sum(kept * branch_ref[k].reshape(shape).astype(F32), axis=0)
        bb = (res * scale).astype(BF16)
        bb_ref[k] = bb.reshape(half, half, imgs, D)
        start(leave(k))
        sums_ref[3] += jnp.sum(bb.astype(F32), axis=0)
        return 0

    lax.fori_loop(0, 4, part, 0)
    out_ref[...] = acc[...].astype(BF16).reshape(out_ref.shape)
    for k in range(4):
        wait(leave(k))


def down_both(origin, norm, unit, inv, branch, wd, dy, small, keep, db, after=()):
    half, _, _, _, imgs, _ = norm.shape
    rows = half * half * imgs
    four = lambda width, dtype: pltpu.VMEM((4, half, half, imgs, width), dtype)
    return kernel_call(
        down_kernel,
        [near((half, half, imgs, 2 * D), BF16), far(norm.shape, BF16), near((4, imgs, D), F32), far(norm.shape, F32)],
        [SMEM] + [HBM] * 8 + [VMEM] * 2,
        [pltpu.VMEM(wd[0].shape, BF16)] * 2
        + [pltpu.VMEM(dy.shape, BF16), pltpu.VMEM(small.shape, F32)]
        + [four(D, BF16), four(D, BF16), four(1, F32), four(D, BF16), four(D, BF16), four(D, F32)]
        + [pltpu.VMEM((rows, 2 * D), F32), pltpu.VMEM((6, 4 * D, 128), F32), pltpu.VMEM((4, D, 2 * D), BF16)]
        + [pltpu.SemaphoreType.DMA((4,)), pltpu.SemaphoreType.DMA((4, 4)), pltpu.SemaphoreType.DMA((2, 4))],
        (origin, norm, unit, inv, branch, *wd, dy, small, keep, db),
        after,
        13,
        44,
    )


def pair_grad_kernel(block, bb_hbm, act_hbm, dg_hbm, norm_hbm, near_hbm, far_hbm, *rest):
    gnear_ref, gfar_ref, hb_ref, p_hbm, near_ref, far_ref, acc, bb_ref, act_ref, dg_ref, norm_ref, p_ref, sem, wsem = rest[-14:]
    rows = bb_hbm.shape[0]
    imgs = hb_ref.shape[0]
    steps = rows // block
    wide = near_ref.shape[0]

    def spot(i):
        return pl.ds(pl.multiple_of(i * block, block), block)

    def enter(i):
        s = i % 2
        pairs = ((act_hbm, act_ref), (dg_hbm, dg_ref), (norm_hbm, norm_ref), (bb_hbm, bb_ref))
        return [dma(a.at[spot(i), :], b.at[s], sem.at[k, s]) for k, (a, b) in enumerate(pairs)]

    def leave(i):
        return dma(p_ref.at[i % 2], p_hbm.at[spot(i), :], sem.at[4, i % 2])

    loads = [dma(near_hbm.at[:, pl.ds(D, D)], near_ref, wsem.at[0]), dma(far_hbm.at[:, pl.ds(D, D)], far_ref, wsem.at[1])]
    start(loads)
    start(enter(0))
    hb_ref[...] = jnp.zeros(hb_ref.shape, F32)
    acc[...] = jnp.zeros(acc.shape, F32)
    wait(loads)

    def body(i, _):
        s = i % 2

        @pl.when(i + 1 < steps)
        def _():
            start(enter(i + 1))

        @pl.when(i >= 2)
        def _():
            leave(i - 2).wait()

        wait(enter(i))
        b = bb_ref[s]
        x = norm_ref[s]
        for j, out_ref in enumerate((near_ref, far_ref)):
            cols = pl.ds(j * wide, wide)
            back = lax.dot_general(b, out_ref[...], COLS, preferred_element_type=F32)
            p = (back * dg_ref[s, :, cols].astype(F32)).astype(BF16)
            p_ref[s, :, cols] = p
            hb_ref[:, cols] += jnp.sum(p.astype(F32).reshape(block // imgs, imgs, wide), axis=0)
            acc[cols, D:] += lax.dot_general(act_ref[s, :, cols], b, ROWS, preferred_element_type=F32)
            acc[cols, :D] += lax.dot_general(p, x, ROWS, preferred_element_type=F32)
        leave(i).start()
        return 0

    lax.fori_loop(0, steps, body, 0)
    gnear_ref[...] = acc[:wide].astype(BF16)
    gfar_ref[...] = acc[wide:].astype(BF16)
    for i in range(max(steps - 2, 0), steps):
        leave(i).wait()


def pair_grad(bb, act, dg, norm, pair, imgs, after=(), block=784):
    rows = bb.shape[0]
    two = lambda width: pltpu.VMEM((2, block, width), BF16)
    return kernel_call(
        functools.partial(pair_grad_kernel, block),
        [near((FF // 2, 2 * D), BF16)] * 2 + [near((imgs, FF), F32), far((rows, FF), BF16)],
        [HBM] * 6,
        [pltpu.VMEM((FF // 2, D), BF16)] * 2
        + [pltpu.VMEM((FF, 2 * D), F32), two(D), two(FF), two(FF), two(D), two(FF)]
        + [pltpu.SemaphoreType.DMA((5, 2)), pltpu.SemaphoreType.DMA((2,))],
        (bb, act, dg, norm, *pair),
        after,
        23,
        44,
    )


def back_one_kernel(block, p_hbm, unit_hbm, inv_hbm, near_hbm, far_hbm, small_hbm, *rest):
    conv_hbm, sums_ref, near_ref, far_ref, small_ref, p_ref, unit_ref, inv_ref, conv_ref, sem, wsem = rest[-11:]
    rows = p_hbm.shape[0]
    imgs = sums_ref.shape[1]
    steps = rows // block
    shape = (block // imgs, imgs, D)
    wide = near_ref.shape[0]

    def spot(i):
        return pl.ds(pl.multiple_of(i * block, block), block)

    def enter(i):
        s = i % 2
        pairs = ((p_hbm, p_ref), (unit_hbm, unit_ref), (inv_hbm, inv_ref))
        return [dma(a.at[spot(i), :], b.at[s], sem.at[k, s]) for k, (a, b) in enumerate(pairs)]

    def leave(i):
        return dma(conv_ref.at[i % 2], conv_hbm.at[spot(i), :], sem.at[3, i % 2])

    loads = [dma(near_hbm.at[:, pl.ds(0, D)], near_ref, wsem.at[0]), dma(far_hbm.at[:, pl.ds(0, D)], far_ref, wsem.at[1]), dma(small_hbm, small_ref, wsem.at[2])]
    start(loads)
    start(enter(0))
    sums_ref[...] = jnp.zeros(sums_ref.shape, F32)
    wait(loads)
    gain = small_ref[GAIN_ONE : GAIN_ONE + 1, :][None]

    def body(i, _):
        s = i % 2

        @pl.when(i + 1 < steps)
        def _():
            start(enter(i + 1))

        @pl.when(i >= 2)
        def _():
            leave(i - 2).wait()

        wait(enter(i))
        back = jnp.dot(p_ref[s, :, :wide], near_ref[...], preferred_element_type=F32)
        back = back + jnp.dot(p_ref[s, :, wide:], far_ref[...], preferred_element_type=F32)
        back = back.reshape(shape)
        unit = unit_ref[s].reshape(shape).astype(F32)
        sums_ref[0] += jnp.sum(back * unit, axis=0)
        sums_ref[1] += jnp.sum(back, axis=0)
        out = norm_back(back, unit, inv_ref[s].reshape(shape[:2] + (1,)), gain)
        sums_ref[2] += jnp.sum(out, axis=0)
        conv_ref[s] = out.reshape(block, D)
        leave(i).start()
        return 0

    lax.fori_loop(0, steps, body, 0)
    for i in range(max(steps - 2, 0), steps):
        leave(i).wait()


def back_one(p, unit, inv, pair, small, imgs, after=(), block=448):
    rows = p.shape[0]
    two = lambda width, dtype: pltpu.VMEM((2, block, width), dtype)
    return kernel_call(
        functools.partial(back_one_kernel, block),
        [far((rows, D), F32), near((3, imgs, D), F32)],
        [HBM] * 6,
        [pltpu.VMEM((FF // 2, D), BF16)] * 2
        + [pltpu.VMEM(small.shape, F32), two(FF, BF16), two(D, BF16), two(1, F32), two(D, F32)]
        + [pltpu.SemaphoreType.DMA((4, 2)), pltpu.SemaphoreType.DMA((3,))],
        (p, unit, inv, *pair, small),
        after,
        10,
        24,
    )


def taps_kernel(groups, conv_hbm, mixed_hbm, *rest):
    g_ref, conv_ref, mixed_ref, sem = rest[-4:]
    side, _, imgs, _ = conv_hbm.shape

    def enter(k):
        lanes = pl.ds(groups[k] * 128, 128)
        return (
            dma(mixed_hbm.at[:, :, :, lanes], mixed_ref.at[k], sem.at[0, k]),
            dma(conv_hbm.at[:, :, :, lanes], conv_ref.at[k], sem.at[1, k]),
        )

    for k in range(len(groups)):
        start(enter(k))
    for k in range(len(groups)):
        wait(enter(k))

        def per_ky(ky, _):
            first = jnp.maximum(3 - ky, 0)
            last = jnp.minimum(side, side + 3 - ky)

            def row(h, acc):
                acc = list(acc)
                for t in range(imgs // 8):
                    at = pl.ds(t * 8, 8)
                    x = [mixed_ref[k, h + ky - 3, w, at] for w in range(side)]
                    for w in range(side):
                        d = conv_ref[k, h, w, at]
                        for kx in range(7):
                            if 0 <= w + kx - 3 < side:
                                acc[kx] = acc[kx] + x[w + kx - 3] * d
                return tuple(acc)

            acc = lax.fori_loop(first, last, row, (jnp.zeros((8, 128), F32),) * 7)
            for kx in range(7):
                g_ref[ky * 7 + kx, :, pl.ds(k * 128, 128)] = jnp.sum(acc[kx], axis=0, keepdims=True)
            return 0

        lax.fori_loop(0, 7, per_ky, 0)


def taps_grad(conv, mixed, groups, after=()):
    lanes = pltpu.VMEM((len(groups),) + conv.shape[:3] + (128,), F32)
    return kernel_call(
        functools.partial(taps_kernel, groups),
        [near((49, 1, 128 * len(groups)), F32)],
        [HBM] * 2,
        [lanes, lanes, pltpu.SemaphoreType.DMA((2, len(groups)))],
        (conv, mixed),
        after,
        4.7 * len(groups),
        20,
    )[0]


def images_kernel(begin, end, conv_hbm, small_hbm, mix_ref, sel_ref, res_hbm, *rest):
    g_hbm, small_ref, conv_ref, taps, res_ref, out_ref, sem, csem = rest[-8:]
    side, _, imgs, _ = conv_hbm.shape
    low = max(begin - 3, 0)
    high = min(end + 3, side)
    load = dma(small_hbm, small_ref, csem.at[side])
    load.start()

    def bring(h):
        return dma(conv_hbm.at[h], conv_ref.at[h], csem.at[h])

    def enter(h):
        return dma(res_hbm.at[h], res_ref.at[h % 2], sem.at[0, h % 2])

    def leave(h):
        return dma(out_ref.at[h % 2], g_hbm.at[h], sem.at[1, h % 2])

    for h in range(low, high):
        bring(h).start()
        if h == min(begin + 3, high - 1):
            enter(begin).start()
    load.wait()
    for t in range(49):
        taps[t] = jnp.broadcast_to(small_ref[t : t + 1, :], (8, D))
    mix = mix_ref[...][None]
    others = 1.0 - mix
    for h in range(low, min(begin + 3, high)):
        bring(h).wait()

    def row(h, _):
        s = h % 2

        @pl.when(h + 1 < end)
        def _():
            enter(h + 1).start()

        @pl.when(h + 3 < high)
        def _():
            bring(h + 3).wait()

        @pl.when(h >= begin + 2)
        def _():
            leave(h - 2).wait()

        enter(h).wait()
        for t in range(imgs // 8):
            at = pl.ds(t * 8, 8)
            for g in range(D // 128):
                lanes = pl.ds(g * 128, 128)
                base = [res_ref[s, w, at, lanes] for w in range(side)]
                acc = conv_rows(conv_ref, taps, h, at, lanes, side, base, True)
                for w in range(side):
                    out_ref[s, w, at, lanes] = acc[w]
        v = out_ref[s]
        part = (others * v).reshape(side * imgs, D)
        upper = part.astype(BF16)
        lower = (part - upper.astype(F32)).astype(BF16)
        back = jnp.dot(sel_ref[...], upper, preferred_element_type=F32)
        back = back + jnp.dot(sel_ref[...], lower, preferred_element_type=F32)
        out_ref[s] = mix * v + back.reshape(side, imgs, D)
        leave(h).start()
        return 0

    lax.fori_loop(begin, end, row, 0)
    for h in range(end - 2, end):
        leave(h).wait()


def images_back(conv, small, mix, sel, res, begin, end, so_far=(), after=()):
    side, _, imgs, _ = conv.shape
    return kernel_call(
        functools.partial(images_kernel, begin, end),
        [far(conv.shape, F32)],
        [HBM, HBM, VMEM, VMEM, HBM] + [HBM] * len(so_far),
        [
            pltpu.VMEM(small.shape, F32),
            pltpu.VMEM(conv.shape, F32),
            pltpu.VMEM((49, 8, D), F32),
            pltpu.VMEM((2, side, imgs, D), F32),
            pltpu.VMEM((2, side, imgs, D), F32),
            pltpu.SemaphoreType.DMA((2, 2)),
            pltpu.SemaphoreType.DMA((side + 1,)),
        ],
        (conv, small, mix, sel, res) + tuple(so_far),
        after,
        22 * (end - begin) / side,
        16,
        {5: 0} if so_far else {},
    )[0]


def join_kernel(first_ref, second_ref, *rest):
    out_ref = rest[-1]
    k = first_ref.shape[0]
    out_ref[:k] = first_ref[...]
    out_ref[k:] = second_ref[...]


def join(first, second, after=()):
    return kernel_call(
        join_kernel,
        [near((2 * first.shape[0],) + first.shape[1:], first.dtype)],
        [VMEM] * 2,
        [],
        (first, second),
        after,
        0.5,
        8,
    )[0]


def fold_kernel(keep_ref, come_ref, *rest):
    stay_ref, leave_ref = rest[-2:]
    k = stay_ref.shape[0]
    stay_ref[...] = keep_ref[:k].astype(F32) + come_ref[:k].astype(F32)
    leave_ref[...] = (keep_ref[k:].astype(F32) + come_ref[k:].astype(F32)).astype(BF16)


def last_kernel(keep_ref, come_ref, *rest):
    sum_ref, square_ref = rest[-2:]
    total = keep_ref[...].astype(F32) + come_ref[...].astype(F32)
    sum_ref[...] = total
    square_ref[...] = jnp.sum(total[0] * total[0], axis=0, keepdims=True)


def fold(keep, come, after=()):
    slots = keep.shape[0]
    rest = keep.shape[1:]
    if slots == 1:
        body = last_kernel
        out = [near(keep.shape, F32), near((1, rest[1]), F32)]
    else:
        body = fold_kernel
        out = [near((slots // 2,) + rest, F32), near((slots // 2,) + rest, BF16)]
    return kernel_call(body, out, [VMEM] * 2, [], (keep, come), after, 0.5, 12)


def swap(x, bit, n):
    return lax.ppermute(x, "dp", [(i, i ^ bit) for i in range(n)])


def is_set(bit):
    return (lax.axis_index("dp") & bit) != 0


def gather_natural(shard, n, order):
    have = shard
    met = []
    for bit in order:
        other = swap(have, bit, n)
        axis = sum(1 for b in met if b > bit)
        mine = is_set(bit)
        have = jnp.stack([jnp.where(mine, other, have), jnp.where(mine, have, other)], axis=axis)
        met.append(bit)
    return have.reshape((n,) + shard.shape)


def scatter_natural(total, n, order):
    left = sorted(order, reverse=True)
    have = total.reshape((2,) * len(left) + total.shape[1:])
    for bit in order:
        axis = left.index(bit)
        mine = is_set(bit).astype(jnp.int32)
        keep = lax.dynamic_index_in_dim(have, mine, axis, keepdims=False)
        send = lax.dynamic_index_in_dim(have, 1 - mine, axis, keepdims=False)
        have = keep.astype(F32) + swap(send.astype(BF16), bit, n).astype(F32)
        left.remove(bit)
    return have


def masks_of(n, order):
    masks = np.zeros(n, np.int32)
    for k, bit in enumerate(order):
        masks += ((np.arange(n, dtype=np.int32) >> k) & 1) * bit
    return masks


def adamw_step(weight, first_mom, second, gradient, step_rate, decay_rate):
    first_mom = BETA_ONE * first_mom + (1.0 - BETA_ONE) * gradient
    second = BETA_TWO * second + (1.0 - BETA_TWO) * gradient * gradient
    first_hat = first_mom / (1.0 - BETA_ONE**STEP)
    second_hat = second / (1.0 - BETA_TWO**STEP)
    weight = weight - step_rate * (first_hat / (jnp.sqrt(second_hat) + ADAM_EPS) + decay_rate * weight)
    return (first_mom, second, weight)


def local(n, images, mix_weight, partner, keep_mask, cotangent, weight_in, weight_out, weight_down, small_params,
          first_in, second_in, first_out, second_out, first_down, second_down, first_small, second_small):
    imgs, side = images.shape[:2]
    half = side // 2
    pixels = side * side * imgs
    me = lax.axis_index("dp")
    bits = [1 << k for k in range(n.bit_length() - 1)]
    deep = FF // n
    aligned = deep % 16 == 0
    p_order = bits[::-1]
    w_order = bits[:2:-1] + [2, 4, 1]
    p_masks = masks_of(n, p_order)
    w_masks = masks_of(n, w_order)

    small = small_params.astype(BF16)
    pair = jnp.concatenate([weight_in, weight_out], axis=1).astype(BF16)[None]
    down = weight_down.astype(BF16)[None]
    small = gather_natural(small, n, bits[1:] + bits[:1]).reshape(-1, D).astype(F32)
    hb = jnp.take(small[HIDDEN_BIAS:OUT_BIAS].reshape(n, deep), me ^ p_masks, axis=0).reshape(1, FF)
    db = small[DOWN_BIAS:].reshape(1, 2 * D)
    spot = jnp.arange(side * imgs, dtype=jnp.int32)
    target = jnp.tile(partner - me * imgs, side) + (spot // imgs) * imgs
    sel = (target[:, None] == spot[None, :]).astype(BF16)
    selt = (target[None, :] == spot[:, None]).astype(BF16)
    mix = jnp.broadcast_to(mix_weight[:, None], (imgs, D))
    keep = jnp.broadcast_to((keep_mask.astype(F32) / (1.0 - DROP_RATE))[:, None], (imgs, D))

    img = images.transpose(1, 2, 0, 3)
    dy = cotangent.transpose(1, 2, 0, 3)
    flat = lambda a: a.reshape(pixels, a.shape[-1])
    paired = lambda a: a.reshape(half, 2, half, 2, imgs, a.shape[-1])
    square = lambda a: a.reshape(side, side, imgs, a.shape[-1])
    def grow(have, order, hop, after=()):
        return join(have, swap(have, order[hop], n), after)

    last = len(bits) - 1
    for hop in range(last - 1):
        pair = grow(pair, p_order, hop)
    for hop in range(last - 2):
        down = grow(down, w_order, hop)
    mixed, *first = conv_forward(small, (img, sel, mix), 0, half)
    pair = grow(pair, p_order, last - 1, first[2:3])
    down = grow(down, w_order, last - 2, first[2:3])
    unit1, inv1, norm1 = conv_forward(small, (mixed,), half, side, tuple(first), (pair, down))
    pair = tuple(x.reshape(FF // 2, 2 * D) for x in (pair, swap(pair, 1, n)))
    act, dg, branch, unit2, inv2, norm2 = hidden_forward(flat(norm1), flat(mixed), pair, small, hb, keep)
    down = grow(down, w_order, last - 1, (norm2,))
    far_down = swap(down, 1, n)
    if aligned:
        origin = me ^ w_masks
        down = tuple(x.reshape(2 * D, 2 * D) for x in (down, far_down))
    else:
        origin = jnp.arange(32, dtype=jnp.int32)
        down = jnp.take(jnp.concatenate([down, far_down]), jnp.asarray(np.argsort(w_masks))[me ^ np.arange(n, dtype=np.int32)], axis=0)
        down = down.reshape(2, 2 * D, 2 * D)

    gd_near, gd_far, gdb = grad_down(origin, paired(norm2), dy, (down[0],))
    out, bb, sums2, res = down_both(
        origin, paired(norm2), paired(unit2), paired(inv2), paired(branch), down, dy, small, keep, db, (gd_near,)
    )
    shards = (n // 2, deep, 2 * D)
    if aligned:
        d_keep = gd_near.reshape(shards)
        d_come = swap(gd_far.reshape(shards), 1, n)
        d_keep, d_send = fold(d_keep, d_come, (bb,))
        d_come = swap(d_send, w_order[-2], n)
    g_near, g_far, ghb, p = pair_grad(flat(bb), act, dg, flat(norm1), pair, imgs, (d_send,) if aligned else ())
    p_keep = g_near.reshape(shards)
    p_come = swap(g_far.reshape(shards), 1, n)
    gate = ()
    if aligned:
        d_keep, d_send = fold(d_keep, d_come, (g_near,))
        d_come = swap(d_send, w_order[-3], n)
        gate = (d_send,)
    back_conv, sums1 = back_one(p, flat(unit1), flat(inv1), pair, small, imgs, gate)
    back_conv = square(back_conv)
    p_keep, p_send = fold(p_keep, p_come, (sums1,))
    p_come = swap(p_send, p_order[-2], n)
    gate = (p_send,)
    if aligned:
        d_keep, d_send = fold(d_keep, d_come, (sums1,))
        d_come = swap(d_send, w_order[-4], n)
        gate = (p_send, d_send)
    part = images_back(back_conv, small, mix, selt, square(res), 0, half, (), gate)
    p_keep, p_send = fold(p_keep, p_come, (part,))
    p_come = swap(p_send, p_order[-3], n)
    gate = (p_send,)
    if aligned:
        d_keep, d_send = fold(d_keep, d_come, (part,))
        d_come = swap(d_send, w_order[-5], n)
        gate = (p_send, d_send)
    images_grad = images_back(back_conv, small, mix, selt, square(res), half, side, (part,), gate)
    p_keep, p_send = fold(p_keep, p_come, (images_grad,))
    p_come = swap(p_send, p_order[-4], n)
    gate = (p_send,)
    if aligned:
        gd, gd_squares = fold(d_keep, d_come, (images_grad,))
        gate = (p_send, gd)
    gk1 = taps_grad(back_conv, mixed, (0, 1), gate)
    p_keep, p_send = fold(p_keep, p_come, (gk1,))
    p_come = swap(p_send, p_order[-5], n)
    gk2 = taps_grad(back_conv, mixed, (2,), (p_send,))
    for bit in p_order[-6::-1]:
        p_keep, p_send = fold(p_keep, p_come)
        p_come = swap(p_send, bit, n)
    gp, gp_squares = fold(p_keep, p_come, (gk2,))
    if not aligned:
        gd = jnp.concatenate([gd_near, gd_far]).reshape(n, deep, 2 * D)
        gd = scatter_natural(gd, n, w_order[::-1])[None]
        gd_squares = jnp.sum(gd[0] * gd[0], axis=0, keepdims=True)
    gd = gd[0]
    gi, go = gp[0, :, :D], gp[0, :, D:]

    one = jnp.sum(sums1, axis=1)
    two = jnp.sum(sums2, axis=1)
    ghb = jnp.take(jnp.sum(ghb, axis=0).reshape(n, deep), jnp.asarray(p_masks)[me ^ np.arange(n, dtype=np.int32)], axis=0)
    total = jnp.concatenate(
        [
            jnp.concatenate([gk1, gk2], axis=2).reshape(49, D),
            one[2:3],
            one[0:2],
            ghb.reshape(4, D),
            two[3:4],
            two[2:3],
            two[0:2],
            jnp.sum(gdb, axis=0).reshape(2, D),
            (gp_squares + gd_squares).reshape(2, D),
        ],
        axis=0,
    )
    for bit in p_order:
        total = total + swap(total, bit, n)
    used = DOWN_BIAS + 2
    gs = total[:used]
    grad_norm = jnp.sqrt(jnp.sum(gs * gs) + jnp.sum(total[used:]))
    factor = CLIP_NORM / jnp.maximum(grad_norm, CLIP_NORM)
    shard_len = small_params.shape[0]
    gs = lax.dynamic_slice_in_dim(gs.reshape(-1), me * shard_len, shard_len)
    position = me * shard_len + jnp.arange(shard_len, dtype=jnp.int32)
    small_rate = jnp.where(position < 54 * D + FF, LAYER_DECAY * RATE_VECTOR, RATE_VECTOR)
    small_decay = jnp.where(position < 49 * D, WEIGHT_DECAY, 0.0)
    new_in = adamw_step(weight_in, first_in, second_in, gi * factor, LAYER_DECAY * RATE_MATRIX, WEIGHT_DECAY)
    new_out = adamw_step(weight_out, first_out, second_out, go * factor, LAYER_DECAY * RATE_MATRIX, WEIGHT_DECAY)
    new_down = adamw_step(weight_down, first_down, second_down, gd * factor, RATE_MATRIX, WEIGHT_DECAY)
    new_small = adamw_step(small_params, first_small, second_small, gs * factor, small_rate, small_decay)
    return (
        out.transpose(2, 0, 1, 3),
        images_grad.transpose(2, 0, 1, 3),
        grad_norm,
        *new_in,
        *new_out,
        *new_down,
        *new_small,
    )


def solution(mesh):
    four = P("dp", None, None, None)
    two = P("dp", None)
    one = P("dp")
    return jax.shard_map(
        functools.partial(local, mesh.shape["dp"]),
        mesh=mesh,
        in_specs=(four, one, one, one, four, two, two, two, one) + (two,) * 6 + (one,) * 2,
        out_specs=(four, four, P()) + (two,) * 9 + (one,) * 3,
        check_vma=False,
    )
```

```python
import functools
import jax
import jax.numpy as jnp
import numpy as np
from jax import lax
from jax.experimental import pallas as pl
from jax.experimental.pallas import tpu as pltpu
from jax.sharding import PartitionSpec as P

STEP = 10
DROP_RATE = 0.2
RATE_MATRIX = 0.05
RATE_VECTOR = 0.3
LAYER_DECAY = 0.8
BETA_ONE = 0.9
BETA_TWO = 0.999
ADAM_EPS = 1e-08
WEIGHT_DECAY = 0.05
CLIP_NORM = 1.0
D = 384
FF = 1536
LN_EPS = 1e-06
F32 = jnp.float32
BF16 = jnp.bfloat16
VMEM = pl.BlockSpec(memory_space=pltpu.VMEM)
SMEM = pl.BlockSpec(memory_space=pltpu.SMEM)
HBM = pl.BlockSpec(memory_space=pltpu.HBM)
ROWS = (((0,), (0,)), ((), ()))
COLS = (((1,), (1,)), ((), ()))
DEPTH_BIAS, GAIN_ONE, BIAS_ONE, HIDDEN_BIAS, OUT_BIAS, LAYER_SCALE, GAIN_TWO, BIAS_TWO, DOWN_BIAS = 49, 50, 51, 52, 56, 57, 58, 59, 60
SQUARES = 62


def near(shape, dtype):
    return jax.ShapeDtypeStruct(shape, dtype)


def far(shape, dtype):
    return pltpu.HBM(shape, dtype)


def held(x):
    return pltpu.with_memory_space_constraint(x, pltpu.HBM)


def dma(src, dst, sem):
    return pltpu.make_async_copy(src, dst, sem)


def start(copies):
    for copy in copies:
        copy.start()


def wait(copies):
    for copy in copies:
        copy.wait()


def kernel_call(body, out, specs, scratch, args, after, us, mib, aliases=None):
    specs = specs + [HBM] * len(after)
    args = tuple(args) + tuple(after)
    args = [held(x) if spec is HBM else x for spec, x in zip(specs, args)]
    return pl.pallas_call(
        body,
        out_shape=tuple(out),
        in_specs=specs,
        out_specs=tuple(HBM if isinstance(x, type(far((8, 128), F32))) else VMEM for x in out),
        scratch_shapes=scratch,
        input_output_aliases=aliases or {},
        cost_estimate=pl.CostEstimate(flops=int(us * 1e9), bytes_accessed=0, transcendentals=0),
        compiler_params=pltpu.CompilerParams(vmem_limit_bytes=mib << 20),
    )(*args)


def norm_of(v):
    c = v - jnp.mean(v, axis=-1, keepdims=True)
    inv = lax.rsqrt(jnp.mean(c * c, axis=-1, keepdims=True) + LN_EPS)
    return c * inv, inv


def norm_back(back, unit, inv, gain):
    scaled = back * gain
    m1 = jnp.mean(scaled, axis=-1, keepdims=True)
    m2 = jnp.mean(scaled * unit, axis=-1, keepdims=True)
    return inv * (scaled - m1 - unit * m2)


def conv_rows(src, taps, h, t, lanes, side, base, flip):
    def one(ky, acc):
        acc = list(acc)
        x = [src[h + ky - 3, w, t, lanes] for w in range(side)]
        for kx in range(7):
            tap = taps[48 - (ky * 7 + kx) if flip else ky * 7 + kx, :, lanes]
            for w in range(side):
                if 0 <= w + kx - 3 < side:
                    acc[w] = acc[w] + x[w + kx - 3] * tap
        return tuple(acc)

    first = jnp.maximum(3 - h, 0)
    last = jnp.minimum(7, side + 3 - h)
    return lax.fori_loop(first, last, one, tuple(base))


def spread(scalars_ref, rows_ref):
    for i in range(rows_ref.shape[0]):
        rows_ref[i : i + 1, :] = jnp.full((1, rows_ref.shape[1]), scalars_ref[i], F32)


def select(row_ref, sel_ref):
    imgs, wide = row_ref.shape
    lane = lax.broadcasted_iota(jnp.int32, (imgs, wide), 1)
    for w in range(wide // imgs):
        sel_ref[w * imgs : (w + 1) * imgs, :] = (lane == row_ref[...] + w * imgs).astype(F32).astype(BF16)


def conv_kernel(begin, end, fresh, *refs):
    if fresh:
        small_hbm, img_hbm, partner_ref, weight_ref = refs[:4]
        mixed_hbm, unit_hbm, inv_hbm, norm_hbm, small_ref, mixed_ref, taps, conv_ref, unit_ref, inv_ref, norm_ref, sem, img_ref, mix_ref, row_ref, sel_ref = refs[-16:]
    else:
        small_hbm, mixed_hbm = refs[:2]
        unit_hbm, inv_hbm, norm_hbm, small_ref, mixed_ref, taps, conv_ref, unit_ref, inv_ref, norm_ref, sem = refs[-11:]
    side, _, imgs, _ = mixed_ref.shape
    low = max(begin - 3, 0)
    high = side if fresh else min(end + 3, side)
    rows = end - begin
    load = dma(small_hbm, small_ref, sem.at[4, 0])
    load.start()

    def enter(h):
        if fresh:
            return dma(img_hbm.at[h], img_ref.at[h], sem.at[3, h])
        return dma(mixed_hbm.at[h], mixed_ref.at[h], sem.at[3, h])

    def store(h):
        return dma(mixed_ref.at[h], mixed_hbm.at[h], sem.at[5, h])

    for h in range(low, high):
        enter(h).start()
    if fresh:
        spread(weight_ref, mix_ref)
        for i in range(imgs):
            row_ref[i : i + 1, :] = jnp.full((1, row_ref.shape[1]), lax.rem(partner_ref[i], imgs), jnp.int32)
        select(row_ref, sel_ref)
    load.wait()
    for t in range(49):
        taps[t] = jnp.broadcast_to(small_ref[t : t + 1, :], (8, D))
    if fresh:
        mix = mix_ref[...][None]
        rest = 1.0 - mix

        def blend(h, _):
            enter(h).wait()
            x = img_ref[h].reshape(side * imgs, D)
            other = jnp.dot(sel_ref[...], x, preferred_element_type=F32).reshape(side, imgs, D)
            mixed_ref[h] = mix * x.reshape(side, imgs, D).astype(F32) + rest * other
            store(h).start()
            return 0

        lax.fori_loop(0, side, blend, 0)
    else:
        for h in range(low, min(begin + 3, high)):
            enter(h).wait()

    def conv(r, _):
        h = r + begin
        if not fresh:

            @pl.when(h + 3 < high)
            def _():
                enter(h + 3).wait()

        for t in range(imgs // 8):
            at = pl.ds(t * 8, 8)
            for g in range(D // 128):
                lanes = pl.ds(g * 128, 128)
                base = jnp.broadcast_to(small_ref[DEPTH_BIAS : DEPTH_BIAS + 1, lanes], (8, 128))
                acc = conv_rows(mixed_ref, taps, h, at, lanes, side, [base] * side, False)
                for w in range(side):
                    conv_ref[r, w, at, lanes] = acc[w]
        return 0

    lax.fori_loop(0, rows, conv, 0)
    gain = small_ref[GAIN_ONE : GAIN_ONE + 1, :][None]
    bias = small_ref[BIAS_ONE : BIAS_ONE + 1, :][None]

    def leave(r):
        return (
            dma(unit_ref.at[r], unit_hbm.at[r + begin], sem.at[0, r]),
            dma(inv_ref.at[r], inv_hbm.at[r + begin], sem.at[1, r]),
            dma(norm_ref.at[r], norm_hbm.at[r + begin], sem.at[2, r]),
        )

    def norm(r, _):
        unit, inv = norm_of(conv_ref[r])
        unit_ref[r] = unit.astype(BF16)
        inv_ref[r] = inv
        norm_ref[r] = (unit * gain + bias).astype(BF16)
        start(leave(r))
        return 0

    lax.fori_loop(0, rows, norm, 0)
    for r in range(rows):
        wait(leave(r))
    if fresh:
        for h in range(side):
            store(h).wait()


def conv_forward(small, inputs, begin, end, so_far=(), after=()):
    fresh = not so_far
    full = inputs[0].shape
    side = full[0]
    thin = full[:3] + (1,)
    rows = end - begin
    out = [far(full, BF16), far(thin, F32), far(full, BF16)]
    scratch = [
        pltpu.VMEM(small.shape, F32),
        pltpu.VMEM(full, F32),
        pltpu.VMEM((49, 8, D), F32),
        pltpu.VMEM((rows,) + full[1:], F32),
        pltpu.VMEM((rows,) + full[1:], BF16),
        pltpu.VMEM((rows,) + thin[1:], F32),
        pltpu.VMEM((rows,) + full[1:], BF16),
        pltpu.SemaphoreType.DMA((6, side)),
    ]
    specs = [HBM] * 2
    if fresh:
        out = [far(full, F32)] + out
        wide = side * full[2]
        scratch += [pltpu.VMEM(full, BF16), pltpu.VMEM((full[2], D), F32), pltpu.VMEM((full[2], wide), jnp.int32), pltpu.VMEM((wide, wide), BF16)]
        specs = [HBM] * 2 + [SMEM] * 2
    return kernel_call(
        functools.partial(conv_kernel, begin, end, fresh),
        out,
        specs + [HBM] * len(so_far),
        scratch,
        (small,) + tuple(inputs) + tuple(so_far),
        after,
        21 * rows / side + 3 * fresh,
        28,
        {2 + k: k for k in range(len(so_far))},
    )


def assembly(origin_ref, near_hbm, far_hbm, whole_ref, sem):
    pieces = origin_ref.shape[0]
    deep = whole_ref.shape[0] // pieces

    def copy(j, src, k):
        to = pl.ds(pl.multiple_of(origin_ref[j] * deep, 16), deep)
        return dma(src.at[pl.ds(k * deep, deep), :], whole_ref.at[to, :], sem)

    return [copy(j, near_hbm if j < pieces // 2 else far_hbm, j % (pieces // 2)) for j in range(pieces)]


def keep_rows(mask_ref, keep_ref):
    for i in range(keep_ref.shape[0]):
        keep_ref[i : i + 1, :] = jnp.full((1, D), mask_ref[i], jnp.int32).astype(F32) / (1.0 - DROP_RATE)


def hidden_kernel(block, origin_ref, norm_hbm, mixed_hbm, near_hbm, far_hbm, small_hbm, mask_ref, *rest):
    act_hbm, dg_hbm, branch_hbm, unit_hbm, inv_hbm, out_hbm = rest[-20:-14]
    pair_ref, small_ref, keep_ref, norm_ref, mixed_ref, act_ref, dg_ref, branch_ref, unit_ref, inv_ref, out_ref, isem, osem, wsem = rest[-14:]
    rows = norm_hbm.shape[0]
    steps = rows // block
    imgs = keep_ref.shape[0]
    shape = (block // imgs, imgs, D)
    wide = FF // 2

    def spot(i):
        return pl.ds(pl.multiple_of(i * block, block), block)

    def enter(i):
        s = i % 2
        return (
            dma(norm_hbm.at[spot(i), :], norm_ref.at[s], isem.at[0, s]),
            dma(mixed_hbm.at[spot(i), :], mixed_ref.at[s], isem.at[1, s]),
        )

    def leave(i):
        s = i % 2
        pairs = ((act_ref, act_hbm), (dg_ref, dg_hbm), (branch_ref, branch_hbm), (unit_ref, unit_hbm), (inv_ref, inv_hbm), (out_ref, out_hbm))
        return [dma(a.at[s], b.at[spot(i), :], osem.at[k, s]) for k, (a, b) in enumerate(pairs)]

    load = dma(small_hbm, small_ref, wsem.at[0])
    start(enter(0))
    load.start()
    pieces_in = assembly(origin_ref, near_hbm, far_hbm, pair_ref, wsem.at[1])
    start(pieces_in)
    wait(pieces_in)
    load.wait()
    keep_rows(mask_ref, keep_ref)
    scale = (keep_ref[...] * small_ref[LAYER_SCALE : LAYER_SCALE + 1, :])[None]
    gain = small_ref[GAIN_TWO : GAIN_TWO + 1, :][None]
    bias = small_ref[BIAS_TWO : BIAS_TWO + 1, :][None]

    def body(i, _):
        s = i % 2

        @pl.when(i + 1 < steps)
        def _():
            start(enter(i + 1))

        @pl.when(i >= 2)
        def _():
            wait(leave(i - 2))

        wait(enter(i))
        x = norm_ref[s]
        branch = jnp.broadcast_to(small_ref[OUT_BIAS : OUT_BIAS + 1, :], (block, D))
        for j in range(2):
            cols = pl.ds(j * wide, wide)
            bias_row = jnp.concatenate([small_ref[HIDDEN_BIAS + 2 * j + k : HIDDEN_BIAS + 2 * j + k + 1, :] for k in range(2)], axis=1)
            pre = lax.dot_general(x, pair_ref[cols, :D], COLS, preferred_element_type=F32) + bias_row
            phi = 0.5 + 0.5 * lax.erf(pre * 0.7071067811865476)
            bell = jnp.exp2(pre * pre * -0.7213475204444817) * 0.3989422804014327
            act = (pre * phi).astype(BF16)
            act_ref[s, :, cols] = act
            dg_ref[s, :, cols] = (phi + pre * bell).astype(BF16)
            branch = branch + jnp.dot(act, pair_ref[cols, D:], preferred_element_type=F32)
        branch_ref[s] = branch.astype(BF16)
        unit, inv = norm_of(mixed_ref[s].reshape(shape) + scale * branch.reshape(shape))
        unit_ref[s] = unit.astype(BF16).reshape(block, D)
        inv_ref[s] = inv.reshape(block, 1)
        out_ref[s] = (unit * gain + bias).astype(BF16).reshape(block, D)
        start(leave(i))
        return 0

    lax.fori_loop(0, steps, body, 0)
    for i in range(max(steps - 2, 0), steps):
        wait(leave(i))


def hidden_forward(origin, norm, mixed, pair, small, mask, after=(), block=448):
    rows = norm.shape[0]
    two = lambda width, dtype: pltpu.VMEM((2, block, width), dtype)
    return kernel_call(
        functools.partial(hidden_kernel, block),
        [far((rows, FF), BF16)] * 2 + [far((rows, D), BF16)] * 2 + [far((rows, 1), F32), far((rows, D), BF16)],
        [SMEM] + [HBM] * 5 + [SMEM],
        [pltpu.VMEM((FF, 2 * D), BF16), pltpu.VMEM(small.shape, F32), pltpu.VMEM((mask.shape[0], D), F32)]
        + [two(D, BF16), two(D, F32), two(FF, BF16), two(FF, BF16)]
        + [two(D, BF16), two(D, BF16), two(1, F32), two(D, BF16)]
        + [pltpu.SemaphoreType.DMA((2, 2)), pltpu.SemaphoreType.DMA((6, 2)), pltpu.SemaphoreType.DMA((3,))],
        (origin, norm, mixed, *pair, small, mask),
        after,
        17,
        32,
    )


def deal(origin_ref, near_ref, far_ref, read):
    pieces = origin_ref.shape[0]
    deep = 2 * near_ref.shape[0] // pieces
    for half_ref, first in ((near_ref, 0), (far_ref, pieces // 2)):

        def move(j, _):
            begin = pl.multiple_of(origin_ref[first + j] * deep, 16)
            to = pl.multiple_of(j * deep, 16)
            for g in range(half_ref.shape[1] // 128):
                half_ref[pl.ds(to, deep), pl.ds(g * 128, 128)] = read(pl.ds(begin, deep), g).astype(BF16)
            return 0

        lax.fori_loop(0, pieces // 2, move, 0)


def down_kernel(home_ref, origin_ref, norm_hbm, unit_hbm, inv_hbm, branch_hbm, near_hbm, far_hbm, dy_hbm, small_hbm, mask_ref, *rest):
    gnear_ref, gfar_ref, gdb_ref, out_ref, bb_hbm, sums_ref, res_hbm = rest[-23:-16]
    wd_ref, dy_ref, small_ref, keep_ref, norm_ref, unit_ref, inv_ref, branch_ref, bb_ref, res_ref, acc, wide, wk, wsem, isem, osem = rest[-16:]
    half, _, _, _, imgs, _ = norm_hbm.shape
    rows = half * half * imgs
    loads = [dma(dy_hbm, dy_ref, wsem.at[1]), dma(small_hbm, small_ref, wsem.at[2])]
    pieces_in = assembly(home_ref, near_hbm, far_hbm, wd_ref, wsem.at[0])
    start(pieces_in)
    start(loads)

    def enter(k):
        pairs = ((norm_hbm, norm_ref), (unit_hbm, unit_ref), (inv_hbm, inv_ref), (branch_hbm, branch_ref))
        return [dma(a.at[:, k // 2, :, k % 2], b.at[k], isem.at[j, k]) for j, (a, b) in enumerate(pairs)]

    def leave(k):
        pairs = ((bb_ref, bb_hbm), (res_ref, res_hbm))
        return [dma(a.at[k], b.at[:, k // 2, :, k % 2], osem.at[j, k]) for j, (a, b) in enumerate(pairs)]

    for k in range(4):
        start(enter(k))
    wait(pieces_in)
    for g in range(6):
        wide[g] = wd_ref[:, pl.ds(g * 128, 128)].astype(F32)
        for k in range(4):
            wk[k, :, pl.ds(g * 128, 128)] = wide[g, pl.ds(k, D, stride=4), :].astype(BF16)
    sums_ref[...] = jnp.zeros(sums_ref.shape, F32)
    shape = (half * half, imgs, D)
    wait(loads)
    keep_rows(mask_ref, keep_ref)
    for k in range(2):
        acc[:, k * D : (k + 1) * D] = jnp.broadcast_to(small_ref[DOWN_BIAS + k : DOWN_BIAS + k + 1, :], (rows, D))
    gdb_ref[...] = jnp.sum(dy_ref[...].astype(F32).reshape(half * half, imgs, 2 * D), axis=0)
    gain = small_ref[GAIN_TWO : GAIN_TWO + 1, :][None]
    keep = keep_ref[...][None]
    scale = keep * small_ref[LAYER_SCALE : LAYER_SCALE + 1, :][None]

    for k in range(4):
        wait(enter(k))
        dy = dy_ref[...].reshape(rows, 2 * D)
        x = norm_ref[k].reshape(rows, D)
        acc[...] += jnp.dot(x, wk[k], preferred_element_type=F32)
        for g in range(6):
            wide[g, pl.ds(k, D, stride=4), :] = lax.dot_general(
                x, dy[:, g * 128 : (g + 1) * 128], ROWS, preferred_element_type=F32
            )
        back = lax.dot_general(dy, wk[k], COLS, preferred_element_type=F32).reshape(shape)
        unit = unit_ref[k].reshape(shape).astype(F32)
        sums_ref[0] += jnp.sum(back * unit, axis=0)
        sums_ref[1] += jnp.sum(back, axis=0)
        res = norm_back(back, unit, inv_ref[k].reshape(half * half, imgs, 1), gain)
        res_ref[k] = res.reshape(half, half, imgs, D)
        kept = res * keep
        sums_ref[2] += jnp.sum(kept * branch_ref[k].reshape(shape).astype(F32), axis=0)
        bb = (res * scale).astype(BF16)
        bb_ref[k] = bb.reshape(half, half, imgs, D)
        start(leave(k))
        sums_ref[3] += jnp.sum(bb.astype(F32), axis=0)

    out_ref[...] = acc[...].astype(BF16).reshape(out_ref.shape)
    deal(origin_ref, gnear_ref, gfar_ref, lambda at, g: wide[g, at, :])
    for k in range(4):
        wait(leave(k))


def down_both(home, origin, norm, unit, inv, branch, wd, dy, small, mask, after=()):
    half, _, _, _, imgs, _ = norm.shape
    rows = half * half * imgs
    four = lambda width, dtype: pltpu.VMEM((4, half, half, imgs, width), dtype)
    return kernel_call(
        down_kernel,
        [near((2 * D, 2 * D), BF16)] * 2
        + [near((imgs, 2 * D), F32), near((half, half, imgs, 2 * D), BF16), far(norm.shape, BF16), near((4, imgs, D), F32), far(norm.shape, F32)],
        [SMEM] * 2 + [HBM] * 8 + [SMEM],
        [pltpu.VMEM((4 * D, 2 * D), BF16), pltpu.VMEM(dy.shape, BF16), pltpu.VMEM(small.shape, F32), pltpu.VMEM((imgs, D), F32)]
        + [four(D, BF16), four(D, BF16), four(1, F32), four(D, BF16), four(D, BF16), four(D, F32)]
        + [pltpu.VMEM((rows, 2 * D), F32), pltpu.VMEM((6, 4 * D, 128), F32), pltpu.VMEM((4, D, 2 * D), BF16)]
        + [pltpu.SemaphoreType.DMA((3,)), pltpu.SemaphoreType.DMA((4, 4)), pltpu.SemaphoreType.DMA((2, 4))],
        (home, origin, norm, unit, inv, branch, *wd, dy, small, mask),
        after,
        20,
        48,
    )


def pair_grad_kernel(block, origin_ref, bb_hbm, act_hbm, dg_hbm, norm_hbm, unit_hbm, inv_hbm, near_hbm, far_hbm, small_hbm, *rest):
    gnear_ref, gfar_ref, hb_ref, sums_ref, conv_hbm = rest[-17:-12]
    pair_ref, small_ref, acc, bb_ref, act_ref, dg_ref, norm_ref, unit_ref, inv_ref, conv_ref, sem, wsem = rest[-12:]
    rows = bb_hbm.shape[0]
    imgs = hb_ref.shape[0]
    steps = rows // block
    wide = FF // 2
    shape = (block // imgs, imgs, D)

    def spot(i):
        return pl.ds(pl.multiple_of(i * block, block), block)

    def enter(i):
        s = i % 2
        pairs = ((act_hbm, act_ref), (dg_hbm, dg_ref), (norm_hbm, norm_ref), (bb_hbm, bb_ref), (unit_hbm, unit_ref), (inv_hbm, inv_ref))
        return [dma(a.at[spot(i), :], b.at[s], sem.at[k, s]) for k, (a, b) in enumerate(pairs)]

    def leave(i):
        return dma(conv_ref.at[i % 2], conv_hbm.at[spot(i), :], sem.at[6, i % 2])

    load = dma(small_hbm, small_ref, wsem.at[0])
    start(enter(0))
    load.start()
    hb_ref[...] = jnp.zeros(hb_ref.shape, F32)
    sums_ref[...] = jnp.zeros(sums_ref.shape, F32)
    acc[...] = jnp.zeros(acc.shape, F32)
    pieces_in = assembly(origin_ref, near_hbm, far_hbm, pair_ref, wsem.at[1])
    start(pieces_in)
    wait(pieces_in)
    load.wait()
    gain = small_ref[GAIN_ONE : GAIN_ONE + 1, :][None]

    def body(i, _):
        s = i % 2

        @pl.when(i + 1 < steps)
        def _():
            start(enter(i + 1))

        @pl.when(i >= 2)
        def _():
            leave(i - 2).wait()

        wait(enter(i))
        b = bb_ref[s]
        x = norm_ref[s]
        back_one = None
        for j in range(2):
            cols = pl.ds(j * wide, wide)
            back = lax.dot_general(b, pair_ref[cols, D:], COLS, preferred_element_type=F32)
            p = (back * dg_ref[s, :, cols].astype(F32)).astype(BF16)
            hb_ref[:, cols] += jnp.sum(p.astype(F32).reshape(block // imgs, imgs, wide), axis=0)
            acc[cols, D:] += lax.dot_general(act_ref[s, :, cols], b, ROWS, preferred_element_type=F32)
            acc[cols, :D] += lax.dot_general(p, x, ROWS, preferred_element_type=F32)
            term = jnp.dot(p, pair_ref[cols, :D], preferred_element_type=F32)
            back_one = term if back_one is None else back_one + term
        back = back_one.reshape(shape)
        unit = unit_ref[s].reshape(shape).astype(F32)
        sums_ref[0] += jnp.sum(back * unit, axis=0)
        sums_ref[1] += jnp.sum(back, axis=0)
        out = norm_back(back, unit, inv_ref[s].reshape(shape[:2] + (1,)), gain)
        sums_ref[2] += jnp.sum(out, axis=0)
        conv_ref[s] = out.reshape(block, D)
        leave(i).start()
        return 0

    lax.fori_loop(0, steps, body, 0)
    deal(origin_ref, gnear_ref, gfar_ref, lambda at, g: acc[at, pl.ds(g * 128, 128)])
    for i in range(max(steps - 2, 0), steps):
        leave(i).wait()


def pair_grad(origin, bb, act, dg, norm, unit, inv, pair, small, imgs, after=(), block=448):
    rows = bb.shape[0]
    two = lambda width, dtype=BF16: pltpu.VMEM((2, block, width), dtype)
    return kernel_call(
        functools.partial(pair_grad_kernel, block),
        [near((FF // 2, 2 * D), BF16)] * 2 + [near((imgs, FF), F32), near((3, imgs, D), F32), far((rows, D), F32)],
        [SMEM] + [HBM] * 9,
        [pltpu.VMEM((FF, 2 * D), BF16), pltpu.VMEM(small.shape, F32), pltpu.VMEM((FF, 2 * D), F32)]
        + [two(D), two(FF), two(FF), two(D), two(D), two(1, F32), two(D, F32)]
        + [pltpu.SemaphoreType.DMA((7, 2)), pltpu.SemaphoreType.DMA((3,))],
        (origin, bb, act, dg, norm, unit, inv, *pair, small),
        after,
        32,
        40,
    )


def taps_kernel(groups, conv_hbm, mixed_hbm, *rest):
    g_ref, conv_ref, mixed_ref, sem = rest[-4:]
    side, _, imgs, _ = conv_hbm.shape

    def enter(k):
        lanes = pl.ds(groups[k] * 128, 128)
        return (
            dma(mixed_hbm.at[:, :, :, lanes], mixed_ref.at[k], sem.at[0, k]),
            dma(conv_hbm.at[:, :, :, lanes], conv_ref.at[k], sem.at[1, k]),
        )

    for k in range(len(groups)):
        start(enter(k))
    for k in range(len(groups)):
        wait(enter(k))

        def per_ky(ky, _):
            first = jnp.maximum(3 - ky, 0)
            last = jnp.minimum(side, side + 3 - ky)

            def row(h, acc):
                acc = list(acc)
                for t in range(imgs // 8):
                    at = pl.ds(t * 8, 8)
                    x = [mixed_ref[k, h + ky - 3, w, at] for w in range(side)]
                    for w in range(side):
                        d = conv_ref[k, h, w, at]
                        for kx in range(7):
                            if 0 <= w + kx - 3 < side:
                                acc[kx] = acc[kx] + x[w + kx - 3] * d
                return tuple(acc)

            acc = lax.fori_loop(first, last, row, (jnp.zeros((8, 128), F32),) * 7)
            for kx in range(7):
                g_ref[ky * 7 + kx, :, pl.ds(k * 128, 128)] = acc[kx]
            return 0

        lax.fori_loop(0, 7, per_ky, 0)


def taps_grad(conv, mixed, groups, after=()):
    lanes = pltpu.VMEM((len(groups),) + conv.shape[:3] + (128,), F32)
    return kernel_call(
        functools.partial(taps_kernel, groups),
        [near((49, 8, 128 * len(groups)), F32)],
        [HBM] * 2,
        [lanes, lanes, pltpu.SemaphoreType.DMA((2, len(groups)))],
        (conv, mixed),
        after,
        4.7 * len(groups),
        20,
    )[0]


def images_kernel(begin, end, conv_hbm, small_hbm, partner_ref, weight_ref, res_hbm, *rest):
    g_hbm, small_ref, conv_ref, taps, res_ref, out_ref, mix_ref, row_ref, sel_ref, sem, csem = rest[-11:]
    side, _, imgs, _ = conv_hbm.shape
    low = max(begin - 3, 0)
    high = min(end + 3, side)
    load = dma(small_hbm, small_ref, csem.at[side])
    load.start()

    def bring(h):
        return dma(conv_hbm.at[h], conv_ref.at[h], csem.at[h])

    def enter(h):
        return dma(res_hbm.at[h], res_ref.at[h % 2], sem.at[0, h % 2])

    def leave(h):
        return dma(out_ref.at[h % 2], g_hbm.at[h], sem.at[1, h % 2])

    for h in range(low, high):
        bring(h).start()
        if h == min(begin + 3, high - 1):
            enter(begin).start()
    spread(weight_ref, mix_ref)
    for i in range(imgs):
        row_ref[pl.ds(lax.rem(partner_ref[i], imgs), 1), :] = jnp.full((1, row_ref.shape[1]), i, jnp.int32)
    select(row_ref, sel_ref)
    load.wait()
    for t in range(49):
        taps[t] = jnp.broadcast_to(small_ref[t : t + 1, :], (8, D))
    mix = mix_ref[...][None]
    others = 1.0 - mix
    for h in range(low, min(begin + 3, high)):
        bring(h).wait()

    def row(h, _):
        s = h % 2

        @pl.when(h + 1 < end)
        def _():
            enter(h + 1).start()

        @pl.when(h + 3 < high)
        def _():
            bring(h + 3).wait()

        @pl.when(h >= begin + 2)
        def _():
            leave(h - 2).wait()

        enter(h).wait()
        for t in range(imgs // 8):
            at = pl.ds(t * 8, 8)
            for g in range(D // 128):
                lanes = pl.ds(g * 128, 128)
                base = [res_ref[s, w, at, lanes] for w in range(side)]
                acc = conv_rows(conv_ref, taps, h, at, lanes, side, base, True)
                for w in range(side):
                    out_ref[s, w, at, lanes] = acc[w]
        v = out_ref[s]
        part = (others * v).reshape(side * imgs, D)
        upper = part.astype(BF16)
        lower = (part - upper.astype(F32)).astype(BF16)
        back = jnp.dot(sel_ref[...], upper, preferred_element_type=F32)
        back = back + jnp.dot(sel_ref[...], lower, preferred_element_type=F32)
        out_ref[s] = mix * v + back.reshape(side, imgs, D)
        leave(h).start()
        return 0

    lax.fori_loop(begin, end, row, 0)
    for h in range(end - 2, end):
        leave(h).wait()


def images_back(conv, small, partner, weight, res, begin, end, so_far=(), after=()):
    side, _, imgs, _ = conv.shape
    return kernel_call(
        functools.partial(images_kernel, begin, end),
        [far(conv.shape, F32)],
        [HBM, HBM, SMEM, SMEM, HBM] + [HBM] * len(so_far),
        [
            pltpu.VMEM(small.shape, F32),
            pltpu.VMEM(conv.shape, F32),
            pltpu.VMEM((49, 8, D), F32),
            pltpu.VMEM((2, side, imgs, D), F32),
            pltpu.VMEM((2, side, imgs, D), F32),
            pltpu.VMEM((imgs, D), F32),
            pltpu.VMEM((imgs, side * imgs), jnp.int32),
            pltpu.VMEM((side * imgs, side * imgs), BF16),
            pltpu.SemaphoreType.DMA((2, 2)),
            pltpu.SemaphoreType.DMA((side + 1,)),
        ],
        (conv, small, partner, weight, res) + tuple(so_far),
        after,
        22 * (end - begin) / side,
        16,
        {5: 0} if so_far else {},
    )[0]


def ready_kernel(in_hbm, out_hbm, down_hbm, *rest):
    pair_ref, low_ref, in_ref, out_ref, down_ref, sem = rest[-6:]
    pairs = ((in_hbm, in_ref), (out_hbm, out_ref), (down_hbm, down_ref))
    copies = [dma(a, b, sem.at[k]) for k, (a, b) in enumerate(pairs)]
    start(copies)
    wait(copies)
    pair_ref[0, :, :D] = in_ref[...].astype(BF16)
    pair_ref[0, :, D:] = out_ref[...].astype(BF16)
    low_ref[0] = down_ref[...].astype(BF16)


def ready(weight_in, weight_out, weight_down, after=()):
    deep = weight_in.shape[0]
    return kernel_call(
        ready_kernel,
        [near((1, deep, 2 * D), BF16)] * 2,
        [HBM] * 3,
        [pltpu.VMEM(x.shape, F32) for x in (weight_in, weight_out, weight_down)] + [pltpu.SemaphoreType.DMA((3,))],
        (weight_in, weight_out, weight_down),
        after,
        0.5,
        8,
    )


def join_kernel(first_ref, second_ref, *rest):
    out_ref = rest[-1]
    k = first_ref.shape[0]
    out_ref[:k] = first_ref[...]
    out_ref[k:] = second_ref[...]


def join(first, second, after=()):
    return kernel_call(
        join_kernel,
        [near((2 * first.shape[0],) + first.shape[1:], first.dtype)],
        [VMEM] * 2,
        [],
        (first, second),
        after,
        0.5,
        8,
    )[0]


def fold_kernel(count, *refs):
    ins, (stay_ref, leave_ref) = refs[: 2 * count], refs[-2:]
    k = stay_ref.shape[0] // count
    for i in range(count):
        keep_ref, come_ref = ins[2 * i], ins[2 * i + 1]
        stay_ref[i * k : (i + 1) * k] = keep_ref[:k].astype(F32) + come_ref[:k].astype(F32)
        leave_ref[i * k : (i + 1) * k] = (keep_ref[k:].astype(F32) + come_ref[k:].astype(F32)).astype(BF16)


def fold(*arrays, after=()):
    slots, deep, wide = arrays[0].shape
    count = len(arrays) // 2
    return kernel_call(
        functools.partial(fold_kernel, count),
        [near((count * slots // 2, deep, wide), F32), near((count * slots // 2, deep, wide), BF16)],
        [VMEM] * len(arrays),
        [],
        arrays,
        after,
        0.5,
        12,
    )


def small_kernel(gk1_ref, gk2_ref, sums1_ref, sums2_ref, hb_ref, db_ref, keep_ref, come_ref, sum_ref, send_ref, total):
    grads = keep_ref[...] + come_ref[...].astype(F32)
    sum_ref[...] = grads
    rows = lambda x: jnp.sum(x, axis=0, keepdims=True)
    for t in range(49):
        total[t : t + 1, :128] = rows(gk1_ref[t])
        total[t : t + 1, 128:] = rows(gk2_ref[t])
    for row, value in (
        (DEPTH_BIAS, sums1_ref[2]),
        (GAIN_ONE, sums1_ref[0]),
        (BIAS_ONE, sums1_ref[1]),
        (OUT_BIAS, sums2_ref[3]),
        (LAYER_SCALE, sums2_ref[2]),
        (GAIN_TWO, sums2_ref[0]),
        (BIAS_TWO, sums2_ref[1]),
    ):
        total[row : row + 1, :] = rows(value)
    for k in range(4):
        total[HIDDEN_BIAS + k : HIDDEN_BIAS + k + 1, :] = rows(hb_ref[:, k * D : (k + 1) * D])
    for k in range(2):
        total[DOWN_BIAS + k : DOWN_BIAS + k + 1, :] = rows(db_ref[:, k * D : (k + 1) * D])
    square = jnp.full((1, D), jnp.sum(grads * grads), F32)
    upper = square.astype(BF16).astype(F32)
    total[SQUARES : SQUARES + 1, :] = upper
    total[SQUARES + 1 : SQUARES + 2, :] = square - upper
    send_ref[...] = total[...].astype(BF16)


def small_total(gk1, gk2, sums1, sums2, hb, db, keep, come):
    return kernel_call(
        small_kernel,
        [near(keep.shape, F32), near((SQUARES + 2, D), BF16)],
        [VMEM] * 8,
        [pltpu.VMEM((SQUARES + 2, D), F32)],
        (gk1, gk2, sums1, sums2, hb, db, keep, come),
        (),
        1,
        8,
    )


def meet_kernel(mine_ref, come_ref, out_ref):
    total = mine_ref[...].astype(F32) + come_ref[...].astype(F32)
    square = total[SQUARES : SQUARES + 1] + total[SQUARES + 1 : SQUARES + 2]
    upper = square.astype(BF16).astype(F32)
    out_ref[...] = total.astype(out_ref.dtype)
    out_ref[SQUARES : SQUARES + 2, :] = jnp.concatenate([upper, square - upper], axis=0).astype(out_ref.dtype)


def meet(mine, come, dtype):
    return kernel_call(meet_kernel, [near(mine.shape, dtype)], [VMEM] * 2, [], (mine, come), (), 0.3, 8)[0]


def adam(weight, first, second, grad, rate, decay):
    first = BETA_ONE * first + (1.0 - BETA_ONE) * grad
    second = BETA_TWO * second + (1.0 - BETA_TWO) * grad * grad
    first_hat = first / (1.0 - BETA_ONE**STEP)
    second_hat = second / (1.0 - BETA_TWO**STEP)
    weight = weight - rate * (first_hat / (jnp.sqrt(second_hat) + ADAM_EPS) + decay * weight)
    return first, second, weight


def adam_kernel(total_ref, grads_ref, *refs):
    ins, outs = refs[:9], refs[9:18]
    norm_ref = refs[18]
    gs = total_ref[:SQUARES]
    norm = jnp.sqrt(jnp.sum(gs * gs) + jnp.sum(total_ref[SQUARES : SQUARES + 2, 0:1]))
    norm_ref[0, 0] = norm
    factor = CLIP_NORM / jnp.maximum(norm, CLIP_NORM)
    grads = (grads_ref[0, :, :D], grads_ref[0, :, D:], grads_ref[1])
    rates = (LAYER_DECAY * RATE_MATRIX, LAYER_DECAY * RATE_MATRIX, RATE_MATRIX)
    for k in range(3):
        new = adam(ins[3 * k][...], ins[3 * k + 1][...], ins[3 * k + 2][...], grads[k] * factor, rates[k], WEIGHT_DECAY)
        for out_ref, value in zip(outs[3 * k : 3 * k + 3], new):
            out_ref[...] = value


def adam_all(total, grads, states):
    return pl.pallas_call(
        adam_kernel,
        out_shape=tuple(near(x.shape, F32) for x in states) + (near((1, 1), F32),),
        in_specs=[VMEM] * 11,
        out_specs=(VMEM,) * 9 + (SMEM,),
        cost_estimate=pl.CostEstimate(flops=int(2e9), bytes_accessed=0, transcendentals=0),
        compiler_params=pltpu.CompilerParams(vmem_limit_bytes=12 << 20),
    )(total, grads, *states)


def swap(x, bit, n):
    return lax.ppermute(x, "dp", [(i, i ^ bit) for i in range(n)])


def is_set(bit):
    return (lax.axis_index("dp") & bit) != 0


def gather_natural(shard, n, order, gates=None):
    have = shard
    met = []
    for hop, bit in enumerate(order):
        if gates and hop in gates:
            have, _ = lax.optimization_barrier((have, gates[hop]))
        other = swap(have, bit, n)
        axis = sum(1 for b in met if b > bit)
        mine = is_set(bit)
        have = jnp.stack([jnp.where(mine, other, have), jnp.where(mine, have, other)], axis=axis)
        met.append(bit)
    return have.reshape((n,) + shard.shape)


def masks_of(n, order):
    masks = np.zeros(n, np.int32)
    for k, bit in enumerate(order):
        masks += ((np.arange(n, dtype=np.int32) >> k) & 1) * bit
    return masks


def local(n, images, mix_weight, partner, keep_mask, cotangent, weight_in, weight_out, weight_down, small_params,
          first_in, second_in, first_out, second_out, first_down, second_down, first_small, second_small):
    imgs, side = images.shape[:2]
    half = side // 2
    pixels = side * side * imgs
    me = lax.axis_index("dp")
    bits = [1 << k for k in range(n.bit_length() - 1)]
    deep = FF // n
    by_hops = n == 32

    pair, down = ready(weight_in, weight_out, weight_down)
    p_origin = d_origin = w_origin = jnp.arange(32, dtype=jnp.int32)
    if by_hops:
        p_order = [16, 8, 4, 2, 1]
        w_order = [16, 8, 2, 4, 1]
        d_order = [16, 2, 8, 4, 1]
        p_origin = me ^ masks_of(n, p_order)
        w_origin = me ^ masks_of(n, w_order)
        d_origin = me ^ masks_of(n, d_order)

    img = images.transpose(1, 2, 0, 3)
    dy = cotangent.transpose(1, 2, 0, 3)
    flat = lambda a: a.reshape(pixels, a.shape[-1])
    paired = lambda a: a.reshape(half, 2, half, 2, imgs, a.shape[-1])
    square = lambda a: a.reshape(side, side, imgs, a.shape[-1])

    cut = [0, 3, 10, side]
    gates = None
    if by_hops:
        gates = {1: pair}
        pair = join(pair, swap(pair, p_order[0], n))
        gates[2] = pair
        down = join(down, swap(down, w_order[0], n))
        gates[3] = down
        pair = join(pair, swap(pair, p_order[1], n))
        gates[4] = pair
    small = gather_natural(small_params.astype(BF16), n, bits[1:] + bits[:1], gates).reshape(-1, D).astype(F32)
    if by_hops:
        down = join(down, swap(down, w_order[1], n))
    mixed, *made = conv_forward(small, (img, partner, mix_weight), cut[0], cut[1])
    for part in (1, 2):
        if by_hops:
            pair = join(pair, swap(pair, p_order[part + 1], n), made[2:3])
            down = join(down, swap(down, w_order[part + 1], n), made[2:3])
        made = conv_forward(small, (mixed,), cut[part], cut[part + 1], tuple(made), (pair, down))
    unit1, inv1, norm1 = made
    if by_hops:
        pair = (pair, swap(pair, p_order[4], n))
        down = (down, swap(down, w_order[4], n))
    else:
        pair, down = (lax.all_gather(x[0], "dp", axis=0, tiled=True).reshape(2, FF // 2, 2 * D) for x in (pair, down))
    pair = tuple(x.reshape(FF // 2, 2 * D) for x in pair)
    down = tuple(x.reshape(FF // 2, 2 * D) for x in down)
    act, dg, branch, unit2, inv2, norm2 = hidden_forward(p_origin, flat(norm1), flat(mixed), pair, small, keep_mask)
    d_near, d_far, gdb, out, bb, sums2, res = down_both(
        w_origin, d_origin, paired(norm2), paired(unit2), paired(inv2), paired(branch), down, dy, small, keep_mask
    )
    shards = (n // 2, deep, 2 * D)
    if by_hops:
        d_keep = d_near.reshape(shards)
        d_come = swap(d_far.reshape(shards), d_order[4], n)
    p_near, p_far, ghb, sums1, back_conv = pair_grad(
        p_origin, flat(bb), act, dg, flat(norm1), flat(unit1), flat(inv1), pair, small, imgs
    )
    back_conv = square(back_conv)
    res = square(res)
    back = functools.partial(images_back, back_conv, small, partner, mix_weight, res)
    if by_hops:
        p_keep = p_near.reshape(shards)
        p_come = swap(p_far.reshape(shards), p_order[4], n)
        d_keep, d_send = fold(d_keep, d_come, after=(sums1,))
        d_come = swap(d_send, d_order[3], n)
        cut = [0, 4, 10, side]
        grad = ()
        for part in range(3):
            grad = (back(cut[part], cut[part + 1], grad, (p_send, d_send) if part else (d_send,)),)
            p_keep, p_send = fold(p_keep, p_come, after=grad)
            p_come = swap(p_send, p_order[3 - part], n)
            if part < 2:
                d_keep, d_send = fold(d_keep, d_come, after=grad)
                d_come = swap(d_send, d_order[2 - part], n)
        gk1 = taps_grad(back_conv, mixed, (0,), (p_send,))
        keep, send = fold(p_keep, p_come, d_keep, d_come, after=(gk1,))
        come = swap(send, p_order[0], n)
        gk2 = taps_grad(back_conv, mixed, (1, 2), (send,))
    else:
        grad = (back(0, side),)
        gk1 = taps_grad(back_conv, mixed, (0,), grad)
        gk2 = taps_grad(back_conv, mixed, (1, 2))
        keep = jnp.stack(
            [
                lax.psum_scatter(jnp.concatenate(x).astype(F32), "dp", scatter_dimension=0, tiled=True)
                for x in ((p_near, p_far), (d_near, d_far))
            ]
        )
        come = jnp.zeros(keep.shape, BF16)

    grads, total = small_total(gk1, gk2, sums1, sums2, ghb, gdb, keep, come)
    for bit in bits[::-1]:
        total = meet(total, swap(total, bit, n), F32 if bit == 1 else BF16)
    states = (weight_in, first_in, second_in, weight_out, first_out, second_out, weight_down, first_down, second_down)
    *news, norm = adam_all(total, grads, states)
    grad_norm = norm[0, 0]
    factor = CLIP_NORM / jnp.maximum(grad_norm, CLIP_NORM)
    shard_len = small_params.shape[0]
    gs = lax.dynamic_slice_in_dim(total[:SQUARES].reshape(-1), me * shard_len, shard_len)
    position = me * shard_len + jnp.arange(shard_len, dtype=jnp.int32)
    small_rate = jnp.where(position < 54 * D + FF, LAYER_DECAY * RATE_VECTOR, RATE_VECTOR)
    small_decay = jnp.where(position < 49 * D, WEIGHT_DECAY, 0.0)
    new_small = adam(small_params, first_small, second_small, gs * factor, small_rate, small_decay)
    return (
        out.transpose(2, 0, 1, 3),
        grad[0].transpose(2, 0, 1, 3),
        grad_norm,
        *news,
        *new_small,
    )


def solution(mesh):
    four = P("dp", None, None, None)
    two = P("dp", None)
    one = P("dp")
    return jax.shard_map(
        functools.partial(local, mesh.shape["dp"]),
        mesh=mesh,
        in_specs=(four, one, one, one, four, two, two, two, one) + (two,) * 6 + (one,) * 2,
        out_specs=(four, four, P()) + (two,) * 9 + (one,) * 3,
        check_vma=False,
    )
```

```python
import functools
import jax
import jax.numpy as jnp
import numpy as np
from jax import lax
from jax.experimental import pallas as pl
from jax.experimental.pallas import tpu as pltpu
from jax.sharding import PartitionSpec as P

STEP = 10
DROP_RATE = 0.2
RATE_MATRIX = 0.05
RATE_VECTOR = 0.3
LAYER_DECAY = 0.8
BETA_ONE = 0.9
BETA_TWO = 0.999
ADAM_EPS = 1e-08
WEIGHT_DECAY = 0.05
CLIP_NORM = 1.0
D = 384
FF = 1536
LN_EPS = 1e-06
F32 = jnp.float32
BF16 = jnp.bfloat16
VMEM = pl.BlockSpec(memory_space=pltpu.VMEM)
SMEM = pl.BlockSpec(memory_space=pltpu.SMEM)
HBM = pl.BlockSpec(memory_space=pltpu.HBM)
ANY = pl.BlockSpec(memory_space=pl.ANY)
ROWS = (((0,), (0,)), ((), ()))
COLS = (((1,), (1,)), ((), ()))
DEPTH_BIAS, GAIN_ONE, BIAS_ONE, HIDDEN_BIAS, OUT_BIAS, LAYER_SCALE, GAIN_TWO, BIAS_TWO, DOWN_BIAS = 49, 50, 51, 52, 56, 57, 58, 59, 60
SQUARES = 62
HALF_PIECES = 16


def near(shape, dtype):
    return jax.ShapeDtypeStruct(shape, dtype)


def far(shape, dtype):
    return pltpu.HBM(shape, dtype)


def held(x):
    return pltpu.with_memory_space_constraint(x, pltpu.HBM)


def dma(src, dst, sem):
    return pltpu.make_async_copy(src, dst, sem)


def start(copies):
    for copy in copies:
        copy.start()


def wait(copies):
    for copy in copies:
        copy.wait()


class Far:
    def __init__(self, array):
        self.array = array


def kernel_call(body, out, specs, scratch, args, after, us, mib, aliases=None):
    specs = specs + [HBM if isinstance(x, Far) else ANY for x in after]
    args = tuple(args) + tuple(x.array if isinstance(x, Far) else x for x in after)
    args = [held(x) if spec is HBM else x for spec, x in zip(specs, args)]
    return pl.pallas_call(
        body,
        out_shape=tuple(out),
        in_specs=specs,
        out_specs=tuple(HBM if isinstance(x, type(far((8, 128), F32))) else VMEM for x in out),
        scratch_shapes=scratch,
        input_output_aliases=aliases or {},
        cost_estimate=pl.CostEstimate(flops=int(us * 1e9), bytes_accessed=0, transcendentals=0),
        compiler_params=pltpu.CompilerParams(vmem_limit_bytes=mib << 20),
    )(*args)


def norm_of(v):
    c = v - jnp.mean(v, axis=-1, keepdims=True)
    inv = lax.rsqrt(jnp.mean(c * c, axis=-1, keepdims=True) + LN_EPS)
    return c * inv, inv


def norm_back(back, unit, inv, gain):
    scaled = back * gain
    m1 = jnp.mean(scaled, axis=-1, keepdims=True)
    m2 = jnp.mean(scaled * unit, axis=-1, keepdims=True)
    return inv * (scaled - m1 - unit * m2)


def every_row(begin, end, side, do):
    for h in range(begin, min(end, 3)):
        do(h, range(3 - h, 7))
    low, high = max(begin, 3), min(end, side - 3)
    if low < high:
        lax.fori_loop(low, high, lambda h, _: do(h, range(7)), 0)
    for h in range(max(begin, side - 3), end):
        do(h, range(side + 3 - h))


def conv_rows(src, sums, taps, h, kys, t, lanes, side, base):
    pairs = side // 2

    def one(ky, acc):
        u, v, w = list(acc[:pairs]), list(acc[pairs : 2 * pairs + 1]), list(acc[2 * pairs + 1 :])
        row = h + ky - 3
        for out, shift, first, count, read in (
            (u, 0, 4, 3, lambda i: src[row, 2 * i, t, lanes]),
            (v, -1, 0, 4, lambda i: src[row, 2 * i + 1, t, lanes]),
            (w, 0, 7, 4, lambda i: sums[row, i, t, lanes]),
        ):
            x = [read(i) for i in range(pairs)]
            for j in range(count):
                tap = taps[ky * 11 + first + j, :, lanes]
                for k in range(len(out)):
                    i = k + shift - 1 + j
                    if 0 <= i < pairs:
                        out[k] = out[k] + x[i] * tap
        return tuple(u + v + w)

    acc = (jnp.zeros((8, 128), F32),) * (3 * pairs + 1)
    for ky in kys:
        acc = one(ky, acc)
    u, v, w = acc[:pairs], acc[pairs : 2 * pairs + 1], acc[2 * pairs + 1 :]
    out = []
    for k in range(pairs):
        out.append(base[2 * k] + (u[k] + v[k]))
        out.append(base[2 * k + 1] + (w[k] - (u[k] + v[k + 1])))
    return out


def fill_taps(small_ref, taps, flip):
    for ky in range(7):
        rows = []
        for kx in range(7):
            k = 48 - (ky * 7 + kx) if flip else ky * 7 + kx
            rows.append(small_ref[k : k + 1, :])
        rows = rows[0::2] + rows[1::2] + [rows[2 * j] + rows[2 * j + 1] for j in range(3)] + [rows[6]]
        for k, value in enumerate(rows):
            taps[ky * 11 + k] = jnp.broadcast_to(value, (8, D))


def add_columns(src, sums, row):
    pairs = sums.shape[1]
    sums[row] = jnp.stack([src[row, 2 * i] + src[row, 2 * i + 1] for i in range(pairs)])


def spread(scalars_ref, rows_ref):
    for i in range(rows_ref.shape[0]):
        rows_ref[i : i + 1, :] = jnp.full((1, rows_ref.shape[1]), scalars_ref[i], F32)


def select(row_ref, sel_ref):
    imgs, wide = row_ref.shape
    lane = lax.broadcasted_iota(jnp.int32, (imgs, wide), 1)
    for w in range(wide // imgs):
        sel_ref[w * imgs : (w + 1) * imgs, :] = (lane == row_ref[...] + w * imgs).astype(F32).astype(BF16)


def conv_kernel(begin, end, fresh, *refs):
    if fresh:
        small_hbm, img_hbm, partner_ref, weight_ref = refs[:4]
        mixed_hbm, unit_hbm, inv_hbm, norm_hbm, token_ref, small_ref, mixed_ref, taps, conv_ref, unit_ref, inv_ref, norm_ref, sem, pair_sums, img_ref, mix_ref, row_ref, sel_ref = refs[-18:]
    else:
        small_hbm, mixed_hbm = refs[:2]
        unit_hbm, inv_hbm, norm_hbm, token_ref, small_ref, mixed_ref, taps, conv_ref, unit_ref, inv_ref, norm_ref, sem, pair_sums = refs[-13:]
    side, _, imgs, _ = mixed_ref.shape
    low = max(begin - 3, 0)
    high = side if fresh else min(end + 3, side)
    rows = end - begin
    load = dma(small_hbm, small_ref, sem.at[4, 0])
    load.start()
    token_ref[...] = jnp.zeros(token_ref.shape, F32)

    def enter(h):
        if fresh:
            return dma(img_hbm.at[h], img_ref.at[h], sem.at[3, h])
        return dma(mixed_hbm.at[h], mixed_ref.at[h], sem.at[3, h])

    def store(h):
        return dma(mixed_ref.at[h], mixed_hbm.at[h], sem.at[5, h])

    for h in range(low, high):
        enter(h).start()
    if fresh:
        spread(weight_ref, mix_ref)
        for i in range(imgs):
            row_ref[i : i + 1, :] = jnp.full((1, row_ref.shape[1]), lax.rem(partner_ref[i], imgs), jnp.int32)
        select(row_ref, sel_ref)
    load.wait()
    fill_taps(small_ref, taps, False)
    if fresh:
        mix = mix_ref[...][None]
        rest = 1.0 - mix

        def blend(h, _):
            enter(h).wait()
            x = img_ref[h].reshape(side * imgs, D)
            other = jnp.dot(sel_ref[...], x, preferred_element_type=F32).reshape(side, imgs, D)
            mixed_ref[h] = mix * x.reshape(side, imgs, D).astype(F32) + rest * other
            add_columns(mixed_ref, pair_sums, h)
            store(h).start()
            return 0

        lax.fori_loop(0, side, blend, 0)
    else:
        for h in range(low, min(begin + 3, high)):
            enter(h).wait()
            add_columns(mixed_ref, pair_sums, h)

    def conv(h, kys):
        r = h - begin
        if not fresh:

            @pl.when(h + 3 < high)
            def _():
                enter(h + 3).wait()
                add_columns(mixed_ref, pair_sums, h + 3)

        for t in range(imgs // 8):
            at = pl.ds(t * 8, 8)
            for g in range(D // 128):
                lanes = pl.ds(g * 128, 128)
                base = jnp.broadcast_to(small_ref[DEPTH_BIAS : DEPTH_BIAS + 1, lanes], (8, 128))
                acc = conv_rows(mixed_ref, pair_sums, taps, h, kys, at, lanes, side, [base] * side)
                for w in range(side):
                    conv_ref[r, w, at, lanes] = acc[w]
        return 0

    every_row(begin, end, side, conv)
    gain = small_ref[GAIN_ONE : GAIN_ONE + 1, :][None]
    bias = small_ref[BIAS_ONE : BIAS_ONE + 1, :][None]

    def leave(r):
        return (
            dma(unit_ref.at[r], unit_hbm.at[r + begin], sem.at[0, r]),
            dma(inv_ref.at[r], inv_hbm.at[r + begin], sem.at[1, r]),
            dma(norm_ref.at[r], norm_hbm.at[r + begin], sem.at[2, r]),
        )

    for r in range(rows):
        unit, inv = norm_of(conv_ref[r])
        unit_ref[r] = unit.astype(BF16)
        inv_ref[r] = inv
        norm_ref[r] = (unit * gain + bias).astype(BF16)
        start(leave(r))
    for r in range(rows):
        wait(leave(r))
    if fresh:
        for h in range(side):
            store(h).wait()


def conv_forward(small, inputs, begin, end, so_far=(), after=()):
    fresh = not so_far
    full = inputs[0].shape
    side = full[0]
    thin = full[:3] + (1,)
    rows = end - begin
    out = [far(full, BF16), far(thin, F32), far(full, BF16), near((8, 128), F32)]
    scratch = [
        pltpu.VMEM(small.shape, F32),
        pltpu.VMEM(full, F32),
        pltpu.VMEM((77, 8, D), F32),
        pltpu.VMEM((rows,) + full[1:], F32),
        pltpu.VMEM((rows,) + full[1:], BF16),
        pltpu.VMEM((rows,) + thin[1:], F32),
        pltpu.VMEM((rows,) + full[1:], BF16),
        pltpu.SemaphoreType.DMA((6, side)),
        pltpu.VMEM((side, side // 2) + full[2:], F32),
    ]
    specs = [HBM] * 2
    if fresh:
        out = [far(full, F32)] + out
        wide = side * full[2]
        scratch += [pltpu.VMEM(full, BF16), pltpu.VMEM((full[2], D), F32), pltpu.VMEM((full[2], wide), jnp.int32), pltpu.VMEM((wide, wide), BF16)]
        specs = [HBM] * 2 + [SMEM] * 2
    return kernel_call(
        functools.partial(conv_kernel, begin, end, fresh),
        out,
        specs + [HBM] * len(so_far),
        scratch,
        (small,) + tuple(inputs) + tuple(so_far),
        after,
        21 * rows / side + 3 * fresh,
        36,
        {2 + k: k for k in range(len(so_far))},
    )


def home(me, masks, j, chips):
    if masks is None:
        return j % HALF_PIECES if chips else j
    device = me ^ masks[j]
    return device // 2 if chips else device


def assembly(me, masks, chips, first, src_hbm, whole_ref, sem):
    deep = src_hbm.shape[0] // HALF_PIECES

    def copy(j):
        to = pl.ds(pl.multiple_of(home(me, masks, first + j, chips) * deep, 16), deep)
        return dma(src_hbm.at[pl.ds(j * deep, deep), :], whole_ref.at[to, :], sem)

    return [copy(j) for j in range(HALF_PIECES)]


def keep_rows(mask_ref, keep_ref):
    for i in range(keep_ref.shape[0]):
        keep_ref[i : i + 1, :] = jnp.full((1, D), mask_ref[i], jnp.int32).astype(F32) / (1.0 - DROP_RATE)


def deal(me, masks, chips, first, out_ref, read):
    deep = out_ref.shape[0] // HALF_PIECES
    for j in range(HALF_PIECES):
        begin = pl.multiple_of(home(me, masks, first + j, chips) * deep, 16)
        for g in range(out_ref.shape[1] // 128):
            out_ref[j * deep : (j + 1) * deep, g * 128 : (g + 1) * 128] = read(pl.ds(begin, deep), g).astype(BF16)


def even_first(rows, deep):
    blocks = [rows[d * deep // D][:, d * deep % D : d * deep % D + deep] for d in range(FF // deep)]
    return jnp.concatenate(blocks[0::2] + blocks[1::2], axis=1)


def even_last(even, odd, k, deep):
    per = D // deep
    blocks = []
    for d in range(per * k, per * k + per):
        source = odd if d % 2 else even
        blocks.append(source[:, d // 2 * deep : d // 2 * deep + deep])
    return jnp.concatenate(blocks, axis=1)


def block_kernel(block, masks, me_ref, norm_hbm, mixed_hbm, pnear_hbm, pfar_hbm, wnear_hbm, wfar_hbm, dy_hbm, small_hbm, mask_ref, *rest):
    act_hbm, dg_hbm, gnear_ref, gfar_ref, gdb_ref, out_ref, bb_hbm, sums_ref, res_hbm = rest[-32:-23]
    pair_ref, small_ref, keep_ref, norm_ref, mixed_ref, act_ref, dg_ref, branch_ref, unit_ref, inv_ref, out2_ref = rest[-23:-12]
    wd_ref, dy_ref, bb_ref, res_ref, acc, wide, wk, isem, osem, wsem, bsem, rsem = rest[-12:]
    rows = norm_hbm.shape[0]
    steps = rows // block
    imgs = keep_ref.shape[0]
    shape = (block // imgs, imgs, D)
    half = dy_hbm.shape[0]

    def spot(i):
        return pl.ds(pl.multiple_of(i * block, block), block)

    def enter(i):
        s = i % 2
        return (
            dma(norm_hbm.at[spot(i), :], norm_ref.at[s], isem.at[0, s]),
            dma(mixed_hbm.at[spot(i), :], mixed_ref.at[s], isem.at[1, s]),
        )

    def leave(i):
        s = i % 2
        pairs = ((act_ref, act_hbm), (dg_ref, dg_hbm))
        return [dma(a.at[s], b.at[spot(i), :], osem.at[k, s]) for k, (a, b) in enumerate(pairs)]

    me = me_ref[0]
    p_masks, w_masks, d_masks = masks
    load = dma(small_hbm, small_ref, wsem.at[0])
    start(enter(0))
    load.start()
    half_rows = FF // 2
    mine = 0 if p_masks is None else me % 2
    pair_in = []
    for src, first, which in ((pnear_hbm, 0, mine), (pfar_hbm, HALF_PIECES, 1 - mine)):
        to = pair_ref.at[pl.ds(pl.multiple_of(which * half_rows, half_rows), half_rows), :]
        pair_in += assembly(me, p_masks, True, first, src, to, wsem.at[1])
    start(pair_in)
    down_in = assembly(me, w_masks, False, 0, wnear_hbm, wd_ref, wsem.at[2])
    down_in += assembly(me, w_masks, False, HALF_PIECES, wfar_hbm, wd_ref, wsem.at[2])
    dy_in = dma(dy_hbm, dy_ref, wsem.at[3])
    wait(pair_in)
    start(down_in)
    dy_in.start()
    load.wait()
    keep_rows(mask_ref, keep_ref)
    keep = keep_ref[...][None]
    scale = keep * small_ref[LAYER_SCALE : LAYER_SCALE + 1, :][None]
    gain = small_ref[GAIN_TWO : GAIN_TWO + 1, :][None]
    bias = small_ref[BIAS_TWO : BIAS_TWO + 1, :][None]
    bias_rows = [small_ref[HIDDEN_BIAS + k : HIDDEN_BIAS + k + 1, :] for k in range(FF // D)]
    hidden_bias = jnp.concatenate(bias_rows, axis=1) if p_masks is None else even_first(bias_rows, FF // len(p_masks))
    chunk = FF // 2

    def body(i, _):
        s = i % 2

        @pl.when(i + 1 < steps)
        def _():
            start(enter(i + 1))

        @pl.when(i >= 2)
        def _():
            wait(leave(i - 2))

        wait(enter(i))
        x = norm_ref[s]
        branch = jnp.broadcast_to(small_ref[OUT_BIAS : OUT_BIAS + 1, :], (block, D))

        def hidden(j):
            cols = slice(j * chunk, (j + 1) * chunk)
            return lax.dot_general(x, pair_ref[cols, :D], COLS, preferred_element_type=F32) + hidden_bias[:, cols]

        pre = hidden(0)
        for j in range(FF // chunk):
            after = hidden(j + 1) if j + 1 < FF // chunk else None
            cols = slice(j * chunk, (j + 1) * chunk)
            phi = 0.5 + 0.5 * lax.erf(pre * 0.7071067811865476)
            bell = jnp.exp2(pre * pre * -0.7213475204444817) * 0.3989422804014327
            act = (pre * phi).astype(BF16)
            act_ref[s, :, cols] = act
            dg_ref[s, :, cols] = (phi + pre * bell).astype(BF16)
            branch = branch + jnp.dot(act, pair_ref[cols, D:], preferred_element_type=F32)
            pre = after
        start(leave(i))
        split = branch_ref.shape[1:]
        branch_ref[i] = branch.astype(BF16).reshape(split)
        unit, inv = norm_of(mixed_ref[s].reshape(shape) + scale * branch.reshape(shape))
        unit_ref[i] = unit.astype(BF16).reshape(split)
        inv_ref[i] = inv.reshape(split[:-1] + (1,))
        out2_ref[i] = (unit * gain + bias).astype(BF16).reshape(split)
        return 0

    lax.fori_loop(0, steps, body, 0)

    wait(down_in)
    for g in range(6):
        wide[g] = wd_ref[:, pl.ds(g * 128, 128)].astype(F32)
        for k in range(4):
            wk[k, :, pl.ds(g * 128, 128)] = wide[g, pl.ds(k, D, stride=4), :].astype(BF16)
    sums_ref[...] = jnp.zeros(sums_ref.shape, F32)
    rows = half * half * imgs
    shape = (half * half, imgs, D)
    for k in range(2):
        acc[:, k * D : (k + 1) * D] = jnp.broadcast_to(small_ref[DOWN_BIAS + k : DOWN_BIAS + k + 1, :], (rows, D))
    dy_in.wait()
    gdb_ref[...] = jnp.sum(dy_ref[...].astype(F32).reshape(half * half, imgs, 2 * D), axis=0)

    def give(k):
        pairs = ((bb_ref, bb_hbm), (res_ref, res_hbm))
        return [dma(a.at[k], b.at[:, k // 2, :, k % 2], rsem.at[j, k]) for j, (a, b) in enumerate(pairs)]

    for k in range(4):
        dy = dy_ref[...].reshape(rows, 2 * D)
        x = out2_ref[:, k // 2, :, k % 2].reshape(rows, D)
        back = lax.dot_general(dy, wk[k], COLS, preferred_element_type=F32).reshape(shape)
        acc[...] += jnp.dot(x, wk[k], preferred_element_type=F32)
        gd = lax.dot_general(x, dy, ROWS, preferred_element_type=F32)
        for g in range(6):
            wide[g, pl.ds(k, D, stride=4), :] = gd[:, g * 128 : (g + 1) * 128]
        unit = unit_ref[:, k // 2, :, k % 2].reshape(shape).astype(F32)
        sums_ref[0] += jnp.sum(back * unit, axis=0)
        sums_ref[1] += jnp.sum(back, axis=0)
        res = norm_back(back, unit, inv_ref[:, k // 2, :, k % 2].reshape(half * half, imgs, 1), gain)
        res_ref[k] = res.astype(BF16).reshape(half, half, imgs, D)
        sums_ref[2] += jnp.sum(res * keep * branch_ref[:, k // 2, :, k % 2].reshape(shape).astype(F32), axis=0)
        bb = (res * scale).astype(BF16)
        bb_ref[k] = bb.reshape(half, half, imgs, D)
        start(give(k))
        sums_ref[3] += jnp.sum(bb.astype(F32), axis=0)

    out_ref[...] = acc[...].astype(BF16).reshape(out_ref.shape)
    deal(me, d_masks, False, 0, gnear_ref, lambda at, g: wide[g, at, :])
    deal(me, d_masks, False, HALF_PIECES, gfar_ref, lambda at, g: wide[g, at, :])
    for k in range(4):
        wait(give(k))
    for i in range(max(steps - 2, 0), steps):
        wait(leave(i))


def block_both(masks, me, norm, mixed, pair, down, dy, small, mask, after=(), block=448):
    rows = norm.shape[0]
    half, _, imgs, _ = dy.shape
    area = half * half * imgs
    six = (half, 2, half, 2, imgs)
    two = lambda width, dtype: pltpu.VMEM((2, block, width), dtype)
    whole = lambda width, dtype: pltpu.VMEM(six + (width,), dtype)
    part = pltpu.VMEM((4, half, half, imgs, D), BF16)
    return kernel_call(
        functools.partial(block_kernel, block, masks),
        [far((rows, FF), BF16)] * 2
        + [near((2 * D, 2 * D), BF16)] * 2
        + [near((imgs, 2 * D), F32), near((half, half, imgs, 2 * D), BF16)]
        + [far(six + (D,), BF16), near((4, imgs, D), F32), far(six + (D,), BF16)],
        [SMEM] + [HBM] * 2 + [ANY, HBM] * 2 + [HBM] * 2 + [SMEM],
        [pltpu.VMEM((FF, 2 * D), BF16), pltpu.VMEM(small.shape, F32), pltpu.VMEM((imgs, D), F32)]
        + [two(D, BF16), two(D, F32), two(FF, BF16), two(FF, BF16)]
        + [whole(D, BF16), whole(D, BF16), whole(1, F32), whole(D, BF16)]
        + [pltpu.VMEM((4 * D, 2 * D), BF16), pltpu.VMEM(dy.shape, BF16), part, part]
        + [pltpu.VMEM((area, 2 * D), F32), pltpu.VMEM((6, 4 * D, 128), F32), pltpu.VMEM((4, D, 2 * D), BF16)]
        + [pltpu.SemaphoreType.DMA((2, 2)), pltpu.SemaphoreType.DMA((2, 2)), pltpu.SemaphoreType.DMA((4,))]
        + [pltpu.SemaphoreType.DMA((1,)), pltpu.SemaphoreType.DMA((2, 4))],
        (me, norm, mixed, *pair, *down, dy, small, mask),
        after,
        34,
        58,
    )


def pair_grad_kernel(block, first, masks, me_ref, bb_hbm, act_hbm, dg_hbm, norm_hbm, pair_hbm, *rest):
    g_ref, hb_ref, p_hbm, pair_ref, acc, bb_ref, act_ref, dg_ref, norm_ref, p_ref, sem, osem, wsem = rest[-13:]
    rows = bb_hbm.shape[0]
    imgs = hb_ref.shape[0]
    steps = rows // block
    wide = FF // 2
    me = me_ref[0]
    which = 0 if masks is None else me % 2
    which = 1 - which if first else which
    lanes = pl.ds(pl.multiple_of(which * wide, wide), wide)

    def spot(i):
        return pl.ds(pl.multiple_of(i * block, block), block)

    def enter(i):
        s = i % 2
        return (
            dma(bb_hbm.at[spot(i), :], bb_ref.at[s], sem.at[0, s]),
            dma(dg_hbm.at[spot(i), lanes], dg_ref.at[s], sem.at[1, s]),
            dma(act_hbm.at[spot(i), lanes], act_ref.at[s], sem.at[2, s]),
            dma(norm_hbm.at[spot(i), :], norm_ref.at[s], sem.at[3, s]),
        )

    def leave(i):
        return dma(p_ref.at[i % 2], p_hbm.at[spot(i), :], osem.at[i % 2])

    pair_in = assembly(me, masks, True, first, pair_hbm, pair_ref, wsem.at[0])
    start(pair_in)
    start(enter(0))
    hb_ref[...] = jnp.zeros(hb_ref.shape, F32)
    acc[...] = jnp.zeros(acc.shape, F32)
    wait(pair_in)

    def body(i, _):
        s = i % 2

        @pl.when(i + 1 < steps)
        def _():
            start(enter(i + 1))

        @pl.when(i >= 2)
        def _():
            leave(i - 2).wait()

        wait(enter(i))
        b = bb_ref[s]
        back = lax.dot_general(b, pair_ref[:, D:], COLS, preferred_element_type=F32)
        acc[:, D:] += lax.dot_general(act_ref[s], b, ROWS, preferred_element_type=F32)
        p = (back * dg_ref[s].astype(F32)).astype(BF16)
        p_ref[s] = p
        hb_ref[...] += jnp.sum(p.astype(F32).reshape(block // imgs, imgs, wide), axis=0)
        acc[:, :D] += lax.dot_general(p, norm_ref[s], ROWS, preferred_element_type=F32)
        leave(i).start()
        return 0

    lax.fori_loop(0, steps, body, 0)
    deal(me, masks, True, first, g_ref, lambda at, g: acc[at, pl.ds(g * 128, 128)])
    for i in range(max(steps - 2, 0), steps):
        leave(i).wait()


def pair_grad(first, masks, me, bb, act, dg, norm, pair, imgs, after=(), block=448):
    rows = bb.shape[0]
    wide = FF // 2
    two = lambda width: pltpu.VMEM((2, block, width), BF16)
    return kernel_call(
        functools.partial(pair_grad_kernel, block, first, masks),
        [near((wide, 2 * D), BF16), near((imgs, wide), F32), far((rows, wide), BF16)],
        [SMEM] + [HBM] * 5,
        [pltpu.VMEM((wide, 2 * D), BF16), pltpu.VMEM((wide, 2 * D), F32)]
        + [two(D), two(wide), two(wide), two(D), two(wide)]
        + [pltpu.SemaphoreType.DMA((4, 2)), pltpu.SemaphoreType.DMA((2,)), pltpu.SemaphoreType.DMA((1,))],
        (me, bb, act, dg, norm, pair),
        after,
        13,
        28,
    )


def back_one_kernel(block, masks, me_ref, pnear_hbm, pfar_hbm, unit_hbm, inv_hbm, near_hbm, far_hbm, small_hbm, *rest):
    conv_hbm, sums_ref, near_ref, far_ref, small_ref, pnear_ref, pfar_ref, unit_ref, inv_ref, conv_ref, sem, wsem = rest[-12:]
    rows = pnear_hbm.shape[0]
    imgs = sums_ref.shape[1]
    steps = rows // block
    shape = (block // imgs, imgs, D)

    def spot(i):
        return pl.ds(pl.multiple_of(i * block, block), block)

    def enter(i):
        s = i % 2
        pairs = ((pnear_hbm, pnear_ref), (pfar_hbm, pfar_ref), (unit_hbm, unit_ref), (inv_hbm, inv_ref))
        return [dma(a.at[spot(i), :], b.at[s], sem.at[k, s]) for k, (a, b) in enumerate(pairs)]

    def leave(i):
        return dma(conv_ref.at[i % 2], conv_hbm.at[spot(i), :], sem.at[4, i % 2])

    load = dma(small_hbm, small_ref, wsem.at[0])
    left = pl.ds(0, D)
    pair_in = assembly(me_ref[0], masks, True, 0, near_hbm.at[:, left], near_ref, wsem.at[1])
    pair_in += assembly(me_ref[0], masks, True, HALF_PIECES, far_hbm.at[:, left], far_ref, wsem.at[1])
    start(pair_in)
    start(enter(0))
    load.start()
    sums_ref[...] = jnp.zeros(sums_ref.shape, F32)
    wait(pair_in)
    load.wait()
    gain = small_ref[GAIN_ONE : GAIN_ONE + 1, :][None]

    def body(i, _):
        s = i % 2

        @pl.when(i + 1 < steps)
        def _():
            start(enter(i + 1))

        @pl.when(i >= 2)
        def _():
            leave(i - 2).wait()

        wait(enter(i))
        back = jnp.dot(pnear_ref[s], near_ref[...], preferred_element_type=F32)
        back = (back + jnp.dot(pfar_ref[s], far_ref[...], preferred_element_type=F32)).reshape(shape)
        unit = unit_ref[s].reshape(shape).astype(F32)
        sums_ref[0] += jnp.sum(back * unit, axis=0)
        sums_ref[1] += jnp.sum(back, axis=0)
        out = norm_back(back, unit, inv_ref[s].reshape(shape[:2] + (1,)), gain)
        sums_ref[2] += jnp.sum(out, axis=0)
        conv_ref[s] = out.astype(BF16).reshape(block, D)
        leave(i).start()
        return 0

    lax.fori_loop(0, steps, body, 0)
    for i in range(max(steps - 2, 0), steps):
        leave(i).wait()


def back_one(masks, me, p, unit, inv, pair, small, imgs, after=(), block=784):
    rows = unit.shape[0]
    wide = FF // 2
    two = lambda width, dtype: pltpu.VMEM((2, block, width), dtype)
    return kernel_call(
        functools.partial(back_one_kernel, block, masks),
        [far((rows, D), BF16), near((3, imgs, D), F32)],
        [SMEM] + [HBM] * 7,
        [pltpu.VMEM((wide, D), BF16)] * 2
        + [pltpu.VMEM(small.shape, F32)]
        + [two(wide, BF16), two(wide, BF16), two(D, BF16), two(1, F32), two(D, BF16)]
        + [pltpu.SemaphoreType.DMA((5, 2)), pltpu.SemaphoreType.DMA((2,))],
        (me, *p, unit, inv, *pair, small),
        after,
        11,
        32,
    )


def taps_kernel(groups, conv_hbm, mixed_hbm, *rest):
    g_ref, conv_ref, mixed_ref, sums, even, odd, last, sem = rest[-8:]
    side, _, imgs, _ = conv_hbm.shape
    pairs = side // 2

    def enter(k):
        lanes = pl.ds(groups[k] * 128, 128)
        return (
            dma(mixed_hbm.at[:, :, :, lanes], mixed_ref.at[k], sem.at[0, k]),
            dma(conv_hbm.at[:, :, :, lanes], conv_ref.at[k], sem.at[1, k]),
        )

    for k in range(len(groups)):
        start(enter(k))
    for k in range(len(groups)):
        wait(enter(k))

        def prepare(h, _):
            x = [mixed_ref[k, h, w] for w in range(side)]
            d = [conv_ref[k, h, w].astype(F32) for w in range(side)]
            for i in range(pairs):
                sums[h, i] = x[2 * i] + x[2 * i + 1]
                last[h, i] = d[2 * i + 1]
                even[h, i] = d[2 * i] - d[2 * i + 1]
                odd[h, i + 1] = (d[2 * i + 2] if i + 1 < pairs else jnp.zeros_like(d[0])) - d[2 * i + 1]
            odd[h, 0] = d[0]
            return 0

        lax.fori_loop(0, side, prepare, 0)
        for ky in range(7):
            first = max(3 - ky, 0)
            count = min(side, side + 3 - ky) - first

            def row(h, acc):
                acc = list(acc)
                for t in range(imgs // 8):
                    at = pl.ds(t * 8, 8)
                    for begin, shift, taps, length, read_x, read_d in (
                        (4, 0, 3, pairs, lambda i: mixed_ref[k, h + ky - 3, 2 * i, at], lambda i: even[h, i, at]),
                        (0, -1, 4, pairs + 1, lambda i: mixed_ref[k, h + ky - 3, 2 * i + 1, at], lambda i: odd[h, i, at]),
                        (7, 0, 4, pairs, lambda i: sums[h + ky - 3, i, at], lambda i: last[h, i, at]),
                    ):
                        x = [read_x(i) for i in range(pairs)]
                        for a in range(length):
                            d = read_d(a)
                            for j in range(taps):
                                i = a + shift - 1 + j
                                if 0 <= i < pairs:
                                    acc[begin + j] = acc[begin + j] + x[i] * d
                return tuple(acc)

            acc = lax.fori_loop(
                0, count // 2, lambda r, acc: row(first + 2 * r + 1, row(first + 2 * r, acc)), (jnp.zeros((8, 128), F32),) * 11
            )
            if count % 2:
                acc = row(first + count - 1, acc)
            even_taps = [acc[j] + acc[7 + j] for j in range(4)]
            odd_taps = [acc[4 + j] + acc[7 + j] for j in range(3)]
            for kx in range(7):
                value = odd_taps[kx // 2] if kx % 2 else even_taps[kx // 2]
                g_ref[ky * 7 + kx, :, pl.ds(k * 128, 128)] = value


def taps_grad(conv, mixed, groups, after=()):
    side, _, imgs, _ = conv.shape
    lanes = lambda dtype: pltpu.VMEM((len(groups),) + conv.shape[:3] + (128,), dtype)
    part = lambda columns: pltpu.VMEM((side, columns, imgs, 128), F32)
    return kernel_call(
        functools.partial(taps_kernel, groups),
        [near((49, 8, 128 * len(groups)), F32)],
        [HBM] * 2,
        [lanes(BF16), lanes(F32), part(side // 2), part(side // 2), part(side // 2 + 1), part(side // 2), pltpu.SemaphoreType.DMA((2, len(groups)))],
        (conv, mixed),
        after,
        4.7 * len(groups),
        28,
    )[0]


def images_kernel(begin, end, conv_hbm, small_hbm, partner_ref, weight_ref, res_hbm, *rest):
    g_hbm, token_ref, small_ref, raw_ref, conv_ref, taps, res_ref, out_ref, mix_ref, row_ref, sel_ref, rest_ref, sem, csem, pair_sums = rest[-15:]
    side, _, imgs, _ = conv_hbm.shape
    low = max(begin - 3, 0)
    high = min(end + 3, side)
    load = dma(small_hbm, small_ref, csem.at[side])
    load.start()
    token_ref[...] = jnp.zeros(token_ref.shape, F32)

    def bring(h):
        return dma(conv_hbm.at[h], raw_ref.at[h], csem.at[h])

    def widen(h):
        bring(h).wait()
        conv_ref[h] = raw_ref[h].astype(F32)
        add_columns(conv_ref, pair_sums, h)

    def enter(h):
        return dma(res_hbm.at[h], res_ref.at[h % 2], sem.at[0, h % 2])

    def leave(h):
        return dma(out_ref.at[h - begin], g_hbm.at[h], sem.at[1, 0])

    for h in range(low, high):
        bring(h).start()
        if h == min(begin + 3, high - 1):
            enter(begin).start()
    spread(weight_ref, mix_ref)
    for i in range(imgs):
        row_ref[pl.ds(lax.rem(partner_ref[i], imgs), 1), :] = jnp.full((1, row_ref.shape[1]), i, jnp.int32)
    select(row_ref, sel_ref)
    load.wait()
    fill_taps(small_ref, taps, True)
    mix = mix_ref[...][None]
    others = 1.0 - mix
    for h in range(low, min(begin + 3, high)):
        widen(h)

    def row(h, kys):
        s = h % 2

        @pl.when(h + 1 < end)
        def _():
            enter(h + 1).start()

        @pl.when(h + 3 < high)
        def _():
            widen(h + 3)

        enter(h).wait()
        rest_ref[...] = res_ref[s].astype(F32)
        for t in range(imgs // 8):
            at = pl.ds(t * 8, 8)
            for g in range(D // 128):
                lanes = pl.ds(g * 128, 128)
                base = [rest_ref[w, at, lanes] for w in range(side)]
                acc = conv_rows(conv_ref, pair_sums, taps, h, kys, at, lanes, side, base)
                for w in range(side):
                    out_ref[h - begin, w, at, lanes] = acc[w]
        return 0

    every_row(begin, end, side, row)
    for r in range(end - begin):
        v = out_ref[r]
        part = (others * v).reshape(side * imgs, D)
        upper = part.astype(BF16)
        lower = (part - upper.astype(F32)).astype(BF16)
        back = jnp.dot(sel_ref[...], upper, preferred_element_type=F32)
        back = back + jnp.dot(sel_ref[...], lower, preferred_element_type=F32)
        out_ref[r] = mix * v + back.reshape(side, imgs, D)
        leave(begin + r).start()
    for h in range(begin, end):
        leave(h).wait()


def images_back(conv, small, partner, weight, res, begin, end, so_far=(), after=()):
    side, _, imgs, _ = conv.shape
    return kernel_call(
        functools.partial(images_kernel, begin, end),
        [far(conv.shape, F32), near((8, 128), F32)],
        [HBM, HBM, SMEM, SMEM, HBM] + [HBM] * len(so_far),
        [
            pltpu.VMEM(small.shape, F32),
            pltpu.VMEM(conv.shape, BF16),
            pltpu.VMEM(conv.shape, F32),
            pltpu.VMEM((77, 8, D), F32),
            pltpu.VMEM((2, side, imgs, D), BF16),
            pltpu.VMEM((end - begin, side, imgs, D), F32),
            pltpu.VMEM((imgs, D), F32),
            pltpu.VMEM((imgs, side * imgs), jnp.int32),
            pltpu.VMEM((side * imgs, side * imgs), BF16),
            pltpu.VMEM((side, imgs, D), F32),
            pltpu.SemaphoreType.DMA((2, 2)),
            pltpu.SemaphoreType.DMA((side + 1,)),
            pltpu.VMEM((side, side // 2, imgs, D), F32),
        ],
        (conv, small, partner, weight, res) + tuple(so_far),
        after,
        22 * (end - begin) / side,
        28,
        {5: 0} if so_far else {},
    )


def ready_kernel(in_hbm, out_hbm, down_hbm, *rest):
    pair_ref, low_ref, in_ref, out_ref, down_ref, sem = rest[-6:]
    pairs = ((in_hbm, in_ref), (out_hbm, out_ref), (down_hbm, down_ref))
    copies = [dma(a, b, sem.at[k]) for k, (a, b) in enumerate(pairs)]
    start(copies)
    wait(copies)
    pair_ref[0, :, :D] = in_ref[...].astype(BF16)
    pair_ref[0, :, D:] = out_ref[...].astype(BF16)
    low_ref[0] = down_ref[...].astype(BF16)


def ready(weight_in, weight_out, weight_down, after=()):
    deep = weight_in.shape[0]
    return kernel_call(
        ready_kernel,
        [near((1, deep, 2 * D), BF16)] * 2,
        [HBM] * 3,
        [pltpu.VMEM(x.shape, F32) for x in (weight_in, weight_out, weight_down)] + [pltpu.SemaphoreType.DMA((3,))],
        (weight_in, weight_out, weight_down),
        after,
        0.5,
        8,
    )


def join_kernel(first_ref, second_ref, *rest):
    out_ref = rest[-1]
    k = first_ref.shape[0]
    out_ref[:k] = first_ref[...]
    out_ref[k:] = second_ref[...]


def join(first, second, after=()):
    return kernel_call(
        join_kernel,
        [near((2 * first.shape[0],) + first.shape[1:], first.dtype)],
        [VMEM] * 2,
        [],
        (first, second),
        after,
        0.5,
        8,
    )[0]


def fold_kernel(count, *refs):
    ins, (stay_ref, leave_ref) = refs[: 2 * count], refs[-2:]
    k = stay_ref.shape[0] // count
    for i in range(count):
        keep_ref, come_ref = ins[2 * i], ins[2 * i + 1]
        stay_ref[i * k : (i + 1) * k] = keep_ref[:k].astype(F32) + come_ref[:k].astype(F32)
        leave_ref[i * k : (i + 1) * k] = (keep_ref[k:].astype(F32) + come_ref[k:].astype(F32)).astype(BF16)


def fold(*arrays, after=()):
    slots, deep, wide = arrays[0].shape
    count = len(arrays) // 2
    return kernel_call(
        functools.partial(fold_kernel, count),
        [near((count * slots // 2, deep, wide), F32), near((count * slots // 2, deep, wide), BF16)],
        [VMEM] * len(arrays),
        [],
        arrays,
        after,
        0.5,
        12,
    )


def small_kernel(hops, me_ref, gk_ref, sums1_ref, sums2_ref, near_ref, far_ref, db_ref, keep_ref, come_ref, sum_ref, send_ref, total):
    grads = keep_ref[...] + come_ref[...].astype(F32)
    sum_ref[...] = grads
    rows = lambda x: jnp.sum(x, axis=0, keepdims=True)
    for t in range(49):
        total[t : t + 1, :] = rows(gk_ref[t])
    for row, value in (
        (DEPTH_BIAS, sums1_ref[2]),
        (GAIN_ONE, sums1_ref[0]),
        (BIAS_ONE, sums1_ref[1]),
        (OUT_BIAS, sums2_ref[3]),
        (LAYER_SCALE, sums2_ref[2]),
        (GAIN_TWO, sums2_ref[0]),
        (BIAS_TWO, sums2_ref[1]),
    ):
        total[row : row + 1, :] = rows(value)
    mine, other = rows(near_ref[...]), rows(far_ref[...])
    if hops:
        odd_device = (me_ref[0] % 2).astype(F32)
        even = mine * (1.0 - odd_device) + other * odd_device
        odd = other * (1.0 - odd_device) + mine * odd_device
    for k in range(4):
        if hops:
            value = even_last(even, odd, k, FF // hops)
        else:
            value = (mine, other)[k // 2][:, k % 2 * D : k % 2 * D + D]
        total[HIDDEN_BIAS + k : HIDDEN_BIAS + k + 1, :] = value
    for k in range(2):
        total[DOWN_BIAS + k : DOWN_BIAS + k + 1, :] = rows(db_ref[:, k * D : (k + 1) * D])
    square = jnp.full((1, D), jnp.sum(grads * grads), F32)
    upper = square.astype(BF16).astype(F32)
    total[SQUARES : SQUARES + 1, :] = upper
    total[SQUARES + 1 : SQUARES + 2, :] = square - upper
    send_ref[...] = total[...].astype(BF16)


def small_total(hops, me, gk, sums1, sums2, near_hb, far_hb, db, keep, come):
    return kernel_call(
        functools.partial(small_kernel, hops),
        [near(keep.shape, F32), near((SQUARES + 2, D), BF16)],
        [SMEM] + [VMEM] * 8,
        [pltpu.VMEM((SQUARES + 2, D), F32)],
        (me, gk, sums1, sums2, near_hb, far_hb, db, keep, come),
        (),
        1,
        8,
    )


def meet_kernel(*refs):
    arrays, out_ref = refs[:-1], refs[-1]
    sums = [x[...].astype(F32) for x in arrays]
    while len(sums) > 1:
        sums = [a + b for a, b in zip(sums[::2], sums[1::2])]
    total = sums[0]
    square = total[SQUARES : SQUARES + 1] + total[SQUARES + 1 : SQUARES + 2]
    upper = square.astype(BF16).astype(F32)
    out_ref[...] = total.astype(out_ref.dtype)
    out_ref[SQUARES : SQUARES + 2, :] = jnp.concatenate([upper, square - upper], axis=0).astype(out_ref.dtype)


def meet(arrays, dtype):
    return kernel_call(meet_kernel, [near(arrays[0].shape, dtype)], [VMEM] * len(arrays), [], arrays, (), 0.3, 8)[0]


def adam(weight, first, second, grad, rate, decay):
    first = BETA_ONE * first + (1.0 - BETA_ONE) * grad
    second = BETA_TWO * second + (1.0 - BETA_TWO) * grad * grad
    first_hat = first / (1.0 - BETA_ONE**STEP)
    second_hat = second / (1.0 - BETA_TWO**STEP)
    weight = weight - rate * (first_hat / (jnp.sqrt(second_hat) + ADAM_EPS) + decay * weight)
    return first, second, weight


def adam_kernel(total_ref, grads_ref, *refs):
    ins, outs = refs[:9], refs[9:18]
    norm_ref = refs[18]
    gs = total_ref[:SQUARES]
    norm = jnp.sqrt(jnp.sum(gs * gs) + jnp.sum(total_ref[SQUARES : SQUARES + 2, 0:1]))
    norm_ref[0, 0] = norm
    factor = CLIP_NORM / jnp.maximum(norm, CLIP_NORM)
    grads = (grads_ref[0, :, :D], grads_ref[0, :, D:], grads_ref[1])
    rates = (LAYER_DECAY * RATE_MATRIX, LAYER_DECAY * RATE_MATRIX, RATE_MATRIX)
    for k in range(3):
        new = adam(ins[3 * k][...], ins[3 * k + 1][...], ins[3 * k + 2][...], grads[k] * factor, rates[k], WEIGHT_DECAY)
        for out_ref, value in zip(outs[3 * k : 3 * k + 3], new):
            out_ref[...] = value


def adam_all(total, grads, states):
    return pl.pallas_call(
        adam_kernel,
        out_shape=tuple(near(x.shape, F32) for x in states) + (near((1, 1), F32),),
        in_specs=[VMEM] * 11,
        out_specs=(VMEM,) * 9 + (SMEM,),
        cost_estimate=pl.CostEstimate(flops=int(2e9), bytes_accessed=0, transcendentals=0),
        compiler_params=pltpu.CompilerParams(vmem_limit_bytes=12 << 20),
    )(total, grads, *states)


def swap(x, bit, n):
    return lax.ppermute(x, "dp", [(i, i ^ bit) for i in range(n)])


def is_set(bit):
    return (lax.axis_index("dp") & bit) != 0


def gather_natural(shard, n, order, gates=None):
    have = shard
    met = []
    for hop, bit in enumerate(order):
        if gates and hop in gates:
            have, _ = lax.optimization_barrier((have, gates[hop]))
        other = swap(have, bit, n)
        axis = sum(1 for b in met if b > bit)
        mine = is_set(bit)
        have = jnp.stack([jnp.where(mine, other, have), jnp.where(mine, have, other)], axis=axis)
        met.append(bit)
    return have.reshape((n,) + shard.shape)


def masks_of(n, order):
    return tuple(sum(bit for k, bit in enumerate(order) if j >> k & 1) for j in range(n))


def local(n, images, mix_weight, partner, keep_mask, cotangent, weight_in, weight_out, weight_down, small_params,
          first_in, second_in, first_out, second_out, first_down, second_down, first_small, second_small):
    imgs, side = images.shape[:2]
    half = side // 2
    pixels = side * side * imgs
    me = lax.axis_index("dp")
    bits = [1 << k for k in range(n.bit_length() - 1)]
    deep = FF // n
    by_hops = n == 32

    pair, down = ready(weight_in, weight_out, weight_down)
    mine = me[None].astype(jnp.int32)
    p_masks = w_masks = d_masks = None
    if by_hops:
        p_order = [16, 8, 4, 2, 1]
        w_order = [16, 8, 2, 4, 1]
        d_order = [16, 2, 8, 4, 1]
        p_masks, w_masks, d_masks = (masks_of(n, order) for order in (p_order, w_order, d_order))

    img = images.transpose(1, 2, 0, 3)
    dy = cotangent.transpose(1, 2, 0, 3)
    flat = lambda a: a.reshape(pixels, a.shape[-1])
    square = lambda a: a.reshape(side, side, imgs, a.shape[-1])

    cut = [0, 3, 10, side]
    gates = None
    if by_hops:
        gates = {1: pair}
        pair = join(pair, swap(pair, p_order[0], n))
        gates[2] = pair
        down = join(down, swap(down, w_order[0], n))
        gates[3] = down
        pair = join(pair, swap(pair, p_order[1], n))
        gates[4] = pair
    small = gather_natural(small_params.astype(BF16), n, bits[1:] + bits[:1], gates).reshape(-1, D).astype(F32)
    if by_hops:
        down = join(down, swap(down, w_order[1], n))
    mixed, *made, token = conv_forward(small, (img, partner, mix_weight), cut[0], cut[1])
    for part in (1, 2):
        if by_hops:
            pair = join(pair, swap(pair, p_order[part + 1], n), (token,))
            down = join(down, swap(down, w_order[part + 1], n), (token,))
        *made, token = conv_forward(small, (mixed,), cut[part], cut[part + 1], tuple(made), (pair, down))
    unit1, inv1, norm1 = made
    if by_hops:
        pair = (pair, swap(pair, p_order[4], n))
        down = (down, swap(down, w_order[4], n))
    else:
        pair, down = (lax.all_gather(x[0], "dp", axis=0, tiled=True).reshape(2, FF // 2, 2 * D) for x in (pair, down))
    pair = tuple(x.reshape(FF // 2, 2 * D) for x in pair)
    down = tuple(x.reshape(FF // 2, 2 * D) for x in down)
    act, dg, d_near, d_far, gdb, out, bb, sums2, res = block_both(
        (p_masks, w_masks, d_masks), mine, flat(norm1), flat(mixed), pair, down, dy, small, keep_mask
    )
    shards = (n // 2, deep, 2 * D)
    if by_hops:
        d_keep = d_near.reshape(shards)
        d_come = swap(d_far.reshape(shards), d_order[4], n)
    grads_of = lambda which, after: pair_grad(
        16 * which, p_masks, mine, flat(bb), act, dg, flat(norm1), pair[which], imgs, after
    )
    p_far, far_hb, far_p = grads_of(1, ())
    if by_hops:
        d_keep, d_send = fold(d_keep, d_come, after=(far_hb,))
        d_come = swap(d_send, d_order[3], n)
        p_come = swap(p_far.reshape(shards), p_order[4], n)
    p_near, near_hb, near_p = grads_of(0, (d_send,) if by_hops else (far_hb,))
    p_gate = ()
    if by_hops:
        p_keep, p_send = fold(p_near.reshape(shards), p_come, after=(near_hb,))
        p_come = swap(p_send, p_order[3], n)
        d_keep, d_send = fold(d_keep, d_come, after=(near_hb,))
        d_come = swap(d_send, d_order[2], n)
        p_gate = (p_send, d_send)
    back_conv, sums1 = back_one(p_masks, mine, (near_p, far_p), flat(unit1), flat(inv1), pair, small, imgs, p_gate)
    back_conv = square(back_conv)
    res = square(res)
    back = functools.partial(images_back, back_conv, small, partner, mix_weight, res)
    if by_hops:
        p_keep, p_send = fold(p_keep, p_come, after=(sums1,))
        p_come = swap(p_send, p_order[2], n)
        d_keep, d_send = fold(d_keep, d_come, after=(sums1,))
        d_come = swap(d_send, d_order[1], n)
        grad, token = back(0, half, (), (p_send, d_send))
        p_keep, p_send = fold(p_keep, p_come, after=(token,))
        p_come = swap(p_send, p_order[1], n)
        grad, token = back(half, side, (grad,), (p_send,))
        keep, send = fold(p_keep, p_come, d_keep, d_come, after=(token,))
        come = swap(send, p_order[0], n)
        gk = taps_grad(back_conv, mixed, (0, 1, 2), (send,))
    else:
        grad, _ = back(0, side)
        gk = taps_grad(back_conv, mixed, (0, 1, 2))
        keep = jnp.stack(
            [
                lax.psum_scatter(jnp.concatenate(x).astype(F32), "dp", scatter_dimension=0, tiled=True)
                for x in ((p_near, p_far), (d_near, d_far))
            ]
        )
        come = jnp.zeros(keep.shape, BF16)

    grads, total = small_total(n if by_hops else 0, mine, gk, sums1, sums2, near_hb, far_hb, gdb, keep, come)
    rounds = [bits[k : k + 2] for k in range(1, len(bits), 2)] + [bits[:1]]
    for step, pair_bits in enumerate(rounds):
        others = [pair_bits[0], pair_bits[-1], sum(pair_bits)] if len(pair_bits) == 2 else pair_bits
        arrays = (total,) + tuple(swap(total, other, n) for other in others)
        total = meet(arrays, F32 if step == len(rounds) - 1 else BF16)
    states = (weight_in, first_in, second_in, weight_out, first_out, second_out, weight_down, first_down, second_down)
    *news, norm = adam_all(total, grads, states)
    grad_norm = norm[0, 0]
    factor = CLIP_NORM / jnp.maximum(grad_norm, CLIP_NORM)
    shard_len = small_params.shape[0]
    gs = lax.dynamic_slice_in_dim(total[:SQUARES].reshape(-1), me * shard_len, shard_len)
    position = me * shard_len + jnp.arange(shard_len, dtype=jnp.int32)
    small_rate = jnp.where(position < 54 * D + FF, LAYER_DECAY * RATE_VECTOR, RATE_VECTOR)
    small_decay = jnp.where(position < 49 * D, WEIGHT_DECAY, 0.0)
    new_small = adam(small_params, first_small, second_small, gs * factor, small_rate, small_decay)
    return (
        out.transpose(2, 0, 1, 3),
        grad.transpose(2, 0, 1, 3),
        grad_norm,
        *news,
        *new_small,
    )


def solution(mesh):
    four = P("dp", None, None, None)
    two = P("dp", None)
    one = P("dp")
    return jax.shard_map(
        functools.partial(local, mesh.shape["dp"]),
        mesh=mesh,
        in_specs=(four, one, one, one, four, two, two, two, one) + (two,) * 6 + (one,) * 2,
        out_specs=(four, four, P()) + (two,) * 9 + (one,) * 3,
        check_vma=False,
    )
```

```python
import functools
import jax
import jax.numpy as jnp
import numpy as np
from jax import lax
from jax.experimental import pallas as pl
from jax.experimental.pallas import tpu as pltpu
from jax.sharding import PartitionSpec as P

STEP = 10
DROP_RATE = 0.2
RATE_MATRIX = 0.05
RATE_VECTOR = 0.3
LAYER_DECAY = 0.8
BETA_ONE = 0.9
BETA_TWO = 0.999
ADAM_EPS = 1e-08
WEIGHT_DECAY = 0.05
CLIP_NORM = 1.0
D = 384
FF = 1536
LN_EPS = 1e-06
F32 = jnp.float32
BF16 = jnp.bfloat16
VMEM = pl.BlockSpec(memory_space=pltpu.VMEM)
SMEM = pl.BlockSpec(memory_space=pltpu.SMEM)
HBM = pl.BlockSpec(memory_space=pltpu.HBM)
ANY = pl.BlockSpec(memory_space=pl.ANY)
ROWS = (((0,), (0,)), ((), ()))
COLS = (((1,), (1,)), ((), ()))
DEPTH_BIAS, GAIN_ONE, BIAS_ONE, HIDDEN_BIAS, OUT_BIAS, LAYER_SCALE, GAIN_TWO, BIAS_TWO, DOWN_BIAS = 49, 50, 51, 52, 56, 57, 58, 59, 60
SQUARES = 62
HALF_PIECES = 16


def near(shape, dtype):
    return jax.ShapeDtypeStruct(shape, dtype)


def far(shape, dtype):
    return pltpu.HBM(shape, dtype)


def held(x):
    return pltpu.with_memory_space_constraint(x, pltpu.HBM)


def dma(src, dst, sem):
    return pltpu.make_async_copy(src, dst, sem)


def start(copies):
    for copy in copies:
        copy.start()


def wait(copies):
    for copy in copies:
        copy.wait()


class Far:
    def __init__(self, array):
        self.array = array


def kernel_call(body, out, specs, scratch, args, after, us, mib, aliases=None):
    specs = specs + [HBM if isinstance(x, Far) else ANY for x in after]
    args = tuple(args) + tuple(x.array if isinstance(x, Far) else x for x in after)
    args = [held(x) if spec is HBM else x for spec, x in zip(specs, args)]
    return pl.pallas_call(
        body,
        out_shape=tuple(out),
        in_specs=specs,
        out_specs=tuple(HBM if isinstance(x, type(far((8, 128), F32))) else VMEM for x in out),
        scratch_shapes=scratch,
        input_output_aliases=aliases or {},
        cost_estimate=pl.CostEstimate(flops=int(us * 1e9), bytes_accessed=0, transcendentals=0),
        compiler_params=pltpu.CompilerParams(vmem_limit_bytes=mib << 20),
    )(*args)


def norm_of(v):
    c = v - jnp.mean(v, axis=-1, keepdims=True)
    inv = lax.rsqrt(jnp.mean(c * c, axis=-1, keepdims=True) + LN_EPS)
    return c * inv, inv


def norm_back(back, unit, inv, gain):
    scaled = back * gain
    m1 = jnp.mean(scaled, axis=-1, keepdims=True)
    m2 = jnp.mean(scaled * unit, axis=-1, keepdims=True)
    return inv * (scaled - m1 - unit * m2)


def tile_of(k, imgs):
    groups = imgs // 8
    return pl.ds(pl.multiple_of(k % groups * 8, 8), 8), pl.ds(pl.multiple_of(k // groups * 128, 128), 128)


def tiles(h, imgs, tile):
    count = imgs // 8 * (D // 128)
    if isinstance(h, int):
        return lax.fori_loop(0, count, tile, 0)
    for k in range(count):
        tile(k, 0)
    return 0


def every_row(begin, end, side, do):
    for h in range(begin, min(end, 3)):
        do(h, range(3 - h, 7))
    low, high = max(begin, 3), min(end, side - 3)
    if low < high:
        lax.fori_loop(low, high, lambda h, _: do(h, range(7)), 0)
    for h in range(max(begin, side - 3), end):
        do(h, range(side + 3 - h))


def conv_rows(src, sums, taps, h, kys, t, lanes, side, base):
    pairs = side // 2

    def one(ky, acc):
        u, v, w = list(acc[:pairs]), list(acc[pairs : 2 * pairs + 1]), list(acc[2 * pairs + 1 :])
        row = h + ky - 3
        for out, shift, first, count, read in (
            (u, 0, 4, 3, lambda i: src[row, 2 * i, t, lanes]),
            (v, -1, 0, 4, lambda i: src[row, 2 * i + 1, t, lanes]),
            (w, 0, 7, 4, lambda i: sums[row, i, t, lanes]),
        ):
            x = [read(i) for i in range(pairs)]
            for j in range(count):
                tap = taps[ky * 11 + first + j, :, lanes]
                for k in range(len(out)):
                    i = k + shift - 1 + j
                    if 0 <= i < pairs:
                        out[k] = out[k] + x[i] * tap
        return tuple(u + v + w)

    acc = (jnp.zeros((8, 128), F32),) * (3 * pairs + 1)
    for ky in kys:
        acc = one(ky, acc)
    u, v, w = acc[:pairs], acc[pairs : 2 * pairs + 1], acc[2 * pairs + 1 :]
    out = []
    for k in range(pairs):
        out.append(base[2 * k] + (u[k] + v[k]))
        out.append(base[2 * k + 1] + (w[k] - (u[k] + v[k + 1])))
    return out


def fill_taps(small_ref, taps, flip):
    for ky in range(7):
        rows = []
        for kx in range(7):
            k = 48 - (ky * 7 + kx) if flip else ky * 7 + kx
            rows.append(small_ref[k : k + 1, :])
        rows = rows[0::2] + rows[1::2] + [rows[2 * j] + rows[2 * j + 1] for j in range(3)] + [rows[6]]
        for k, value in enumerate(rows):
            taps[ky * 11 + k] = jnp.broadcast_to(value, (8, D))


def add_columns(src, sums, row):
    pairs = sums.shape[1]
    sums[row] = jnp.stack([src[row, 2 * i] + src[row, 2 * i + 1] for i in range(pairs)])


def spread(scalars_ref, rows_ref):
    for i in range(rows_ref.shape[0]):
        rows_ref[i : i + 1, :] = jnp.full((1, rows_ref.shape[1]), scalars_ref[i], F32)


def select(row_ref, sel_ref):
    imgs, wide = row_ref.shape
    lane = lax.broadcasted_iota(jnp.int32, (imgs, wide), 1)
    for w in range(wide // imgs):
        sel_ref[w * imgs : (w + 1) * imgs, :] = (lane == row_ref[...] + w * imgs).astype(F32).astype(BF16)


def conv_kernel(begin, end, fresh, *refs):
    if fresh:
        small_hbm, img_hbm, partner_ref, weight_ref = refs[:4]
        mixed_hbm, unit_hbm, inv_hbm, norm_hbm, token_ref, small_ref, mixed_ref, taps, conv_ref, unit_ref, inv_ref, norm_ref, sem, pair_sums, img_ref, mix_ref, row_ref, sel_ref = refs[-18:]
    else:
        small_hbm, mixed_hbm = refs[:2]
        unit_hbm, inv_hbm, norm_hbm, token_ref, small_ref, mixed_ref, taps, conv_ref, unit_ref, inv_ref, norm_ref, sem, pair_sums = refs[-13:]
    side, _, imgs, _ = mixed_ref.shape
    low = max(begin - 3, 0)
    high = side if fresh else min(end + 3, side)
    rows = end - begin
    load = dma(small_hbm, small_ref, sem.at[4, 0])
    load.start()
    token_ref[...] = jnp.zeros(token_ref.shape, F32)

    def enter(h):
        if fresh:
            return dma(img_hbm.at[h], img_ref.at[h], sem.at[3, h])
        return dma(mixed_hbm.at[h], mixed_ref.at[h], sem.at[3, h])

    def store(h):
        return dma(mixed_ref.at[h], mixed_hbm.at[h], sem.at[5, h])

    for h in range(low, high):
        enter(h).start()
    if fresh:
        spread(weight_ref, mix_ref)
        for i in range(imgs):
            row_ref[i : i + 1, :] = jnp.full((1, row_ref.shape[1]), lax.rem(partner_ref[i], imgs), jnp.int32)
        select(row_ref, sel_ref)
    load.wait()
    fill_taps(small_ref, taps, False)
    if fresh:
        mix = mix_ref[...][None]
        rest = 1.0 - mix

        def blend(h, _):
            enter(h).wait()
            x = img_ref[h].reshape(side * imgs, D)
            other = jnp.dot(sel_ref[...], x, preferred_element_type=F32).reshape(side, imgs, D)
            mixed_ref[h] = mix * x.reshape(side, imgs, D).astype(F32) + rest * other
            add_columns(mixed_ref, pair_sums, h)
            store(h).start()
            return 0

        lax.fori_loop(0, side, blend, 0)
    else:
        for h in range(low, min(begin + 3, high)):
            enter(h).wait()
            add_columns(mixed_ref, pair_sums, h)

    def conv(h, kys):
        r = h - begin
        if not fresh:

            @pl.when(h + 3 < high)
            def _():
                enter(h + 3).wait()
                add_columns(mixed_ref, pair_sums, h + 3)

        def tile(k, _):
            at, lanes = tile_of(k, imgs)
            base = jnp.broadcast_to(small_ref[DEPTH_BIAS : DEPTH_BIAS + 1, lanes], (8, 128))
            acc = conv_rows(mixed_ref, pair_sums, taps, h, kys, at, lanes, side, [base] * side)
            for w in range(side):
                conv_ref[r, w, at, lanes] = acc[w]
            return 0

        return tiles(h, imgs, tile)

    every_row(begin, end, side, conv)
    gain = small_ref[GAIN_ONE : GAIN_ONE + 1, :][None]
    bias = small_ref[BIAS_ONE : BIAS_ONE + 1, :][None]

    def leave(r):
        return (
            dma(unit_ref.at[r], unit_hbm.at[r + begin], sem.at[0, r]),
            dma(inv_ref.at[r], inv_hbm.at[r + begin], sem.at[1, r]),
            dma(norm_ref.at[r], norm_hbm.at[r + begin], sem.at[2, r]),
        )

    def norm(r):
        unit, inv = norm_of(conv_ref[r])
        unit_ref[r] = unit.astype(BF16)
        inv_ref[r] = inv
        norm_ref[r] = (unit * gain + bias).astype(BF16)
        start(leave(r))

    def two(i, _):
        norm(2 * i)
        norm(2 * i + 1)
        return 0

    lax.fori_loop(0, rows // 2, two, 0)
    if rows % 2:
        norm(rows - 1)
    for r in range(rows):
        wait(leave(r))
    if fresh:
        for h in range(side):
            store(h).wait()


def conv_forward(small, inputs, begin, end, so_far=(), after=()):
    fresh = not so_far
    full = inputs[0].shape
    side = full[0]
    thin = full[:3] + (1,)
    rows = end - begin
    out = [far(full, BF16), far(thin, F32), far(full, BF16), near((8, 128), F32)]
    scratch = [
        pltpu.VMEM(small.shape, F32),
        pltpu.VMEM(full, F32),
        pltpu.VMEM((77, 8, D), F32),
        pltpu.VMEM((rows,) + full[1:], F32),
        pltpu.VMEM((rows,) + full[1:], BF16),
        pltpu.VMEM((rows,) + thin[1:], F32),
        pltpu.VMEM((rows,) + full[1:], BF16),
        pltpu.SemaphoreType.DMA((6, side)),
        pltpu.VMEM((side, side // 2) + full[2:], F32),
    ]
    specs = [HBM] * 2
    if fresh:
        out = [far(full, F32)] + out
        wide = side * full[2]
        scratch += [pltpu.VMEM(full, BF16), pltpu.VMEM((full[2], D), F32), pltpu.VMEM((full[2], wide), jnp.int32), pltpu.VMEM((wide, wide), BF16)]
        specs = [HBM] * 2 + [SMEM] * 2
    return kernel_call(
        functools.partial(conv_kernel, begin, end, fresh),
        out,
        specs + [HBM] * len(so_far),
        scratch,
        (small,) + tuple(inputs) + tuple(so_far),
        after,
        21 * rows / side + 3 * fresh,
        36,
        {2 + k: k for k in range(len(so_far))},
    )


def home(me, order, j, chips):
    if order is None:
        return j % HALF_PIECES if chips else j
    device = me
    for k, bit in enumerate(order):
        device = device ^ (((j >> k) & 1) * bit)
    return device >> 1 if chips else device


def keep_rows(mask_ref, keep_ref):
    for i in range(keep_ref.shape[0]):
        keep_ref[i : i + 1, :] = jnp.full((1, D), mask_ref[i], jnp.int32).astype(F32) / (1.0 - DROP_RATE)


def assembly(me, order, chips, first, src_hbm, whole_ref, sem):
    deep = src_hbm.shape[0] // HALF_PIECES

    def copy(j, _):
        to = pl.ds(pl.multiple_of(home(me, order, first + j, chips) * deep, 16), deep)
        dma(src_hbm.at[pl.ds(pl.multiple_of(j * deep, 16), deep), :], whole_ref.at[to, :], sem).start()
        return 0

    lax.fori_loop(0, HALF_PIECES, copy, 0)
    return dma(src_hbm, whole_ref.at[pl.ds(0, src_hbm.shape[0]), :], sem)


def deal(me, order, chips, first, out_ref, read):
    deep = out_ref.shape[0] // HALF_PIECES

    def move(j, _):
        begin = pl.multiple_of(home(me, order, first + j, chips) * deep, 16)
        to = pl.ds(pl.multiple_of(j * deep, 16), deep)
        for g in range(out_ref.shape[1] // 128):
            out_ref[to, g * 128 : (g + 1) * 128] = read(pl.ds(begin, deep), g).astype(BF16)
        return 0

    lax.fori_loop(0, HALF_PIECES, move, 0)


def even_first(rows, deep):
    blocks = [rows[d * deep // D][:, d * deep % D : d * deep % D + deep] for d in range(FF // deep)]
    return jnp.concatenate(blocks[0::2] + blocks[1::2], axis=1)


def even_last(even, odd, k, deep):
    per = D // deep
    blocks = []
    for d in range(per * k, per * k + per):
        source = odd if d % 2 else even
        blocks.append(source[:, d // 2 * deep : d // 2 * deep + deep])
    return jnp.concatenate(blocks, axis=1)


def block_kernel(block, masks, me_ref, norm_hbm, mixed_hbm, pnear_hbm, pfar_hbm, wnear_hbm, wfar_hbm, dy_hbm, small_hbm, mask_ref, *rest):
    act_hbm, dg_hbm, gnear_ref, gfar_ref, gdb_ref, out_ref, bb_hbm, sums_ref, res_hbm = rest[-32:-23]
    pair_ref, small_ref, keep_ref, norm_ref, mixed_ref, act_ref, dg_ref, branch_ref, unit_ref, inv_ref, out2_ref = rest[-23:-12]
    wd_ref, dy_ref, bb_ref, res_ref, acc, wide, wk, isem, osem, wsem, bsem, rsem = rest[-12:]
    rows = norm_hbm.shape[0]
    steps = rows // block
    imgs = keep_ref.shape[0]
    shape = (block // imgs, imgs, D)
    half = dy_hbm.shape[0]

    def spot(i):
        return pl.ds(pl.multiple_of(i * block, block), block)

    def enter(i):
        s = i % 2
        return (
            dma(norm_hbm.at[spot(i), :], norm_ref.at[s], isem.at[0, s]),
            dma(mixed_hbm.at[spot(i), :], mixed_ref.at[s], isem.at[1, s]),
        )

    def leave(i):
        s = i % 2
        pairs = ((act_ref, act_hbm), (dg_ref, dg_hbm))
        return [dma(a.at[s], b.at[spot(i), :], osem.at[k, s]) for k, (a, b) in enumerate(pairs)]

    me = me_ref[0]
    p_masks, w_masks, d_masks = masks
    load = dma(small_hbm, small_ref, wsem.at[0])
    start(enter(0))
    load.start()
    half_rows = FF // 2
    mine = 0 if p_masks is None else me % 2
    pair_in = []
    for src, first, which in ((pnear_hbm, 0, mine), (pfar_hbm, HALF_PIECES, 1 - mine)):
        to = pair_ref.at[pl.ds(pl.multiple_of(which * half_rows, half_rows), half_rows), :]
        pair_in.append(assembly(me, p_masks, True, first, src, to, wsem.at[1]))
    dy_in = dma(dy_hbm, dy_ref, wsem.at[3])
    wait(pair_in)
    down_in = [
        assembly(me, w_masks, False, first, src, wd_ref, wsem.at[2]) for first, src in ((0, wnear_hbm), (HALF_PIECES, wfar_hbm))
    ]
    dy_in.start()
    load.wait()
    keep_rows(mask_ref, keep_ref)
    keep = keep_ref[...][None]
    scale = keep * small_ref[LAYER_SCALE : LAYER_SCALE + 1, :][None]
    gain = small_ref[GAIN_TWO : GAIN_TWO + 1, :][None]
    bias = small_ref[BIAS_TWO : BIAS_TWO + 1, :][None]
    bias_rows = [small_ref[HIDDEN_BIAS + k : HIDDEN_BIAS + k + 1, :] for k in range(FF // D)]
    hidden_bias = jnp.concatenate(bias_rows, axis=1) if p_masks is None else even_first(bias_rows, FF >> len(p_masks))
    chunk = FF // 2

    def body(i, _):
        s = i % 2

        @pl.when(i + 1 < steps)
        def _():
            start(enter(i + 1))

        @pl.when(i >= 2)
        def _():
            wait(leave(i - 2))

        wait(enter(i))
        x = norm_ref[s]
        branch = jnp.broadcast_to(small_ref[OUT_BIAS : OUT_BIAS + 1, :], (block, D))

        def hidden(j):
            cols = slice(j * chunk, (j + 1) * chunk)
            return lax.dot_general(x, pair_ref[cols, :D], COLS, preferred_element_type=F32) + hidden_bias[:, cols]

        pre = hidden(0)
        for j in range(FF // chunk):
            after = hidden(j + 1) if j + 1 < FF // chunk else None
            cols = slice(j * chunk, (j + 1) * chunk)
            phi = 0.5 + 0.5 * lax.erf(pre * 0.7071067811865476)
            bell = jnp.exp2(pre * pre * -0.7213475204444817) * 0.3989422804014327
            act = (pre * phi).astype(BF16)
            act_ref[s, :, cols] = act
            dg_ref[s, :, cols] = (phi + pre * bell).astype(BF16)
            branch = branch + jnp.dot(act, pair_ref[cols, D:], preferred_element_type=F32)
            pre = after
        start(leave(i))
        split = branch_ref.shape[1:]
        branch_ref[i] = branch.astype(BF16).reshape(split)
        unit, inv = norm_of(mixed_ref[s].reshape(shape) + scale * branch.reshape(shape))
        unit_ref[i] = unit.astype(BF16).reshape(split)
        inv_ref[i] = inv.reshape(split[:-1] + (1,))
        out2_ref[i] = (unit * gain + bias).astype(BF16).reshape(split)
        return 0

    lax.fori_loop(0, steps, body, 0)

    wait(down_in)
    for g in range(6):
        wide[g] = wd_ref[:, pl.ds(g * 128, 128)].astype(F32)
        for k in range(4):
            wk[k, :, pl.ds(g * 128, 128)] = wide[g, pl.ds(k, D, stride=4), :].astype(BF16)
    sums_ref[...] = jnp.zeros(sums_ref.shape, F32)
    rows = half * half * imgs
    shape = (half * half, imgs, D)
    for k in range(2):
        acc[:, k * D : (k + 1) * D] = jnp.broadcast_to(small_ref[DOWN_BIAS + k : DOWN_BIAS + k + 1, :], (rows, D))
    dy_in.wait()
    gdb_ref[...] = jnp.sum(dy_ref[...].astype(F32).reshape(half * half, imgs, 2 * D), axis=0)

    def give(k):
        pairs = ((bb_ref, bb_hbm), (res_ref, res_hbm))
        return [dma(a.at[k], b.at[:, k // 2, :, k % 2], rsem.at[j, k]) for j, (a, b) in enumerate(pairs)]

    def quarter(k):
        dy = dy_ref[...].reshape(rows, 2 * D)
        x = out2_ref[:, k // 2, :, k % 2].reshape(rows, D)
        back = lax.dot_general(dy, wk[k], COLS, preferred_element_type=F32).reshape(shape)
        acc[...] += jnp.dot(x, wk[k], preferred_element_type=F32)
        gd = lax.dot_general(x, dy, ROWS, preferred_element_type=F32)
        for g in range(6):
            wide[g, pl.ds(k, D, stride=4), :] = gd[:, g * 128 : (g + 1) * 128]
        unit = unit_ref[:, k // 2, :, k % 2].reshape(shape).astype(F32)
        sums_ref[0] += jnp.sum(back * unit, axis=0)
        sums_ref[1] += jnp.sum(back, axis=0)
        res = norm_back(back, unit, inv_ref[:, k // 2, :, k % 2].reshape(half * half, imgs, 1), gain)
        res_ref[k] = res.astype(BF16).reshape(half, half, imgs, D)
        sums_ref[2] += jnp.sum(res * keep * branch_ref[:, k // 2, :, k % 2].reshape(shape).astype(F32), axis=0)
        bb = (res * scale).astype(BF16)
        bb_ref[k] = bb.reshape(half, half, imgs, D)
        start(give(k))
        sums_ref[3] += jnp.sum(bb.astype(F32), axis=0)

    def half_of(a, _):
        quarter(2 * a)
        quarter(2 * a + 1)
        return 0

    lax.fori_loop(0, 2, half_of, 0)
    out_ref[...] = acc[...].astype(BF16).reshape(out_ref.shape)
    deal(me, d_masks, False, 0, gnear_ref, lambda at, g: wide[g, at, :])
    deal(me, d_masks, False, HALF_PIECES, gfar_ref, lambda at, g: wide[g, at, :])
    for k in range(4):
        wait(give(k))
    for i in range(max(steps - 2, 0), steps):
        wait(leave(i))


def block_both(masks, me, norm, mixed, pair, down, dy, small, mask, after=(), block=448):
    rows = norm.shape[0]
    half, _, imgs, _ = dy.shape
    area = half * half * imgs
    six = (half, 2, half, 2, imgs)
    two = lambda width, dtype: pltpu.VMEM((2, block, width), dtype)
    whole = lambda width, dtype: pltpu.VMEM(six + (width,), dtype)
    part = pltpu.VMEM((4, half, half, imgs, D), BF16)
    return kernel_call(
        functools.partial(block_kernel, block, masks),
        [far((rows, FF), BF16)] * 2
        + [near((2 * D, 2 * D), BF16)] * 2
        + [near((imgs, 2 * D), F32), near((half, half, imgs, 2 * D), BF16)]
        + [far(six + (D,), BF16), near((4, imgs, D), F32), far(six + (D,), BF16)],
        [SMEM] + [HBM] * 2 + [ANY, HBM] * 2 + [HBM] * 2 + [SMEM],
        [pltpu.VMEM((FF, 2 * D), BF16), pltpu.VMEM(small.shape, F32), pltpu.VMEM((imgs, D), F32)]
        + [two(D, BF16), two(D, F32), two(FF, BF16), two(FF, BF16)]
        + [whole(D, BF16), whole(D, BF16), whole(1, F32), whole(D, BF16)]
        + [pltpu.VMEM((4 * D, 2 * D), BF16), pltpu.VMEM(dy.shape, BF16), part, part]
        + [pltpu.VMEM((area, 2 * D), F32), pltpu.VMEM((6, 4 * D, 128), F32), pltpu.VMEM((4, D, 2 * D), BF16)]
        + [pltpu.SemaphoreType.DMA((2, 2)), pltpu.SemaphoreType.DMA((2, 2)), pltpu.SemaphoreType.DMA((4,))]
        + [pltpu.SemaphoreType.DMA((1,)), pltpu.SemaphoreType.DMA((2, 4))],
        (me, norm, mixed, *pair, *down, dy, small, mask),
        after,
        34,
        58,
    )


def pair_grad_kernel(block, first, masks, me_ref, bb_hbm, act_hbm, dg_hbm, norm_hbm, pair_hbm, *rest):
    g_ref, hb_ref, p_hbm, pair_ref, acc, bb_ref, act_ref, dg_ref, norm_ref, p_ref, sem, osem, wsem = rest[-13:]
    rows = bb_hbm.shape[0]
    imgs = hb_ref.shape[0]
    steps = rows // block
    wide = FF // 2
    me = me_ref[0]
    which = 0 if masks is None else me % 2
    which = 1 - which if first else which
    lanes = pl.ds(pl.multiple_of(which * wide, wide), wide)

    def spot(i):
        return pl.ds(pl.multiple_of(i * block, block), block)

    def enter(i):
        s = i % 2
        return (
            dma(bb_hbm.at[spot(i), :], bb_ref.at[s], sem.at[0, s]),
            dma(dg_hbm.at[spot(i), lanes], dg_ref.at[s], sem.at[1, s]),
            dma(act_hbm.at[spot(i), lanes], act_ref.at[s], sem.at[2, s]),
            dma(norm_hbm.at[spot(i), :], norm_ref.at[s], sem.at[3, s]),
        )

    def leave(i):
        return dma(p_ref.at[i % 2], p_hbm.at[spot(i), :], osem.at[i % 2])

    pair_in = [assembly(me, masks, True, first, pair_hbm, pair_ref, wsem.at[0])]
    start(enter(0))
    hb_ref[...] = jnp.zeros(hb_ref.shape, F32)
    acc[...] = jnp.zeros(acc.shape, F32)
    wait(pair_in)

    def body(i, _):
        s = i % 2

        @pl.when(i + 1 < steps)
        def _():
            start(enter(i + 1))

        @pl.when(i >= 2)
        def _():
            leave(i - 2).wait()

        wait(enter(i))
        b = bb_ref[s]
        back = lax.dot_general(b, pair_ref[:, D:], COLS, preferred_element_type=F32)
        acc[:, D:] += lax.dot_general(act_ref[s], b, ROWS, preferred_element_type=F32)
        p = (back * dg_ref[s].astype(F32)).astype(BF16)
        p_ref[s] = p
        hb_ref[...] += jnp.sum(p.astype(F32).reshape(block // imgs, imgs, wide), axis=0)
        acc[:, :D] += lax.dot_general(p, norm_ref[s], ROWS, preferred_element_type=F32)
        leave(i).start()
        return 0

    lax.fori_loop(0, steps, body, 0)
    deal(me, masks, True, first, g_ref, lambda at, g: acc[at, pl.ds(g * 128, 128)])
    for i in range(max(steps - 2, 0), steps):
        leave(i).wait()


def pair_grad(first, masks, me, bb, act, dg, norm, pair, imgs, after=(), block=448):
    rows = bb.shape[0]
    wide = FF // 2
    two = lambda width: pltpu.VMEM((2, block, width), BF16)
    return kernel_call(
        functools.partial(pair_grad_kernel, block, first, masks),
        [near((wide, 2 * D), BF16), near((imgs, wide), F32), far((rows, wide), BF16)],
        [SMEM] + [HBM] * 5,
        [pltpu.VMEM((wide, 2 * D), BF16), pltpu.VMEM((wide, 2 * D), F32)]
        + [two(D), two(wide), two(wide), two(D), two(wide)]
        + [pltpu.SemaphoreType.DMA((4, 2)), pltpu.SemaphoreType.DMA((2,)), pltpu.SemaphoreType.DMA((1,))],
        (me, bb, act, dg, norm, pair),
        after,
        13,
        28,
    )


def back_one_kernel(block, masks, me_ref, pnear_hbm, pfar_hbm, unit_hbm, inv_hbm, near_hbm, far_hbm, small_hbm, *rest):
    conv_hbm, sums_ref, near_ref, far_ref, small_ref, pnear_ref, pfar_ref, unit_ref, inv_ref, conv_ref, sem, wsem = rest[-12:]
    rows = pnear_hbm.shape[0]
    imgs = sums_ref.shape[1]
    steps = rows // block
    shape = (block // imgs, imgs, D)

    def spot(i):
        return pl.ds(pl.multiple_of(i * block, block), block)

    def enter(i):
        s = i % 2
        pairs = ((pnear_hbm, pnear_ref), (pfar_hbm, pfar_ref), (unit_hbm, unit_ref), (inv_hbm, inv_ref))
        return [dma(a.at[spot(i), :], b.at[s], sem.at[k, s]) for k, (a, b) in enumerate(pairs)]

    def leave(i):
        return dma(conv_ref.at[i % 2], conv_hbm.at[spot(i), :], sem.at[4, i % 2])

    load = dma(small_hbm, small_ref, wsem.at[0])
    left = pl.ds(0, D)
    pair_in = [
        assembly(me_ref[0], masks, True, first, src.at[:, left], dst, wsem.at[1])
        for first, src, dst in ((0, near_hbm, near_ref), (HALF_PIECES, far_hbm, far_ref))
    ]
    start(enter(0))
    load.start()
    sums_ref[...] = jnp.zeros(sums_ref.shape, F32)
    wait(pair_in)
    load.wait()
    gain = small_ref[GAIN_ONE : GAIN_ONE + 1, :][None]

    def body(i, _):
        s = i % 2

        @pl.when(i + 1 < steps)
        def _():
            start(enter(i + 1))

        @pl.when(i >= 2)
        def _():
            leave(i - 2).wait()

        wait(enter(i))
        back = jnp.dot(pnear_ref[s], near_ref[...], preferred_element_type=F32)
        back = (back + jnp.dot(pfar_ref[s], far_ref[...], preferred_element_type=F32)).reshape(shape)
        unit = unit_ref[s].reshape(shape).astype(F32)
        sums_ref[0] += jnp.sum(back * unit, axis=0)
        sums_ref[1] += jnp.sum(back, axis=0)
        out = norm_back(back, unit, inv_ref[s].reshape(shape[:2] + (1,)), gain)
        sums_ref[2] += jnp.sum(out, axis=0)
        conv_ref[s] = out.astype(BF16).reshape(block, D)
        leave(i).start()
        return 0

    lax.fori_loop(0, steps, body, 0)
    for i in range(max(steps - 2, 0), steps):
        leave(i).wait()


def back_one(masks, me, p, unit, inv, pair, small, imgs, after=(), block=784):
    rows = unit.shape[0]
    wide = FF // 2
    two = lambda width, dtype: pltpu.VMEM((2, block, width), dtype)
    return kernel_call(
        functools.partial(back_one_kernel, block, masks),
        [far((rows, D), BF16), near((3, imgs, D), F32)],
        [SMEM] + [HBM] * 7,
        [pltpu.VMEM((wide, D), BF16)] * 2
        + [pltpu.VMEM(small.shape, F32)]
        + [two(wide, BF16), two(wide, BF16), two(D, BF16), two(1, F32), two(D, BF16)]
        + [pltpu.SemaphoreType.DMA((5, 2)), pltpu.SemaphoreType.DMA((2,))],
        (me, *p, unit, inv, *pair, small),
        after,
        11,
        32,
    )


def taps_kernel(groups, conv_hbm, mixed_hbm, *rest):
    g_ref, conv_ref, mixed_ref, sums, even, odd, last, sem = rest[-8:]
    side, _, imgs, _ = conv_hbm.shape
    pairs = side // 2

    def enter(k):
        lanes = pl.ds(pl.multiple_of((k + groups[0]) * 128, 128), 128)
        return (
            dma(mixed_hbm.at[:, :, :, lanes], mixed_ref.at[k], sem.at[0, k]),
            dma(conv_hbm.at[:, :, :, lanes], conv_ref.at[k], sem.at[1, k]),
        )

    for k in range(len(groups)):
        start(enter(k))
    def group(k, _):
        wait(enter(k))

        def prepare(h, _):
            x = [mixed_ref[k, h, w] for w in range(side)]
            d = [conv_ref[k, h, w].astype(F32) for w in range(side)]
            for i in range(pairs):
                sums[h, i] = x[2 * i] + x[2 * i + 1]
                last[h, i] = d[2 * i + 1]
                even[h, i] = d[2 * i] - d[2 * i + 1]
                odd[h, i + 1] = (d[2 * i + 2] if i + 1 < pairs else jnp.zeros_like(d[0])) - d[2 * i + 1]
            odd[h, 0] = d[0]
            return 0

        lax.fori_loop(0, side, prepare, 0)
        for ky in range(7):
            first = max(3 - ky, 0)
            count = min(side, side + 3 - ky) - first

            def row(h, acc):
                acc = list(acc)
                for t in range(imgs // 8):
                    at = pl.ds(t * 8, 8)
                    for begin, shift, taps, length, read_x, read_d in (
                        (4, 0, 3, pairs, lambda i: mixed_ref[k, h + ky - 3, 2 * i, at], lambda i: even[h, i, at]),
                        (0, -1, 4, pairs + 1, lambda i: mixed_ref[k, h + ky - 3, 2 * i + 1, at], lambda i: odd[h, i, at]),
                        (7, 0, 4, pairs, lambda i: sums[h + ky - 3, i, at], lambda i: last[h, i, at]),
                    ):
                        x = [read_x(i) for i in range(pairs)]
                        for a in range(length):
                            d = read_d(a)
                            for j in range(taps):
                                i = a + shift - 1 + j
                                if 0 <= i < pairs:
                                    acc[begin + j] = acc[begin + j] + x[i] * d
                return tuple(acc)

            acc = lax.fori_loop(
                0, count // 2, lambda r, acc: row(first + 2 * r + 1, row(first + 2 * r, acc)), (jnp.zeros((8, 128), F32),) * 11
            )
            if count % 2:
                acc = row(first + count - 1, acc)
            even_taps = [acc[j] + acc[7 + j] for j in range(4)]
            odd_taps = [acc[4 + j] + acc[7 + j] for j in range(3)]
            for kx in range(7):
                value = odd_taps[kx // 2] if kx % 2 else even_taps[kx // 2]
                g_ref[ky * 7 + kx, :, pl.ds(pl.multiple_of(k * 128, 128), 128)] = value
        return 0

    lax.fori_loop(0, len(groups), group, 0)


def taps_grad(conv, mixed, groups, after=()):
    side, _, imgs, _ = conv.shape
    lanes = lambda dtype: pltpu.VMEM((len(groups),) + conv.shape[:3] + (128,), dtype)
    part = lambda columns: pltpu.VMEM((side, columns, imgs, 128), F32)
    return kernel_call(
        functools.partial(taps_kernel, groups),
        [near((49, 8, 128 * len(groups)), F32)],
        [HBM] * 2,
        [lanes(BF16), lanes(F32), part(side // 2), part(side // 2), part(side // 2 + 1), part(side // 2), pltpu.SemaphoreType.DMA((2, len(groups)))],
        (conv, mixed),
        after,
        4.7 * len(groups),
        28,
    )[0]


def images_kernel(begin, end, conv_hbm, small_hbm, partner_ref, weight_ref, res_hbm, *rest):
    g_hbm, token_ref, small_ref, raw_ref, conv_ref, taps, res_ref, out_ref, mix_ref, row_ref, sel_ref, rest_ref, sem, csem, pair_sums = rest[-15:]
    side, _, imgs, _ = conv_hbm.shape
    low = max(begin - 3, 0)
    high = min(end + 3, side)
    load = dma(small_hbm, small_ref, csem.at[side])
    load.start()
    token_ref[...] = jnp.zeros(token_ref.shape, F32)

    def bring(h):
        return dma(conv_hbm.at[h], raw_ref.at[h], csem.at[h])

    def widen(h):
        bring(h).wait()
        conv_ref[h] = raw_ref[h].astype(F32)
        add_columns(conv_ref, pair_sums, h)

    def enter(h):
        return dma(res_hbm.at[h], res_ref.at[h % 2], sem.at[0, h % 2])

    def leave(h):
        return dma(out_ref.at[h - begin], g_hbm.at[h], sem.at[1, 0])

    for h in range(low, high):
        bring(h).start()
        if h == min(begin + 3, high - 1):
            enter(begin).start()
    spread(weight_ref, mix_ref)
    for i in range(imgs):
        row_ref[pl.ds(lax.rem(partner_ref[i], imgs), 1), :] = jnp.full((1, row_ref.shape[1]), i, jnp.int32)
    select(row_ref, sel_ref)
    load.wait()
    fill_taps(small_ref, taps, True)
    mix = mix_ref[...][None]
    others = 1.0 - mix
    for h in range(low, min(begin + 3, high)):
        widen(h)

    def row(h, kys):
        s = h % 2

        @pl.when(h + 1 < end)
        def _():
            enter(h + 1).start()

        @pl.when(h + 3 < high)
        def _():
            widen(h + 3)

        enter(h).wait()
        rest_ref[...] = res_ref[s].astype(F32)
        def tile(k, _):
            at, lanes = tile_of(k, imgs)
            base = [rest_ref[w, at, lanes] for w in range(side)]
            acc = conv_rows(conv_ref, pair_sums, taps, h, kys, at, lanes, side, base)
            for w in range(side):
                out_ref[h - begin, w, at, lanes] = acc[w]
            return 0

        return tiles(h, imgs, tile)

    every_row(begin, end, side, row)
    def unmix(r):
        v = out_ref[r]
        part = (others * v).reshape(side * imgs, D)
        upper = part.astype(BF16)
        lower = (part - upper.astype(F32)).astype(BF16)
        back = jnp.dot(sel_ref[...], upper, preferred_element_type=F32)
        back = back + jnp.dot(sel_ref[...], lower, preferred_element_type=F32)
        out_ref[r] = mix * v + back.reshape(side, imgs, D)
        leave(begin + r).start()

    for r in range(end - begin):
        unmix(r)
    for h in range(begin, end):
        leave(h).wait()


def images_back(conv, small, partner, weight, res, begin, end, so_far=(), after=()):
    side, _, imgs, _ = conv.shape
    return kernel_call(
        functools.partial(images_kernel, begin, end),
        [far(conv.shape, F32), near((8, 128), F32)],
        [HBM, HBM, SMEM, SMEM, HBM] + [HBM] * len(so_far),
        [
            pltpu.VMEM(small.shape, F32),
            pltpu.VMEM(conv.shape, BF16),
            pltpu.VMEM(conv.shape, F32),
            pltpu.VMEM((77, 8, D), F32),
            pltpu.VMEM((2, side, imgs, D), BF16),
            pltpu.VMEM((end - begin, side, imgs, D), F32),
            pltpu.VMEM((imgs, D), F32),
            pltpu.VMEM((imgs, side * imgs), jnp.int32),
            pltpu.VMEM((side * imgs, side * imgs), BF16),
            pltpu.VMEM((side, imgs, D), F32),
            pltpu.SemaphoreType.DMA((2, 2)),
            pltpu.SemaphoreType.DMA((side + 1,)),
            pltpu.VMEM((side, side // 2, imgs, D), F32),
        ],
        (conv, small, partner, weight, res) + tuple(so_far),
        after,
        22 * (end - begin) / side,
        28,
        {5: 0} if so_far else {},
    )


def ready_kernel(in_hbm, out_hbm, down_hbm, *rest):
    pair_ref, low_ref, in_ref, out_ref, down_ref, sem = rest[-6:]
    pairs = ((in_hbm, in_ref), (out_hbm, out_ref), (down_hbm, down_ref))
    copies = [dma(a, b, sem.at[k]) for k, (a, b) in enumerate(pairs)]
    start(copies)
    wait(copies)
    pair_ref[0, :, :D] = in_ref[...].astype(BF16)
    pair_ref[0, :, D:] = out_ref[...].astype(BF16)
    low_ref[0] = down_ref[...].astype(BF16)


def ready(weight_in, weight_out, weight_down, after=()):
    deep = weight_in.shape[0]
    return kernel_call(
        ready_kernel,
        [near((1, deep, 2 * D), BF16)] * 2,
        [HBM] * 3,
        [pltpu.VMEM(x.shape, F32) for x in (weight_in, weight_out, weight_down)] + [pltpu.SemaphoreType.DMA((3,))],
        (weight_in, weight_out, weight_down),
        after,
        0.5,
        8,
    )


def join_kernel(first_ref, second_ref, *rest):
    out_ref = rest[-1]
    k = first_ref.shape[0]
    out_ref[:k] = first_ref[...]
    out_ref[k:] = second_ref[...]


def join(first, second, after=()):
    return kernel_call(
        join_kernel,
        [near((2 * first.shape[0],) + first.shape[1:], first.dtype)],
        [VMEM] * 2,
        [],
        (first, second),
        after,
        0.5,
        8,
    )[0]


def fold_kernel(count, *refs):
    ins, (stay_ref, leave_ref) = refs[: 2 * count], refs[-2:]
    k = stay_ref.shape[0] // count
    for i in range(count):
        keep_ref, come_ref = ins[2 * i], ins[2 * i + 1]
        stay_ref[i * k : (i + 1) * k] = keep_ref[:k].astype(F32) + come_ref[:k].astype(F32)
        leave_ref[i * k : (i + 1) * k] = (keep_ref[k:].astype(F32) + come_ref[k:].astype(F32)).astype(BF16)


def fold(*arrays, after=()):
    slots, deep, wide = arrays[0].shape
    count = len(arrays) // 2
    return kernel_call(
        functools.partial(fold_kernel, count),
        [near((count * slots // 2, deep, wide), F32), near((count * slots // 2, deep, wide), BF16)],
        [VMEM] * len(arrays),
        [],
        arrays,
        after,
        0.5,
        12,
    )


def small_kernel(hops, me_ref, gk_ref, sums1_ref, sums2_ref, near_ref, far_ref, db_ref, keep_ref, come_ref, sum_ref, send_ref, total):
    grads = keep_ref[...] + come_ref[...].astype(F32)
    sum_ref[...] = grads
    rows = lambda x: jnp.sum(x, axis=0, keepdims=True)
    for t in range(49):
        total[t : t + 1, :] = rows(gk_ref[t])
    for row, value in (
        (DEPTH_BIAS, sums1_ref[2]),
        (GAIN_ONE, sums1_ref[0]),
        (BIAS_ONE, sums1_ref[1]),
        (OUT_BIAS, sums2_ref[3]),
        (LAYER_SCALE, sums2_ref[2]),
        (GAIN_TWO, sums2_ref[0]),
        (BIAS_TWO, sums2_ref[1]),
    ):
        total[row : row + 1, :] = rows(value)
    mine, other = rows(near_ref[...]), rows(far_ref[...])
    if hops:
        odd_device = (me_ref[0] % 2).astype(F32)
        even = mine * (1.0 - odd_device) + other * odd_device
        odd = other * (1.0 - odd_device) + mine * odd_device
    for k in range(4):
        if hops:
            value = even_last(even, odd, k, FF // hops)
        else:
            value = (mine, other)[k // 2][:, k % 2 * D : k % 2 * D + D]
        total[HIDDEN_BIAS + k : HIDDEN_BIAS + k + 1, :] = value
    for k in range(2):
        total[DOWN_BIAS + k : DOWN_BIAS + k + 1, :] = rows(db_ref[:, k * D : (k + 1) * D])
    square = jnp.full((1, D), jnp.sum(grads * grads), F32)
    upper = square.astype(BF16).astype(F32)
    total[SQUARES : SQUARES + 1, :] = upper
    total[SQUARES + 1 : SQUARES + 2, :] = square - upper
    send_ref[...] = total[...].astype(BF16)


def small_total(hops, me, gk, sums1, sums2, near_hb, far_hb, db, keep, come):
    return kernel_call(
        functools.partial(small_kernel, hops),
        [near(keep.shape, F32), near((SQUARES + 2, D), BF16)],
        [SMEM] + [VMEM] * 8,
        [pltpu.VMEM((SQUARES + 2, D), F32)],
        (me, gk, sums1, sums2, near_hb, far_hb, db, keep, come),
        (),
        1,
        8,
    )


def meet_kernel(*refs):
    arrays, out_ref = refs[:-1], refs[-1]
    sums = [x[...].astype(F32) for x in arrays]
    while len(sums) > 1:
        sums = [a + b for a, b in zip(sums[::2], sums[1::2])]
    total = sums[0]
    square = total[SQUARES : SQUARES + 1] + total[SQUARES + 1 : SQUARES + 2]
    upper = square.astype(BF16).astype(F32)
    out_ref[...] = total.astype(out_ref.dtype)
    out_ref[SQUARES : SQUARES + 2, :] = jnp.concatenate([upper, square - upper], axis=0).astype(out_ref.dtype)


def meet(arrays, dtype):
    return kernel_call(meet_kernel, [near(arrays[0].shape, dtype)], [VMEM] * len(arrays), [], arrays, (), 0.3, 8)[0]


def adam(weight, first, second, grad, rate, decay):
    first = BETA_ONE * first + (1.0 - BETA_ONE) * grad
    second = BETA_TWO * second + (1.0 - BETA_TWO) * grad * grad
    first_hat = first / (1.0 - BETA_ONE**STEP)
    second_hat = second / (1.0 - BETA_TWO**STEP)
    weight = weight - rate * (first_hat / (jnp.sqrt(second_hat) + ADAM_EPS) + decay * weight)
    return first, second, weight


def adam_kernel(total_ref, grads_ref, *refs):
    ins, outs = refs[:9], refs[9:18]
    norm_ref = refs[18]
    gs = total_ref[:SQUARES]
    norm = jnp.sqrt(jnp.sum(gs * gs) + jnp.sum(total_ref[SQUARES : SQUARES + 2, 0:1]))
    norm_ref[0, 0] = norm
    factor = CLIP_NORM / jnp.maximum(norm, CLIP_NORM)
    grads = (grads_ref[0, :, :D], grads_ref[0, :, D:], grads_ref[1])
    rates = (LAYER_DECAY * RATE_MATRIX, LAYER_DECAY * RATE_MATRIX, RATE_MATRIX)
    for k in range(3):
        new = adam(ins[3 * k][...], ins[3 * k + 1][...], ins[3 * k + 2][...], grads[k] * factor, rates[k], WEIGHT_DECAY)
        for out_ref, value in zip(outs[3 * k : 3 * k + 3], new):
            out_ref[...] = value


def adam_all(total, grads, states):
    return pl.pallas_call(
        adam_kernel,
        out_shape=tuple(near(x.shape, F32) for x in states) + (near((1, 1), F32),),
        in_specs=[VMEM] * 11,
        out_specs=(VMEM,) * 9 + (SMEM,),
        cost_estimate=pl.CostEstimate(flops=int(2e9), bytes_accessed=0, transcendentals=0),
        compiler_params=pltpu.CompilerParams(vmem_limit_bytes=12 << 20),
    )(total, grads, *states)


def swap(x, bit, n):
    return lax.ppermute(x, "dp", [(i, i ^ bit) for i in range(n)])


def is_set(bit):
    return (lax.axis_index("dp") & bit) != 0


def gather_natural(shard, n, order, gates=None):
    have = shard
    met = []
    for hop, bit in enumerate(order):
        if gates and hop in gates:
            have, _ = lax.optimization_barrier((have, gates[hop]))
        other = swap(have, bit, n)
        axis = sum(1 for b in met if b > bit)
        mine = is_set(bit)
        have = jnp.stack([jnp.where(mine, other, have), jnp.where(mine, have, other)], axis=axis)
        met.append(bit)
    return have.reshape((n,) + shard.shape)


def local(n, images, mix_weight, partner, keep_mask, cotangent, weight_in, weight_out, weight_down, small_params,
          first_in, second_in, first_out, second_out, first_down, second_down, first_small, second_small):
    imgs, side = images.shape[:2]
    half = side // 2
    pixels = side * side * imgs
    me = lax.axis_index("dp")
    bits = [1 << k for k in range(n.bit_length() - 1)]
    deep = FF // n
    by_hops = n == 32

    pair, down = ready(weight_in, weight_out, weight_down)
    mine = me[None].astype(jnp.int32)
    p_masks = w_masks = d_masks = None
    if by_hops:
        p_order = [16, 8, 4, 2, 1]
        w_order = [16, 8, 2, 4, 1]
        d_order = [16, 2, 8, 4, 1]
        p_masks, w_masks, d_masks = p_order, w_order, d_order

    img = images.transpose(1, 2, 0, 3)
    dy = cotangent.transpose(1, 2, 0, 3)
    flat = lambda a: a.reshape(pixels, a.shape[-1])
    square = lambda a: a.reshape(side, side, imgs, a.shape[-1])

    cut = [0, 3, 10, side]
    gates = None
    if by_hops:
        gates = {0: pair}
        pair = join(pair, swap(pair, p_order[0], n))
        gates[2] = pair
        down = join(down, swap(down, w_order[0], n))
        pair = join(pair, swap(pair, p_order[1], n))
        gates[4] = pair
    small = gather_natural(small_params.astype(BF16), n, bits[1:] + bits[:1], gates).reshape(-1, D).astype(F32)
    if by_hops:
        down = join(down, swap(down, w_order[1], n))
    mixed, *made, token = conv_forward(small, (img, partner, mix_weight), cut[0], cut[1])
    for part in (1, 2):
        if by_hops:
            pair = join(pair, swap(pair, p_order[part + 1], n), (token,))
            down = join(down, swap(down, w_order[part + 1], n), (token,))
        *made, token = conv_forward(small, (mixed,), cut[part], cut[part + 1], tuple(made), (pair, down))
    unit1, inv1, norm1 = made
    if by_hops:
        pair = (pair, swap(pair, p_order[4], n))
        down = (down, swap(down, w_order[4], n))
    else:
        pair, down = (lax.all_gather(x[0], "dp", axis=0, tiled=True).reshape(2, FF // 2, 2 * D) for x in (pair, down))
    pair = tuple(x.reshape(FF // 2, 2 * D) for x in pair)
    down = tuple(x.reshape(FF // 2, 2 * D) for x in down)
    act, dg, d_near, d_far, gdb, out, bb, sums2, res = block_both(
        (p_masks, w_masks, d_masks), mine, flat(norm1), flat(mixed), pair, down, dy, small, keep_mask
    )
    shards = (n // 2, deep, 2 * D)
    if by_hops:
        d_keep = d_near.reshape(shards)
        d_come = swap(d_far.reshape(shards), d_order[4], n)
    grads_of = lambda which, after: pair_grad(
        16 * which, p_masks, mine, flat(bb), act, dg, flat(norm1), pair[which], imgs, after
    )
    p_far, far_hb, far_p = grads_of(1, ())
    if by_hops:
        d_keep, d_send = fold(d_keep, d_come, after=(far_hb,))
        d_come = swap(d_send, d_order[3], n)
        p_come = swap(p_far.reshape(shards), p_order[4], n)
    p_near, near_hb, near_p = grads_of(0, (d_send,) if by_hops else (far_hb,))
    p_gate = ()
    if by_hops:
        p_keep, p_send = fold(p_near.reshape(shards), p_come, after=(near_hb,))
        p_come = swap(p_send, p_order[3], n)
        d_keep, d_send = fold(d_keep, d_come, after=(near_hb,))
        d_come = swap(d_send, d_order[2], n)
        p_gate = (p_send, d_send)
    back_conv, sums1 = back_one(p_masks, mine, (near_p, far_p), flat(unit1), flat(inv1), pair, small, imgs, p_gate)
    back_conv = square(back_conv)
    res = square(res)
    back = functools.partial(images_back, back_conv, small, partner, mix_weight, res)
    if by_hops:
        p_keep, p_send = fold(p_keep, p_come, after=(sums1,))
        p_come = swap(p_send, p_order[2], n)
        d_keep, d_send = fold(d_keep, d_come, after=(sums1,))
        d_come = swap(d_send, d_order[1], n)
        grad, token = back(0, half, (), (p_send, d_send))
        p_keep, p_send = fold(p_keep, p_come, after=(token,))
        p_come = swap(p_send, p_order[1], n)
        grad, token = back(half, side, (grad,), (p_send,))
        keep, send = fold(p_keep, p_come, d_keep, d_come, after=(token,))
        come = swap(send, p_order[0], n)
        gk = taps_grad(back_conv, mixed, (0, 1, 2), (send,))
    else:
        grad, _ = back(0, side)
        gk = taps_grad(back_conv, mixed, (0, 1, 2))
        keep = jnp.stack(
            [
                lax.psum_scatter(jnp.concatenate(x).astype(F32), "dp", scatter_dimension=0, tiled=True)
                for x in ((p_near, p_far), (d_near, d_far))
            ]
        )
        come = jnp.zeros(keep.shape, BF16)

    grads, total = small_total(n if by_hops else 0, mine, gk, sums1, sums2, near_hb, far_hb, gdb, keep, come)
    rounds = [bits[k : k + 2] for k in range(1, len(bits), 2)] + [bits[:1]]
    for step, pair_bits in enumerate(rounds):
        others = [pair_bits[0], pair_bits[-1], sum(pair_bits)] if len(pair_bits) == 2 else pair_bits
        arrays = (total,) + tuple(swap(total, other, n) for other in others)
        total = meet(arrays, F32 if step == len(rounds) - 1 else BF16)
    states = (weight_in, first_in, second_in, weight_out, first_out, second_out, weight_down, first_down, second_down)
    *news, norm = adam_all(total, grads, states)
    grad_norm = norm[0, 0]
    factor = CLIP_NORM / jnp.maximum(grad_norm, CLIP_NORM)
    shard_len = small_params.shape[0]
    gs = lax.dynamic_slice_in_dim(total[:SQUARES].reshape(-1), me * shard_len, shard_len)
    position = me * shard_len + jnp.arange(shard_len, dtype=jnp.int32)
    small_rate = jnp.where(position < 54 * D + FF, LAYER_DECAY * RATE_VECTOR, RATE_VECTOR)
    small_decay = jnp.where(position < 49 * D, WEIGHT_DECAY, 0.0)
    new_small = adam(small_params, first_small, second_small, gs * factor, small_rate, small_decay)
    return (
        out.transpose(2, 0, 1, 3),
        grad.transpose(2, 0, 1, 3),
        grad_norm,
        *news,
        *new_small,
    )


def solution(mesh):
    four = P("dp", None, None, None)
    two = P("dp", None)
    one = P("dp")
    return jax.shard_map(
        functools.partial(local, mesh.shape["dp"]),
        mesh=mesh,
        in_specs=(four, one, one, one, four, two, two, two, one) + (two,) * 6 + (one,) * 2,
        out_specs=(four, four, P()) + (two,) * 9 + (one,) * 3,
        check_vma=False,
    )
```

```python
import functools
import jax
import jax.numpy as jnp
import numpy as np
from jax import lax
from jax.experimental import pallas as pl
from jax.experimental.pallas import tpu as pltpu
from jax.sharding import PartitionSpec as P

STEP = 10
DROP_RATE = 0.2
RATE_MATRIX = 0.05
RATE_VECTOR = 0.3
LAYER_DECAY = 0.8
BETA_ONE = 0.9
BETA_TWO = 0.999
ADAM_EPS = 1e-08
WEIGHT_DECAY = 0.05
CLIP_NORM = 1.0
D = 384
FF = 1536
LN_EPS = 1e-06
F32 = jnp.float32
BF16 = jnp.bfloat16
VMEM = pl.BlockSpec(memory_space=pltpu.VMEM)
SMEM = pl.BlockSpec(memory_space=pltpu.SMEM)
HBM = pl.BlockSpec(memory_space=pltpu.HBM)
ANY = pl.BlockSpec(memory_space=pl.ANY)
ROWS = (((0,), (0,)), ((), ()))
COLS = (((1,), (1,)), ((), ()))
DEPTH_BIAS, GAIN_ONE, BIAS_ONE, HIDDEN_BIAS, OUT_BIAS, LAYER_SCALE, GAIN_TWO, BIAS_TWO, DOWN_BIAS = 49, 50, 51, 52, 56, 57, 58, 59, 60
SQUARES = 62
HALF_PIECES = 16


def near(shape, dtype):
    return jax.ShapeDtypeStruct(shape, dtype)


def far(shape, dtype):
    return pltpu.HBM(shape, dtype)


def held(x):
    return pltpu.with_memory_space_constraint(x, pltpu.HBM)


def dma(src, dst, sem):
    return pltpu.make_async_copy(src, dst, sem)


def start(copies):
    for copy in copies:
        copy.start()


def wait(copies):
    for copy in copies:
        copy.wait()


class Far:
    def __init__(self, array):
        self.array = array


def kernel_call(body, out, specs, scratch, args, after, us, mib, aliases=None):
    specs = specs + [HBM if isinstance(x, Far) else ANY for x in after]
    args = tuple(args) + tuple(x.array if isinstance(x, Far) else x for x in after)
    args = [held(x) if spec is HBM else x for spec, x in zip(specs, args)]
    return pl.pallas_call(
        body,
        out_shape=tuple(out),
        in_specs=specs,
        out_specs=tuple(HBM if isinstance(x, type(far((8, 128), F32))) else VMEM for x in out),
        scratch_shapes=scratch,
        input_output_aliases=aliases or {},
        cost_estimate=pl.CostEstimate(flops=int(us * 1e9), bytes_accessed=0, transcendentals=0),
        compiler_params=pltpu.CompilerParams(vmem_limit_bytes=mib << 20),
    )(*args)


def norm_of(v):
    c = v - jnp.mean(v, axis=-1, keepdims=True)
    inv = lax.rsqrt(jnp.mean(c * c, axis=-1, keepdims=True) + LN_EPS)
    return c * inv, inv


def norm_back(back, unit, inv, gain):
    scaled = back * gain
    m1 = jnp.mean(scaled, axis=-1, keepdims=True)
    m2 = jnp.mean(scaled * unit, axis=-1, keepdims=True)
    return inv * (scaled - m1 - unit * m2)


def tile_of(k, imgs):
    groups = imgs // 8
    return pl.ds(pl.multiple_of(k % groups * 8, 8), 8), pl.ds(pl.multiple_of(k // groups * 128, 128), 128)


def tiles(h, imgs, tile, loop):
    count = imgs // 8 * (D // 128)
    if loop and isinstance(h, int):
        return lax.fori_loop(0, count, tile, 0)
    for k in range(count):
        tile(k, 0)
    return 0


def every_row(begin, end, side, do):
    for h in range(begin, min(end, 3)):
        do(h, range(3 - h, 7))
    low, high = max(begin, 3), min(end, side - 3)
    if low < high:
        lax.fori_loop(low, high, lambda h, _: do(h, range(7)), 0)
    for h in range(max(begin, side - 3), end):
        do(h, range(side + 3 - h))


def conv_rows(src, sums, taps, h, kys, t, lanes, side, base):
    pairs = side // 2

    def one(ky, acc):
        u, v, w = list(acc[:pairs]), list(acc[pairs : 2 * pairs + 1]), list(acc[2 * pairs + 1 :])
        row = h + ky - 3
        for out, shift, first, count, read in (
            (u, 0, 4, 3, lambda i: src[row, 2 * i, t, lanes]),
            (v, -1, 0, 4, lambda i: src[row, 2 * i + 1, t, lanes]),
            (w, 0, 7, 4, lambda i: sums[row, i, t, lanes]),
        ):
            x = [read(i) for i in range(pairs)]
            for j in range(count):
                tap = taps[ky * 11 + first + j, :, lanes]
                for k in range(len(out)):
                    i = k + shift - 1 + j
                    if 0 <= i < pairs:
                        out[k] = out[k] + x[i] * tap
        return tuple(u + v + w)

    acc = (jnp.zeros((8, 128), F32),) * (3 * pairs + 1)
    for ky in kys:
        acc = one(ky, acc)
    u, v, w = acc[:pairs], acc[pairs : 2 * pairs + 1], acc[2 * pairs + 1 :]
    out = []
    for k in range(pairs):
        out.append(base[2 * k] + (u[k] + v[k]))
        out.append(base[2 * k + 1] + (w[k] - (u[k] + v[k + 1])))
    return out


def fill_taps(small_ref, taps, flip):
    for ky in range(7):
        rows = []
        for kx in range(7):
            k = 48 - (ky * 7 + kx) if flip else ky * 7 + kx
            rows.append(small_ref[k : k + 1, :])
        rows = rows[0::2] + rows[1::2] + [rows[2 * j] + rows[2 * j + 1] for j in range(3)] + [rows[6]]
        for k, value in enumerate(rows):
            taps[ky * 11 + k] = jnp.broadcast_to(value, (8, D))


def add_columns(src, sums, row):
    pairs = sums.shape[1]
    sums[row] = jnp.stack([src[row, 2 * i] + src[row, 2 * i + 1] for i in range(pairs)])


def spread(scalars_ref, rows_ref):
    for i in range(rows_ref.shape[0]):
        rows_ref[i : i + 1, :] = jnp.full((1, rows_ref.shape[1]), scalars_ref[i], F32)


def select(row_ref, sel_ref):
    imgs, wide = row_ref.shape
    lane = lax.broadcasted_iota(jnp.int32, (imgs, wide), 1)
    for w in range(wide // imgs):
        sel_ref[w * imgs : (w + 1) * imgs, :] = (lane == row_ref[...] + w * imgs).astype(F32).astype(BF16)


def conv_kernel(begin, end, fresh, *refs):
    if fresh:
        small_hbm, img_hbm, partner_ref, weight_ref = refs[:4]
        mixed_hbm, unit_hbm, inv_hbm, norm_hbm, token_ref, small_ref, mixed_ref, taps, conv_ref, unit_ref, inv_ref, norm_ref, sem, pair_sums, img_ref, mix_ref, row_ref, sel_ref = refs[-18:]
    else:
        small_hbm, mixed_hbm = refs[:2]
        unit_hbm, inv_hbm, norm_hbm, token_ref, small_ref, mixed_ref, taps, conv_ref, unit_ref, inv_ref, norm_ref, sem, pair_sums = refs[-13:]
    side, _, imgs, _ = mixed_ref.shape
    low = max(begin - 3, 0)
    high = side if fresh else min(end + 3, side)
    rows = end - begin
    load = dma(small_hbm, small_ref, sem.at[4, 0])
    load.start()
    token_ref[...] = jnp.zeros(token_ref.shape, F32)

    def enter(h):
        if fresh:
            return dma(img_hbm.at[h], img_ref.at[h], sem.at[3, h])
        return dma(mixed_hbm.at[h], mixed_ref.at[h], sem.at[3, h])

    def store(h):
        return dma(mixed_ref.at[h], mixed_hbm.at[h], sem.at[5, h])

    for h in range(low, high):
        enter(h).start()
    if fresh:
        spread(weight_ref, mix_ref)
        for i in range(imgs):
            row_ref[i : i + 1, :] = jnp.full((1, row_ref.shape[1]), lax.rem(partner_ref[i], imgs), jnp.int32)
        select(row_ref, sel_ref)
    load.wait()
    fill_taps(small_ref, taps, False)
    if fresh:
        mix = mix_ref[...][None]
        rest = 1.0 - mix

        def blend(h, _):
            enter(h).wait()
            x = img_ref[h].reshape(side * imgs, D)
            other = jnp.dot(sel_ref[...], x, preferred_element_type=F32).reshape(side, imgs, D)
            mixed_ref[h] = mix * x.reshape(side, imgs, D).astype(F32) + rest * other
            add_columns(mixed_ref, pair_sums, h)
            store(h).start()
            return 0

        lax.fori_loop(0, side, blend, 0)
    else:
        for h in range(low, min(begin + 3, high)):
            enter(h).wait()
            add_columns(mixed_ref, pair_sums, h)

    def conv(h, kys):
        r = h - begin
        if not fresh:

            @pl.when(h + 3 < high)
            def _():
                enter(h + 3).wait()
                add_columns(mixed_ref, pair_sums, h + 3)

        def tile(k, _):
            at, lanes = tile_of(k, imgs)
            base = jnp.broadcast_to(small_ref[DEPTH_BIAS : DEPTH_BIAS + 1, lanes], (8, 128))
            acc = conv_rows(mixed_ref, pair_sums, taps, h, kys, at, lanes, side, [base] * side)
            for w in range(side):
                conv_ref[r, w, at, lanes] = acc[w]
            return 0

        return tiles(h, imgs, tile, True)

    every_row(begin, end, side, conv)
    gain = small_ref[GAIN_ONE : GAIN_ONE + 1, :][None]
    bias = small_ref[BIAS_ONE : BIAS_ONE + 1, :][None]

    def leave(r):
        return (
            dma(unit_ref.at[r], unit_hbm.at[r + begin], sem.at[0, r]),
            dma(inv_ref.at[r], inv_hbm.at[r + begin], sem.at[1, r]),
            dma(norm_ref.at[r], norm_hbm.at[r + begin], sem.at[2, r]),
        )

    def norm(r):
        unit, inv = norm_of(conv_ref[r])
        unit_ref[r] = unit.astype(BF16)
        inv_ref[r] = inv
        norm_ref[r] = (unit * gain + bias).astype(BF16)
        start(leave(r))

    def two(i, _):
        norm(2 * i)
        norm(2 * i + 1)
        return 0

    lax.fori_loop(0, rows // 2, two, 0)
    if rows % 2:
        norm(rows - 1)
    for r in range(rows):
        wait(leave(r))
    if fresh:
        for h in range(side):
            store(h).wait()


def conv_forward(small, inputs, begin, end, so_far=(), after=()):
    fresh = not so_far
    full = inputs[0].shape
    side = full[0]
    thin = full[:3] + (1,)
    rows = end - begin
    out = [far(full, BF16), far(thin, F32), far(full, BF16), near((8, 128), F32)]
    scratch = [
        pltpu.VMEM(small.shape, F32),
        pltpu.VMEM(full, F32),
        pltpu.VMEM((77, 8, D), F32),
        pltpu.VMEM((rows,) + full[1:], F32),
        pltpu.VMEM((rows,) + full[1:], BF16),
        pltpu.VMEM((rows,) + thin[1:], F32),
        pltpu.VMEM((rows,) + full[1:], BF16),
        pltpu.SemaphoreType.DMA((6, side)),
        pltpu.VMEM((side, side // 2) + full[2:], F32),
    ]
    specs = [HBM] * 2
    if fresh:
        out = [far(full, F32)] + out
        wide = side * full[2]
        scratch += [pltpu.VMEM(full, BF16), pltpu.VMEM((full[2], D), F32), pltpu.VMEM((full[2], wide), jnp.int32), pltpu.VMEM((wide, wide), BF16)]
        specs = [HBM] * 2 + [SMEM] * 2
    return kernel_call(
        functools.partial(conv_kernel, begin, end, fresh),
        out,
        specs + [HBM] * len(so_far),
        scratch,
        (small,) + tuple(inputs) + tuple(so_far),
        after,
        21 * rows / side + 3 * fresh,
        36,
        {2 + k: k for k in range(len(so_far))},
    )


def home(me, order, j, chips):
    if order is None:
        return j % HALF_PIECES if chips else j
    device = me
    for k, bit in enumerate(order):
        device = device ^ (((j >> k) & 1) * bit)
    return device >> 1 if chips else device


def keep_rows(mask_ref, keep_ref):
    for i in range(keep_ref.shape[0]):
        keep_ref[i : i + 1, :] = jnp.full((1, D), mask_ref[i], jnp.int32).astype(F32) / (1.0 - DROP_RATE)


def assembly(me, order, chips, first, src_hbm, whole_ref, sem):
    deep = src_hbm.shape[0] // HALF_PIECES

    def copy(j, _):
        to = pl.ds(pl.multiple_of(home(me, order, first + j, chips) * deep, 16), deep)
        dma(src_hbm.at[pl.ds(pl.multiple_of(j * deep, 16), deep), :], whole_ref.at[to, :], sem).start()
        return 0

    lax.fori_loop(0, HALF_PIECES, copy, 0)
    return dma(src_hbm, whole_ref.at[pl.ds(0, src_hbm.shape[0]), :], sem)


def deal(me, order, chips, first, out_ref, read):
    deep = out_ref.shape[0] // HALF_PIECES

    def move(j, _):
        begin = pl.multiple_of(home(me, order, first + j, chips) * deep, 16)
        to = pl.ds(pl.multiple_of(j * deep, 16), deep)
        for g in range(out_ref.shape[1] // 128):
            out_ref[to, g * 128 : (g + 1) * 128] = read(pl.ds(begin, deep), g).astype(BF16)
        return 0

    lax.fori_loop(0, HALF_PIECES, move, 0)


def even_first(rows, deep):
    blocks = [rows[d * deep // D][:, d * deep % D : d * deep % D + deep] for d in range(FF // deep)]
    return jnp.concatenate(blocks[0::2] + blocks[1::2], axis=1)


def even_last(even, odd, k, deep):
    per = D // deep
    blocks = []
    for d in range(per * k, per * k + per):
        source = odd if d % 2 else even
        blocks.append(source[:, d // 2 * deep : d // 2 * deep + deep])
    return jnp.concatenate(blocks, axis=1)


def block_kernel(block, masks, me_ref, norm_hbm, mixed_hbm, pnear_hbm, pfar_hbm, wnear_hbm, wfar_hbm, dy_hbm, small_hbm, mask_ref, *rest):
    act_hbm, dg_hbm, gnear_ref, gfar_ref, gdb_ref, out_ref, bb_hbm, sums_ref, res_hbm = rest[-32:-23]
    pair_ref, small_ref, keep_ref, norm_ref, mixed_ref, act_ref, dg_ref, branch_ref, unit_ref, inv_ref, out2_ref = rest[-23:-12]
    wd_ref, dy_ref, bb_ref, res_ref, acc, wide, wk, isem, osem, wsem, bsem, rsem = rest[-12:]
    rows = norm_hbm.shape[0]
    steps = rows // block
    imgs = keep_ref.shape[0]
    shape = (block // imgs, imgs, D)
    half = dy_hbm.shape[0]

    def spot(i):
        return pl.ds(pl.multiple_of(i * block, block), block)

    def enter(i):
        s = i % 2
        return (
            dma(norm_hbm.at[spot(i), :], norm_ref.at[s], isem.at[0, s]),
            dma(mixed_hbm.at[spot(i), :], mixed_ref.at[s], isem.at[1, s]),
        )

    def leave(i):
        s = i % 2
        pairs = ((act_ref, act_hbm), (dg_ref, dg_hbm))
        return [dma(a.at[s], b.at[spot(i), :], osem.at[k, s]) for k, (a, b) in enumerate(pairs)]

    me = me_ref[0]
    p_masks, w_masks, d_masks = masks
    load = dma(small_hbm, small_ref, wsem.at[0])
    start(enter(0))
    load.start()
    half_rows = FF // 2
    mine = 0 if p_masks is None else me % 2
    pair_in = []
    for src, first, which in ((pnear_hbm, 0, mine), (pfar_hbm, HALF_PIECES, 1 - mine)):
        to = pair_ref.at[pl.ds(pl.multiple_of(which * half_rows, half_rows), half_rows), :]
        pair_in.append(assembly(me, p_masks, True, first, src, to, wsem.at[1]))
    dy_in = dma(dy_hbm, dy_ref, wsem.at[3])
    wait(pair_in)
    down_in = [
        assembly(me, w_masks, False, first, src, wd_ref, wsem.at[2]) for first, src in ((0, wnear_hbm), (HALF_PIECES, wfar_hbm))
    ]
    dy_in.start()
    load.wait()
    keep_rows(mask_ref, keep_ref)
    keep = keep_ref[...][None]
    scale = keep * small_ref[LAYER_SCALE : LAYER_SCALE + 1, :][None]
    gain = small_ref[GAIN_TWO : GAIN_TWO + 1, :][None]
    bias = small_ref[BIAS_TWO : BIAS_TWO + 1, :][None]
    bias_rows = [small_ref[HIDDEN_BIAS + k : HIDDEN_BIAS + k + 1, :] for k in range(FF // D)]
    hidden_bias = jnp.concatenate(bias_rows, axis=1) if p_masks is None else even_first(bias_rows, FF >> len(p_masks))
    chunk = FF // 2

    def body(i, _):
        s = i % 2

        @pl.when(i + 1 < steps)
        def _():
            start(enter(i + 1))

        @pl.when(i >= 2)
        def _():
            wait(leave(i - 2))

        wait(enter(i))
        x = norm_ref[s]
        branch = jnp.broadcast_to(small_ref[OUT_BIAS : OUT_BIAS + 1, :], (block, D))

        def hidden(j):
            cols = slice(j * chunk, (j + 1) * chunk)
            return lax.dot_general(x, pair_ref[cols, :D], COLS, preferred_element_type=F32) + hidden_bias[:, cols]

        pre = hidden(0)
        for j in range(FF // chunk):
            after = hidden(j + 1) if j + 1 < FF // chunk else None
            cols = slice(j * chunk, (j + 1) * chunk)
            phi = 0.5 + 0.5 * lax.erf(pre * 0.7071067811865476)
            bell = jnp.exp2(pre * pre * -0.7213475204444817) * 0.3989422804014327
            act = (pre * phi).astype(BF16)
            act_ref[s, :, cols] = act
            dg_ref[s, :, cols] = (phi + pre * bell).astype(BF16)
            branch = branch + jnp.dot(act, pair_ref[cols, D:], preferred_element_type=F32)
            pre = after
        start(leave(i))
        split = branch_ref.shape[1:]
        branch_ref[i] = branch.astype(BF16).reshape(split)
        unit, inv = norm_of(mixed_ref[s].reshape(shape) + scale * branch.reshape(shape))
        unit_ref[i] = unit.astype(BF16).reshape(split)
        inv_ref[i] = inv.reshape(split[:-1] + (1,))
        out2_ref[i] = (unit * gain + bias).astype(BF16).reshape(split)
        return 0

    lax.fori_loop(0, steps, body, 0)

    wait(down_in)
    for g in range(6):
        wide[g] = wd_ref[:, pl.ds(g * 128, 128)].astype(F32)
        for k in range(4):
            wk[k, :, pl.ds(g * 128, 128)] = wide[g, pl.ds(k, D, stride=4), :].astype(BF16)
    sums_ref[...] = jnp.zeros(sums_ref.shape, F32)
    rows = half * half * imgs
    shape = (half * half, imgs, D)
    for k in range(2):
        acc[:, k * D : (k + 1) * D] = jnp.broadcast_to(small_ref[DOWN_BIAS + k : DOWN_BIAS + k + 1, :], (rows, D))
    dy_in.wait()
    gdb_ref[...] = jnp.sum(dy_ref[...].astype(F32).reshape(half * half, imgs, 2 * D), axis=0)

    def give(k):
        pairs = ((bb_ref, bb_hbm), (res_ref, res_hbm))
        return [dma(a.at[k], b.at[:, k // 2, :, k % 2], rsem.at[j, k]) for j, (a, b) in enumerate(pairs)]

    def quarter(k):
        dy = dy_ref[...].reshape(rows, 2 * D)
        x = out2_ref[:, k // 2, :, k % 2].reshape(rows, D)
        back = lax.dot_general(dy, wk[k], COLS, preferred_element_type=F32).reshape(shape)
        acc[...] += jnp.dot(x, wk[k], preferred_element_type=F32)
        gd = lax.dot_general(x, dy, ROWS, preferred_element_type=F32)
        for g in range(6):
            wide[g, pl.ds(k, D, stride=4), :] = gd[:, g * 128 : (g + 1) * 128]
        unit = unit_ref[:, k // 2, :, k % 2].reshape(shape).astype(F32)
        sums_ref[0] += jnp.sum(back * unit, axis=0)
        sums_ref[1] += jnp.sum(back, axis=0)
        res = norm_back(back, unit, inv_ref[:, k // 2, :, k % 2].reshape(half * half, imgs, 1), gain)
        res_ref[k] = res.astype(BF16).reshape(half, half, imgs, D)
        sums_ref[2] += jnp.sum(res * keep * branch_ref[:, k // 2, :, k % 2].reshape(shape).astype(F32), axis=0)
        bb = (res * scale).astype(BF16)
        bb_ref[k] = bb.reshape(half, half, imgs, D)
        start(give(k))
        sums_ref[3] += jnp.sum(bb.astype(F32), axis=0)

    for k in range(4):
        quarter(k)
    out_ref[...] = acc[...].astype(BF16).reshape(out_ref.shape)
    deal(me, d_masks, False, 0, gnear_ref, lambda at, g: wide[g, at, :])
    deal(me, d_masks, False, HALF_PIECES, gfar_ref, lambda at, g: wide[g, at, :])
    for k in range(4):
        wait(give(k))
    for i in range(max(steps - 2, 0), steps):
        wait(leave(i))


def block_both(masks, me, norm, mixed, pair, down, dy, small, mask, after=(), block=448):
    rows = norm.shape[0]
    half, _, imgs, _ = dy.shape
    area = half * half * imgs
    six = (half, 2, half, 2, imgs)
    two = lambda width, dtype: pltpu.VMEM((2, block, width), dtype)
    whole = lambda width, dtype: pltpu.VMEM(six + (width,), dtype)
    part = pltpu.VMEM((4, half, half, imgs, D), BF16)
    return kernel_call(
        functools.partial(block_kernel, block, masks),
        [far((rows, FF), BF16)] * 2
        + [near((2 * D, 2 * D), BF16)] * 2
        + [near((imgs, 2 * D), F32), near((half, half, imgs, 2 * D), BF16)]
        + [far(six + (D,), BF16), near((4, imgs, D), F32), far(six + (D,), BF16)],
        [SMEM] + [HBM] * 2 + [ANY, HBM] * 2 + [HBM] * 2 + [SMEM],
        [pltpu.VMEM((FF, 2 * D), BF16), pltpu.VMEM(small.shape, F32), pltpu.VMEM((imgs, D), F32)]
        + [two(D, BF16), two(D, F32), two(FF, BF16), two(FF, BF16)]
        + [whole(D, BF16), whole(D, BF16), whole(1, F32), whole(D, BF16)]
        + [pltpu.VMEM((4 * D, 2 * D), BF16), pltpu.VMEM(dy.shape, BF16), part, part]
        + [pltpu.VMEM((area, 2 * D), F32), pltpu.VMEM((6, 4 * D, 128), F32), pltpu.VMEM((4, D, 2 * D), BF16)]
        + [pltpu.SemaphoreType.DMA((2, 2)), pltpu.SemaphoreType.DMA((2, 2)), pltpu.SemaphoreType.DMA((4,))]
        + [pltpu.SemaphoreType.DMA((1,)), pltpu.SemaphoreType.DMA((2, 4))],
        (me, norm, mixed, *pair, *down, dy, small, mask),
        after,
        34,
        58,
    )


def pair_grad_kernel(block, first, masks, me_ref, bb_hbm, act_hbm, dg_hbm, norm_hbm, pair_hbm, *rest):
    g_ref, hb_ref, p_hbm, pair_ref, acc, bb_ref, act_ref, dg_ref, norm_ref, p_ref, sem, osem, wsem = rest[-13:]
    rows = bb_hbm.shape[0]
    imgs = hb_ref.shape[0]
    steps = rows // block
    wide = FF // 2
    me = me_ref[0]
    which = 0 if masks is None else me % 2
    which = 1 - which if first else which
    lanes = pl.ds(pl.multiple_of(which * wide, wide), wide)

    def spot(i):
        return pl.ds(pl.multiple_of(i * block, block), block)

    def enter(i):
        s = i % 2
        return (
            dma(bb_hbm.at[spot(i), :], bb_ref.at[s], sem.at[0, s]),
            dma(dg_hbm.at[spot(i), lanes], dg_ref.at[s], sem.at[1, s]),
            dma(act_hbm.at[spot(i), lanes], act_ref.at[s], sem.at[2, s]),
            dma(norm_hbm.at[spot(i), :], norm_ref.at[s], sem.at[3, s]),
        )

    def leave(i):
        return dma(p_ref.at[i % 2], p_hbm.at[spot(i), :], osem.at[i % 2])

    pair_in = [assembly(me, masks, True, first, pair_hbm, pair_ref, wsem.at[0])]
    start(enter(0))
    hb_ref[...] = jnp.zeros(hb_ref.shape, F32)
    acc[...] = jnp.zeros(acc.shape, F32)
    wait(pair_in)

    def body(i, _):
        s = i % 2

        @pl.when(i + 1 < steps)
        def _():
            start(enter(i + 1))

        @pl.when(i >= 2)
        def _():
            leave(i - 2).wait()

        wait(enter(i))
        b = bb_ref[s]
        back = lax.dot_general(b, pair_ref[:, D:], COLS, preferred_element_type=F32)
        acc[:, D:] += lax.dot_general(act_ref[s], b, ROWS, preferred_element_type=F32)
        p = (back * dg_ref[s].astype(F32)).astype(BF16)
        p_ref[s] = p
        hb_ref[...] += jnp.sum(p.astype(F32).reshape(block // imgs, imgs, wide), axis=0)
        acc[:, :D] += lax.dot_general(p, norm_ref[s], ROWS, preferred_element_type=F32)
        leave(i).start()
        return 0

    lax.fori_loop(0, steps, body, 0)
    deal(me, masks, True, first, g_ref, lambda at, g: acc[at, pl.ds(g * 128, 128)])
    for i in range(max(steps - 2, 0), steps):
        leave(i).wait()


def pair_grad(first, masks, me, bb, act, dg, norm, pair, imgs, after=(), block=448):
    rows = bb.shape[0]
    wide = FF // 2
    two = lambda width: pltpu.VMEM((2, block, width), BF16)
    return kernel_call(
        functools.partial(pair_grad_kernel, block, first, masks),
        [near((wide, 2 * D), BF16), near((imgs, wide), F32), far((rows, wide), BF16)],
        [SMEM] + [HBM] * 5,
        [pltpu.VMEM((wide, 2 * D), BF16), pltpu.VMEM((wide, 2 * D), F32)]
        + [two(D), two(wide), two(wide), two(D), two(wide)]
        + [pltpu.SemaphoreType.DMA((4, 2)), pltpu.SemaphoreType.DMA((2,)), pltpu.SemaphoreType.DMA((1,))],
        (me, bb, act, dg, norm, pair),
        after,
        13,
        28,
    )


def back_one_kernel(block, masks, me_ref, pnear_hbm, pfar_hbm, unit_hbm, inv_hbm, near_hbm, far_hbm, small_hbm, *rest):
    conv_hbm, sums_ref, near_ref, far_ref, small_ref, pnear_ref, pfar_ref, unit_ref, inv_ref, conv_ref, sem, wsem = rest[-12:]
    rows = pnear_hbm.shape[0]
    imgs = sums_ref.shape[1]
    steps = rows // block
    shape = (block // imgs, imgs, D)

    def spot(i):
        return pl.ds(pl.multiple_of(i * block, block), block)

    def enter(i):
        s = i % 2
        pairs = ((pnear_hbm, pnear_ref), (pfar_hbm, pfar_ref), (unit_hbm, unit_ref), (inv_hbm, inv_ref))
        return [dma(a.at[spot(i), :], b.at[s], sem.at[k, s]) for k, (a, b) in enumerate(pairs)]

    def leave(i):
        return dma(conv_ref.at[i % 2], conv_hbm.at[spot(i), :], sem.at[4, i % 2])

    load = dma(small_hbm, small_ref, wsem.at[0])
    left = pl.ds(0, D)
    pair_in = [
        assembly(me_ref[0], masks, True, first, src.at[:, left], dst, wsem.at[1])
        for first, src, dst in ((0, near_hbm, near_ref), (HALF_PIECES, far_hbm, far_ref))
    ]
    start(enter(0))
    load.start()
    sums_ref[...] = jnp.zeros(sums_ref.shape, F32)
    wait(pair_in)
    load.wait()
    gain = small_ref[GAIN_ONE : GAIN_ONE + 1, :][None]

    def body(i, _):
        s = i % 2

        @pl.when(i + 1 < steps)
        def _():
            start(enter(i + 1))

        @pl.when(i >= 2)
        def _():
            leave(i - 2).wait()

        wait(enter(i))
        back = jnp.dot(pnear_ref[s], near_ref[...], preferred_element_type=F32)
        back = (back + jnp.dot(pfar_ref[s], far_ref[...], preferred_element_type=F32)).reshape(shape)
        unit = unit_ref[s].reshape(shape).astype(F32)
        sums_ref[0] += jnp.sum(back * unit, axis=0)
        sums_ref[1] += jnp.sum(back, axis=0)
        out = norm_back(back, unit, inv_ref[s].reshape(shape[:2] + (1,)), gain)
        sums_ref[2] += jnp.sum(out, axis=0)
        conv_ref[s] = out.astype(BF16).reshape(block, D)
        leave(i).start()
        return 0

    lax.fori_loop(0, steps, body, 0)
    for i in range(max(steps - 2, 0), steps):
        leave(i).wait()


def back_one(masks, me, p, unit, inv, pair, small, imgs, after=(), block=784):
    rows = unit.shape[0]
    wide = FF // 2
    two = lambda width, dtype: pltpu.VMEM((2, block, width), dtype)
    return kernel_call(
        functools.partial(back_one_kernel, block, masks),
        [far((rows, D), BF16), near((3, imgs, D), F32)],
        [SMEM] + [HBM] * 7,
        [pltpu.VMEM((wide, D), BF16)] * 2
        + [pltpu.VMEM(small.shape, F32)]
        + [two(wide, BF16), two(wide, BF16), two(D, BF16), two(1, F32), two(D, BF16)]
        + [pltpu.SemaphoreType.DMA((5, 2)), pltpu.SemaphoreType.DMA((2,))],
        (me, *p, unit, inv, *pair, small),
        after,
        11,
        32,
    )


def taps_kernel(groups, conv_hbm, mixed_hbm, *rest):
    g_ref, conv_ref, mixed_ref, sums, even, odd, last, sem = rest[-8:]
    side, _, imgs, _ = conv_hbm.shape
    pairs = side // 2

    def enter(k):
        lanes = pl.ds(pl.multiple_of((k + groups[0]) * 128, 128), 128)
        return (
            dma(mixed_hbm.at[:, :, :, lanes], mixed_ref.at[k], sem.at[0, k]),
            dma(conv_hbm.at[:, :, :, lanes], conv_ref.at[k], sem.at[1, k]),
        )

    for k in range(len(groups)):
        start(enter(k))
    def group(k, _):
        wait(enter(k))

        def prepare(h, _):
            x = [mixed_ref[k, h, w] for w in range(side)]
            d = [conv_ref[k, h, w].astype(F32) for w in range(side)]
            for i in range(pairs):
                sums[h, i] = x[2 * i] + x[2 * i + 1]
                last[h, i] = d[2 * i + 1]
                even[h, i] = d[2 * i] - d[2 * i + 1]
                odd[h, i + 1] = (d[2 * i + 2] if i + 1 < pairs else jnp.zeros_like(d[0])) - d[2 * i + 1]
            odd[h, 0] = d[0]
            return 0

        lax.fori_loop(0, side, prepare, 0)
        for ky in range(7):
            first = max(3 - ky, 0)
            count = min(side, side + 3 - ky) - first

            def row(h, acc):
                acc = list(acc)
                for t in range(imgs // 8):
                    at = pl.ds(t * 8, 8)
                    for begin, shift, taps, length, read_x, read_d in (
                        (4, 0, 3, pairs, lambda i: mixed_ref[k, h + ky - 3, 2 * i, at], lambda i: even[h, i, at]),
                        (0, -1, 4, pairs + 1, lambda i: mixed_ref[k, h + ky - 3, 2 * i + 1, at], lambda i: odd[h, i, at]),
                        (7, 0, 4, pairs, lambda i: sums[h + ky - 3, i, at], lambda i: last[h, i, at]),
                    ):
                        x = [read_x(i) for i in range(pairs)]
                        for a in range(length):
                            d = read_d(a)
                            for j in range(taps):
                                i = a + shift - 1 + j
                                if 0 <= i < pairs:
                                    acc[begin + j] = acc[begin + j] + x[i] * d
                return tuple(acc)

            acc = lax.fori_loop(
                0, count // 2, lambda r, acc: row(first + 2 * r + 1, row(first + 2 * r, acc)), (jnp.zeros((8, 128), F32),) * 11
            )
            if count % 2:
                acc = row(first + count - 1, acc)
            even_taps = [acc[j] + acc[7 + j] for j in range(4)]
            odd_taps = [acc[4 + j] + acc[7 + j] for j in range(3)]
            for kx in range(7):
                value = odd_taps[kx // 2] if kx % 2 else even_taps[kx // 2]
                g_ref[ky * 7 + kx, :, pl.ds(pl.multiple_of(k * 128, 128), 128)] = value
        return 0

    lax.fori_loop(0, len(groups), group, 0)


def taps_grad(conv, mixed, groups, after=()):
    side, _, imgs, _ = conv.shape
    lanes = lambda dtype: pltpu.VMEM((len(groups),) + conv.shape[:3] + (128,), dtype)
    part = lambda columns: pltpu.VMEM((side, columns, imgs, 128), F32)
    return kernel_call(
        functools.partial(taps_kernel, groups),
        [near((49, 8, 128 * len(groups)), F32)],
        [HBM] * 2,
        [lanes(BF16), lanes(F32), part(side // 2), part(side // 2), part(side // 2 + 1), part(side // 2), pltpu.SemaphoreType.DMA((2, len(groups)))],
        (conv, mixed),
        after,
        4.7 * len(groups),
        28,
    )[0]


def images_kernel(begin, end, conv_hbm, small_hbm, partner_ref, weight_ref, res_hbm, *rest):
    g_hbm, token_ref, small_ref, raw_ref, conv_ref, taps, res_ref, out_ref, mix_ref, row_ref, sel_ref, rest_ref, sem, csem, pair_sums, rsem = rest[-16:]
    side, _, imgs, _ = conv_hbm.shape
    low = max(begin - 3, 0)
    high = min(end + 3, side)
    load = dma(small_hbm, small_ref, csem.at[side])
    load.start()
    token_ref[...] = jnp.zeros(token_ref.shape, F32)

    def bring(h):
        return dma(conv_hbm.at[h], raw_ref.at[h], csem.at[h])

    def widen(h):
        bring(h).wait()
        conv_ref[h] = raw_ref[h].astype(F32)
        add_columns(conv_ref, pair_sums, h)

    def enter(h):
        return dma(res_hbm.at[h], res_ref.at[h - begin], rsem.at[h - begin])

    def leave(h):
        return dma(out_ref.at[h - begin], g_hbm.at[h], sem.at[1, 0])

    for h in range(low, high):
        bring(h).start()
        if h == min(begin + 3, high - 1):
            for r in range(begin, end):
                enter(r).start()
    spread(weight_ref, mix_ref)
    for i in range(imgs):
        row_ref[pl.ds(lax.rem(partner_ref[i], imgs), 1), :] = jnp.full((1, row_ref.shape[1]), i, jnp.int32)
    select(row_ref, sel_ref)
    load.wait()
    fill_taps(small_ref, taps, True)
    mix = mix_ref[...][None]
    others = 1.0 - mix
    for h in range(low, min(begin + 3, high)):
        widen(h)

    def row(h, kys):
        @pl.when(h + 3 < high)
        def _():
            widen(h + 3)

        enter(h).wait()
        rest_ref[...] = res_ref[h - begin].astype(F32)

        def tile(k, _):
            at, lanes = tile_of(k, imgs)
            base = [rest_ref[w, at, lanes] for w in range(side)]
            acc = conv_rows(conv_ref, pair_sums, taps, h, kys, at, lanes, side, base)
            for w in range(side):
                out_ref[h - begin, w, at, lanes] = acc[w]
            return 0

        return tiles(h, imgs, tile, False)

    every_row(begin, end, side, row)

    def unmix(r):
        v = out_ref[r]
        part = (others * v).reshape(side * imgs, D)
        upper = part.astype(BF16)
        lower = (part - upper.astype(F32)).astype(BF16)
        back = jnp.dot(sel_ref[...], upper, preferred_element_type=F32)
        back = back + jnp.dot(sel_ref[...], lower, preferred_element_type=F32)
        out_ref[r] = mix * v + back.reshape(side, imgs, D)
        leave(begin + r).start()

    def two(i, _):
        unmix(2 * i)
        unmix(2 * i + 1)
        return 0

    lax.fori_loop(0, (end - begin) // 2, two, 0)
    for h in range(begin, end):
        leave(h).wait()


def images_back(conv, small, partner, weight, res, begin, end, so_far=(), after=()):
    side, _, imgs, _ = conv.shape
    return kernel_call(
        functools.partial(images_kernel, begin, end),
        [far(conv.shape, F32), near((8, 128), F32)],
        [HBM, HBM, SMEM, SMEM, HBM] + [HBM] * len(so_far),
        [
            pltpu.VMEM(small.shape, F32),
            pltpu.VMEM(conv.shape, BF16),
            pltpu.VMEM(conv.shape, F32),
            pltpu.VMEM((77, 8, D), F32),
            pltpu.VMEM((end - begin, side, imgs, D), BF16),
            pltpu.VMEM((end - begin, side, imgs, D), F32),
            pltpu.VMEM((imgs, D), F32),
            pltpu.VMEM((imgs, side * imgs), jnp.int32),
            pltpu.VMEM((side * imgs, side * imgs), BF16),
            pltpu.VMEM((side, imgs, D), F32),
            pltpu.SemaphoreType.DMA((2, 2)),
            pltpu.SemaphoreType.DMA((side + 1,)),
            pltpu.VMEM((side, side // 2, imgs, D), F32),
            pltpu.SemaphoreType.DMA((end - begin,)),
        ],
        (conv, small, partner, weight, res) + tuple(so_far),
        after,
        22 * (end - begin) / side,
        28,
        {5: 0} if so_far else {},
    )


def ready_kernel(in_hbm, out_hbm, down_hbm, *rest):
    pair_ref, low_ref, in_ref, out_ref, down_ref, sem = rest[-6:]
    pairs = ((in_hbm, in_ref), (out_hbm, out_ref), (down_hbm, down_ref))
    copies = [dma(a, b, sem.at[k]) for k, (a, b) in enumerate(pairs)]
    start(copies)
    wait(copies)
    pair_ref[0, :, :D] = in_ref[...].astype(BF16)
    pair_ref[0, :, D:] = out_ref[...].astype(BF16)
    low_ref[0] = down_ref[...].astype(BF16)


def ready(weight_in, weight_out, weight_down, after=()):
    deep = weight_in.shape[0]
    return kernel_call(
        ready_kernel,
        [near((1, deep, 2 * D), BF16)] * 2,
        [HBM] * 3,
        [pltpu.VMEM(x.shape, F32) for x in (weight_in, weight_out, weight_down)] + [pltpu.SemaphoreType.DMA((3,))],
        (weight_in, weight_out, weight_down),
        after,
        0.5,
        8,
    )


def join_kernel(first_ref, second_ref, *rest):
    out_ref = rest[-1]
    k = first_ref.shape[0]
    out_ref[:k] = first_ref[...]
    out_ref[k:] = second_ref[...]


def join(first, second, after=()):
    return kernel_call(
        join_kernel,
        [near((2 * first.shape[0],) + first.shape[1:], first.dtype)],
        [VMEM] * 2,
        [],
        (first, second),
        after,
        0.5,
        8,
    )[0]


def fold_kernel(count, *refs):
    ins, (stay_ref, leave_ref) = refs[: 2 * count], refs[-2:]
    k = stay_ref.shape[0] // count
    for i in range(count):
        keep_ref, come_ref = ins[2 * i], ins[2 * i + 1]
        stay_ref[i * k : (i + 1) * k] = keep_ref[:k].astype(F32) + come_ref[:k].astype(F32)
        leave_ref[i * k : (i + 1) * k] = (keep_ref[k:].astype(F32) + come_ref[k:].astype(F32)).astype(BF16)


def fold(*arrays, after=()):
    slots, deep, wide = arrays[0].shape
    count = len(arrays) // 2
    return kernel_call(
        functools.partial(fold_kernel, count),
        [near((count * slots // 2, deep, wide), F32), near((count * slots // 2, deep, wide), BF16)],
        [VMEM] * len(arrays),
        [],
        arrays,
        after,
        0.5,
        12,
    )


def part_kernel(*refs):
    ins, outs = refs[:4], refs[-4:]
    for i in range(2):
        keep_ref, come_ref = ins[2 * i], ins[2 * i + 1]
        for slot, out_ref in enumerate(outs):
            out_ref[i] = (keep_ref[slot].astype(F32) + come_ref[slot].astype(F32)).astype(out_ref.dtype)


def part(p_keep, p_come, d_keep, d_come, after=()):
    shape = (2,) + p_keep.shape[1:]
    return kernel_call(
        part_kernel,
        [near(shape, F32)] + [near(shape, BF16)] * 3,
        [VMEM] * 4,
        [],
        (p_keep, p_come, d_keep, d_come),
        after,
        0.5,
        12,
    )


def small_kernel(hops, me_ref, gk_ref, sums1_ref, sums2_ref, near_ref, far_ref, db_ref, keep_ref, *rest):
    sum_ref, send_ref, total = rest[-3:]
    grads = keep_ref[...]
    for come_ref in rest[:-3]:
        grads = grads + come_ref[...].astype(F32)
    sum_ref[...] = grads
    rows = lambda x: jnp.sum(x, axis=0, keepdims=True)
    for t in range(49):
        total[t : t + 1, :] = rows(gk_ref[t])
    for row, value in (
        (DEPTH_BIAS, sums1_ref[2]),
        (GAIN_ONE, sums1_ref[0]),
        (BIAS_ONE, sums1_ref[1]),
        (OUT_BIAS, sums2_ref[3]),
        (LAYER_SCALE, sums2_ref[2]),
        (GAIN_TWO, sums2_ref[0]),
        (BIAS_TWO, sums2_ref[1]),
    ):
        total[row : row + 1, :] = rows(value)
    mine, other = rows(near_ref[...]), rows(far_ref[...])
    if hops:
        odd_device = (me_ref[0] % 2).astype(F32)
        even = mine * (1.0 - odd_device) + other * odd_device
        odd = other * (1.0 - odd_device) + mine * odd_device
    for k in range(4):
        if hops:
            value = even_last(even, odd, k, FF // hops)
        else:
            value = (mine, other)[k // 2][:, k % 2 * D : k % 2 * D + D]
        total[HIDDEN_BIAS + k : HIDDEN_BIAS + k + 1, :] = value
    for k in range(2):
        total[DOWN_BIAS + k : DOWN_BIAS + k + 1, :] = rows(db_ref[:, k * D : (k + 1) * D])
    square = jnp.full((1, D), jnp.sum(grads * grads), F32)
    upper = square.astype(BF16).astype(F32)
    total[SQUARES : SQUARES + 1, :] = upper
    total[SQUARES + 1 : SQUARES + 2, :] = square - upper
    send_ref[...] = total[...].astype(BF16)


def small_total(hops, me, gk, sums1, sums2, near_hb, far_hb, db, keep, *come):
    return kernel_call(
        functools.partial(small_kernel, hops),
        [near(keep.shape, F32), near((SQUARES + 2, D), BF16)],
        [SMEM] + [VMEM] * (7 + len(come)),
        [pltpu.VMEM((SQUARES + 2, D), F32)],
        (me, gk, sums1, sums2, near_hb, far_hb, db, keep, *come),
        (),
        1,
        8,
    )


def meet_kernel(*refs):
    arrays, out_ref = refs[:-1], refs[-1]
    sums = [x[...].astype(F32) for x in arrays]
    while len(sums) > 1:
        sums = [a + b for a, b in zip(sums[::2], sums[1::2])]
    total = sums[0]
    square = total[SQUARES : SQUARES + 1] + total[SQUARES + 1 : SQUARES + 2]
    upper = square.astype(BF16).astype(F32)
    out_ref[...] = total.astype(out_ref.dtype)
    out_ref[SQUARES : SQUARES + 2, :] = jnp.concatenate([upper, square - upper], axis=0).astype(out_ref.dtype)


def meet(arrays, dtype):
    return kernel_call(meet_kernel, [near(arrays[0].shape, dtype)], [VMEM] * len(arrays), [], arrays, (), 0.3, 8)[0]


def adam(weight, first, second, grad, rate, decay):
    first = BETA_ONE * first + (1.0 - BETA_ONE) * grad
    second = BETA_TWO * second + (1.0 - BETA_TWO) * grad * grad
    first_hat = first / (1.0 - BETA_ONE**STEP)
    second_hat = second / (1.0 - BETA_TWO**STEP)
    weight = weight - rate * (first_hat / (jnp.sqrt(second_hat) + ADAM_EPS) + decay * weight)
    return first, second, weight


def adam_kernel(total_ref, grads_ref, *refs):
    ins, outs = refs[:9], refs[9:18]
    norm_ref = refs[18]
    gs = total_ref[:SQUARES]
    norm = jnp.sqrt(jnp.sum(gs * gs) + jnp.sum(total_ref[SQUARES : SQUARES + 2, 0:1]))
    norm_ref[0, 0] = norm
    factor = CLIP_NORM / jnp.maximum(norm, CLIP_NORM)
    grads = (grads_ref[0, :, :D], grads_ref[0, :, D:], grads_ref[1])
    rates = (LAYER_DECAY * RATE_MATRIX, LAYER_DECAY * RATE_MATRIX, RATE_MATRIX)
    for k in range(3):
        new = adam(ins[3 * k][...], ins[3 * k + 1][...], ins[3 * k + 2][...], grads[k] * factor, rates[k], WEIGHT_DECAY)
        for out_ref, value in zip(outs[3 * k : 3 * k + 3], new):
            out_ref[...] = value


def adam_all(total, grads, states):
    return pl.pallas_call(
        adam_kernel,
        out_shape=tuple(near(x.shape, F32) for x in states) + (near((1, 1), F32),),
        in_specs=[VMEM] * 11,
        out_specs=(VMEM,) * 9 + (SMEM,),
        cost_estimate=pl.CostEstimate(flops=int(2e9), bytes_accessed=0, transcendentals=0),
        compiler_params=pltpu.CompilerParams(vmem_limit_bytes=12 << 20),
    )(total, grads, *states)


def swap(x, bit, n):
    return lax.ppermute(x, "dp", [(i, i ^ bit) for i in range(n)])


def is_set(bit):
    return (lax.axis_index("dp") & bit) != 0


def gather_natural(shard, n, order, gates=None):
    have = shard
    met = []
    for hop, bit in enumerate(order):
        if gates and hop in gates:
            have, _ = lax.optimization_barrier((have, gates[hop]))
        other = swap(have, bit, n)
        axis = sum(1 for b in met if b > bit)
        mine = is_set(bit)
        have = jnp.stack([jnp.where(mine, other, have), jnp.where(mine, have, other)], axis=axis)
        met.append(bit)
    return have.reshape((n,) + shard.shape)


def local(n, images, mix_weight, partner, keep_mask, cotangent, weight_in, weight_out, weight_down, small_params,
          first_in, second_in, first_out, second_out, first_down, second_down, first_small, second_small):
    imgs, side = images.shape[:2]
    half = side // 2
    pixels = side * side * imgs
    me = lax.axis_index("dp")
    bits = [1 << k for k in range(n.bit_length() - 1)]
    deep = FF // n
    by_hops = n == 32

    pair, down = ready(weight_in, weight_out, weight_down)
    mine = me[None].astype(jnp.int32)
    p_masks = w_masks = d_masks = None
    if by_hops:
        p_order = [16, 8, 4, 2, 1]
        w_order = [16, 8, 2, 4, 1]
        d_order = p_order
        p_masks, w_masks, d_masks = p_order, w_order, d_order

    img = images.transpose(1, 2, 0, 3)
    dy = cotangent.transpose(1, 2, 0, 3)
    flat = lambda a: a.reshape(pixels, a.shape[-1])
    square = lambda a: a.reshape(side, side, imgs, a.shape[-1])

    cut = [0, 3, 10, side]
    gates = None
    if by_hops:
        gates = {0: pair}
        pair = join(pair, swap(pair, p_order[0], n))
        gates[2] = pair
        down = join(down, swap(down, w_order[0], n))
        pair = join(pair, swap(pair, p_order[1], n))
        gates[4] = pair
    small = gather_natural(small_params.astype(BF16), n, bits[1:] + bits[:1], gates).reshape(-1, D).astype(F32)
    if by_hops:
        down = join(down, swap(down, w_order[1], n))
    mixed, *made, token = conv_forward(small, (img, partner, mix_weight), cut[0], cut[1])
    for piece in (1, 2):
        if by_hops:
            pair = join(pair, swap(pair, p_order[piece + 1], n), (token,))
            down = join(down, swap(down, w_order[piece + 1], n), (token,))
        *made, token = conv_forward(small, (mixed,), cut[piece], cut[piece + 1], tuple(made), (pair, down))
    unit1, inv1, norm1 = made
    if by_hops:
        pair = (pair, swap(pair, p_order[4], n))
        down = (down, swap(down, w_order[4], n))
    else:
        pair, down = (lax.all_gather(x[0], "dp", axis=0, tiled=True).reshape(2, FF // 2, 2 * D) for x in (pair, down))
    pair = tuple(x.reshape(FF // 2, 2 * D) for x in pair)
    down = tuple(x.reshape(FF // 2, 2 * D) for x in down)
    act, dg, d_near, d_far, gdb, out, bb, sums2, res = block_both(
        (p_masks, w_masks, d_masks), mine, flat(norm1), flat(mixed), pair, down, dy, small, keep_mask
    )
    shards = (n // 2, deep, 2 * D)
    if by_hops:
        d_keep = d_near.reshape(shards)
        d_come = swap(d_far.reshape(shards), d_order[4], n)
    grads_of = lambda which, after: pair_grad(
        16 * which, p_masks, mine, flat(bb), act, dg, flat(norm1), pair[which], imgs, after
    )
    p_far, far_hb, far_p = grads_of(1, ())
    if by_hops:
        d_keep, d_send = fold(d_keep, d_come, after=(far_hb,))
        d_come = swap(d_send, d_order[3], n)
        p_come = swap(p_far.reshape(shards), p_order[4], n)
    p_near, near_hb, near_p = grads_of(0, (d_send,) if by_hops else (far_hb,))
    p_gate = ()
    if by_hops:
        p_keep, p_send = fold(p_near.reshape(shards), p_come, after=(near_hb,))
        p_come = swap(p_send, p_order[3], n)
        d_keep, d_send = fold(d_keep, d_come, after=(near_hb,))
        d_come = swap(d_send, d_order[2], n)
        p_gate = (p_send, d_send)
    back_conv, sums1 = back_one(p_masks, mine, (near_p, far_p), flat(unit1), flat(inv1), pair, small, imgs, p_gate)
    back_conv = square(back_conv)
    res = square(res)
    back = functools.partial(images_back, back_conv, small, partner, mix_weight, res)
    if by_hops:
        p_keep, p_send = fold(p_keep, p_come, after=(sums1,))
        p_come = swap(p_send, p_order[2], n)
        grad, token = back(0, side, (), (p_send,))
        keep, *send = part(p_keep, p_come, d_keep, d_come, after=(token,))
        come = [swap(x, bits, n) for x, bits in zip(send, (16, 8, 24))]
        gk = taps_grad(back_conv, mixed, (0, 1, 2), tuple(send))
    else:
        grad, _ = back(0, side)
        gk = taps_grad(back_conv, mixed, (0, 1, 2))
        keep = jnp.stack(
            [
                lax.psum_scatter(jnp.concatenate(x).astype(F32), "dp", scatter_dimension=0, tiled=True)
                for x in ((p_near, p_far), (d_near, d_far))
            ]
        )
        come = ()

    grads, total = small_total(n if by_hops else 0, mine, gk, sums1, sums2, near_hb, far_hb, gdb, keep, *come)
    rounds = [bits[k : k + 2] for k in range(1, len(bits), 2)] + [bits[:1]]
    for step, pair_bits in enumerate(rounds):
        others = [pair_bits[0], pair_bits[-1], sum(pair_bits)] if len(pair_bits) == 2 else pair_bits
        arrays = (total,) + tuple(swap(total, other, n) for other in others)
        total = meet(arrays, F32 if step == len(rounds) - 1 else BF16)
    states = (weight_in, first_in, second_in, weight_out, first_out, second_out, weight_down, first_down, second_down)
    *news, norm = adam_all(total, grads, states)
    grad_norm = norm[0, 0]
    factor = CLIP_NORM / jnp.maximum(grad_norm, CLIP_NORM)
    shard_len = small_params.shape[0]
    gs = lax.dynamic_slice_in_dim(total[:SQUARES].reshape(-1), me * shard_len, shard_len)
    position = me * shard_len + jnp.arange(shard_len, dtype=jnp.int32)
    small_rate = jnp.where(position < 54 * D + FF, LAYER_DECAY * RATE_VECTOR, RATE_VECTOR)
    small_decay = jnp.where(position < 49 * D, WEIGHT_DECAY, 0.0)
    new_small = adam(small_params, first_small, second_small, gs * factor, small_rate, small_decay)
    return (
        out.transpose(2, 0, 1, 3),
        grad.transpose(2, 0, 1, 3),
        grad_norm,
        *news,
        *new_small,
    )


def solution(mesh):
    four = P("dp", None, None, None)
    two = P("dp", None)
    one = P("dp")
    return jax.shard_map(
        functools.partial(local, mesh.shape["dp"]),
        mesh=mesh,
        in_specs=(four, one, one, one, four, two, two, two, one) + (two,) * 6 + (one,) * 2,
        out_specs=(four, four, P()) + (two,) * 9 + (one,) * 3,
        check_vma=False,
    )
```

```python
import functools
import jax
import jax.numpy as jnp
import numpy as np
from jax import lax
from jax.experimental import pallas as pl
from jax.experimental.pallas import tpu as pltpu
from jax.sharding import PartitionSpec as P

STEP = 10
DROP_RATE = 0.2
RATE_MATRIX = 0.05
RATE_VECTOR = 0.3
LAYER_DECAY = 0.8
BETA_ONE = 0.9
BETA_TWO = 0.999
ADAM_EPS = 1e-08
WEIGHT_DECAY = 0.05
CLIP_NORM = 1.0
D = 384
FF = 1536
LN_EPS = 1e-06
F32 = jnp.float32
BF16 = jnp.bfloat16
VMEM = pl.BlockSpec(memory_space=pltpu.VMEM)
SMEM = pl.BlockSpec(memory_space=pltpu.SMEM)
HBM = pl.BlockSpec(memory_space=pltpu.HBM)
ANY = pl.BlockSpec(memory_space=pl.ANY)
ROWS = (((0,), (0,)), ((), ()))
COLS = (((1,), (1,)), ((), ()))
DEPTH_BIAS, GAIN_ONE, BIAS_ONE, HIDDEN_BIAS, OUT_BIAS, LAYER_SCALE, GAIN_TWO, BIAS_TWO, DOWN_BIAS = 49, 50, 51, 52, 56, 57, 58, 59, 60
SQUARES = 62
HALF_PIECES = 16


def near(shape, dtype):
    return jax.ShapeDtypeStruct(shape, dtype)


def far(shape, dtype):
    return pltpu.HBM(shape, dtype)


def held(x):
    return pltpu.with_memory_space_constraint(x, pltpu.HBM)


def dma(src, dst, sem):
    return pltpu.make_async_copy(src, dst, sem)


def start(copies):
    for copy in copies:
        copy.start()


def wait(copies):
    for copy in copies:
        copy.wait()


class Far:
    def __init__(self, array):
        self.array = array


def kernel_call(body, out, specs, scratch, args, after, us, mib, aliases=None):
    specs = specs + [HBM if isinstance(x, Far) else ANY for x in after]
    args = tuple(args) + tuple(x.array if isinstance(x, Far) else x for x in after)
    args = [held(x) if spec is HBM else x for spec, x in zip(specs, args)]
    return pl.pallas_call(
        body,
        out_shape=tuple(out),
        in_specs=specs,
        out_specs=tuple(HBM if isinstance(x, type(far((8, 128), F32))) else VMEM for x in out),
        scratch_shapes=scratch,
        input_output_aliases=aliases or {},
        cost_estimate=pl.CostEstimate(flops=int(us * 1e9), bytes_accessed=0, transcendentals=0),
        compiler_params=pltpu.CompilerParams(vmem_limit_bytes=mib << 20),
    )(*args)


def norm_of(v):
    c = v - jnp.mean(v, axis=-1, keepdims=True)
    inv = lax.rsqrt(jnp.mean(c * c, axis=-1, keepdims=True) + LN_EPS)
    return c * inv, inv


def norm_back(back, unit, inv, gain):
    scaled = back * gain
    m1 = jnp.mean(scaled, axis=-1, keepdims=True)
    m2 = jnp.mean(scaled * unit, axis=-1, keepdims=True)
    return inv * (scaled - m1 - unit * m2)


def tile_of(k, imgs):
    groups = imgs // 8
    return pl.ds(pl.multiple_of(k % groups * 8, 8), 8), pl.ds(pl.multiple_of(k // groups * 128, 128), 128)


def tiles(h, imgs, tile, loop):
    count = imgs // 8 * (D // 128)
    if loop and isinstance(h, int):
        return lax.fori_loop(0, count, tile, 0)
    for k in range(count):
        tile(k, 0)
    return 0


def every_row(begin, end, side, do):
    for h in range(begin, min(end, 3)):
        do(h, range(3 - h, 7))
    low, high = max(begin, 3), min(end, side - 3)
    if low < high:
        lax.fori_loop(low, high, lambda h, _: do(h, range(7)), 0)
    for h in range(max(begin, side - 3), end):
        do(h, range(side + 3 - h))


def conv_rows(src, sums, taps, h, kys, t, lanes, side, base):
    pairs = side // 2

    def one(ky, acc):
        u, v, w = list(acc[:pairs]), list(acc[pairs : 2 * pairs + 1]), list(acc[2 * pairs + 1 :])
        row = h + ky - 3
        for out, shift, first, count, read in (
            (u, 0, 4, 3, lambda i: src[row, 2 * i, t, lanes]),
            (v, -1, 0, 4, lambda i: src[row, 2 * i + 1, t, lanes]),
            (w, 0, 7, 4, lambda i: sums[row, i, t, lanes]),
        ):
            x = [read(i) for i in range(pairs)]
            for j in range(count):
                tap = taps[ky * 11 + first + j, :, lanes]
                for k in range(len(out)):
                    i = k + shift - 1 + j
                    if 0 <= i < pairs:
                        out[k] = out[k] + x[i] * tap
        return tuple(u + v + w)

    acc = (jnp.zeros((8, 128), F32),) * (3 * pairs + 1)
    for ky in kys:
        acc = one(ky, acc)
    u, v, w = acc[:pairs], acc[pairs : 2 * pairs + 1], acc[2 * pairs + 1 :]
    out = []
    for k in range(pairs):
        out.append(base[2 * k] + (u[k] + v[k]))
        out.append(base[2 * k + 1] + (w[k] - (u[k] + v[k + 1])))
    return out


def fill_taps(small_ref, taps, flip):
    for ky in range(7):
        rows = []
        for kx in range(7):
            k = 48 - (ky * 7 + kx) if flip else ky * 7 + kx
            rows.append(small_ref[k : k + 1, :])
        rows = rows[0::2] + rows[1::2] + [rows[2 * j] + rows[2 * j + 1] for j in range(3)] + [rows[6]]
        for k, value in enumerate(rows):
            taps[ky * 11 + k] = jnp.broadcast_to(value, (8, D))


def add_columns(src, sums, row):
    pairs = sums.shape[1]
    sums[row] = jnp.stack([src[row, 2 * i] + src[row, 2 * i + 1] for i in range(pairs)])


def spread(scalars_ref, rows_ref):
    for i in range(rows_ref.shape[0]):
        rows_ref[i : i + 1, :] = jnp.full((1, rows_ref.shape[1]), scalars_ref[i], F32)


def select(row_ref, sel_ref):
    imgs, wide = row_ref.shape
    lane = lax.broadcasted_iota(jnp.int32, (imgs, wide), 1)
    for w in range(wide // imgs):
        sel_ref[w * imgs : (w + 1) * imgs, :] = (lane == row_ref[...] + w * imgs).astype(F32).astype(BF16)


def conv_kernel(begin, end, fresh, *refs):
    if fresh:
        small_hbm, img_hbm, partner_ref, weight_ref = refs[:4]
        mixed_hbm, unit_hbm, inv_hbm, norm_hbm, token_ref, small_ref, mixed_ref, taps, conv_ref, unit_ref, inv_ref, norm_ref, sem, pair_sums, img_ref, mix_ref, row_ref, sel_ref = refs[-18:]
    else:
        small_hbm, mixed_hbm = refs[:2]
        unit_hbm, inv_hbm, norm_hbm, token_ref, small_ref, mixed_ref, taps, conv_ref, unit_ref, inv_ref, norm_ref, sem, pair_sums = refs[-13:]
    side, _, imgs, _ = mixed_ref.shape
    low = max(begin - 3, 0)
    high = side if fresh else min(end + 3, side)
    rows = end - begin
    load = dma(small_hbm, small_ref, sem.at[4, 0])
    load.start()
    token_ref[...] = jnp.zeros(token_ref.shape, F32)

    def enter(h):
        if fresh:
            return dma(img_hbm.at[h], img_ref.at[h], sem.at[3, h])
        return dma(mixed_hbm.at[h], mixed_ref.at[h], sem.at[3, h])

    def store(h):
        return dma(mixed_ref.at[h], mixed_hbm.at[h], sem.at[5, h])

    for h in range(low, high):
        enter(h).start()
    if fresh:
        spread(weight_ref, mix_ref)
        for i in range(imgs):
            row_ref[i : i + 1, :] = jnp.full((1, row_ref.shape[1]), lax.rem(partner_ref[i], imgs), jnp.int32)
        select(row_ref, sel_ref)
    load.wait()
    fill_taps(small_ref, taps, False)
    if fresh:
        mix = mix_ref[...][None]
        rest = 1.0 - mix

        def blend(h, _):
            enter(h).wait()
            x = img_ref[h].reshape(side * imgs, D)
            other = jnp.dot(sel_ref[...], x, preferred_element_type=F32).reshape(side, imgs, D)
            mixed_ref[h] = mix * x.reshape(side, imgs, D).astype(F32) + rest * other
            add_columns(mixed_ref, pair_sums, h)
            store(h).start()
            return 0

        lax.fori_loop(0, side, blend, 0)
    else:
        for h in range(low, min(begin + 3, high)):
            enter(h).wait()
            add_columns(mixed_ref, pair_sums, h)

    def conv(h, kys):
        r = h - begin
        if not fresh:

            @pl.when(h + 3 < high)
            def _():
                enter(h + 3).wait()
                add_columns(mixed_ref, pair_sums, h + 3)

        def tile(k, _):
            at, lanes = tile_of(k, imgs)
            base = jnp.broadcast_to(small_ref[DEPTH_BIAS : DEPTH_BIAS + 1, lanes], (8, 128))
            acc = conv_rows(mixed_ref, pair_sums, taps, h, kys, at, lanes, side, [base] * side)
            for w in range(side):
                conv_ref[r, w, at, lanes] = acc[w]
            return 0

        return tiles(h, imgs, tile, True)

    every_row(begin, end, side, conv)
    gain = small_ref[GAIN_ONE : GAIN_ONE + 1, :][None]
    bias = small_ref[BIAS_ONE : BIAS_ONE + 1, :][None]

    def leave(r):
        return (
            dma(unit_ref.at[r], unit_hbm.at[r + begin], sem.at[0, r]),
            dma(inv_ref.at[r], inv_hbm.at[r + begin], sem.at[1, r]),
            dma(norm_ref.at[r], norm_hbm.at[r + begin], sem.at[2, r]),
        )

    def norm(r):
        unit, inv = norm_of(conv_ref[r])
        unit_ref[r] = unit.astype(BF16)
        inv_ref[r] = inv
        norm_ref[r] = (unit * gain + bias).astype(BF16)
        start(leave(r))

    def two(i, _):
        norm(2 * i)
        norm(2 * i + 1)
        return 0

    lax.fori_loop(0, rows // 2, two, 0)
    if rows % 2:
        norm(rows - 1)
    for r in range(rows):
        wait(leave(r))
    if fresh:
        for h in range(side):
            store(h).wait()


def conv_forward(small, inputs, begin, end, so_far=(), after=()):
    fresh = not so_far
    full = inputs[0].shape
    side = full[0]
    thin = full[:3] + (1,)
    rows = end - begin
    out = [far(full, BF16), far(thin, F32), far(full, BF16), near((8, 128), F32)]
    scratch = [
        pltpu.VMEM(small.shape, F32),
        pltpu.VMEM(full, F32),
        pltpu.VMEM((77, 8, D), F32),
        pltpu.VMEM((rows,) + full[1:], F32),
        pltpu.VMEM((rows,) + full[1:], BF16),
        pltpu.VMEM((rows,) + thin[1:], F32),
        pltpu.VMEM((rows,) + full[1:], BF16),
        pltpu.SemaphoreType.DMA((6, side)),
        pltpu.VMEM((side, side // 2) + full[2:], F32),
    ]
    specs = [HBM] * 2
    if fresh:
        out = [far(full, F32)] + out
        wide = side * full[2]
        scratch += [pltpu.VMEM(full, BF16), pltpu.VMEM((full[2], D), F32), pltpu.VMEM((full[2], wide), jnp.int32), pltpu.VMEM((wide, wide), BF16)]
        specs = [HBM] * 2 + [SMEM] * 2
    return kernel_call(
        functools.partial(conv_kernel, begin, end, fresh),
        out,
        specs + [HBM] * len(so_far),
        scratch,
        (small,) + tuple(inputs) + tuple(so_far),
        after,
        21 * rows / side + 3 * fresh,
        36,
        {2 + k: k for k in range(len(so_far))},
    )


def home(me, order, j, chips):
    if order is None:
        return j % HALF_PIECES if chips else j
    device = me
    for k, bit in enumerate(order):
        device = device ^ (((j >> k) & 1) * bit)
    return device >> 1 if chips else device


def keep_rows(mask_ref, keep_ref):
    for i in range(keep_ref.shape[0]):
        keep_ref[i : i + 1, :] = jnp.full((1, D), mask_ref[i], jnp.int32).astype(F32) / (1.0 - DROP_RATE)


def assembly(me, order, chips, first, src_hbm, whole_ref, sem):
    deep = src_hbm.shape[0] // HALF_PIECES

    def copy(j, _):
        to = pl.ds(pl.multiple_of(home(me, order, first + j, chips) * deep, 16), deep)
        dma(src_hbm.at[pl.ds(pl.multiple_of(j * deep, 16), deep), :], whole_ref.at[to, :], sem).start()
        return 0

    lax.fori_loop(0, HALF_PIECES, copy, 0)
    return dma(src_hbm, whole_ref.at[pl.ds(0, src_hbm.shape[0]), :], sem)


def deal(me, order, chips, first, out_ref, read):
    deep = out_ref.shape[0] // HALF_PIECES

    def move(j, _):
        begin = pl.multiple_of(home(me, order, first + j, chips) * deep, 16)
        to = pl.ds(pl.multiple_of(j * deep, 16), deep)
        for g in range(out_ref.shape[1] // 128):
            out_ref[to, g * 128 : (g + 1) * 128] = read(pl.ds(begin, deep), g).astype(BF16)
        return 0

    lax.fori_loop(0, HALF_PIECES, move, 0)


def even_first(rows, deep):
    blocks = [rows[d * deep // D][:, d * deep % D : d * deep % D + deep] for d in range(FF // deep)]
    return jnp.concatenate(blocks[0::2] + blocks[1::2], axis=1)


def even_last(even, odd, k, deep):
    per = D // deep
    blocks = []
    for d in range(per * k, per * k + per):
        source = odd if d % 2 else even
        blocks.append(source[:, d // 2 * deep : d // 2 * deep + deep])
    return jnp.concatenate(blocks, axis=1)


def block_kernel(block, masks, me_ref, norm_hbm, mixed_hbm, pnear_hbm, pfar_hbm, wnear_hbm, wfar_hbm, dy_hbm, small_hbm, mask_ref, *rest):
    act_hbm, dg_hbm, gnear_ref, gfar_ref, gdb_ref, out_ref, bb_hbm, sums_ref, res_hbm = rest[-32:-23]
    pair_ref, small_ref, keep_ref, norm_ref, mixed_ref, act_ref, dg_ref, branch_ref, unit_ref, inv_ref, out2_ref = rest[-23:-12]
    wd_ref, dy_ref, bb_ref, res_ref, acc, wide, wk, isem, osem, wsem, bsem, rsem = rest[-12:]
    rows = norm_hbm.shape[0]
    steps = rows // block
    imgs = keep_ref.shape[0]
    shape = (block // imgs, imgs, D)
    half = dy_hbm.shape[0]

    def spot(i):
        return pl.ds(pl.multiple_of(i * block, block), block)

    def enter(i):
        s = i % 2
        return (
            dma(norm_hbm.at[spot(i), :], norm_ref.at[s], isem.at[0, s]),
            dma(mixed_hbm.at[spot(i), :], mixed_ref.at[s], isem.at[1, s]),
        )

    def leave(i):
        s = i % 2
        pairs = ((act_ref, act_hbm), (dg_ref, dg_hbm))
        return [dma(a.at[s], b.at[spot(i), :], osem.at[k, s]) for k, (a, b) in enumerate(pairs)]

    me = me_ref[0]
    p_masks, w_masks, d_masks = masks
    load = dma(small_hbm, small_ref, wsem.at[0])
    start(enter(0))
    load.start()
    half_rows = FF // 2
    mine = 0 if p_masks is None else me % 2
    pair_in = []
    for src, first, which in ((pnear_hbm, 0, mine), (pfar_hbm, HALF_PIECES, 1 - mine)):
        to = pair_ref.at[pl.ds(pl.multiple_of(which * half_rows, half_rows), half_rows), :]
        pair_in.append(assembly(me, p_masks, True, first, src, to, wsem.at[1]))
    dy_in = dma(dy_hbm, dy_ref, wsem.at[3])
    wait(pair_in)
    down_in = [
        assembly(me, w_masks, False, first, src, wd_ref, wsem.at[2]) for first, src in ((0, wnear_hbm), (HALF_PIECES, wfar_hbm))
    ]
    dy_in.start()
    load.wait()
    keep_rows(mask_ref, keep_ref)
    keep = keep_ref[...][None]
    scale = keep * small_ref[LAYER_SCALE : LAYER_SCALE + 1, :][None]
    gain = small_ref[GAIN_TWO : GAIN_TWO + 1, :][None]
    bias = small_ref[BIAS_TWO : BIAS_TWO + 1, :][None]
    bias_rows = [small_ref[HIDDEN_BIAS + k : HIDDEN_BIAS + k + 1, :] for k in range(FF // D)]
    hidden_bias = jnp.concatenate(bias_rows, axis=1) if p_masks is None else even_first(bias_rows, FF >> len(p_masks))
    chunk = FF // 2

    def body(i, _):
        s = i % 2

        @pl.when(i + 1 < steps)
        def _():
            start(enter(i + 1))

        @pl.when(i >= 2)
        def _():
            wait(leave(i - 2))

        wait(enter(i))
        x = norm_ref[s]
        branch = jnp.broadcast_to(small_ref[OUT_BIAS : OUT_BIAS + 1, :], (block, D))

        def hidden(j):
            cols = slice(j * chunk, (j + 1) * chunk)
            return lax.dot_general(x, pair_ref[cols, :D], COLS, preferred_element_type=F32) + hidden_bias[:, cols]

        pre = hidden(0)
        for j in range(FF // chunk):
            after = hidden(j + 1) if j + 1 < FF // chunk else None
            cols = slice(j * chunk, (j + 1) * chunk)
            phi = 0.5 + 0.5 * lax.erf(pre * 0.7071067811865476)
            bell = jnp.exp2(pre * pre * -0.7213475204444817) * 0.3989422804014327
            act = (pre * phi).astype(BF16)
            act_ref[s, :, cols] = act
            dg_ref[s, :, cols] = (phi + pre * bell).astype(BF16)
            branch = branch + jnp.dot(act, pair_ref[cols, D:], preferred_element_type=F32)
            pre = after
        start(leave(i))
        split = branch_ref.shape[1:]
        branch_ref[i] = branch.astype(BF16).reshape(split)
        unit, inv = norm_of(mixed_ref[s].reshape(shape) + scale * branch.reshape(shape))
        unit_ref[i] = unit.astype(BF16).reshape(split)
        inv_ref[i] = inv.reshape(split[:-1] + (1,))
        out2_ref[i] = (unit * gain + bias).astype(BF16).reshape(split)
        return 0

    lax.fori_loop(0, steps, body, 0)

    wait(down_in)
    for g in range(6):
        wide[g] = wd_ref[:, pl.ds(g * 128, 128)].astype(F32)
        for k in range(4):
            wk[k // 2, pl.ds(k % 2 * D, D), pl.ds(g * 128, 128)] = wide[g, pl.ds(k, D, stride=4), :].astype(BF16)
    sums_ref[...] = jnp.zeros(sums_ref.shape, F32)
    rows = half * half * imgs
    shape = (half * half, imgs, D)
    for k in range(2):
        acc[:, k * D : (k + 1) * D] = jnp.broadcast_to(small_ref[DOWN_BIAS + k : DOWN_BIAS + k + 1, :], (rows, D))
    dy_in.wait()
    gdb_ref[...] = jnp.sum(dy_ref[...].astype(F32).reshape(half * half, imgs, 2 * D), axis=0)

    def give(k):
        pairs = ((bb_ref, bb_hbm), (res_ref, res_hbm))
        return [dma(a.at[k], b.at[:, k // 2, :, k % 2], rsem.at[j, k]) for j, (a, b) in enumerate(pairs)]

    for a in range(2):
        dy = dy_ref[...].reshape(rows, 2 * D)
        x = jnp.concatenate([out2_ref[:, a, :, b].reshape(rows, D) for b in range(2)], axis=1)
        both = lax.dot_general(dy, wk[a], COLS, preferred_element_type=F32)
        acc[...] += jnp.dot(x, wk[a], preferred_element_type=F32)
        gd = lax.dot_general(x, dy, ROWS, preferred_element_type=F32)
        for b in range(2):
            k = 2 * a + b
            for g in range(6):
                wide[g, pl.ds(k, D, stride=4), :] = gd[b * D : (b + 1) * D, g * 128 : (g + 1) * 128]
            back = both[:, b * D : (b + 1) * D].reshape(shape)
            unit = unit_ref[:, a, :, b].reshape(shape).astype(F32)
            sums_ref[0] += jnp.sum(back * unit, axis=0)
            sums_ref[1] += jnp.sum(back, axis=0)
            res = norm_back(back, unit, inv_ref[:, a, :, b].reshape(half * half, imgs, 1), gain)
            res_ref[k] = res.astype(BF16).reshape(half, half, imgs, D)
            sums_ref[2] += jnp.sum(res * keep * branch_ref[:, a, :, b].reshape(shape).astype(F32), axis=0)
            bb = (res * scale).astype(BF16)
            bb_ref[k] = bb.reshape(half, half, imgs, D)
            start(give(k))
            sums_ref[3] += jnp.sum(bb.astype(F32), axis=0)

    out_ref[...] = acc[...].astype(BF16).reshape(out_ref.shape)
    deal(me, d_masks, False, 0, gnear_ref, lambda at, g: wide[g, at, :])
    deal(me, d_masks, False, HALF_PIECES, gfar_ref, lambda at, g: wide[g, at, :])
    for k in range(4):
        wait(give(k))
    for i in range(max(steps - 2, 0), steps):
        wait(leave(i))


def block_both(masks, me, norm, mixed, pair, down, dy, small, mask, after=(), block=448):
    rows = norm.shape[0]
    half, _, imgs, _ = dy.shape
    area = half * half * imgs
    six = (half, 2, half, 2, imgs)
    two = lambda width, dtype: pltpu.VMEM((2, block, width), dtype)
    whole = lambda width, dtype: pltpu.VMEM(six + (width,), dtype)
    part = pltpu.VMEM((4, half, half, imgs, D), BF16)
    return kernel_call(
        functools.partial(block_kernel, block, masks),
        [far((rows, FF), BF16)] * 2
        + [near((2 * D, 2 * D), BF16)] * 2
        + [near((imgs, 2 * D), F32), near((half, half, imgs, 2 * D), BF16)]
        + [far(six + (D,), BF16), near((4, imgs, D), F32), far(six + (D,), BF16)],
        [SMEM] + [HBM] * 2 + [ANY, HBM] * 2 + [HBM] * 2 + [SMEM],
        [pltpu.VMEM((FF, 2 * D), BF16), pltpu.VMEM(small.shape, F32), pltpu.VMEM((imgs, D), F32)]
        + [two(D, BF16), two(D, F32), two(FF, BF16), two(FF, BF16)]
        + [whole(D, BF16), whole(D, BF16), whole(1, F32), whole(D, BF16)]
        + [pltpu.VMEM((4 * D, 2 * D), BF16), pltpu.VMEM(dy.shape, BF16), part, part]
        + [pltpu.VMEM((area, 2 * D), F32), pltpu.VMEM((6, 4 * D, 128), F32), pltpu.VMEM((2, 2 * D, 2 * D), BF16)]
        + [pltpu.SemaphoreType.DMA((2, 2)), pltpu.SemaphoreType.DMA((2, 2)), pltpu.SemaphoreType.DMA((4,))]
        + [pltpu.SemaphoreType.DMA((1,)), pltpu.SemaphoreType.DMA((2, 4))],
        (me, norm, mixed, *pair, *down, dy, small, mask),
        after,
        34,
        58,
    )


def pair_grad_kernel(block, first, masks, me_ref, bb_hbm, act_hbm, dg_hbm, norm_hbm, pair_hbm, *rest):
    g_ref, hb_ref, p_hbm, pair_ref, acc, turned, bb_ref, act_ref, dg_ref, norm_ref, p_ref, sem, osem, wsem = rest[-14:]
    rows = bb_hbm.shape[0]
    imgs = hb_ref.shape[0]
    steps = rows // block
    wide = FF // 2
    me = me_ref[0]
    which = 0 if masks is None else me % 2
    which = 1 - which if first else which
    lanes = pl.ds(pl.multiple_of(which * wide, wide), wide)

    def spot(i):
        return pl.ds(pl.multiple_of(i * block, block), block)

    def enter(i):
        s = i % 2
        return (
            dma(bb_hbm.at[spot(i), :], bb_ref.at[s], sem.at[0, s]),
            dma(dg_hbm.at[spot(i), lanes], dg_ref.at[s], sem.at[1, s]),
            dma(act_hbm.at[spot(i), lanes], act_ref.at[s], sem.at[2, s]),
            dma(norm_hbm.at[spot(i), :], norm_ref.at[s], sem.at[3, s]),
        )

    def leave(i):
        return dma(p_ref.at[i % 2], p_hbm.at[spot(i), :], osem.at[i % 2])

    pair_in = [assembly(me, masks, True, first, pair_hbm, pair_ref, wsem.at[0])]
    start(enter(0))
    hb_ref[...] = jnp.zeros(hb_ref.shape, F32)
    acc[...] = jnp.zeros(acc.shape, F32)
    wait(pair_in)

    def body(i, _):
        s = i % 2

        @pl.when(i + 1 < steps)
        def _():
            start(enter(i + 1))

        @pl.when(i >= 2)
        def _():
            leave(i - 2).wait()

        wait(enter(i))
        b = bb_ref[s]
        back = lax.dot_general(b, pair_ref[:, D:], COLS, preferred_element_type=F32)
        acc[D:, :] += lax.dot_general(b, act_ref[s], ROWS, preferred_element_type=F32)
        p = (back * dg_ref[s].astype(F32)).astype(BF16)
        p_ref[s] = p
        hb_ref[...] += jnp.sum(p.astype(F32).reshape(block // imgs, imgs, wide), axis=0)
        acc[:D, :] += lax.dot_general(norm_ref[s], p, ROWS, preferred_element_type=F32)
        leave(i).start()
        return 0

    lax.fori_loop(0, steps, body, 0)
    turned[...] = acc[...].T
    deal(me, masks, True, first, g_ref, lambda at, g: turned[at, pl.ds(g * 128, 128)])
    for i in range(max(steps - 2, 0), steps):
        leave(i).wait()


def pair_grad(first, masks, me, bb, act, dg, norm, pair, imgs, after=(), block=784):
    rows = bb.shape[0]
    wide = FF // 2
    two = lambda width: pltpu.VMEM((2, block, width), BF16)
    return kernel_call(
        functools.partial(pair_grad_kernel, block, first, masks),
        [near((wide, 2 * D), BF16), near((imgs, wide), F32), far((rows, wide), BF16)],
        [SMEM] + [HBM] * 5,
        [pltpu.VMEM((wide, 2 * D), BF16), pltpu.VMEM((2 * D, wide), F32), pltpu.VMEM((wide, 2 * D), F32)]
        + [two(D), two(wide), two(wide), two(D), two(wide)]
        + [pltpu.SemaphoreType.DMA((4, 2)), pltpu.SemaphoreType.DMA((2,)), pltpu.SemaphoreType.DMA((1,))],
        (me, bb, act, dg, norm, pair),
        after,
        13,
        44,
    )


def back_one_kernel(block, masks, me_ref, pnear_hbm, pfar_hbm, unit_hbm, inv_hbm, near_hbm, far_hbm, small_hbm, *rest):
    conv_hbm, sums_ref, near_ref, far_ref, small_ref, pnear_ref, pfar_ref, unit_ref, inv_ref, conv_ref, sem, wsem = rest[-12:]
    rows = pnear_hbm.shape[0]
    imgs = sums_ref.shape[1]
    steps = rows // block
    shape = (block // imgs, imgs, D)

    def spot(i):
        return pl.ds(pl.multiple_of(i * block, block), block)

    def enter(i):
        s = i % 2
        pairs = ((pnear_hbm, pnear_ref), (pfar_hbm, pfar_ref), (unit_hbm, unit_ref), (inv_hbm, inv_ref))
        return [dma(a.at[spot(i), :], b.at[s], sem.at[k, s]) for k, (a, b) in enumerate(pairs)]

    def leave(i):
        return dma(conv_ref.at[i % 2], conv_hbm.at[spot(i), :], sem.at[4, i % 2])

    load = dma(small_hbm, small_ref, wsem.at[0])
    left = pl.ds(0, D)
    pair_in = [
        assembly(me_ref[0], masks, True, first, src.at[:, left], dst, wsem.at[1])
        for first, src, dst in ((0, near_hbm, near_ref), (HALF_PIECES, far_hbm, far_ref))
    ]
    start(enter(0))
    load.start()
    sums_ref[...] = jnp.zeros(sums_ref.shape, F32)
    wait(pair_in)
    load.wait()
    gain = small_ref[GAIN_ONE : GAIN_ONE + 1, :][None]

    def body(i, _):
        s = i % 2

        @pl.when(i + 1 < steps)
        def _():
            start(enter(i + 1))

        @pl.when(i >= 2)
        def _():
            leave(i - 2).wait()

        wait(enter(i))
        back = jnp.dot(pnear_ref[s], near_ref[...], preferred_element_type=F32)
        back = (back + jnp.dot(pfar_ref[s], far_ref[...], preferred_element_type=F32)).reshape(shape)
        unit = unit_ref[s].reshape(shape).astype(F32)
        sums_ref[0] += jnp.sum(back * unit, axis=0)
        sums_ref[1] += jnp.sum(back, axis=0)
        out = norm_back(back, unit, inv_ref[s].reshape(shape[:2] + (1,)), gain)
        sums_ref[2] += jnp.sum(out, axis=0)
        conv_ref[s] = out.astype(BF16).reshape(block, D)
        leave(i).start()
        return 0

    lax.fori_loop(0, steps, body, 0)
    for i in range(max(steps - 2, 0), steps):
        leave(i).wait()


def back_one(masks, me, p, unit, inv, pair, small, imgs, after=(), block=784):
    rows = unit.shape[0]
    wide = FF // 2
    two = lambda width, dtype: pltpu.VMEM((2, block, width), dtype)
    return kernel_call(
        functools.partial(back_one_kernel, block, masks),
        [far((rows, D), BF16), near((3, imgs, D), F32)],
        [SMEM] + [HBM] * 7,
        [pltpu.VMEM((wide, D), BF16)] * 2
        + [pltpu.VMEM(small.shape, F32)]
        + [two(wide, BF16), two(wide, BF16), two(D, BF16), two(1, F32), two(D, BF16)]
        + [pltpu.SemaphoreType.DMA((5, 2)), pltpu.SemaphoreType.DMA((2,))],
        (me, *p, unit, inv, *pair, small),
        after,
        11,
        32,
    )


def taps_kernel(groups, conv_hbm, mixed_hbm, *rest):
    g_ref, conv_ref, mixed_ref, sums, even, odd, last, sem = rest[-8:]
    side, _, imgs, _ = conv_hbm.shape
    pairs = side // 2

    def enter(k):
        lanes = pl.ds(pl.multiple_of((k + groups[0]) * 128, 128), 128)
        return (
            dma(mixed_hbm.at[:, :, :, lanes], mixed_ref.at[k], sem.at[0, k]),
            dma(conv_hbm.at[:, :, :, lanes], conv_ref.at[k], sem.at[1, k]),
        )

    for k in range(len(groups)):
        start(enter(k))
    def group(k, _):
        wait(enter(k))

        def prepare(h, _):
            x = [mixed_ref[k, h, w] for w in range(side)]
            d = [conv_ref[k, h, w].astype(F32) for w in range(side)]
            for i in range(pairs):
                sums[h, i] = x[2 * i] + x[2 * i + 1]
                last[h, i] = d[2 * i + 1]
                even[h, i] = d[2 * i] - d[2 * i + 1]
                odd[h, i + 1] = (d[2 * i + 2] if i + 1 < pairs else jnp.zeros_like(d[0])) - d[2 * i + 1]
            odd[h, 0] = d[0]
            return 0

        lax.fori_loop(0, side, prepare, 0)
        for ky in range(7):
            first = max(3 - ky, 0)
            count = min(side, side + 3 - ky) - first

            def row(h, acc):
                acc = list(acc)
                for t in range(imgs // 8):
                    at = pl.ds(t * 8, 8)
                    for begin, shift, taps, length, read_x, read_d in (
                        (4, 0, 3, pairs, lambda i: mixed_ref[k, h + ky - 3, 2 * i, at], lambda i: even[h, i, at]),
                        (0, -1, 4, pairs + 1, lambda i: mixed_ref[k, h + ky - 3, 2 * i + 1, at], lambda i: odd[h, i, at]),
                        (7, 0, 4, pairs, lambda i: sums[h + ky - 3, i, at], lambda i: last[h, i, at]),
                    ):
                        x = [read_x(i) for i in range(pairs)]
                        for a in range(length):
                            d = read_d(a)
                            for j in range(taps):
                                i = a + shift - 1 + j
                                if 0 <= i < pairs:
                                    acc[begin + j] = acc[begin + j] + x[i] * d
                return tuple(acc)

            acc = lax.fori_loop(
                0, count // 2, lambda r, acc: row(first + 2 * r + 1, row(first + 2 * r, acc)), (jnp.zeros((8, 128), F32),) * 11
            )
            if count % 2:
                acc = row(first + count - 1, acc)
            even_taps = [acc[j] + acc[7 + j] for j in range(4)]
            odd_taps = [acc[4 + j] + acc[7 + j] for j in range(3)]
            for kx in range(7):
                value = odd_taps[kx // 2] if kx % 2 else even_taps[kx // 2]
                g_ref[ky * 7 + kx, :, pl.ds(pl.multiple_of(k * 128, 128), 128)] = value
        return 0

    lax.fori_loop(0, len(groups), group, 0)


def taps_grad(conv, mixed, groups, after=()):
    side, _, imgs, _ = conv.shape
    lanes = lambda dtype: pltpu.VMEM((len(groups),) + conv.shape[:3] + (128,), dtype)
    part = lambda columns: pltpu.VMEM((side, columns, imgs, 128), F32)
    return kernel_call(
        functools.partial(taps_kernel, groups),
        [near((49, 8, 128 * len(groups)), F32)],
        [HBM] * 2,
        [lanes(BF16), lanes(F32), part(side // 2), part(side // 2), part(side // 2 + 1), part(side // 2), pltpu.SemaphoreType.DMA((2, len(groups)))],
        (conv, mixed),
        after,
        4.7 * len(groups),
        28,
    )[0]


def images_kernel(begin, end, conv_hbm, small_hbm, partner_ref, weight_ref, res_hbm, *rest):
    g_hbm, token_ref, small_ref, raw_ref, conv_ref, taps, res_ref, out_ref, mix_ref, row_ref, sel_ref, rest_ref, sem, csem, pair_sums, rsem = rest[-16:]
    side, _, imgs, _ = conv_hbm.shape
    low = max(begin - 3, 0)
    high = min(end + 3, side)
    load = dma(small_hbm, small_ref, csem.at[side])
    load.start()
    token_ref[...] = jnp.zeros(token_ref.shape, F32)

    def bring(h):
        return dma(conv_hbm.at[h], raw_ref.at[h], csem.at[h])

    def widen(h):
        bring(h).wait()
        conv_ref[h] = raw_ref[h].astype(F32)
        add_columns(conv_ref, pair_sums, h)

    def enter(h):
        return dma(res_hbm.at[h], res_ref.at[h - begin], rsem.at[h - begin])

    def leave(h):
        return dma(out_ref.at[h - begin], g_hbm.at[h], sem.at[1, 0])

    for h in range(low, high):
        bring(h).start()
        if h == min(begin + 3, high - 1):
            for r in range(begin, end):
                enter(r).start()
    spread(weight_ref, mix_ref)
    for i in range(imgs):
        row_ref[pl.ds(lax.rem(partner_ref[i], imgs), 1), :] = jnp.full((1, row_ref.shape[1]), i, jnp.int32)
    select(row_ref, sel_ref)
    load.wait()
    fill_taps(small_ref, taps, True)
    mix = mix_ref[...][None]
    others = 1.0 - mix
    for h in range(low, min(begin + 3, high)):
        widen(h)

    def row(h, kys):
        @pl.when(h + 3 < high)
        def _():
            widen(h + 3)

        enter(h).wait()
        rest_ref[...] = res_ref[h - begin].astype(F32)

        def tile(k, _):
            at, lanes = tile_of(k, imgs)
            base = [rest_ref[w, at, lanes] for w in range(side)]
            acc = conv_rows(conv_ref, pair_sums, taps, h, kys, at, lanes, side, base)
            for w in range(side):
                out_ref[h - begin, w, at, lanes] = acc[w]
            return 0

        return tiles(h, imgs, tile, False)

    every_row(begin, end, side, row)

    def unmix(r):
        v = out_ref[r]
        part = (others * v).reshape(side * imgs, D)
        upper = part.astype(BF16)
        lower = (part - upper.astype(F32)).astype(BF16)
        back = jnp.dot(sel_ref[...], upper, preferred_element_type=F32)
        back = back + jnp.dot(sel_ref[...], lower, preferred_element_type=F32)
        out_ref[r] = mix * v + back.reshape(side, imgs, D)
        leave(begin + r).start()

    def two(i, _):
        unmix(2 * i)
        unmix(2 * i + 1)
        return 0

    lax.fori_loop(0, (end - begin) // 2, two, 0)
    for h in range(begin, end):
        leave(h).wait()


def images_back(conv, small, partner, weight, res, begin, end, so_far=(), after=()):
    side, _, imgs, _ = conv.shape
    return kernel_call(
        functools.partial(images_kernel, begin, end),
        [far(conv.shape, F32), near((8, 128), F32)],
        [HBM, HBM, SMEM, SMEM, HBM] + [HBM] * len(so_far),
        [
            pltpu.VMEM(small.shape, F32),
            pltpu.VMEM(conv.shape, BF16),
            pltpu.VMEM(conv.shape, F32),
            pltpu.VMEM((77, 8, D), F32),
            pltpu.VMEM((end - begin, side, imgs, D), BF16),
            pltpu.VMEM((end - begin, side, imgs, D), F32),
            pltpu.VMEM((imgs, D), F32),
            pltpu.VMEM((imgs, side * imgs), jnp.int32),
            pltpu.VMEM((side * imgs, side * imgs), BF16),
            pltpu.VMEM((side, imgs, D), F32),
            pltpu.SemaphoreType.DMA((2, 2)),
            pltpu.SemaphoreType.DMA((side + 1,)),
            pltpu.VMEM((side, side // 2, imgs, D), F32),
            pltpu.SemaphoreType.DMA((end - begin,)),
        ],
        (conv, small, partner, weight, res) + tuple(so_far),
        after,
        22 * (end - begin) / side,
        28,
        {5: 0} if so_far else {},
    )


def ready_kernel(in_hbm, out_hbm, down_hbm, *rest):
    pair_ref, low_ref, in_ref, out_ref, down_ref, sem = rest[-6:]
    pairs = ((in_hbm, in_ref), (out_hbm, out_ref), (down_hbm, down_ref))
    copies = [dma(a, b, sem.at[k]) for k, (a, b) in enumerate(pairs)]
    start(copies)
    wait(copies)
    pair_ref[0, :, :D] = in_ref[...].astype(BF16)
    pair_ref[0, :, D:] = out_ref[...].astype(BF16)
    low_ref[0] = down_ref[...].astype(BF16)


def ready(weight_in, weight_out, weight_down, after=()):
    deep = weight_in.shape[0]
    return kernel_call(
        ready_kernel,
        [near((1, deep, 2 * D), BF16)] * 2,
        [HBM] * 3,
        [pltpu.VMEM(x.shape, F32) for x in (weight_in, weight_out, weight_down)] + [pltpu.SemaphoreType.DMA((3,))],
        (weight_in, weight_out, weight_down),
        after,
        0.5,
        8,
    )


def join_kernel(first_ref, second_ref, *rest):
    out_ref = rest[-1]
    k = first_ref.shape[0]
    out_ref[:k] = first_ref[...]
    out_ref[k:] = second_ref[...]


def join(first, second, after=()):
    return kernel_call(
        join_kernel,
        [near((2 * first.shape[0],) + first.shape[1:], first.dtype)],
        [VMEM] * 2,
        [],
        (first, second),
        after,
        0.5,
        8,
    )[0]


def fold_kernel(count, *refs):
    ins, (stay_ref, leave_ref) = refs[: 2 * count], refs[-2:]
    k = stay_ref.shape[0] // count
    for i in range(count):
        keep_ref, come_ref = ins[2 * i], ins[2 * i + 1]
        stay_ref[i * k : (i + 1) * k] = keep_ref[:k].astype(F32) + come_ref[:k].astype(F32)
        leave_ref[i * k : (i + 1) * k] = (keep_ref[k:].astype(F32) + come_ref[k:].astype(F32)).astype(BF16)


def fold(*arrays, after=()):
    slots, deep, wide = arrays[0].shape
    count = len(arrays) // 2
    return kernel_call(
        functools.partial(fold_kernel, count),
        [near((count * slots // 2, deep, wide), F32), near((count * slots // 2, deep, wide), BF16)],
        [VMEM] * len(arrays),
        [],
        arrays,
        after,
        0.5,
        12,
    )


def part_kernel(*refs):
    ins, outs = refs[:4], refs[-4:]
    for i in range(2):
        keep_ref, come_ref = ins[2 * i], ins[2 * i + 1]
        for slot, out_ref in enumerate(outs):
            out_ref[i] = (keep_ref[slot].astype(F32) + come_ref[slot].astype(F32)).astype(out_ref.dtype)


def part(p_keep, p_come, d_keep, d_come, after=()):
    shape = (2,) + p_keep.shape[1:]
    return kernel_call(
        part_kernel,
        [near(shape, F32)] + [near(shape, BF16)] * 3,
        [VMEM] * 4,
        [],
        (p_keep, p_come, d_keep, d_come),
        after,
        0.5,
        12,
    )


def small_kernel(hops, me_ref, gk_ref, sums1_ref, sums2_ref, near_ref, far_ref, db_ref, keep_ref, *rest):
    sum_ref, send_ref, total = rest[-3:]
    grads = keep_ref[...]
    for come_ref in rest[:-3]:
        grads = grads + come_ref[...].astype(F32)
    sum_ref[...] = grads
    rows = lambda x: jnp.sum(x, axis=0, keepdims=True)
    for t in range(49):
        total[t : t + 1, :] = rows(gk_ref[t])
    for row, value in (
        (DEPTH_BIAS, sums1_ref[2]),
        (GAIN_ONE, sums1_ref[0]),
        (BIAS_ONE, sums1_ref[1]),
        (OUT_BIAS, sums2_ref[3]),
        (LAYER_SCALE, sums2_ref[2]),
        (GAIN_TWO, sums2_ref[0]),
        (BIAS_TWO, sums2_ref[1]),
    ):
        total[row : row + 1, :] = rows(value)
    mine, other = rows(near_ref[...]), rows(far_ref[...])
    if hops:
        odd_device = (me_ref[0] % 2).astype(F32)
        even = mine * (1.0 - odd_device) + other * odd_device
        odd = other * (1.0 - odd_device) + mine * odd_device
    for k in range(4):
        if hops:
            value = even_last(even, odd, k, FF // hops)
        else:
            value = (mine, other)[k // 2][:, k % 2 * D : k % 2 * D + D]
        total[HIDDEN_BIAS + k : HIDDEN_BIAS + k + 1, :] = value
    for k in range(2):
        total[DOWN_BIAS + k : DOWN_BIAS + k + 1, :] = rows(db_ref[:, k * D : (k + 1) * D])
    square = jnp.full((1, D), jnp.sum(grads * grads), F32)
    upper = square.astype(BF16).astype(F32)
    total[SQUARES : SQUARES + 1, :] = upper
    total[SQUARES + 1 : SQUARES + 2, :] = square - upper
    send_ref[...] = total[...].astype(BF16)


def small_total(hops, me, gk, sums1, sums2, near_hb, far_hb, db, keep, *come):
    return kernel_call(
        functools.partial(small_kernel, hops),
        [near(keep.shape, F32), near((SQUARES + 2, D), BF16)],
        [SMEM] + [VMEM] * (7 + len(come)),
        [pltpu.VMEM((SQUARES + 2, D), F32)],
        (me, gk, sums1, sums2, near_hb, far_hb, db, keep, *come),
        (),
        1,
        8,
    )


def meet_kernel(*refs):
    arrays, out_ref = refs[:-1], refs[-1]
    sums = [x[...].astype(F32) for x in arrays]
    while len(sums) > 1:
        sums = [a + b for a, b in zip(sums[::2], sums[1::2])]
    total = sums[0]
    square = total[SQUARES : SQUARES + 1] + total[SQUARES + 1 : SQUARES + 2]
    upper = square.astype(BF16).astype(F32)
    out_ref[...] = total.astype(out_ref.dtype)
    out_ref[SQUARES : SQUARES + 2, :] = jnp.concatenate([upper, square - upper], axis=0).astype(out_ref.dtype)


def meet(arrays, dtype):
    return kernel_call(meet_kernel, [near(arrays[0].shape, dtype)], [VMEM] * len(arrays), [], arrays, (), 0.3, 8)[0]


def adam(weight, first, second, grad, rate, decay):
    first = BETA_ONE * first + (1.0 - BETA_ONE) * grad
    second = BETA_TWO * second + (1.0 - BETA_TWO) * grad * grad
    first_hat = first / (1.0 - BETA_ONE**STEP)
    second_hat = second / (1.0 - BETA_TWO**STEP)
    weight = weight - rate * (first_hat / (jnp.sqrt(second_hat) + ADAM_EPS) + decay * weight)
    return first, second, weight


def adam_kernel(total_ref, grads_ref, *refs):
    ins, outs = refs[:9], refs[9:18]
    norm_ref = refs[18]
    gs = total_ref[:SQUARES]
    norm = jnp.sqrt(jnp.sum(gs * gs) + jnp.sum(total_ref[SQUARES : SQUARES + 2, 0:1]))
    norm_ref[0, 0] = norm
    factor = CLIP_NORM / jnp.maximum(norm, CLIP_NORM)
    grads = (grads_ref[0, :, :D], grads_ref[0, :, D:], grads_ref[1])
    rates = (LAYER_DECAY * RATE_MATRIX, LAYER_DECAY * RATE_MATRIX, RATE_MATRIX)
    for k in range(3):
        new = adam(ins[3 * k][...], ins[3 * k + 1][...], ins[3 * k + 2][...], grads[k] * factor, rates[k], WEIGHT_DECAY)
        for out_ref, value in zip(outs[3 * k : 3 * k + 3], new):
            out_ref[...] = value


def adam_all(total, grads, states):
    return pl.pallas_call(
        adam_kernel,
        out_shape=tuple(near(x.shape, F32) for x in states) + (near((1, 1), F32),),
        in_specs=[VMEM] * 11,
        out_specs=(VMEM,) * 9 + (SMEM,),
        cost_estimate=pl.CostEstimate(flops=int(2e9), bytes_accessed=0, transcendentals=0),
        compiler_params=pltpu.CompilerParams(vmem_limit_bytes=12 << 20),
    )(total, grads, *states)


def swap(x, bit, n):
    return lax.ppermute(x, "dp", [(i, i ^ bit) for i in range(n)])


def is_set(bit):
    return (lax.axis_index("dp") & bit) != 0


def gather_natural(shard, n, order, gates=None):
    have = shard
    met = []
    for hop, bit in enumerate(order):
        if gates and hop in gates:
            have, _ = lax.optimization_barrier((have, gates[hop]))
        other = swap(have, bit, n)
        axis = sum(1 for b in met if b > bit)
        mine = is_set(bit)
        have = jnp.stack([jnp.where(mine, other, have), jnp.where(mine, have, other)], axis=axis)
        met.append(bit)
    return have.reshape((n,) + shard.shape)


def local(n, images, mix_weight, partner, keep_mask, cotangent, weight_in, weight_out, weight_down, small_params,
          first_in, second_in, first_out, second_out, first_down, second_down, first_small, second_small):
    imgs, side = images.shape[:2]
    half = side // 2
    pixels = side * side * imgs
    me = lax.axis_index("dp")
    bits = [1 << k for k in range(n.bit_length() - 1)]
    deep = FF // n
    by_hops = n == 32

    pair, down = ready(weight_in, weight_out, weight_down)
    mine = me[None].astype(jnp.int32)
    p_masks = w_masks = d_masks = None
    if by_hops:
        p_order = [16, 8, 4, 2, 1]
        w_order = [16, 8, 2, 4, 1]
        d_order = p_order
        p_masks, w_masks, d_masks = p_order, w_order, d_order

    img = images.transpose(1, 2, 0, 3)
    dy = cotangent.transpose(1, 2, 0, 3)
    flat = lambda a: a.reshape(pixels, a.shape[-1])
    square = lambda a: a.reshape(side, side, imgs, a.shape[-1])

    cut = [0, 3, 10, side]
    gates = None
    if by_hops:
        gates = {1: pair}
        pair = join(pair, swap(pair, p_order[0], n))
        gates[3] = pair
        down = join(down, swap(down, w_order[0], n))
        pair = join(pair, swap(pair, p_order[1], n))
        gates[4] = pair
    small = gather_natural(small_params.astype(BF16), n, bits[1:] + bits[:1], gates).reshape(-1, D).astype(F32)
    if by_hops:
        down = join(down, swap(down, w_order[1], n))
    mixed, *made, token = conv_forward(small, (img, partner, mix_weight), cut[0], cut[1])
    for piece in (1, 2):
        if by_hops:
            pair = join(pair, swap(pair, p_order[piece + 1], n), (token,))
            down = join(down, swap(down, w_order[piece + 1], n), (token,))
        *made, token = conv_forward(small, (mixed,), cut[piece], cut[piece + 1], tuple(made), (pair, down))
    unit1, inv1, norm1 = made
    if by_hops:
        pair = (pair, swap(pair, p_order[4], n))
        down = (down, swap(down, w_order[4], n))
    else:
        pair, down = (lax.all_gather(x[0], "dp", axis=0, tiled=True).reshape(2, FF // 2, 2 * D) for x in (pair, down))
    pair = tuple(x.reshape(FF // 2, 2 * D) for x in pair)
    down = tuple(x.reshape(FF // 2, 2 * D) for x in down)
    act, dg, d_near, d_far, gdb, out, bb, sums2, res = block_both(
        (p_masks, w_masks, d_masks), mine, flat(norm1), flat(mixed), pair, down, dy, small, keep_mask
    )
    shards = (n // 2, deep, 2 * D)
    if by_hops:
        d_keep = d_near.reshape(shards)
        d_come = swap(d_far.reshape(shards), d_order[4], n)
    grads_of = lambda which, after: pair_grad(
        16 * which, p_masks, mine, flat(bb), act, dg, flat(norm1), pair[which], imgs, after
    )
    p_far, far_hb, far_p = grads_of(1, ())
    if by_hops:
        d_keep, d_send = fold(d_keep, d_come, after=(far_hb,))
        d_come = swap(d_send, d_order[3], n)
        p_come = swap(p_far.reshape(shards), p_order[4], n)
    p_near, near_hb, near_p = grads_of(0, (d_send,) if by_hops else (far_hb,))
    p_gate = ()
    if by_hops:
        p_keep, p_send = fold(p_near.reshape(shards), p_come, after=(near_hb,))
        p_come = swap(p_send, p_order[3], n)
        d_keep, d_send = fold(d_keep, d_come, after=(near_hb,))
        d_come = swap(d_send, d_order[2], n)
        p_gate = (p_send, d_send)
    back_conv, sums1 = back_one(p_masks, mine, (near_p, far_p), flat(unit1), flat(inv1), pair, small, imgs, p_gate)
    back_conv = square(back_conv)
    res = square(res)
    back = functools.partial(images_back, back_conv, small, partner, mix_weight, res)
    if by_hops:
        p_keep, p_send = fold(p_keep, p_come, after=(sums1,))
        p_come = swap(p_send, p_order[2], n)
        grad, token = back(0, side, (), (p_send,))
        keep, *send = part(p_keep, p_come, d_keep, d_come, after=(token,))
        come = [swap(x, bits, n) for x, bits in zip(send, (16, 8, 24))]
        gk = taps_grad(back_conv, mixed, (0, 1, 2), tuple(send))
    else:
        grad, _ = back(0, side)
        gk = taps_grad(back_conv, mixed, (0, 1, 2))
        keep = jnp.stack(
            [
                lax.psum_scatter(jnp.concatenate(x).astype(F32), "dp", scatter_dimension=0, tiled=True)
                for x in ((p_near, p_far), (d_near, d_far))
            ]
        )
        come = ()

    grads, total = small_total(n if by_hops else 0, mine, gk, sums1, sums2, near_hb, far_hb, gdb, keep, *come)
    rounds = [bits[k : k + 2] for k in range(1, len(bits), 2)] + [bits[:1]]
    for step, pair_bits in enumerate(rounds):
        others = [pair_bits[0], pair_bits[-1], sum(pair_bits)] if len(pair_bits) == 2 else pair_bits
        arrays = (total,) + tuple(swap(total, other, n) for other in others)
        total = meet(arrays, F32 if step == len(rounds) - 1 else BF16)
    states = (weight_in, first_in, second_in, weight_out, first_out, second_out, weight_down, first_down, second_down)
    *news, norm = adam_all(total, grads, states)
    grad_norm = norm[0, 0]
    factor = CLIP_NORM / jnp.maximum(grad_norm, CLIP_NORM)
    shard_len = small_params.shape[0]
    gs = lax.dynamic_slice_in_dim(total[:SQUARES].reshape(-1), me * shard_len, shard_len)
    position = me * shard_len + jnp.arange(shard_len, dtype=jnp.int32)
    small_rate = jnp.where(position < 54 * D + FF, LAYER_DECAY * RATE_VECTOR, RATE_VECTOR)
    small_decay = jnp.where(position < 49 * D, WEIGHT_DECAY, 0.0)
    new_small = adam(small_params, first_small, second_small, gs * factor, small_rate, small_decay)
    return (
        out.transpose(2, 0, 1, 3),
        grad.transpose(2, 0, 1, 3),
        grad_norm,
        *news,
        *new_small,
    )


def solution(mesh):
    four = P("dp", None, None, None)
    two = P("dp", None)
    one = P("dp")
    return jax.shard_map(
        functools.partial(local, mesh.shape["dp"]),
        mesh=mesh,
        in_specs=(four, one, one, one, four, two, two, two, one) + (two,) * 6 + (one,) * 2,
        out_specs=(four, four, P()) + (two,) * 9 + (one,) * 3,
        check_vma=False,
    )
```

```python
import functools
import jax
import jax.numpy as jnp
import numpy as np
from jax import lax
from jax.experimental import pallas as pl
from jax.experimental.pallas import tpu as pltpu
from jax.sharding import PartitionSpec as P

STEP = 10
DROP_RATE = 0.2
RATE_MATRIX = 0.05
RATE_VECTOR = 0.3
LAYER_DECAY = 0.8
BETA_ONE = 0.9
BETA_TWO = 0.999
ADAM_EPS = 1e-08
WEIGHT_DECAY = 0.05
CLIP_NORM = 1.0
D = 384
FF = 1536
LN_EPS = 1e-06
F32 = jnp.float32
BF16 = jnp.bfloat16
VMEM = pl.BlockSpec(memory_space=pltpu.VMEM)
SMEM = pl.BlockSpec(memory_space=pltpu.SMEM)
HBM = pl.BlockSpec(memory_space=pltpu.HBM)
ANY = pl.BlockSpec(memory_space=pl.ANY)
ROWS = (((0,), (0,)), ((), ()))
COLS = (((1,), (1,)), ((), ()))
DEPTH_BIAS, GAIN_ONE, BIAS_ONE, HIDDEN_BIAS, OUT_BIAS, LAYER_SCALE, GAIN_TWO, BIAS_TWO, DOWN_BIAS = 49, 50, 51, 52, 56, 57, 58, 59, 60
SQUARES = 62
HALF_PIECES = 16


def near(shape, dtype):
    return jax.ShapeDtypeStruct(shape, dtype)


def far(shape, dtype):
    return pltpu.HBM(shape, dtype)


def held(x):
    return pltpu.with_memory_space_constraint(x, pltpu.HBM)


def dma(src, dst, sem):
    return pltpu.make_async_copy(src, dst, sem)


def start(copies):
    for copy in copies:
        copy.start()


def wait(copies):
    for copy in copies:
        copy.wait()


class Far:
    def __init__(self, array):
        self.array = array


def kernel_call(body, out, specs, scratch, args, after, us, mib, aliases=None):
    specs = specs + [HBM if isinstance(x, Far) else ANY for x in after]
    args = tuple(args) + tuple(x.array if isinstance(x, Far) else x for x in after)
    args = [held(x) if spec is HBM else x for spec, x in zip(specs, args)]
    return pl.pallas_call(
        body,
        out_shape=tuple(out),
        in_specs=specs,
        out_specs=tuple(HBM if isinstance(x, type(far((8, 128), F32))) else VMEM for x in out),
        scratch_shapes=scratch,
        input_output_aliases=aliases or {},
        cost_estimate=pl.CostEstimate(flops=int(us * 1e9), bytes_accessed=0, transcendentals=0),
        compiler_params=pltpu.CompilerParams(vmem_limit_bytes=mib << 20),
    )(*args)


def norm_of(v):
    c = v - jnp.mean(v, axis=-1, keepdims=True)
    inv = lax.rsqrt(jnp.mean(c * c, axis=-1, keepdims=True) + LN_EPS)
    return c * inv, inv


def norm_back(back, unit, inv, gain):
    scaled = back * gain
    m1 = jnp.mean(scaled, axis=-1, keepdims=True)
    m2 = jnp.mean(scaled * unit, axis=-1, keepdims=True)
    return inv * (scaled - m1 - unit * m2)


def tile_of(k, imgs):
    groups = imgs // 8
    return pl.ds(pl.multiple_of(k % groups * 8, 8), 8), pl.ds(pl.multiple_of(k // groups * 128, 128), 128)


def tiles(h, imgs, tile, loop):
    count = imgs // 8 * (D // 128)
    if loop and isinstance(h, int):
        return lax.fori_loop(0, count, tile, 0)
    for k in range(count):
        tile(k, 0)
    return 0


def every_row(begin, end, side, do):
    for h in range(begin, min(end, 3)):
        do(h, range(3 - h, 7))
    low, high = max(begin, 3), min(end, side - 3)
    if low < high:
        lax.fori_loop(low, high, lambda h, _: do(h, range(7)), 0)
    for h in range(max(begin, side - 3), end):
        do(h, range(side + 3 - h))


def conv_rows(src, sums, taps, h, kys, t, lanes, side, base):
    pairs = side // 2

    def one(ky, acc):
        u, v, w = list(acc[:pairs]), list(acc[pairs : 2 * pairs + 1]), list(acc[2 * pairs + 1 :])
        row = h + ky - 3
        for out, shift, first, count, read in (
            (u, 0, 4, 3, lambda i: src[row, 2 * i, t, lanes]),
            (v, -1, 0, 4, lambda i: src[row, 2 * i + 1, t, lanes]),
            (w, 0, 7, 4, lambda i: sums[row, i, t, lanes]),
        ):
            x = [read(i) for i in range(pairs)]
            for j in range(count):
                tap = taps[ky * 11 + first + j, :, lanes]
                for k in range(len(out)):
                    i = k + shift - 1 + j
                    if 0 <= i < pairs:
                        out[k] = out[k] + x[i] * tap
        return tuple(u + v + w)

    acc = (jnp.zeros((8, 128), F32),) * (3 * pairs + 1)
    for ky in kys:
        acc = one(ky, acc)
    u, v, w = acc[:pairs], acc[pairs : 2 * pairs + 1], acc[2 * pairs + 1 :]
    out = []
    for k in range(pairs):
        out.append(base[2 * k] + (u[k] + v[k]))
        out.append(base[2 * k + 1] + (w[k] - (u[k] + v[k + 1])))
    return out


def fill_taps(small_ref, taps, flip):
    for ky in range(7):
        rows = []
        for kx in range(7):
            k = 48 - (ky * 7 + kx) if flip else ky * 7 + kx
            rows.append(small_ref[k : k + 1, :])
        rows = rows[0::2] + rows[1::2] + [rows[2 * j] + rows[2 * j + 1] for j in range(3)] + [rows[6]]
        for k, value in enumerate(rows):
            taps[ky * 11 + k] = jnp.broadcast_to(value, (8, D))


def add_columns(src, sums, row):
    pairs = sums.shape[1]
    sums[row] = jnp.stack([src[row, 2 * i] + src[row, 2 * i + 1] for i in range(pairs)])


def spread(scalars_ref, rows_ref):
    for i in range(rows_ref.shape[0]):
        rows_ref[i : i + 1, :] = jnp.full((1, rows_ref.shape[1]), scalars_ref[i], F32)


def select(row_ref, sel_ref):
    imgs, wide = row_ref.shape
    lane = lax.broadcasted_iota(jnp.int32, (imgs, wide), 1)
    for w in range(wide // imgs):
        sel_ref[w * imgs : (w + 1) * imgs, :] = (lane == row_ref[...] + w * imgs).astype(F32).astype(BF16)


def conv_kernel(begin, end, fresh, *refs):
    if fresh:
        small_hbm, img_hbm, partner_ref, weight_ref = refs[:4]
        mixed_hbm, unit_hbm, inv_hbm, norm_hbm, token_ref, small_ref, mixed_ref, taps, conv_ref, unit_ref, inv_ref, norm_ref, sem, pair_sums, img_ref, mix_ref, row_ref, sel_ref = refs[-18:]
    else:
        small_hbm, mixed_hbm = refs[:2]
        unit_hbm, inv_hbm, norm_hbm, token_ref, small_ref, mixed_ref, taps, conv_ref, unit_ref, inv_ref, norm_ref, sem, pair_sums = refs[-13:]
    side, _, imgs, _ = mixed_ref.shape
    low = max(begin - 3, 0)
    high = side if fresh else min(end + 3, side)
    rows = end - begin
    load = dma(small_hbm, small_ref, sem.at[4, 0])
    load.start()
    token_ref[...] = jnp.zeros(token_ref.shape, F32)

    def enter(h):
        if fresh:
            return dma(img_hbm.at[h], img_ref.at[h], sem.at[3, h])
        return dma(mixed_hbm.at[h], mixed_ref.at[h], sem.at[3, h])

    def store(h):
        return dma(mixed_ref.at[h], mixed_hbm.at[h], sem.at[5, h])

    for h in range(low, high):
        enter(h).start()
    if fresh:
        spread(weight_ref, mix_ref)
        for i in range(imgs):
            row_ref[i : i + 1, :] = jnp.full((1, row_ref.shape[1]), lax.rem(partner_ref[i], imgs), jnp.int32)
        select(row_ref, sel_ref)
    load.wait()
    fill_taps(small_ref, taps, False)
    if fresh:
        mix = mix_ref[...][None]
        rest = 1.0 - mix

        def blend(h, _):
            enter(h).wait()
            x = img_ref[h].reshape(side * imgs, D)
            other = jnp.dot(sel_ref[...], x, preferred_element_type=F32).reshape(side, imgs, D)
            mixed_ref[h] = mix * x.reshape(side, imgs, D).astype(F32) + rest * other
            add_columns(mixed_ref, pair_sums, h)
            store(h).start()
            return 0

        lax.fori_loop(0, side, blend, 0)
    else:
        for h in range(low, min(begin + 3, high)):
            enter(h).wait()
            add_columns(mixed_ref, pair_sums, h)

    def conv(h, kys):
        r = h - begin
        if not fresh:

            @pl.when(h + 3 < high)
            def _():
                enter(h + 3).wait()
                add_columns(mixed_ref, pair_sums, h + 3)

        def tile(k, _):
            at, lanes = tile_of(k, imgs)
            base = jnp.broadcast_to(small_ref[DEPTH_BIAS : DEPTH_BIAS + 1, lanes], (8, 128))
            acc = conv_rows(mixed_ref, pair_sums, taps, h, kys, at, lanes, side, [base] * side)
            for w in range(side):
                conv_ref[r, w, at, lanes] = acc[w]
            return 0

        return tiles(h, imgs, tile, True)

    every_row(begin, end, side, conv)
    gain = small_ref[GAIN_ONE : GAIN_ONE + 1, :][None]
    bias = small_ref[BIAS_ONE : BIAS_ONE + 1, :][None]

    def leave(r):
        return (
            dma(unit_ref.at[r], unit_hbm.at[r + begin], sem.at[0, r]),
            dma(inv_ref.at[r], inv_hbm.at[r + begin], sem.at[1, r]),
            dma(norm_ref.at[r], norm_hbm.at[r + begin], sem.at[2, r]),
        )

    def norm(r):
        unit, inv = norm_of(conv_ref[r])
        unit_ref[r] = unit.astype(BF16)
        inv_ref[r] = inv
        norm_ref[r] = (unit * gain + bias).astype(BF16)
        start(leave(r))

    def two(i, _):
        norm(2 * i)
        norm(2 * i + 1)
        return 0

    lax.fori_loop(0, rows // 2, two, 0)
    if rows % 2:
        norm(rows - 1)
    for r in range(rows):
        wait(leave(r))
    if fresh:
        for h in range(side):
            store(h).wait()


def conv_forward(small, inputs, begin, end, so_far=(), after=()):
    fresh = not so_far
    full = inputs[0].shape
    side = full[0]
    thin = full[:3] + (1,)
    rows = end - begin
    out = [far(full, BF16), far(thin, F32), far(full, BF16), near((8, 128), F32)]
    scratch = [
        pltpu.VMEM(small.shape, F32),
        pltpu.VMEM(full, F32),
        pltpu.VMEM((77, 8, D), F32),
        pltpu.VMEM((rows,) + full[1:], F32),
        pltpu.VMEM((rows,) + full[1:], BF16),
        pltpu.VMEM((rows,) + thin[1:], F32),
        pltpu.VMEM((rows,) + full[1:], BF16),
        pltpu.SemaphoreType.DMA((6, side)),
        pltpu.VMEM((side, side // 2) + full[2:], F32),
    ]
    specs = [HBM] * 2
    if fresh:
        out = [far(full, F32)] + out
        wide = side * full[2]
        scratch += [pltpu.VMEM(full, BF16), pltpu.VMEM((full[2], D), F32), pltpu.VMEM((full[2], wide), jnp.int32), pltpu.VMEM((wide, wide), BF16)]
        specs = [HBM] * 2 + [SMEM] * 2
    return kernel_call(
        functools.partial(conv_kernel, begin, end, fresh),
        out,
        specs + [HBM] * len(so_far),
        scratch,
        (small,) + tuple(inputs) + tuple(so_far),
        after,
        21 * rows / side + 3 * fresh,
        36,
        {2 + k: k for k in range(len(so_far))},
    )


def home(me, order, j, chips):
    if order is None:
        return j % HALF_PIECES if chips else j
    device = me
    for k, bit in enumerate(order):
        device = device ^ (((j >> k) & 1) * bit)
    return device >> 1 if chips else device


def keep_rows(mask_ref, keep_ref):
    for i in range(keep_ref.shape[0]):
        keep_ref[i : i + 1, :] = jnp.full((1, D), mask_ref[i], jnp.int32).astype(F32) / (1.0 - DROP_RATE)


def assembly(me, order, chips, first, src_hbm, whole_ref, sem):
    deep = src_hbm.shape[0] // HALF_PIECES

    def copy(j, _):
        to = pl.ds(pl.multiple_of(home(me, order, first + j, chips) * deep, 16), deep)
        dma(src_hbm.at[pl.ds(pl.multiple_of(j * deep, 16), deep), :], whole_ref.at[to, :], sem).start()
        return 0

    lax.fori_loop(0, HALF_PIECES, copy, 0)
    return dma(src_hbm, whole_ref.at[pl.ds(0, src_hbm.shape[0]), :], sem)


def deal(me, order, chips, first, out_ref, read):
    deep = out_ref.shape[0] // HALF_PIECES

    def move(j, _):
        begin = pl.multiple_of(home(me, order, first + j, chips) * deep, 16)
        to = pl.ds(pl.multiple_of(j * deep, 16), deep)
        for g in range(out_ref.shape[1] // 128):
            out_ref[to, g * 128 : (g + 1) * 128] = read(pl.ds(begin, deep), g).astype(BF16)
        return 0

    lax.fori_loop(0, HALF_PIECES, move, 0)


def even_first(rows, deep):
    blocks = [rows[d * deep // D][:, d * deep % D : d * deep % D + deep] for d in range(FF // deep)]
    return jnp.concatenate(blocks[0::2] + blocks[1::2], axis=1)


def even_last(even, odd, k, deep):
    per = D // deep
    blocks = []
    for d in range(per * k, per * k + per):
        source = odd if d % 2 else even
        blocks.append(source[:, d // 2 * deep : d // 2 * deep + deep])
    return jnp.concatenate(blocks, axis=1)


def block_kernel(block, masks, me_ref, norm_hbm, mixed_hbm, pnear_hbm, pfar_hbm, wnear_hbm, wfar_hbm, dy_hbm, small_hbm, mask_ref, *rest):
    act_hbm, dg_hbm, gnear_ref, gfar_ref, gdb_ref, out_ref, bb_hbm, sums_ref, res_hbm = rest[-32:-23]
    pair_ref, small_ref, keep_ref, norm_ref, mixed_ref, act_ref, dg_ref, branch_ref, unit_ref, inv_ref, out2_ref = rest[-23:-12]
    wd_ref, dy_ref, bb_ref, res_ref, acc, wide, wk, isem, osem, wsem, bsem, rsem = rest[-12:]
    rows = norm_hbm.shape[0]
    steps = rows // block
    imgs = keep_ref.shape[0]
    shape = (block // imgs, imgs, D)
    half = dy_hbm.shape[0]

    def spot(i):
        return pl.ds(pl.multiple_of(i * block, block), block)

    def enter(i):
        s = i % 2
        return (
            dma(norm_hbm.at[spot(i), :], norm_ref.at[s], isem.at[0, s]),
            dma(mixed_hbm.at[spot(i), :], mixed_ref.at[s], isem.at[1, s]),
        )

    def leave(i):
        s = i % 2
        pairs = ((act_ref, act_hbm), (dg_ref, dg_hbm))
        return [dma(a.at[s], b.at[spot(i), :], osem.at[k, s]) for k, (a, b) in enumerate(pairs)]

    me = me_ref[0]
    p_masks, w_masks, d_masks = masks
    load = dma(small_hbm, small_ref, wsem.at[0])
    start(enter(0))
    load.start()
    half_rows = FF // 2
    mine = 0 if p_masks is None else me % 2
    pair_in = []
    for src, first, which in ((pnear_hbm, 0, mine), (pfar_hbm, HALF_PIECES, 1 - mine)):
        to = pair_ref.at[pl.ds(pl.multiple_of(which * half_rows, half_rows), half_rows), :]
        pair_in.append(assembly(me, p_masks, True, first, src, to, wsem.at[1]))
    dy_in = dma(dy_hbm, dy_ref, wsem.at[3])
    wait(pair_in)
    down_in = [
        assembly(me, w_masks, False, first, src, wd_ref, wsem.at[2]) for first, src in ((0, wnear_hbm), (HALF_PIECES, wfar_hbm))
    ]
    dy_in.start()
    load.wait()
    keep_rows(mask_ref, keep_ref)
    keep = keep_ref[...][None]
    scale = keep * small_ref[LAYER_SCALE : LAYER_SCALE + 1, :][None]
    gain = small_ref[GAIN_TWO : GAIN_TWO + 1, :][None]
    bias = small_ref[BIAS_TWO : BIAS_TWO + 1, :][None]
    bias_rows = [small_ref[HIDDEN_BIAS + k : HIDDEN_BIAS + k + 1, :] for k in range(FF // D)]
    hidden_bias = jnp.concatenate(bias_rows, axis=1) if p_masks is None else even_first(bias_rows, FF >> len(p_masks))
    chunk = FF // 2

    def body(i, _):
        s = i % 2

        @pl.when(i + 1 < steps)
        def _():
            start(enter(i + 1))

        @pl.when(i >= 2)
        def _():
            wait(leave(i - 2))

        wait(enter(i))
        x = norm_ref[s]
        branch = jnp.broadcast_to(small_ref[OUT_BIAS : OUT_BIAS + 1, :], (block, D))

        def hidden(j):
            cols = slice(j * chunk, (j + 1) * chunk)
            return lax.dot_general(x, pair_ref[cols, :D], COLS, preferred_element_type=F32) + hidden_bias[:, cols]

        pre = hidden(0)
        for j in range(FF // chunk):
            after = hidden(j + 1) if j + 1 < FF // chunk else None
            cols = slice(j * chunk, (j + 1) * chunk)
            phi = 0.5 + 0.5 * lax.erf(pre * 0.7071067811865476)
            bell = jnp.exp2(pre * pre * -0.7213475204444817) * 0.3989422804014327
            act = (pre * phi).astype(BF16)
            act_ref[s, :, cols] = act
            dg_ref[s, :, cols] = (phi + pre * bell).astype(BF16)
            branch = branch + jnp.dot(act, pair_ref[cols, D:], preferred_element_type=F32)
            pre = after
        start(leave(i))
        split = branch_ref.shape[1:]
        branch_ref[i] = branch.astype(BF16).reshape(split)
        unit, inv = norm_of(mixed_ref[s].reshape(shape) + scale * branch.reshape(shape))
        unit_ref[i] = unit.astype(BF16).reshape(split)
        inv_ref[i] = inv.reshape(split[:-1] + (1,))
        out2_ref[i] = (unit * gain + bias).astype(BF16).reshape(split)
        return 0

    lax.fori_loop(0, steps, body, 0)

    wait(down_in)
    for g in range(6):
        wide[g] = wd_ref[:, pl.ds(g * 128, 128)].astype(F32)
        for k in range(4):
            wk[k // 2, pl.ds(k % 2 * D, D), pl.ds(g * 128, 128)] = wide[g, pl.ds(k, D, stride=4), :].astype(BF16)
    sums_ref[...] = jnp.zeros(sums_ref.shape, F32)
    rows = half * half * imgs
    shape = (half * half, imgs, D)
    for k in range(2):
        acc[:, k * D : (k + 1) * D] = jnp.broadcast_to(small_ref[DOWN_BIAS + k : DOWN_BIAS + k + 1, :], (rows, D))
    dy_in.wait()
    gdb_ref[...] = jnp.sum(dy_ref[...].astype(F32).reshape(half * half, imgs, 2 * D), axis=0)

    def give(k):
        pairs = ((bb_ref, bb_hbm), (res_ref, res_hbm))
        return [dma(a.at[k], b.at[:, k // 2, :, k % 2], rsem.at[j, k]) for j, (a, b) in enumerate(pairs)]

    for a in range(2):
        dy = dy_ref[...].reshape(rows, 2 * D)
        x = jnp.concatenate([out2_ref[:, a, :, b].reshape(rows, D) for b in range(2)], axis=1)
        both = lax.dot_general(dy, wk[a], COLS, preferred_element_type=F32)
        acc[...] += jnp.dot(x, wk[a], preferred_element_type=F32)
        gd = lax.dot_general(x, dy, ROWS, preferred_element_type=F32)
        for b in range(2):
            k = 2 * a + b
            for g in range(6):
                wide[g, pl.ds(k, D, stride=4), :] = gd[b * D : (b + 1) * D, g * 128 : (g + 1) * 128]
            back = both[:, b * D : (b + 1) * D].reshape(shape)
            unit = unit_ref[:, a, :, b].reshape(shape).astype(F32)
            sums_ref[0] += jnp.sum(back * unit, axis=0)
            sums_ref[1] += jnp.sum(back, axis=0)
            res = norm_back(back, unit, inv_ref[:, a, :, b].reshape(half * half, imgs, 1), gain)
            res_ref[k] = res.astype(BF16).reshape(half, half, imgs, D)
            sums_ref[2] += jnp.sum(res * keep * branch_ref[:, a, :, b].reshape(shape).astype(F32), axis=0)
            bb = (res * scale).astype(BF16)
            bb_ref[k] = bb.reshape(half, half, imgs, D)
            start(give(k))
            sums_ref[3] += jnp.sum(bb.astype(F32), axis=0)

    out_ref[...] = acc[...].astype(BF16).reshape(out_ref.shape)
    deal(me, d_masks, False, 0, gnear_ref, lambda at, g: wide[g, at, :])
    deal(me, d_masks, False, HALF_PIECES, gfar_ref, lambda at, g: wide[g, at, :])
    for k in range(4):
        wait(give(k))
    for i in range(max(steps - 2, 0), steps):
        wait(leave(i))


def block_both(masks, me, norm, mixed, pair, down, dy, small, mask, after=(), block=448):
    rows = norm.shape[0]
    half, _, imgs, _ = dy.shape
    area = half * half * imgs
    six = (half, 2, half, 2, imgs)
    two = lambda width, dtype: pltpu.VMEM((2, block, width), dtype)
    whole = lambda width, dtype: pltpu.VMEM(six + (width,), dtype)
    part = pltpu.VMEM((4, half, half, imgs, D), BF16)
    return kernel_call(
        functools.partial(block_kernel, block, masks),
        [far((rows, FF), BF16)] * 2
        + [near((2 * D, 2 * D), BF16)] * 2
        + [near((imgs, 2 * D), F32), near((half, half, imgs, 2 * D), BF16)]
        + [far(six + (D,), BF16), near((4, imgs, D), F32), far(six + (D,), BF16)],
        [SMEM] + [HBM] * 2 + [ANY, HBM] * 2 + [HBM] * 2 + [SMEM],
        [pltpu.VMEM((FF, 2 * D), BF16), pltpu.VMEM(small.shape, F32), pltpu.VMEM((imgs, D), F32)]
        + [two(D, BF16), two(D, F32), two(FF, BF16), two(FF, BF16)]
        + [whole(D, BF16), whole(D, BF16), whole(1, F32), whole(D, BF16)]
        + [pltpu.VMEM((4 * D, 2 * D), BF16), pltpu.VMEM(dy.shape, BF16), part, part]
        + [pltpu.VMEM((area, 2 * D), F32), pltpu.VMEM((6, 4 * D, 128), F32), pltpu.VMEM((2, 2 * D, 2 * D), BF16)]
        + [pltpu.SemaphoreType.DMA((2, 2)), pltpu.SemaphoreType.DMA((2, 2)), pltpu.SemaphoreType.DMA((4,))]
        + [pltpu.SemaphoreType.DMA((1,)), pltpu.SemaphoreType.DMA((2, 4))],
        (me, norm, mixed, *pair, *down, dy, small, mask),
        after,
        34,
        58,
    )


def pair_grad_kernel(block, first, masks, me_ref, bb_hbm, act_hbm, dg_hbm, norm_hbm, pair_hbm, *rest):
    g_ref, hb_ref, p_hbm, pair_ref, acc, turned, bb_ref, act_ref, dg_ref, norm_ref, p_ref, sem, osem, wsem = rest[-14:]
    rows = bb_hbm.shape[0]
    imgs = hb_ref.shape[0]
    steps = rows // block
    wide = FF // 2
    me = me_ref[0]
    which = 0 if masks is None else me % 2
    which = 1 - which if first else which
    lanes = pl.ds(pl.multiple_of(which * wide, wide), wide)

    def spot(i):
        return pl.ds(pl.multiple_of(i * block, block), block)

    def enter(i):
        s = i % 2
        return (
            dma(bb_hbm.at[spot(i), :], bb_ref.at[s], sem.at[0, s]),
            dma(dg_hbm.at[spot(i), lanes], dg_ref.at[s], sem.at[1, s]),
            dma(act_hbm.at[spot(i), lanes], act_ref.at[s], sem.at[2, s]),
            dma(norm_hbm.at[spot(i), :], norm_ref.at[s], sem.at[3, s]),
        )

    def leave(i):
        return dma(p_ref.at[i % 2], p_hbm.at[spot(i), :], osem.at[i % 2])

    pair_in = [assembly(me, masks, True, first, pair_hbm, pair_ref, wsem.at[0])]
    start(enter(0))
    hb_ref[...] = jnp.zeros(hb_ref.shape, F32)
    acc[...] = jnp.zeros(acc.shape, F32)
    wait(pair_in)

    def body(i, _):
        s = i % 2

        @pl.when(i + 1 < steps)
        def _():
            start(enter(i + 1))

        @pl.when(i >= 2)
        def _():
            leave(i - 2).wait()

        wait(enter(i))
        b = bb_ref[s]
        back = lax.dot_general(b, pair_ref[:, D:], COLS, preferred_element_type=F32)
        acc[D:, :] += lax.dot_general(b, act_ref[s], ROWS, preferred_element_type=F32)
        p = (back * dg_ref[s].astype(F32)).astype(BF16)
        p_ref[s] = p
        hb_ref[...] += jnp.sum(p.astype(F32).reshape(block // imgs, imgs, wide), axis=0)
        acc[:D, :] += lax.dot_general(norm_ref[s], p, ROWS, preferred_element_type=F32)
        leave(i).start()
        return 0

    lax.fori_loop(0, steps, body, 0)
    turned[...] = acc[...].T
    deal(me, masks, True, first, g_ref, lambda at, g: turned[at, pl.ds(g * 128, 128)])
    for i in range(max(steps - 2, 0), steps):
        leave(i).wait()


def pair_grad(first, masks, me, bb, act, dg, norm, pair, imgs, after=(), block=784):
    rows = bb.shape[0]
    wide = FF // 2
    two = lambda width: pltpu.VMEM((2, block, width), BF16)
    return kernel_call(
        functools.partial(pair_grad_kernel, block, first, masks),
        [near((wide, 2 * D), BF16), near((imgs, wide), F32), far((rows, wide), BF16)],
        [SMEM] + [HBM] * 5,
        [pltpu.VMEM((wide, 2 * D), BF16), pltpu.VMEM((2 * D, wide), F32), pltpu.VMEM((wide, 2 * D), F32)]
        + [two(D), two(wide), two(wide), two(D), two(wide)]
        + [pltpu.SemaphoreType.DMA((4, 2)), pltpu.SemaphoreType.DMA((2,)), pltpu.SemaphoreType.DMA((1,))],
        (me, bb, act, dg, norm, pair),
        after,
        13,
        44,
    )


def back_one_kernel(block, masks, me_ref, pnear_hbm, pfar_hbm, unit_hbm, inv_hbm, near_hbm, far_hbm, small_hbm, *rest):
    conv_hbm, sums_ref, near_ref, far_ref, small_ref, pnear_ref, pfar_ref, unit_ref, inv_ref, conv_ref, sem, wsem = rest[-12:]
    rows = pnear_hbm.shape[0]
    imgs = sums_ref.shape[1]
    steps = rows // block
    shape = (block // imgs, imgs, D)

    def spot(i):
        return pl.ds(pl.multiple_of(i * block, block), block)

    def enter(i):
        s = i % 2
        pairs = ((pnear_hbm, pnear_ref), (pfar_hbm, pfar_ref), (unit_hbm, unit_ref), (inv_hbm, inv_ref))
        return [dma(a.at[spot(i), :], b.at[s], sem.at[k, s]) for k, (a, b) in enumerate(pairs)]

    def leave(i):
        return dma(conv_ref.at[i % 2], conv_hbm.at[spot(i), :], sem.at[4, i % 2])

    load = dma(small_hbm, small_ref, wsem.at[0])
    left = pl.ds(0, D)
    pair_in = [
        assembly(me_ref[0], masks, True, first, src.at[:, left], dst, wsem.at[1])
        for first, src, dst in ((0, near_hbm, near_ref), (HALF_PIECES, far_hbm, far_ref))
    ]
    start(enter(0))
    load.start()
    sums_ref[...] = jnp.zeros(sums_ref.shape, F32)
    wait(pair_in)
    load.wait()
    gain = small_ref[GAIN_ONE : GAIN_ONE + 1, :][None]

    def body(i, _):
        s = i % 2

        @pl.when(i + 1 < steps)
        def _():
            start(enter(i + 1))

        @pl.when(i >= 2)
        def _():
            leave(i - 2).wait()

        wait(enter(i))
        back = jnp.dot(pnear_ref[s], near_ref[...], preferred_element_type=F32)
        back = (back + jnp.dot(pfar_ref[s], far_ref[...], preferred_element_type=F32)).reshape(shape)
        unit = unit_ref[s].reshape(shape).astype(F32)
        sums_ref[0] += jnp.sum(back * unit, axis=0)
        sums_ref[1] += jnp.sum(back, axis=0)
        out = norm_back(back, unit, inv_ref[s].reshape(shape[:2] + (1,)), gain)
        sums_ref[2] += jnp.sum(out, axis=0)
        conv_ref[s] = out.astype(BF16).reshape(block, D)
        leave(i).start()
        return 0

    lax.fori_loop(0, steps, body, 0)
    for i in range(max(steps - 2, 0), steps):
        leave(i).wait()


def back_one(masks, me, p, unit, inv, pair, small, imgs, after=(), block=784):
    rows = unit.shape[0]
    wide = FF // 2
    two = lambda width, dtype: pltpu.VMEM((2, block, width), dtype)
    return kernel_call(
        functools.partial(back_one_kernel, block, masks),
        [far((rows, D), BF16), near((3, imgs, D), F32)],
        [SMEM] + [HBM] * 7,
        [pltpu.VMEM((wide, D), BF16)] * 2
        + [pltpu.VMEM(small.shape, F32)]
        + [two(wide, BF16), two(wide, BF16), two(D, BF16), two(1, F32), two(D, BF16)]
        + [pltpu.SemaphoreType.DMA((5, 2)), pltpu.SemaphoreType.DMA((2,))],
        (me, *p, unit, inv, *pair, small),
        after,
        11,
        32,
    )


def taps_kernel(groups, conv_hbm, mixed_hbm, *rest):
    g_ref, conv_ref, mixed_ref, sums, even, odd, last, sem = rest[-8:]
    side, _, imgs, _ = conv_hbm.shape
    pairs = side // 2

    def enter(k):
        lanes = pl.ds(pl.multiple_of((k + groups[0]) * 128, 128), 128)
        return (
            dma(mixed_hbm.at[:, :, :, lanes], mixed_ref.at[k], sem.at[0, k]),
            dma(conv_hbm.at[:, :, :, lanes], conv_ref.at[k], sem.at[1, k]),
        )

    for k in range(len(groups)):
        start(enter(k))
    def group(k, _):
        wait(enter(k))

        def prepare(h, _):
            x = [mixed_ref[k, h, w] for w in range(side)]
            d = [conv_ref[k, h, w].astype(F32) for w in range(side)]
            for i in range(pairs):
                sums[h, i] = x[2 * i] + x[2 * i + 1]
                last[h, i] = d[2 * i + 1]
                even[h, i] = d[2 * i] - d[2 * i + 1]
                odd[h, i + 1] = (d[2 * i + 2] if i + 1 < pairs else jnp.zeros_like(d[0])) - d[2 * i + 1]
            odd[h, 0] = d[0]
            return 0

        lax.fori_loop(0, side, prepare, 0)
        for ky in range(7):
            first = max(3 - ky, 0)
            count = min(side, side + 3 - ky) - first

            def row(h, acc):
                acc = list(acc)
                for t in range(imgs // 8):
                    at = pl.ds(t * 8, 8)
                    for begin, shift, taps, length, read_x, read_d in (
                        (4, 0, 3, pairs, lambda i: mixed_ref[k, h + ky - 3, 2 * i, at], lambda i: even[h, i, at]),
                        (0, -1, 4, pairs + 1, lambda i: mixed_ref[k, h + ky - 3, 2 * i + 1, at], lambda i: odd[h, i, at]),
                        (7, 0, 4, pairs, lambda i: sums[h + ky - 3, i, at], lambda i: last[h, i, at]),
                    ):
                        x = [read_x(i) for i in range(pairs)]
                        for a in range(length):
                            d = read_d(a)
                            for j in range(taps):
                                i = a + shift - 1 + j
                                if 0 <= i < pairs:
                                    acc[begin + j] = acc[begin + j] + x[i] * d
                return tuple(acc)

            acc = lax.fori_loop(
                0, count // 2, lambda r, acc: row(first + 2 * r + 1, row(first + 2 * r, acc)), (jnp.zeros((8, 128), F32),) * 11
            )
            if count % 2:
                acc = row(first + count - 1, acc)
            even_taps = [acc[j] + acc[7 + j] for j in range(4)]
            odd_taps = [acc[4 + j] + acc[7 + j] for j in range(3)]
            for kx in range(7):
                value = odd_taps[kx // 2] if kx % 2 else even_taps[kx // 2]
                g_ref[ky * 7 + kx, :, pl.ds(pl.multiple_of(k * 128, 128), 128)] = value
        return 0

    lax.fori_loop(0, len(groups), group, 0)


def taps_grad(conv, mixed, groups, after=()):
    side, _, imgs, _ = conv.shape
    lanes = lambda dtype: pltpu.VMEM((len(groups),) + conv.shape[:3] + (128,), dtype)
    part = lambda columns: pltpu.VMEM((side, columns, imgs, 128), F32)
    return kernel_call(
        functools.partial(taps_kernel, groups),
        [near((49, 8, 128 * len(groups)), F32)],
        [HBM] * 2,
        [lanes(BF16), lanes(F32), part(side // 2), part(side // 2), part(side // 2 + 1), part(side // 2), pltpu.SemaphoreType.DMA((2, len(groups)))],
        (conv, mixed),
        after,
        4.7 * len(groups),
        28,
    )[0]


def images_kernel(begin, end, conv_hbm, small_hbm, partner_ref, weight_ref, res_hbm, *rest):
    g_hbm, token_ref, small_ref, raw_ref, conv_ref, taps, res_ref, out_ref, mix_ref, row_ref, sel_ref, rest_ref, sem, csem, pair_sums, rsem = rest[-16:]
    side, _, imgs, _ = conv_hbm.shape
    low = max(begin - 3, 0)
    high = min(end + 3, side)
    load = dma(small_hbm, small_ref, csem.at[side])
    load.start()
    token_ref[...] = jnp.zeros(token_ref.shape, F32)

    def bring(h):
        return dma(conv_hbm.at[h], raw_ref.at[h], csem.at[h])

    def widen(h):
        bring(h).wait()
        conv_ref[h] = raw_ref[h].astype(F32)
        add_columns(conv_ref, pair_sums, h)

    def enter(h):
        return dma(res_hbm.at[h], res_ref.at[h - begin], rsem.at[h - begin])

    def leave(h):
        return dma(out_ref.at[h - begin], g_hbm.at[h], sem.at[1, 0])

    for h in range(low, high):
        bring(h).start()
        if h == min(begin + 3, high - 1):
            for r in range(begin, end):
                enter(r).start()
    spread(weight_ref, mix_ref)
    for i in range(imgs):
        row_ref[pl.ds(lax.rem(partner_ref[i], imgs), 1), :] = jnp.full((1, row_ref.shape[1]), i, jnp.int32)
    select(row_ref, sel_ref)
    load.wait()
    fill_taps(small_ref, taps, True)
    mix = mix_ref[...][None]
    others = 1.0 - mix
    for h in range(low, min(begin + 3, high)):
        widen(h)

    def row(h, kys):
        @pl.when(h + 3 < high)
        def _():
            widen(h + 3)

        enter(h).wait()
        rest_ref[...] = res_ref[h - begin].astype(F32)

        def tile(k, _):
            at, lanes = tile_of(k, imgs)
            base = [rest_ref[w, at, lanes] for w in range(side)]
            acc = conv_rows(conv_ref, pair_sums, taps, h, kys, at, lanes, side, base)
            for w in range(side):
                out_ref[h - begin, w, at, lanes] = acc[w]
            return 0

        return tiles(h, imgs, tile, False)

    every_row(begin, end, side, row)

    def unmix(r):
        v = out_ref[r]
        part = (others * v).reshape(side * imgs, D)
        upper = part.astype(BF16)
        lower = (part - upper.astype(F32)).astype(BF16)
        back = jnp.dot(sel_ref[...], upper, preferred_element_type=F32)
        back = back + jnp.dot(sel_ref[...], lower, preferred_element_type=F32)
        out_ref[r] = mix * v + back.reshape(side, imgs, D)
        leave(begin + r).start()

    def two(i, _):
        unmix(2 * i)
        unmix(2 * i + 1)
        return 0

    lax.fori_loop(0, (end - begin) // 2, two, 0)
    for h in range(begin, end):
        leave(h).wait()


def images_back(conv, small, partner, weight, res, begin, end, so_far=(), after=()):
    side, _, imgs, _ = conv.shape
    return kernel_call(
        functools.partial(images_kernel, begin, end),
        [far(conv.shape, F32), near((8, 128), F32)],
        [HBM, HBM, SMEM, SMEM, HBM] + [HBM] * len(so_far),
        [
            pltpu.VMEM(small.shape, F32),
            pltpu.VMEM(conv.shape, BF16),
            pltpu.VMEM(conv.shape, F32),
            pltpu.VMEM((77, 8, D), F32),
            pltpu.VMEM((end - begin, side, imgs, D), BF16),
            pltpu.VMEM((end - begin, side, imgs, D), F32),
            pltpu.VMEM((imgs, D), F32),
            pltpu.VMEM((imgs, side * imgs), jnp.int32),
            pltpu.VMEM((side * imgs, side * imgs), BF16),
            pltpu.VMEM((side, imgs, D), F32),
            pltpu.SemaphoreType.DMA((2, 2)),
            pltpu.SemaphoreType.DMA((side + 1,)),
            pltpu.VMEM((side, side // 2, imgs, D), F32),
            pltpu.SemaphoreType.DMA((end - begin,)),
        ],
        (conv, small, partner, weight, res) + tuple(so_far),
        after,
        22 * (end - begin) / side,
        28,
        {5: 0} if so_far else {},
    )


def ready_kernel(in_hbm, out_hbm, down_hbm, *rest):
    pair_ref, low_ref, in_ref, out_ref, down_ref, sem = rest[-6:]
    pairs = ((in_hbm, in_ref), (out_hbm, out_ref), (down_hbm, down_ref))
    copies = [dma(a, b, sem.at[k]) for k, (a, b) in enumerate(pairs)]
    start(copies)
    wait(copies)
    pair_ref[0, :, :D] = in_ref[...].astype(BF16)
    pair_ref[0, :, D:] = out_ref[...].astype(BF16)
    low_ref[0] = down_ref[...].astype(BF16)


def ready(weight_in, weight_out, weight_down, after=()):
    deep = weight_in.shape[0]
    return kernel_call(
        ready_kernel,
        [near((1, deep, 2 * D), BF16)] * 2,
        [HBM] * 3,
        [pltpu.VMEM(x.shape, F32) for x in (weight_in, weight_out, weight_down)] + [pltpu.SemaphoreType.DMA((3,))],
        (weight_in, weight_out, weight_down),
        after,
        0.5,
        8,
    )


def join_kernel(first_ref, second_ref, *rest):
    out_ref = rest[-1]
    k = first_ref.shape[0]
    out_ref[:k] = first_ref[...]
    out_ref[k:] = second_ref[...]


def join(first, second, after=()):
    return kernel_call(
        join_kernel,
        [near((2 * first.shape[0],) + first.shape[1:], first.dtype)],
        [VMEM] * 2,
        [],
        (first, second),
        after,
        0.5,
        8,
    )[0]


def fold_kernel(count, *refs):
    ins, (stay_ref, leave_ref) = refs[: 2 * count], refs[-2:]
    k = stay_ref.shape[0] // count
    for i in range(count):
        keep_ref, come_ref = ins[2 * i], ins[2 * i + 1]
        stay_ref[i * k : (i + 1) * k] = keep_ref[:k].astype(F32) + come_ref[:k].astype(F32)
        leave_ref[i * k : (i + 1) * k] = (keep_ref[k:].astype(F32) + come_ref[k:].astype(F32)).astype(BF16)


def fold(*arrays, after=()):
    slots, deep, wide = arrays[0].shape
    count = len(arrays) // 2
    return kernel_call(
        functools.partial(fold_kernel, count),
        [near((count * slots // 2, deep, wide), F32), near((count * slots // 2, deep, wide), BF16)],
        [VMEM] * len(arrays),
        [],
        arrays,
        after,
        0.5,
        12,
    )


def part_kernel(*refs):
    ins, outs = refs[:4], refs[-4:]
    for i in range(2):
        keep_ref, come_ref = ins[2 * i], ins[2 * i + 1]
        for slot, out_ref in enumerate(outs):
            out_ref[i] = (keep_ref[slot].astype(F32) + come_ref[slot].astype(F32)).astype(out_ref.dtype)


def part(p_keep, p_come, d_keep, d_come, after=()):
    shape = (2,) + p_keep.shape[1:]
    return kernel_call(
        part_kernel,
        [near(shape, F32)] + [near(shape, BF16)] * 3,
        [VMEM] * 4,
        [],
        (p_keep, p_come, d_keep, d_come),
        after,
        0.5,
        12,
    )


def small_kernel(hops, me_ref, gk_ref, sums1_ref, sums2_ref, near_ref, far_ref, db_ref, keep_ref, *rest):
    sum_ref, send_ref, total = rest[-3:]
    grads = keep_ref[...]
    for come_ref in rest[:-3]:
        grads = grads + come_ref[...].astype(F32)
    sum_ref[...] = grads
    rows = lambda x: jnp.sum(x, axis=0, keepdims=True)
    for t in range(49):
        total[t : t + 1, :] = rows(gk_ref[t])
    for row, value in (
        (DEPTH_BIAS, sums1_ref[2]),
        (GAIN_ONE, sums1_ref[0]),
        (BIAS_ONE, sums1_ref[1]),
        (OUT_BIAS, sums2_ref[3]),
        (LAYER_SCALE, sums2_ref[2]),
        (GAIN_TWO, sums2_ref[0]),
        (BIAS_TWO, sums2_ref[1]),
    ):
        total[row : row + 1, :] = rows(value)
    mine, other = rows(near_ref[...]), rows(far_ref[...])
    if hops:
        odd_device = (me_ref[0] % 2).astype(F32)
        even = mine * (1.0 - odd_device) + other * odd_device
        odd = other * (1.0 - odd_device) + mine * odd_device
    for k in range(4):
        if hops:
            value = even_last(even, odd, k, FF // hops)
        else:
            value = (mine, other)[k // 2][:, k % 2 * D : k % 2 * D + D]
        total[HIDDEN_BIAS + k : HIDDEN_BIAS + k + 1, :] = value
    for k in range(2):
        total[DOWN_BIAS + k : DOWN_BIAS + k + 1, :] = rows(db_ref[:, k * D : (k + 1) * D])
    square = jnp.full((1, D), jnp.sum(grads * grads), F32)
    upper = square.astype(BF16).astype(F32)
    total[SQUARES : SQUARES + 1, :] = upper
    total[SQUARES + 1 : SQUARES + 2, :] = square - upper
    send_ref[...] = total[...].astype(BF16)


def small_total(hops, me, gk, sums1, sums2, near_hb, far_hb, db, keep, *come):
    return kernel_call(
        functools.partial(small_kernel, hops),
        [near(keep.shape, F32), near((SQUARES + 2, D), BF16)],
        [SMEM] + [VMEM] * (7 + len(come)),
        [pltpu.VMEM((SQUARES + 2, D), F32)],
        (me, gk, sums1, sums2, near_hb, far_hb, db, keep, *come),
        (),
        1,
        8,
    )


def meet_kernel(*refs):
    arrays, out_ref = refs[:-1], refs[-1]
    sums = [x[...].astype(F32) for x in arrays]
    while len(sums) > 1:
        sums = [a + b for a, b in zip(sums[::2], sums[1::2])]
    total = sums[0]
    square = total[SQUARES : SQUARES + 1] + total[SQUARES + 1 : SQUARES + 2]
    upper = square.astype(BF16).astype(F32)
    out_ref[...] = total.astype(out_ref.dtype)
    out_ref[SQUARES : SQUARES + 2, :] = jnp.concatenate([upper, square - upper], axis=0).astype(out_ref.dtype)


def meet(arrays, dtype):
    return kernel_call(meet_kernel, [near(arrays[0].shape, dtype)], [VMEM] * len(arrays), [], arrays, (), 0.3, 8)[0]


def adam(weight, first, second, grad, rate, decay):
    first = BETA_ONE * first + (1.0 - BETA_ONE) * grad
    second = BETA_TWO * second + (1.0 - BETA_TWO) * grad * grad
    first_hat = first / (1.0 - BETA_ONE**STEP)
    second_hat = second / (1.0 - BETA_TWO**STEP)
    weight = weight - rate * (first_hat / (jnp.sqrt(second_hat) + ADAM_EPS) + decay * weight)
    return first, second, weight


def adam_kernel(total_ref, grads_ref, *refs):
    ins, outs = refs[:9], refs[9:18]
    norm_ref = refs[18]
    gs = total_ref[:SQUARES]
    norm = jnp.sqrt(jnp.sum(gs * gs) + jnp.sum(total_ref[SQUARES : SQUARES + 2, 0:1]))
    norm_ref[0, 0] = norm
    factor = CLIP_NORM / jnp.maximum(norm, CLIP_NORM)
    grads = (grads_ref[0, :, :D], grads_ref[0, :, D:], grads_ref[1])
    rates = (LAYER_DECAY * RATE_MATRIX, LAYER_DECAY * RATE_MATRIX, RATE_MATRIX)
    for k in range(3):
        new = adam(ins[3 * k][...], ins[3 * k + 1][...], ins[3 * k + 2][...], grads[k] * factor, rates[k], WEIGHT_DECAY)
        for out_ref, value in zip(outs[3 * k : 3 * k + 3], new):
            out_ref[...] = value


def adam_all(total, grads, states):
    return pl.pallas_call(
        adam_kernel,
        out_shape=tuple(near(x.shape, F32) for x in states) + (near((1, 1), F32),),
        in_specs=[VMEM] * 11,
        out_specs=(VMEM,) * 9 + (SMEM,),
        cost_estimate=pl.CostEstimate(flops=int(2e9), bytes_accessed=0, transcendentals=0),
        compiler_params=pltpu.CompilerParams(vmem_limit_bytes=12 << 20),
    )(total, grads, *states)


def swap(x, bit, n):
    return lax.ppermute(x, "dp", [(i, i ^ bit) for i in range(n)])


def is_set(bit):
    return (lax.axis_index("dp") & bit) != 0


def gather_natural(shard, n, order, gates=None):
    have = shard
    met = []
    for hop, bit in enumerate(order):
        if gates and hop in gates:
            have, _ = lax.optimization_barrier((have, gates[hop]))
        other = swap(have, bit, n)
        axis = sum(1 for b in met if b > bit)
        mine = is_set(bit)
        have = jnp.stack([jnp.where(mine, other, have), jnp.where(mine, have, other)], axis=axis)
        met.append(bit)
    return have.reshape((n,) + shard.shape)


def local(n, images, mix_weight, partner, keep_mask, cotangent, weight_in, weight_out, weight_down, small_params,
          first_in, second_in, first_out, second_out, first_down, second_down, first_small, second_small):
    imgs, side = images.shape[:2]
    half = side // 2
    pixels = side * side * imgs
    me = lax.axis_index("dp")
    bits = [1 << k for k in range(n.bit_length() - 1)]
    deep = FF // n
    by_hops = n == 32

    pair, down = ready(weight_in, weight_out, weight_down)
    mine = me[None].astype(jnp.int32)
    p_masks = w_masks = d_masks = None
    if by_hops:
        p_order = [16, 8, 4, 2, 1]
        w_order = [16, 8, 2, 4, 1]
        d_order = p_order
        p_masks, w_masks, d_masks = p_order, w_order, d_order

    img = images.transpose(1, 2, 0, 3)
    dy = cotangent.transpose(1, 2, 0, 3)
    flat = lambda a: a.reshape(pixels, a.shape[-1])
    square = lambda a: a.reshape(side, side, imgs, a.shape[-1])

    cut = [0, 3, 12, side]
    gates = None
    if by_hops:
        gates = {1: pair}
        pair = join(pair, swap(pair, p_order[0], n))
        gates[3] = pair
        down = join(down, swap(down, w_order[0], n))
        pair = join(pair, swap(pair, p_order[1], n))
        gates[4] = pair
    small = gather_natural(small_params.astype(BF16), n, bits[1:] + bits[:1], gates).reshape(-1, D).astype(F32)
    if by_hops:
        down = join(down, swap(down, w_order[1], n))
    mixed, *made, token = conv_forward(small, (img, partner, mix_weight), cut[0], cut[1])
    for piece in (1, 2):
        if by_hops:
            pair = join(pair, swap(pair, p_order[piece + 1], n), (token,))
            down = join(down, swap(down, w_order[piece + 1], n), (token,))
        *made, token = conv_forward(small, (mixed,), cut[piece], cut[piece + 1], tuple(made), (pair, down))
    unit1, inv1, norm1 = made
    if by_hops:
        pair = (pair, swap(pair, p_order[4], n))
        down = (down, swap(down, w_order[4], n))
    else:
        pair, down = (lax.all_gather(x[0], "dp", axis=0, tiled=True).reshape(2, FF // 2, 2 * D) for x in (pair, down))
    pair = tuple(x.reshape(FF // 2, 2 * D) for x in pair)
    down = tuple(x.reshape(FF // 2, 2 * D) for x in down)
    act, dg, d_near, d_far, gdb, out, bb, sums2, res = block_both(
        (p_masks, w_masks, d_masks), mine, flat(norm1), flat(mixed), pair, down, dy, small, keep_mask
    )
    shards = (n // 2, deep, 2 * D)
    if by_hops:
        d_keep = d_near.reshape(shards)
        d_come = swap(d_far.reshape(shards), d_order[4], n)
    grads_of = lambda which, after: pair_grad(
        16 * which, p_masks, mine, flat(bb), act, dg, flat(norm1), pair[which], imgs, after
    )
    p_far, far_hb, far_p = grads_of(1, ())
    if by_hops:
        d_keep, d_send = fold(d_keep, d_come, after=(far_hb,))
        d_come = swap(d_send, d_order[3], n)
        p_come = swap(p_far.reshape(shards), p_order[4], n)
    p_near, near_hb, near_p = grads_of(0, (d_send,) if by_hops else (far_hb,))
    p_gate = ()
    if by_hops:
        p_keep, p_send = fold(p_near.reshape(shards), p_come, after=(near_hb,))
        p_come = swap(p_send, p_order[3], n)
        d_keep, d_send = fold(d_keep, d_come, after=(near_hb,))
        d_come = swap(d_send, d_order[2], n)
        p_gate = (p_send, d_send)
    back_conv, sums1 = back_one(p_masks, mine, (near_p, far_p), flat(unit1), flat(inv1), pair, small, imgs, p_gate)
    back_conv = square(back_conv)
    res = square(res)
    back = functools.partial(images_back, back_conv, small, partner, mix_weight, res)
    if by_hops:
        p_keep, p_send = fold(p_keep, p_come, after=(sums1,))
        p_come = swap(p_send, p_order[2], n)
        grad, token = back(0, side, (), (p_send,))
        keep, *send = part(p_keep, p_come, d_keep, d_come, after=(token,))
        come = [swap(x, bits, n) for x, bits in zip(send, (16, 8, 24))]
        gk = taps_grad(back_conv, mixed, (0, 1, 2), tuple(send))
    else:
        grad, _ = back(0, side)
        gk = taps_grad(back_conv, mixed, (0, 1, 2))
        keep = jnp.stack(
            [
                lax.psum_scatter(jnp.concatenate(x).astype(F32), "dp", scatter_dimension=0, tiled=True)
                for x in ((p_near, p_far), (d_near, d_far))
            ]
        )
        come = ()

    grads, total = small_total(n if by_hops else 0, mine, gk, sums1, sums2, near_hb, far_hb, gdb, keep, *come)
    rounds = [bits[k : k + 2] for k in range(1, len(bits), 2)] + [bits[:1]]
    for step, pair_bits in enumerate(rounds):
        others = [pair_bits[0], pair_bits[-1], sum(pair_bits)] if len(pair_bits) == 2 else pair_bits
        arrays = (total,) + tuple(swap(total, other, n) for other in others)
        total = meet(arrays, F32 if step == len(rounds) - 1 else BF16)
    states = (weight_in, first_in, second_in, weight_out, first_out, second_out, weight_down, first_down, second_down)
    *news, norm = adam_all(total, grads, states)
    grad_norm = norm[0, 0]
    factor = CLIP_NORM / jnp.maximum(grad_norm, CLIP_NORM)
    shard_len = small_params.shape[0]
    gs = lax.dynamic_slice_in_dim(total[:SQUARES].reshape(-1), me * shard_len, shard_len)
    position = me * shard_len + jnp.arange(shard_len, dtype=jnp.int32)
    small_rate = jnp.where(position < 54 * D + FF, LAYER_DECAY * RATE_VECTOR, RATE_VECTOR)
    small_decay = jnp.where(position < 49 * D, WEIGHT_DECAY, 0.0)
    new_small = adam(small_params, first_small, second_small, gs * factor, small_rate, small_decay)
    return (
        out.transpose(2, 0, 1, 3),
        grad.transpose(2, 0, 1, 3),
        grad_norm,
        *news,
        *new_small,
    )


def solution(mesh):
    four = P("dp", None, None, None)
    two = P("dp", None)
    one = P("dp")
    return jax.shard_map(
        functools.partial(local, mesh.shape["dp"]),
        mesh=mesh,
        in_specs=(four, one, one, one, four, two, two, two, one) + (two,) * 6 + (one,) * 2,
        out_specs=(four, four, P()) + (two,) * 9 + (one,) * 3,
        check_vma=False,
    )
```

```python
import functools
import jax
import jax.numpy as jnp
import numpy as np
from jax import lax
from jax.experimental import pallas as pl
from jax.experimental.pallas import tpu as pltpu
from jax.sharding import PartitionSpec as P

STEP = 10
DROP_RATE = 0.2
RATE_MATRIX = 0.05
RATE_VECTOR = 0.3
LAYER_DECAY = 0.8
BETA_ONE = 0.9
BETA_TWO = 0.999
ADAM_EPS = 1e-08
WEIGHT_DECAY = 0.05
CLIP_NORM = 1.0
D = 384
FF = 1536
LN_EPS = 1e-06
F32 = jnp.float32
BF16 = jnp.bfloat16
VMEM = pl.BlockSpec(memory_space=pltpu.VMEM)
SMEM = pl.BlockSpec(memory_space=pltpu.SMEM)
HBM = pl.BlockSpec(memory_space=pltpu.HBM)
ANY = pl.BlockSpec(memory_space=pl.ANY)
ROWS = (((0,), (0,)), ((), ()))
COLS = (((1,), (1,)), ((), ()))
DEPTH_BIAS, GAIN_ONE, BIAS_ONE, HIDDEN_BIAS, OUT_BIAS, LAYER_SCALE, GAIN_TWO, BIAS_TWO, DOWN_BIAS = 49, 50, 51, 52, 56, 57, 58, 59, 60
SQUARES = 62
HALF_PIECES = 16


def near(shape, dtype):
    return jax.ShapeDtypeStruct(shape, dtype)


def far(shape, dtype):
    return pltpu.HBM(shape, dtype)


def held(x):
    return pltpu.with_memory_space_constraint(x, pltpu.HBM)


def dma(src, dst, sem):
    return pltpu.make_async_copy(src, dst, sem)


def start(copies):
    for copy in copies:
        copy.start()


def wait(copies):
    for copy in copies:
        copy.wait()


class Far:
    def __init__(self, array):
        self.array = array


def kernel_call(body, out, specs, scratch, args, after, us, mib, aliases=None):
    specs = specs + [HBM if isinstance(x, Far) else ANY for x in after]
    args = tuple(args) + tuple(x.array if isinstance(x, Far) else x for x in after)
    args = [held(x) if spec is HBM else x for spec, x in zip(specs, args)]
    return pl.pallas_call(
        body,
        out_shape=tuple(out),
        in_specs=specs,
        out_specs=tuple(HBM if isinstance(x, type(far((8, 128), F32))) else VMEM for x in out),
        scratch_shapes=scratch,
        input_output_aliases=aliases or {},
        cost_estimate=pl.CostEstimate(flops=int(us * 1e9), bytes_accessed=0, transcendentals=0),
        compiler_params=pltpu.CompilerParams(vmem_limit_bytes=mib << 20),
    )(*args)


def norm_of(v):
    c = v - jnp.mean(v, axis=-1, keepdims=True)
    inv = lax.rsqrt(jnp.mean(c * c, axis=-1, keepdims=True) + LN_EPS)
    return c * inv, inv


def norm_back(back, unit, inv, gain):
    scaled = back * gain
    m1 = jnp.mean(scaled, axis=-1, keepdims=True)
    m2 = jnp.mean(scaled * unit, axis=-1, keepdims=True)
    return inv * (scaled - m1 - unit * m2)


def tile_of(k, imgs):
    groups = imgs // 8
    return pl.ds(pl.multiple_of(k % groups * 8, 8), 8), pl.ds(pl.multiple_of(k // groups * 128, 128), 128)


def tiles(h, imgs, tile, loop):
    count = imgs // 8 * (D // 128)
    if loop and isinstance(h, int):
        return lax.fori_loop(0, count, tile, 0)
    for k in range(count):
        tile(k, 0)
    return 0


def every_row(begin, end, side, do):
    for h in range(begin, min(end, 3)):
        do(h, range(3 - h, 7))
    low, high = max(begin, 3), min(end, side - 3)
    if low < high:
        lax.fori_loop(low, high, lambda h, _: do(h, range(7)), 0)
    for h in range(max(begin, side - 3), end):
        do(h, range(side + 3 - h))


def conv_rows(src, sums, taps, h, kys, t, lanes, side, base):
    pairs = side // 2

    def one(ky, acc):
        u, v, w = list(acc[:pairs]), list(acc[pairs : 2 * pairs + 1]), list(acc[2 * pairs + 1 :])
        row = h + ky - 3
        for out, shift, first, count, read in (
            (u, 0, 4, 3, lambda i: src[row, 2 * i, t, lanes]),
            (v, -1, 0, 4, lambda i: src[row, 2 * i + 1, t, lanes]),
            (w, 0, 7, 4, lambda i: sums[row, i, t, lanes]),
        ):
            x = [read(i) for i in range(pairs)]
            for j in range(count):
                tap = taps[ky * 11 + first + j, :, lanes]
                for k in range(len(out)):
                    i = k + shift - 1 + j
                    if 0 <= i < pairs:
                        out[k] = out[k] + x[i] * tap
        return tuple(u + v + w)

    acc = (jnp.zeros((8, 128), F32),) * (3 * pairs + 1)
    for ky in kys:
        acc = one(ky, acc)
    u, v, w = acc[:pairs], acc[pairs : 2 * pairs + 1], acc[2 * pairs + 1 :]
    out = []
    for k in range(pairs):
        out.append(base[2 * k] + (u[k] + v[k]))
        out.append(base[2 * k + 1] + (w[k] - (u[k] + v[k + 1])))
    return out


def fill_taps(small_ref, taps, flip):
    for ky in range(7):
        rows = []
        for kx in range(7):
            k = 48 - (ky * 7 + kx) if flip else ky * 7 + kx
            rows.append(small_ref[k : k + 1, :])
        rows = rows[0::2] + rows[1::2] + [rows[2 * j] + rows[2 * j + 1] for j in range(3)] + [rows[6]]
        for k, value in enumerate(rows):
            taps[ky * 11 + k] = jnp.broadcast_to(value, (8, D))


def add_columns(src, sums, row):
    pairs = sums.shape[1]
    sums[row] = jnp.stack([src[row, 2 * i] + src[row, 2 * i + 1] for i in range(pairs)])


def spread(scalars_ref, rows_ref):
    for i in range(rows_ref.shape[0]):
        rows_ref[i : i + 1, :] = jnp.full((1, rows_ref.shape[1]), scalars_ref[i], F32)


def select(row_ref, sel_ref):
    imgs, wide = row_ref.shape
    lane = lax.broadcasted_iota(jnp.int32, (imgs, wide), 1)
    for w in range(wide // imgs):
        sel_ref[w * imgs : (w + 1) * imgs, :] = (lane == row_ref[...] + w * imgs).astype(F32).astype(BF16)


def conv_kernel(begin, end, fresh, *refs):
    if fresh:
        small_hbm, img_hbm, partner_ref, weight_ref = refs[:4]
        mixed_hbm, unit_hbm, inv_hbm, norm_hbm, token_ref, small_ref, mixed_ref, taps, conv_ref, unit_ref, inv_ref, norm_ref, sem, pair_sums, img_ref, mix_ref, row_ref, sel_ref = refs[-18:]
    else:
        small_hbm, mixed_hbm = refs[:2]
        unit_hbm, inv_hbm, norm_hbm, token_ref, small_ref, mixed_ref, taps, conv_ref, unit_ref, inv_ref, norm_ref, sem, pair_sums = refs[-13:]
    side, _, imgs, _ = mixed_ref.shape
    low = max(begin - 3, 0)
    high = side if fresh else min(end + 3, side)
    rows = end - begin
    load = dma(small_hbm, small_ref, sem.at[4, 0])
    load.start()
    token_ref[...] = jnp.zeros(token_ref.shape, F32)

    def enter(h):
        if fresh:
            return dma(img_hbm.at[h], img_ref.at[h], sem.at[3, h])
        return dma(mixed_hbm.at[h], mixed_ref.at[h], sem.at[3, h])

    def store(h):
        return dma(mixed_ref.at[h], mixed_hbm.at[h], sem.at[5, h])

    for h in range(low, high):
        enter(h).start()
    if fresh:
        spread(weight_ref, mix_ref)
        for i in range(imgs):
            row_ref[i : i + 1, :] = jnp.full((1, row_ref.shape[1]), lax.rem(partner_ref[i], imgs), jnp.int32)
        select(row_ref, sel_ref)
    load.wait()
    fill_taps(small_ref, taps, False)
    if fresh:
        mix = mix_ref[...][None]
        rest = 1.0 - mix

        def blend(h, _):
            enter(h).wait()
            x = img_ref[h].reshape(side * imgs, D)
            other = jnp.dot(sel_ref[...], x, preferred_element_type=F32).reshape(side, imgs, D)
            mixed_ref[h] = mix * x.reshape(side, imgs, D).astype(F32) + rest * other
            add_columns(mixed_ref, pair_sums, h)
            store(h).start()
            return 0

        lax.fori_loop(0, side, blend, 0)
    else:
        for h in range(low, min(begin + 3, high)):
            enter(h).wait()
            add_columns(mixed_ref, pair_sums, h)

    def conv(h, kys):
        r = h - begin
        if not fresh:

            @pl.when(h + 3 < high)
            def _():
                enter(h + 3).wait()
                add_columns(mixed_ref, pair_sums, h + 3)

        def tile(k, _):
            at, lanes = tile_of(k, imgs)
            base = jnp.broadcast_to(small_ref[DEPTH_BIAS : DEPTH_BIAS + 1, lanes], (8, 128))
            acc = conv_rows(mixed_ref, pair_sums, taps, h, kys, at, lanes, side, [base] * side)
            for w in range(side):
                conv_ref[r, w, at, lanes] = acc[w]
            return 0

        return tiles(h, imgs, tile, begin == 0)

    every_row(begin, end, side, conv)
    gain = small_ref[GAIN_ONE : GAIN_ONE + 1, :][None]
    bias = small_ref[BIAS_ONE : BIAS_ONE + 1, :][None]

    def leave(r):
        return (
            dma(unit_ref.at[r], unit_hbm.at[r + begin], sem.at[0, r]),
            dma(inv_ref.at[r], inv_hbm.at[r + begin], sem.at[1, r]),
            dma(norm_ref.at[r], norm_hbm.at[r + begin], sem.at[2, r]),
        )

    def norm(r):
        unit, inv = norm_of(conv_ref[r])
        unit_ref[r] = unit.astype(BF16)
        inv_ref[r] = inv
        norm_ref[r] = (unit * gain + bias).astype(BF16)
        start(leave(r))

    def two(i, _):
        norm(2 * i)
        norm(2 * i + 1)
        return 0

    lax.fori_loop(0, rows // 2, two, 0)
    if rows % 2:
        norm(rows - 1)
    for r in range(rows):
        wait(leave(r))
    if fresh:
        for h in range(side):
            store(h).wait()


def conv_forward(small, inputs, begin, end, so_far=(), after=()):
    fresh = not so_far
    full = inputs[0].shape
    side = full[0]
    thin = full[:3] + (1,)
    rows = end - begin
    out = [far(full, BF16), far(thin, F32), far(full, BF16), near((8, 128), F32)]
    scratch = [
        pltpu.VMEM(small.shape, F32),
        pltpu.VMEM(full, F32),
        pltpu.VMEM((77, 8, D), F32),
        pltpu.VMEM((rows,) + full[1:], F32),
        pltpu.VMEM((rows,) + full[1:], BF16),
        pltpu.VMEM((rows,) + thin[1:], F32),
        pltpu.VMEM((rows,) + full[1:], BF16),
        pltpu.SemaphoreType.DMA((6, side)),
        pltpu.VMEM((side, side // 2) + full[2:], F32),
    ]
    specs = [HBM] * 2
    if fresh:
        out = [far(full, F32)] + out
        wide = side * full[2]
        scratch += [pltpu.VMEM(full, BF16), pltpu.VMEM((full[2], D), F32), pltpu.VMEM((full[2], wide), jnp.int32), pltpu.VMEM((wide, wide), BF16)]
        specs = [HBM] * 2 + [SMEM] * 2
    return kernel_call(
        functools.partial(conv_kernel, begin, end, fresh),
        out,
        specs + [HBM] * len(so_far),
        scratch,
        (small,) + tuple(inputs) + tuple(so_far),
        after,
        21 * rows / side + 3 * fresh,
        36,
        {2 + k: k for k in range(len(so_far))},
    )


def home(me, order, j, chips):
    if order is None:
        return j % HALF_PIECES if chips else j
    device = me
    for k, bit in enumerate(order):
        device = device ^ (((j >> k) & 1) * bit)
    return device >> 1 if chips else device


def keep_rows(mask_ref, keep_ref):
    for i in range(keep_ref.shape[0]):
        keep_ref[i : i + 1, :] = jnp.full((1, D), mask_ref[i], jnp.int32).astype(F32) / (1.0 - DROP_RATE)


def assembly(me, order, chips, first, src_hbm, whole_ref, sem):
    deep = src_hbm.shape[0] // HALF_PIECES

    def copy(j, _):
        to = pl.ds(pl.multiple_of(home(me, order, first + j, chips) * deep, 16), deep)
        dma(src_hbm.at[pl.ds(pl.multiple_of(j * deep, 16), deep), :], whole_ref.at[to, :], sem).start()
        return 0

    lax.fori_loop(0, HALF_PIECES, copy, 0)
    return dma(src_hbm, whole_ref.at[pl.ds(0, src_hbm.shape[0]), :], sem)


def deal(me, order, chips, first, out_ref, read):
    deep = out_ref.shape[0] // HALF_PIECES

    def move(j, _):
        begin = pl.multiple_of(home(me, order, first + j, chips) * deep, 16)
        to = pl.ds(pl.multiple_of(j * deep, 16), deep)
        for g in range(out_ref.shape[1] // 128):
            out_ref[to, g * 128 : (g + 1) * 128] = read(pl.ds(begin, deep), g).astype(BF16)
        return 0

    lax.fori_loop(0, HALF_PIECES, move, 0)


def even_first(rows, deep):
    blocks = [rows[d * deep // D][:, d * deep % D : d * deep % D + deep] for d in range(FF // deep)]
    return jnp.concatenate(blocks[0::2] + blocks[1::2], axis=1)


def even_last(even, odd, k, deep):
    per = D // deep
    blocks = []
    for d in range(per * k, per * k + per):
        source = odd if d % 2 else even
        blocks.append(source[:, d // 2 * deep : d // 2 * deep + deep])
    return jnp.concatenate(blocks, axis=1)


def block_kernel(block, masks, me_ref, norm_hbm, mixed_hbm, pnear_hbm, pfar_hbm, wnear_hbm, wfar_hbm, dy_hbm, small_hbm, mask_ref, *rest):
    act_hbm, dg_hbm, gnear_ref, gfar_ref, gdb_ref, out_ref, bb_hbm, sums_ref, res_hbm = rest[-32:-23]
    pair_ref, small_ref, keep_ref, norm_ref, mixed_ref, act_ref, dg_ref, branch_ref, unit_ref, inv_ref, out2_ref = rest[-23:-12]
    wd_ref, dy_ref, bb_ref, res_ref, acc, wide, wk, isem, osem, wsem, bsem, rsem = rest[-12:]
    rows = norm_hbm.shape[0]
    steps = rows // block
    imgs = keep_ref.shape[0]
    shape = (block // imgs, imgs, D)
    half = dy_hbm.shape[0]

    def spot(i):
        return pl.ds(pl.multiple_of(i * block, block), block)

    def enter(i):
        s = i % 2
        return (
            dma(norm_hbm.at[spot(i), :], norm_ref.at[s], isem.at[0, s]),
            dma(mixed_hbm.at[spot(i), :], mixed_ref.at[s], isem.at[1, s]),
        )

    def leave(i):
        s = i % 2
        pairs = ((act_ref, act_hbm), (dg_ref, dg_hbm))
        return [dma(a.at[s], b.at[spot(i), :], osem.at[k, s]) for k, (a, b) in enumerate(pairs)]

    me = me_ref[0]
    p_masks, w_masks, d_masks = masks
    load = dma(small_hbm, small_ref, wsem.at[0])
    start(enter(0))
    load.start()
    half_rows = FF // 2
    mine = 0 if p_masks is None else me % 2
    pair_in = []
    for src, first, which in ((pnear_hbm, 0, mine), (pfar_hbm, HALF_PIECES, 1 - mine)):
        to = pair_ref.at[pl.ds(pl.multiple_of(which * half_rows, half_rows), half_rows), :]
        pair_in.append(assembly(me, p_masks, True, first, src, to, wsem.at[1]))
    dy_in = dma(dy_hbm, dy_ref, wsem.at[3])
    wait(pair_in)
    down_in = [
        assembly(me, w_masks, False, first, src, wd_ref, wsem.at[2]) for first, src in ((0, wnear_hbm), (HALF_PIECES, wfar_hbm))
    ]
    dy_in.start()
    load.wait()
    keep_rows(mask_ref, keep_ref)
    keep = keep_ref[...][None]
    scale = keep * small_ref[LAYER_SCALE : LAYER_SCALE + 1, :][None]
    gain = small_ref[GAIN_TWO : GAIN_TWO + 1, :][None]
    bias = small_ref[BIAS_TWO : BIAS_TWO + 1, :][None]
    bias_rows = [small_ref[HIDDEN_BIAS + k : HIDDEN_BIAS + k + 1, :] for k in range(FF // D)]
    hidden_bias = jnp.concatenate(bias_rows, axis=1) if p_masks is None else even_first(bias_rows, FF >> len(p_masks))
    chunk = FF // 2

    def body(i, _):
        s = i % 2

        @pl.when(i + 1 < steps)
        def _():
            start(enter(i + 1))

        @pl.when(i >= 2)
        def _():
            wait(leave(i - 2))

        wait(enter(i))
        x = norm_ref[s]
        branch = jnp.broadcast_to(small_ref[OUT_BIAS : OUT_BIAS + 1, :], (block, D))

        def hidden(j):
            cols = slice(j * chunk, (j + 1) * chunk)
            return lax.dot_general(x, pair_ref[cols, :D], COLS, preferred_element_type=F32) + hidden_bias[:, cols]

        pre = hidden(0)
        for j in range(FF // chunk):
            after = hidden(j + 1) if j + 1 < FF // chunk else None
            cols = slice(j * chunk, (j + 1) * chunk)
            phi = 0.5 + 0.5 * lax.erf(pre * 0.7071067811865476)
            bell = jnp.exp2(pre * pre * -0.7213475204444817) * 0.3989422804014327
            act = (pre * phi).astype(BF16)
            act_ref[s, :, cols] = act
            dg_ref[s, :, cols] = (phi + pre * bell).astype(BF16)
            branch = branch + jnp.dot(act, pair_ref[cols, D:], preferred_element_type=F32)
            pre = after
        start(leave(i))
        split = branch_ref.shape[1:]
        branch_ref[i] = branch.astype(BF16).reshape(split)
        unit, inv = norm_of(mixed_ref[s].reshape(shape) + scale * branch.reshape(shape))
        unit_ref[i] = unit.astype(BF16).reshape(split)
        inv_ref[i] = inv.reshape(split[:-1] + (1,))
        out2_ref[i] = (unit * gain + bias).astype(BF16).reshape(split)
        return 0

    lax.fori_loop(0, steps, body, 0)

    wait(down_in)
    for g in range(6):
        wide[g] = wd_ref[:, pl.ds(g * 128, 128)].astype(F32)
        for k in range(4):
            wk[k // 2, pl.ds(k % 2 * D, D), pl.ds(g * 128, 128)] = wide[g, pl.ds(k, D, stride=4), :].astype(BF16)
    sums_ref[...] = jnp.zeros(sums_ref.shape, F32)
    rows = half * half * imgs
    shape = (half * half, imgs, D)
    for k in range(2):
        acc[:, k * D : (k + 1) * D] = jnp.broadcast_to(small_ref[DOWN_BIAS + k : DOWN_BIAS + k + 1, :], (rows, D))
    dy_in.wait()
    gdb_ref[...] = jnp.sum(dy_ref[...].astype(F32).reshape(half * half, imgs, 2 * D), axis=0)

    def give(k):
        pairs = ((bb_ref, bb_hbm), (res_ref, res_hbm))
        return [dma(a.at[k], b.at[:, k // 2, :, k % 2], rsem.at[j, k]) for j, (a, b) in enumerate(pairs)]

    for a in range(2):
        dy = dy_ref[...].reshape(rows, 2 * D)
        x = jnp.concatenate([out2_ref[:, a, :, b].reshape(rows, D) for b in range(2)], axis=1)
        both = lax.dot_general(dy, wk[a], COLS, preferred_element_type=F32)
        acc[...] += jnp.dot(x, wk[a], preferred_element_type=F32)
        gd = lax.dot_general(x, dy, ROWS, preferred_element_type=F32)
        for b in range(2):
            k = 2 * a + b
            for g in range(6):
                wide[g, pl.ds(k, D, stride=4), :] = gd[b * D : (b + 1) * D, g * 128 : (g + 1) * 128]
            back = both[:, b * D : (b + 1) * D].reshape(shape)
            unit = unit_ref[:, a, :, b].reshape(shape).astype(F32)
            sums_ref[0] += jnp.sum(back * unit, axis=0)
            sums_ref[1] += jnp.sum(back, axis=0)
            res = norm_back(back, unit, inv_ref[:, a, :, b].reshape(half * half, imgs, 1), gain)
            res_ref[k] = res.astype(BF16).reshape(half, half, imgs, D)
            sums_ref[2] += jnp.sum(res * keep * branch_ref[:, a, :, b].reshape(shape).astype(F32), axis=0)
            bb = (res * scale).astype(BF16)
            bb_ref[k] = bb.reshape(half, half, imgs, D)
            start(give(k))
            sums_ref[3] += jnp.sum(bb.astype(F32), axis=0)

    out_ref[...] = acc[...].astype(BF16).reshape(out_ref.shape)
    deal(me, d_masks, False, 0, gnear_ref, lambda at, g: wide[g, at, :])
    deal(me, d_masks, False, HALF_PIECES, gfar_ref, lambda at, g: wide[g, at, :])
    for k in range(4):
        wait(give(k))
    for i in range(max(steps - 2, 0), steps):
        wait(leave(i))


def block_both(masks, me, norm, mixed, pair, down, dy, small, mask, after=(), block=448):
    rows = norm.shape[0]
    half, _, imgs, _ = dy.shape
    area = half * half * imgs
    six = (half, 2, half, 2, imgs)
    two = lambda width, dtype: pltpu.VMEM((2, block, width), dtype)
    whole = lambda width, dtype: pltpu.VMEM(six + (width,), dtype)
    part = pltpu.VMEM((4, half, half, imgs, D), BF16)
    return kernel_call(
        functools.partial(block_kernel, block, masks),
        [far((rows, FF), BF16)] * 2
        + [near((2 * D, 2 * D), BF16)] * 2
        + [near((imgs, 2 * D), F32), near((half, half, imgs, 2 * D), BF16)]
        + [far(six + (D,), BF16), near((4, imgs, D), F32), far(six + (D,), BF16)],
        [SMEM] + [HBM] * 2 + [ANY, HBM] * 2 + [HBM] * 2 + [SMEM],
        [pltpu.VMEM((FF, 2 * D), BF16), pltpu.VMEM(small.shape, F32), pltpu.VMEM((imgs, D), F32)]
        + [two(D, BF16), two(D, F32), two(FF, BF16), two(FF, BF16)]
        + [whole(D, BF16), whole(D, BF16), whole(1, F32), whole(D, BF16)]
        + [pltpu.VMEM((4 * D, 2 * D), BF16), pltpu.VMEM(dy.shape, BF16), part, part]
        + [pltpu.VMEM((area, 2 * D), F32), pltpu.VMEM((6, 4 * D, 128), F32), pltpu.VMEM((2, 2 * D, 2 * D), BF16)]
        + [pltpu.SemaphoreType.DMA((2, 2)), pltpu.SemaphoreType.DMA((2, 2)), pltpu.SemaphoreType.DMA((4,))]
        + [pltpu.SemaphoreType.DMA((1,)), pltpu.SemaphoreType.DMA((2, 4))],
        (me, norm, mixed, *pair, *down, dy, small, mask),
        after,
        34,
        58,
    )


def pair_grad_kernel(block, first, masks, me_ref, bb_hbm, act_hbm, dg_hbm, norm_hbm, pair_hbm, *rest):
    g_ref, hb_ref, p_hbm, pair_ref, acc, turned, bb_ref, act_ref, dg_ref, norm_ref, p_ref, sem, osem, wsem = rest[-14:]
    rows = bb_hbm.shape[0]
    imgs = hb_ref.shape[0]
    steps = rows // block
    wide = FF // 2
    me = me_ref[0]
    which = 0 if masks is None else me % 2
    which = 1 - which if first else which
    lanes = pl.ds(pl.multiple_of(which * wide, wide), wide)

    def spot(i):
        return pl.ds(pl.multiple_of(i * block, block), block)

    def enter(i):
        s = i % 2
        return (
            dma(bb_hbm.at[spot(i), :], bb_ref.at[s], sem.at[0, s]),
            dma(dg_hbm.at[spot(i), lanes], dg_ref.at[s], sem.at[1, s]),
            dma(act_hbm.at[spot(i), lanes], act_ref.at[s], sem.at[2, s]),
            dma(norm_hbm.at[spot(i), :], norm_ref.at[s], sem.at[3, s]),
        )

    def leave(i):
        return dma(p_ref.at[i % 2], p_hbm.at[spot(i), :], osem.at[i % 2])

    pair_in = [assembly(me, masks, True, first, pair_hbm, pair_ref, wsem.at[0])]
    start(enter(0))
    hb_ref[...] = jnp.zeros(hb_ref.shape, F32)
    acc[...] = jnp.zeros(acc.shape, F32)
    wait(pair_in)

    def body(i, _):
        s = i % 2

        @pl.when(i + 1 < steps)
        def _():
            start(enter(i + 1))

        @pl.when(i >= 2)
        def _():
            leave(i - 2).wait()

        wait(enter(i))
        b = bb_ref[s]
        back = lax.dot_general(b, pair_ref[:, D:], COLS, preferred_element_type=F32)
        acc[D:, :] += lax.dot_general(b, act_ref[s], ROWS, preferred_element_type=F32)
        p = (back * dg_ref[s].astype(F32)).astype(BF16)
        p_ref[s] = p
        hb_ref[...] += jnp.sum(p.astype(F32).reshape(block // imgs, imgs, wide), axis=0)
        acc[:D, :] += lax.dot_general(norm_ref[s], p, ROWS, preferred_element_type=F32)
        leave(i).start()
        return 0

    lax.fori_loop(0, steps, body, 0)
    turned[...] = acc[...].T
    deal(me, masks, True, first, g_ref, lambda at, g: turned[at, pl.ds(g * 128, 128)])
    for i in range(max(steps - 2, 0), steps):
        leave(i).wait()


def pair_grad(first, masks, me, bb, act, dg, norm, pair, imgs, after=(), block=784):
    rows = bb.shape[0]
    wide = FF // 2
    two = lambda width: pltpu.VMEM((2, block, width), BF16)
    return kernel_call(
        functools.partial(pair_grad_kernel, block, first, masks),
        [near((wide, 2 * D), BF16), near((imgs, wide), F32), far((rows, wide), BF16)],
        [SMEM] + [HBM] * 5,
        [pltpu.VMEM((wide, 2 * D), BF16), pltpu.VMEM((2 * D, wide), F32), pltpu.VMEM((wide, 2 * D), F32)]
        + [two(D), two(wide), two(wide), two(D), two(wide)]
        + [pltpu.SemaphoreType.DMA((4, 2)), pltpu.SemaphoreType.DMA((2,)), pltpu.SemaphoreType.DMA((1,))],
        (me, bb, act, dg, norm, pair),
        after,
        13,
        44,
    )


def back_one_kernel(block, masks, me_ref, pnear_hbm, pfar_hbm, unit_hbm, inv_hbm, near_hbm, far_hbm, small_hbm, *rest):
    conv_hbm, sums_ref, near_ref, far_ref, small_ref, pnear_ref, pfar_ref, unit_ref, inv_ref, conv_ref, sem, wsem = rest[-12:]
    rows = pnear_hbm.shape[0]
    imgs = sums_ref.shape[1]
    steps = rows // block
    shape = (block // imgs, imgs, D)

    def spot(i):
        return pl.ds(pl.multiple_of(i * block, block), block)

    def enter(i):
        s = i % 2
        pairs = ((pnear_hbm, pnear_ref), (pfar_hbm, pfar_ref), (unit_hbm, unit_ref), (inv_hbm, inv_ref))
        return [dma(a.at[spot(i), :], b.at[s], sem.at[k, s]) for k, (a, b) in enumerate(pairs)]

    def leave(i):
        return dma(conv_ref.at[i % 2], conv_hbm.at[spot(i), :], sem.at[4, i % 2])

    load = dma(small_hbm, small_ref, wsem.at[0])
    left = pl.ds(0, D)
    pair_in = [
        assembly(me_ref[0], masks, True, first, src.at[:, left], dst, wsem.at[1])
        for first, src, dst in ((0, near_hbm, near_ref), (HALF_PIECES, far_hbm, far_ref))
    ]
    start(enter(0))
    load.start()
    sums_ref[...] = jnp.zeros(sums_ref.shape, F32)
    wait(pair_in)
    load.wait()
    gain = small_ref[GAIN_ONE : GAIN_ONE + 1, :][None]

    def body(i, _):
        s = i % 2

        @pl.when(i + 1 < steps)
        def _():
            start(enter(i + 1))

        @pl.when(i >= 2)
        def _():
            leave(i - 2).wait()

        wait(enter(i))
        back = jnp.dot(pnear_ref[s], near_ref[...], preferred_element_type=F32)
        back = (back + jnp.dot(pfar_ref[s], far_ref[...], preferred_element_type=F32)).reshape(shape)
        unit = unit_ref[s].reshape(shape).astype(F32)
        sums_ref[0] += jnp.sum(back * unit, axis=0)
        sums_ref[1] += jnp.sum(back, axis=0)
        out = norm_back(back, unit, inv_ref[s].reshape(shape[:2] + (1,)), gain)
        sums_ref[2] += jnp.sum(out, axis=0)
        conv_ref[s] = out.astype(BF16).reshape(block, D)
        leave(i).start()
        return 0

    lax.fori_loop(0, steps, body, 0)
    for i in range(max(steps - 2, 0), steps):
        leave(i).wait()


def back_one(masks, me, p, unit, inv, pair, small, imgs, after=(), block=784):
    rows = unit.shape[0]
    wide = FF // 2
    two = lambda width, dtype: pltpu.VMEM((2, block, width), dtype)
    return kernel_call(
        functools.partial(back_one_kernel, block, masks),
        [far((rows, D), BF16), near((3, imgs, D), F32)],
        [SMEM] + [HBM] * 7,
        [pltpu.VMEM((wide, D), BF16)] * 2
        + [pltpu.VMEM(small.shape, F32)]
        + [two(wide, BF16), two(wide, BF16), two(D, BF16), two(1, F32), two(D, BF16)]
        + [pltpu.SemaphoreType.DMA((5, 2)), pltpu.SemaphoreType.DMA((2,))],
        (me, *p, unit, inv, *pair, small),
        after,
        11,
        32,
    )


def taps_kernel(groups, conv_hbm, mixed_hbm, *rest):
    g_ref, conv_ref, mixed_ref, sums, even, odd, last, sem = rest[-8:]
    side, _, imgs, _ = conv_hbm.shape
    pairs = side // 2

    def enter(k):
        lanes = pl.ds(pl.multiple_of((k + groups[0]) * 128, 128), 128)
        return (
            dma(mixed_hbm.at[:, :, :, lanes], mixed_ref.at[k], sem.at[0, k]),
            dma(conv_hbm.at[:, :, :, lanes], conv_ref.at[k], sem.at[1, k]),
        )

    for k in range(len(groups)):
        start(enter(k))
    def group(k, _):
        wait(enter(k))

        def prepare(h, _):
            x = [mixed_ref[k, h, w] for w in range(side)]
            d = [conv_ref[k, h, w].astype(F32) for w in range(side)]
            for i in range(pairs):
                sums[h, i] = x[2 * i] + x[2 * i + 1]
                last[h, i] = d[2 * i + 1]
                even[h, i] = d[2 * i] - d[2 * i + 1]
                odd[h, i + 1] = (d[2 * i + 2] if i + 1 < pairs else jnp.zeros_like(d[0])) - d[2 * i + 1]
            odd[h, 0] = d[0]
            return 0

        lax.fori_loop(0, side, prepare, 0)
        for ky in range(7):
            first = max(3 - ky, 0)
            count = min(side, side + 3 - ky) - first

            def row(h, acc):
                acc = list(acc)
                for t in range(imgs // 8):
                    at = pl.ds(t * 8, 8)
                    for begin, shift, taps, length, read_x, read_d in (
                        (4, 0, 3, pairs, lambda i: mixed_ref[k, h + ky - 3, 2 * i, at], lambda i: even[h, i, at]),
                        (0, -1, 4, pairs + 1, lambda i: mixed_ref[k, h + ky - 3, 2 * i + 1, at], lambda i: odd[h, i, at]),
                        (7, 0, 4, pairs, lambda i: sums[h + ky - 3, i, at], lambda i: last[h, i, at]),
                    ):
                        x = [read_x(i) for i in range(pairs)]
                        for a in range(length):
                            d = read_d(a)
                            for j in range(taps):
                                i = a + shift - 1 + j
                                if 0 <= i < pairs:
                                    acc[begin + j] = acc[begin + j] + x[i] * d
                return tuple(acc)

            acc = lax.fori_loop(
                0, count // 2, lambda r, acc: row(first + 2 * r + 1, row(first + 2 * r, acc)), (jnp.zeros((8, 128), F32),) * 11
            )
            if count % 2:
                acc = row(first + count - 1, acc)
            even_taps = [acc[j] + acc[7 + j] for j in range(4)]
            odd_taps = [acc[4 + j] + acc[7 + j] for j in range(3)]
            for kx in range(7):
                value = odd_taps[kx // 2] if kx % 2 else even_taps[kx // 2]
                g_ref[ky * 7 + kx, :, pl.ds(pl.multiple_of(k * 128, 128), 128)] = value
        return 0

    lax.fori_loop(0, len(groups), group, 0)


def taps_grad(conv, mixed, groups, after=()):
    side, _, imgs, _ = conv.shape
    lanes = lambda dtype: pltpu.VMEM((len(groups),) + conv.shape[:3] + (128,), dtype)
    part = lambda columns: pltpu.VMEM((side, columns, imgs, 128), F32)
    return kernel_call(
        functools.partial(taps_kernel, groups),
        [near((49, 8, 128 * len(groups)), F32)],
        [HBM] * 2,
        [lanes(BF16), lanes(F32), part(side // 2), part(side // 2), part(side // 2 + 1), part(side // 2), pltpu.SemaphoreType.DMA((2, len(groups)))],
        (conv, mixed),
        after,
        4.7 * len(groups),
        28,
    )[0]


def images_kernel(begin, end, conv_hbm, small_hbm, partner_ref, weight_ref, res_hbm, *rest):
    g_hbm, token_ref, small_ref, raw_ref, conv_ref, taps, res_ref, out_ref, mix_ref, row_ref, sel_ref, rest_ref, sem, csem, pair_sums, rsem = rest[-16:]
    side, _, imgs, _ = conv_hbm.shape
    low = max(begin - 3, 0)
    high = min(end + 3, side)
    load = dma(small_hbm, small_ref, csem.at[side])
    load.start()
    token_ref[...] = jnp.zeros(token_ref.shape, F32)

    def bring(h):
        return dma(conv_hbm.at[h], raw_ref.at[h], csem.at[h])

    def widen(h):
        bring(h).wait()
        conv_ref[h] = raw_ref[h].astype(F32)
        add_columns(conv_ref, pair_sums, h)

    def enter(h):
        return dma(res_hbm.at[h], res_ref.at[h - begin], rsem.at[h - begin])

    def leave(h):
        return dma(out_ref.at[h - begin], g_hbm.at[h], sem.at[1, 0])

    for h in range(low, high):
        bring(h).start()
        if h == min(begin + 3, high - 1):
            for r in range(begin, end):
                enter(r).start()
    spread(weight_ref, mix_ref)
    for i in range(imgs):
        row_ref[pl.ds(lax.rem(partner_ref[i], imgs), 1), :] = jnp.full((1, row_ref.shape[1]), i, jnp.int32)
    select(row_ref, sel_ref)
    load.wait()
    fill_taps(small_ref, taps, True)
    mix = mix_ref[...][None]
    others = 1.0 - mix
    for h in range(low, min(begin + 3, high)):
        widen(h)

    def row(h, kys):
        @pl.when(h + 3 < high)
        def _():
            widen(h + 3)

        enter(h).wait()
        rest_ref[...] = res_ref[h - begin].astype(F32)

        def tile(k, _):
            at, lanes = tile_of(k, imgs)
            base = [rest_ref[w, at, lanes] for w in range(side)]
            acc = conv_rows(conv_ref, pair_sums, taps, h, kys, at, lanes, side, base)
            for w in range(side):
                out_ref[h - begin, w, at, lanes] = acc[w]
            return 0

        return tiles(h, imgs, tile, False)

    every_row(begin, end, side, row)

    def unmix(r):
        v = out_ref[r]
        part = (others * v).reshape(side * imgs, D)
        upper = part.astype(BF16)
        lower = (part - upper.astype(F32)).astype(BF16)
        back = jnp.dot(sel_ref[...], upper, preferred_element_type=F32)
        back = back + jnp.dot(sel_ref[...], lower, preferred_element_type=F32)
        out_ref[r] = mix * v + back.reshape(side, imgs, D)
        leave(begin + r).start()

    def two(i, _):
        unmix(2 * i)
        unmix(2 * i + 1)
        return 0

    lax.fori_loop(0, (end - begin) // 2, two, 0)
    for h in range(begin, end):
        leave(h).wait()


def images_back(conv, small, partner, weight, res, begin, end, so_far=(), after=()):
    side, _, imgs, _ = conv.shape
    return kernel_call(
        functools.partial(images_kernel, begin, end),
        [far(conv.shape, F32), near((8, 128), F32)],
        [HBM, HBM, SMEM, SMEM, HBM] + [HBM] * len(so_far),
        [
            pltpu.VMEM(small.shape, F32),
            pltpu.VMEM(conv.shape, BF16),
            pltpu.VMEM(conv.shape, F32),
            pltpu.VMEM((77, 8, D), F32),
            pltpu.VMEM((end - begin, side, imgs, D), BF16),
            pltpu.VMEM((end - begin, side, imgs, D), F32),
            pltpu.VMEM((imgs, D), F32),
            pltpu.VMEM((imgs, side * imgs), jnp.int32),
            pltpu.VMEM((side * imgs, side * imgs), BF16),
            pltpu.VMEM((side, imgs, D), F32),
            pltpu.SemaphoreType.DMA((2, 2)),
            pltpu.SemaphoreType.DMA((side + 1,)),
            pltpu.VMEM((side, side // 2, imgs, D), F32),
            pltpu.SemaphoreType.DMA((end - begin,)),
        ],
        (conv, small, partner, weight, res) + tuple(so_far),
        after,
        22 * (end - begin) / side,
        28,
        {5: 0} if so_far else {},
    )


def ready_kernel(in_hbm, out_hbm, down_hbm, *rest):
    pair_ref, low_ref, in_ref, out_ref, down_ref, sem = rest[-6:]
    pairs = ((in_hbm, in_ref), (out_hbm, out_ref), (down_hbm, down_ref))
    copies = [dma(a, b, sem.at[k]) for k, (a, b) in enumerate(pairs)]
    start(copies)
    wait(copies)
    pair_ref[0, :, :D] = in_ref[...].astype(BF16)
    pair_ref[0, :, D:] = out_ref[...].astype(BF16)
    low_ref[0] = down_ref[...].astype(BF16)


def ready(weight_in, weight_out, weight_down, after=()):
    deep = weight_in.shape[0]
    return kernel_call(
        ready_kernel,
        [near((1, deep, 2 * D), BF16)] * 2,
        [HBM] * 3,
        [pltpu.VMEM(x.shape, F32) for x in (weight_in, weight_out, weight_down)] + [pltpu.SemaphoreType.DMA((3,))],
        (weight_in, weight_out, weight_down),
        after,
        0.5,
        8,
    )


def join_kernel(first_ref, second_ref, *rest):
    out_ref = rest[-1]
    k = first_ref.shape[0]
    out_ref[:k] = first_ref[...]
    out_ref[k:] = second_ref[...]


def join(first, second, after=()):
    return kernel_call(
        join_kernel,
        [near((2 * first.shape[0],) + first.shape[1:], first.dtype)],
        [VMEM] * 2,
        [],
        (first, second),
        after,
        0.5,
        8,
    )[0]


def fold_kernel(count, *refs):
    ins, (stay_ref, leave_ref) = refs[: 2 * count], refs[-2:]
    k = stay_ref.shape[0] // count
    for i in range(count):
        keep_ref, come_ref = ins[2 * i], ins[2 * i + 1]
        stay_ref[i * k : (i + 1) * k] = keep_ref[:k].astype(F32) + come_ref[:k].astype(F32)
        leave_ref[i * k : (i + 1) * k] = (keep_ref[k:].astype(F32) + come_ref[k:].astype(F32)).astype(BF16)


def fold(*arrays, after=()):
    slots, deep, wide = arrays[0].shape
    count = len(arrays) // 2
    return kernel_call(
        functools.partial(fold_kernel, count),
        [near((count * slots // 2, deep, wide), F32), near((count * slots // 2, deep, wide), BF16)],
        [VMEM] * len(arrays),
        [],
        arrays,
        after,
        0.5,
        12,
    )


def part_kernel(*refs):
    ins, outs = refs[:4], refs[-4:]
    for i in range(2):
        keep_ref, come_ref = ins[2 * i], ins[2 * i + 1]
        for slot, out_ref in enumerate(outs):
            out_ref[i] = (keep_ref[slot].astype(F32) + come_ref[slot].astype(F32)).astype(out_ref.dtype)


def part(p_keep, p_come, d_keep, d_come, after=()):
    shape = (2,) + p_keep.shape[1:]
    return kernel_call(
        part_kernel,
        [near(shape, F32)] + [near(shape, BF16)] * 3,
        [VMEM] * 4,
        [],
        (p_keep, p_come, d_keep, d_come),
        after,
        0.5,
        12,
    )


def small_kernel(hops, me_ref, gk_ref, sums1_ref, sums2_ref, near_ref, far_ref, db_ref, keep_ref, *rest):
    sum_ref, send_ref, total = rest[-3:]
    grads = keep_ref[...]
    for come_ref in rest[:-3]:
        grads = grads + come_ref[...].astype(F32)
    sum_ref[...] = grads
    rows = lambda x: jnp.sum(x, axis=0, keepdims=True)
    for t in range(49):
        total[t : t + 1, :] = rows(gk_ref[t])
    for row, value in (
        (DEPTH_BIAS, sums1_ref[2]),
        (GAIN_ONE, sums1_ref[0]),
        (BIAS_ONE, sums1_ref[1]),
        (OUT_BIAS, sums2_ref[3]),
        (LAYER_SCALE, sums2_ref[2]),
        (GAIN_TWO, sums2_ref[0]),
        (BIAS_TWO, sums2_ref[1]),
    ):
        total[row : row + 1, :] = rows(value)
    mine, other = rows(near_ref[...]), rows(far_ref[...])
    if hops:
        odd_device = (me_ref[0] % 2).astype(F32)
        even = mine * (1.0 - odd_device) + other * odd_device
        odd = other * (1.0 - odd_device) + mine * odd_device
    for k in range(4):
        if hops:
            value = even_last(even, odd, k, FF // hops)
        else:
            value = (mine, other)[k // 2][:, k % 2 * D : k % 2 * D + D]
        total[HIDDEN_BIAS + k : HIDDEN_BIAS + k + 1, :] = value
    for k in range(2):
        total[DOWN_BIAS + k : DOWN_BIAS + k + 1, :] = rows(db_ref[:, k * D : (k + 1) * D])
    square = jnp.full((1, D), jnp.sum(grads * grads), F32)
    upper = square.astype(BF16).astype(F32)
    total[SQUARES : SQUARES + 1, :] = upper
    total[SQUARES + 1 : SQUARES + 2, :] = square - upper
    send_ref[...] = total[...].astype(BF16)


def small_total(hops, me, gk, sums1, sums2, near_hb, far_hb, db, keep, *come):
    return kernel_call(
        functools.partial(small_kernel, hops),
        [near(keep.shape, F32), near((SQUARES + 2, D), BF16)],
        [SMEM] + [VMEM] * (7 + len(come)),
        [pltpu.VMEM((SQUARES + 2, D), F32)],
        (me, gk, sums1, sums2, near_hb, far_hb, db, keep, *come),
        (),
        1,
        8,
    )


def meet_kernel(*refs):
    arrays, out_ref = refs[:-1], refs[-1]
    sums = [x[...].astype(F32) for x in arrays]
    while len(sums) > 1:
        sums = [a + b for a, b in zip(sums[::2], sums[1::2])]
    total = sums[0]
    square = total[SQUARES : SQUARES + 1] + total[SQUARES + 1 : SQUARES + 2]
    upper = square.astype(BF16).astype(F32)
    out_ref[...] = total.astype(out_ref.dtype)
    out_ref[SQUARES : SQUARES + 2, :] = jnp.concatenate([upper, square - upper], axis=0).astype(out_ref.dtype)


def meet(arrays, dtype):
    return kernel_call(meet_kernel, [near(arrays[0].shape, dtype)], [VMEM] * len(arrays), [], arrays, (), 0.3, 8)[0]


def adam(weight, first, second, grad, rate, decay):
    first = BETA_ONE * first + (1.0 - BETA_ONE) * grad
    second = BETA_TWO * second + (1.0 - BETA_TWO) * grad * grad
    first_hat = first / (1.0 - BETA_ONE**STEP)
    second_hat = second / (1.0 - BETA_TWO**STEP)
    weight = weight - rate * (first_hat / (jnp.sqrt(second_hat) + ADAM_EPS) + decay * weight)
    return first, second, weight


def adam_kernel(total_ref, grads_ref, *refs):
    ins, outs = refs[:9], refs[9:18]
    norm_ref = refs[18]
    gs = total_ref[:SQUARES]
    norm = jnp.sqrt(jnp.sum(gs * gs) + jnp.sum(total_ref[SQUARES : SQUARES + 2, 0:1]))
    norm_ref[0, 0] = norm
    factor = CLIP_NORM / jnp.maximum(norm, CLIP_NORM)
    grads = (grads_ref[0, :, :D], grads_ref[0, :, D:], grads_ref[1])
    rates = (LAYER_DECAY * RATE_MATRIX, LAYER_DECAY * RATE_MATRIX, RATE_MATRIX)
    for k in range(3):
        new = adam(ins[3 * k][...], ins[3 * k + 1][...], ins[3 * k + 2][...], grads[k] * factor, rates[k], WEIGHT_DECAY)
        for out_ref, value in zip(outs[3 * k : 3 * k + 3], new):
            out_ref[...] = value


def adam_all(total, grads, states):
    return pl.pallas_call(
        adam_kernel,
        out_shape=tuple(near(x.shape, F32) for x in states) + (near((1, 1), F32),),
        in_specs=[VMEM] * 11,
        out_specs=(VMEM,) * 9 + (SMEM,),
        cost_estimate=pl.CostEstimate(flops=int(2e9), bytes_accessed=0, transcendentals=0),
        compiler_params=pltpu.CompilerParams(vmem_limit_bytes=12 << 20),
    )(total, grads, *states)


def swap(x, bit, n):
    return lax.ppermute(x, "dp", [(i, i ^ bit) for i in range(n)])


def is_set(bit):
    return (lax.axis_index("dp") & bit) != 0


def gather_natural(shard, n, order, gates=None):
    have = shard
    met = []
    for hop, bit in enumerate(order):
        if gates and hop in gates:
            have, _ = lax.optimization_barrier((have, gates[hop]))
        other = swap(have, bit, n)
        axis = sum(1 for b in met if b > bit)
        mine = is_set(bit)
        have = jnp.stack([jnp.where(mine, other, have), jnp.where(mine, have, other)], axis=axis)
        met.append(bit)
    return have.reshape((n,) + shard.shape)


def local(n, images, mix_weight, partner, keep_mask, cotangent, weight_in, weight_out, weight_down, small_params,
          first_in, second_in, first_out, second_out, first_down, second_down, first_small, second_small):
    imgs, side = images.shape[:2]
    half = side // 2
    pixels = side * side * imgs
    me = lax.axis_index("dp")
    bits = [1 << k for k in range(n.bit_length() - 1)]
    deep = FF // n
    by_hops = n == 32

    pair, down = ready(weight_in, weight_out, weight_down)
    mine = me[None].astype(jnp.int32)
    p_masks = w_masks = d_masks = None
    if by_hops:
        p_order = [16, 8, 4, 2, 1]
        w_order = [16, 8, 2, 4, 1]
        d_order = p_order
        p_masks, w_masks, d_masks = p_order, w_order, d_order

    img = images.transpose(1, 2, 0, 3)
    dy = cotangent.transpose(1, 2, 0, 3)
    flat = lambda a: a.reshape(pixels, a.shape[-1])
    square = lambda a: a.reshape(side, side, imgs, a.shape[-1])

    cut = [0, 3, 12, side]
    gates = None
    if by_hops:
        gates = {1: pair}
        pair = join(pair, swap(pair, p_order[0], n))
        gates[3] = pair
        down = join(down, swap(down, w_order[0], n))
        pair = join(pair, swap(pair, p_order[1], n))
        gates[4] = pair
    small = gather_natural(small_params.astype(BF16), n, bits[1:] + bits[:1], gates).reshape(-1, D).astype(F32)
    if by_hops:
        down = join(down, swap(down, w_order[1], n))
    mixed, *made, token = conv_forward(small, (img, partner, mix_weight), cut[0], cut[1])
    for piece in (1, 2):
        if by_hops:
            pair = join(pair, swap(pair, p_order[piece + 1], n), (token,))
            down = join(down, swap(down, w_order[piece + 1], n), (token,))
        *made, token = conv_forward(small, (mixed,), cut[piece], cut[piece + 1], tuple(made), (pair, down))
    unit1, inv1, norm1 = made
    if by_hops:
        pair = (pair, swap(pair, p_order[4], n))
        down = (down, swap(down, w_order[4], n))
    else:
        pair, down = (lax.all_gather(x[0], "dp", axis=0, tiled=True).reshape(2, FF // 2, 2 * D) for x in (pair, down))
    pair = tuple(x.reshape(FF // 2, 2 * D) for x in pair)
    down = tuple(x.reshape(FF // 2, 2 * D) for x in down)
    act, dg, d_near, d_far, gdb, out, bb, sums2, res = block_both(
        (p_masks, w_masks, d_masks), mine, flat(norm1), flat(mixed), pair, down, dy, small, keep_mask
    )
    shards = (n // 2, deep, 2 * D)
    if by_hops:
        d_keep = d_near.reshape(shards)
        d_come = swap(d_far.reshape(shards), d_order[4], n)
    grads_of = lambda which, after: pair_grad(
        16 * which, p_masks, mine, flat(bb), act, dg, flat(norm1), pair[which], imgs, after
    )
    p_far, far_hb, far_p = grads_of(1, ())
    if by_hops:
        d_keep, d_send = fold(d_keep, d_come, after=(far_hb,))
        d_come = swap(d_send, d_order[3], n)
        p_come = swap(p_far.reshape(shards), p_order[4], n)
    p_near, near_hb, near_p = grads_of(0, (d_send,) if by_hops else (far_hb,))
    p_gate = ()
    if by_hops:
        p_keep, p_send = fold(p_near.reshape(shards), p_come, after=(near_hb,))
        p_come = swap(p_send, p_order[3], n)
        d_keep, d_send = fold(d_keep, d_come, after=(near_hb,))
        d_come = swap(d_send, d_order[2], n)
        p_gate = (p_send, d_send)
    back_conv, sums1 = back_one(p_masks, mine, (near_p, far_p), flat(unit1), flat(inv1), pair, small, imgs, p_gate)
    back_conv = square(back_conv)
    res = square(res)
    back = functools.partial(images_back, back_conv, small, partner, mix_weight, res)
    if by_hops:
        p_keep, p_send = fold(p_keep, p_come, after=(sums1,))
        p_come = swap(p_send, p_order[2], n)
        grad, token = back(0, side, (), (p_send,))
        keep, *send = part(p_keep, p_come, d_keep, d_come, after=(token,))
        come = [swap(x, bits, n) for x, bits in zip(send, (16, 8, 24))]
        gk = taps_grad(back_conv, mixed, (0, 1, 2), tuple(send))
    else:
        grad, _ = back(0, side)
        gk = taps_grad(back_conv, mixed, (0, 1, 2))
        keep = jnp.stack(
            [
                lax.psum_scatter(jnp.concatenate(x).astype(F32), "dp", scatter_dimension=0, tiled=True)
                for x in ((p_near, p_far), (d_near, d_far))
            ]
        )
        come = ()

    grads, total = small_total(n if by_hops else 0, mine, gk, sums1, sums2, near_hb, far_hb, gdb, keep, *come)
    rounds = [bits[k : k + 2] for k in range(1, len(bits), 2)] + [bits[:1]]
    for step, pair_bits in enumerate(rounds):
        others = [pair_bits[0], pair_bits[-1], sum(pair_bits)] if len(pair_bits) == 2 else pair_bits
        arrays = (total,) + tuple(swap(total, other, n) for other in others)
        total = meet(arrays, F32 if step == len(rounds) - 1 else BF16)
    states = (weight_in, first_in, second_in, weight_out, first_out, second_out, weight_down, first_down, second_down)
    *news, norm = adam_all(total, grads, states)
    grad_norm = norm[0, 0]
    factor = CLIP_NORM / jnp.maximum(grad_norm, CLIP_NORM)
    shard_len = small_params.shape[0]
    gs = lax.dynamic_slice_in_dim(total[:SQUARES].reshape(-1), me * shard_len, shard_len)
    position = me * shard_len + jnp.arange(shard_len, dtype=jnp.int32)
    small_rate = jnp.where(position < 54 * D + FF, LAYER_DECAY * RATE_VECTOR, RATE_VECTOR)
    small_decay = jnp.where(position < 49 * D, WEIGHT_DECAY, 0.0)
    new_small = adam(small_params, first_small, second_small, gs * factor, small_rate, small_decay)
    return (
        out.transpose(2, 0, 1, 3),
        grad.transpose(2, 0, 1, 3),
        grad_norm,
        *news,
        *new_small,
    )


def solution(mesh):
    four = P("dp", None, None, None)
    two = P("dp", None)
    one = P("dp")
    return jax.shard_map(
        functools.partial(local, mesh.shape["dp"]),
        mesh=mesh,
        in_specs=(four, one, one, one, four, two, two, two, one) + (two,) * 6 + (one,) * 2,
        out_specs=(four, four, P()) + (two,) * 9 + (one,) * 3,
        check_vma=False,
    )
```
